32 devices in a mesh: dp: 8 (over y, x, core), tensor: 4 (over z).
Axes of the slice: x: 2, y: 2, z: 4, core: 2. Of those that a mesh axis runs over, the one named last changes fastest.
Arguments:
- layer_input_rows: bfloat16 [512, 32, 768], P('tensor', 'dp'), may hold values from -6 to 6
- sentence_index_row: int32 [32, 512], P('dp'), may hold values from 0 to 7, as said below
- padding_mask: int32 [32, 512], P('dp'), may hold values from 0 to 1, as said below
- output_gradient: bfloat16 [512, 32, 768], P('tensor', 'dp'), may hold values from -6 to 6
- owner_rank: int32 [769], replicated, may hold values from 0 to 7, as said below
- master_state: float32 [4, 1536, 2304], P('tensor', 'dp'), may hold values from -1.5 to 1.5
- first_moment: float32 [4, 1536, 2304], P('tensor', 'dp')
- second_moment: float32 [4, 1536, 2304], P('tensor', 'dp'), as said below
Outputs:
- layer_out: float32 [512, 32, 768], P('tensor', 'dp')
- pooled_mean: float32 [32, 8, 768], P('dp', None, 'tensor')
- input_grad: float32 [512, 32, 768], P('tensor', 'dp')
- new_master: float32 [4, 1536, 2304], P('tensor', 'dp')
- new_first: float32 [4, 1536, 2304], P('tensor', 'dp')
- new_second: float32 [4, 1536, 2304], P('tensor', 'dp')
- norm_grads: float32 [6, 768], P(None, 'tensor')
The draws below stay inside these ranges and needn't reach their ends.
Inputs may be any that keep to these rules, and one draw needn't show every extreme that they name: `owner_rank`: each dp index owns at most 192 blocks, and one of them owns exactly 192. `sentence_index_row`: ids never fall along a row; padding positions carry id 8 - 1 = 7. `padding_mask`: in every row the ones come first and cover at least 320 positions. `second_moment`: positive.
All inputs are finite; a program needn't handle non-finite values.
Results may differ from the reference program's by a relative error of at most 0.017.
Values may be sent and summed in bfloat16 or wider, within the bound.
A program may use at most 192 MiB of HBM per device.

```python
import math
import jax
import jax.numpy as jnp
from jax import lax

MODEL_WIDTH = 768
HEADS = 12
HEAD_DIM = 64
FF = 3072
PACKED_ROW_LENGTH = 512
REPLICA_ROWS = 4
SMAX = 8
BLK = 2304
STEP = 10
TOTAL_PACKED_ROWS = 32
NBLK = 769
CAP = 192
N_DP = 8
N_TENSOR = 4


BETA_ONE = 0.9


BETA_TWO = 0.999


def owner_list(key):
    key_heavy, key_slots, key_order = jax.random.split(key, 3)
    heaviest = jax.random.randint(key_heavy, (), 0, N_DP)
    others = jax.random.permutation(key_slots, (N_DP - 1) * CAP)[:NBLK - CAP] // CAP
    others = (others + (others >= heaviest).astype(others.dtype)).astype(jnp.int32)
    owners = jnp.concatenate([jnp.full((CAP,), heaviest, jnp.int32), others])
    return owners[jax.random.permutation(key_order, NBLK)].astype(jnp.int32)


def slot_layout(key):
    owners = owner_list(key)
    ordinal = jnp.arange(NBLK, dtype=jnp.int32)
    same_owner = owners[:, None] == owners[None, :]
    earlier = ordinal[None, :] < ordinal[:, None]
    ranking = jnp.sum((same_owner & earlier).astype(jnp.int32), axis=1)
    slot_of = owners * CAP + ranking
    wanted = jnp.arange(N_DP * CAP, dtype=jnp.int32)
    matches = slot_of[None, :] == wanted[:, None]
    block_of = jnp.sum(jnp.where(matches, ordinal[None, :], 0), axis=1).astype(jnp.int32)
    return block_of


def entry_tables(block_of):
    width_loc = MODEL_WIDTH // N_TENSOR
    ffn_loc = FF // N_TENSOR
    end_up = MODEL_WIDTH * ffn_loc
    end_down = end_up + ffn_loc * MODEL_WIDTH
    end_qkv = end_down + MODEL_WIDTH * 3 * width_loc
    end_out = end_qkv + width_loc * MODEL_WIDTH
    token_position = block_of[:, None] * BLK + jnp.arange(BLK, dtype=jnp.int32)[None, :]
    offset = token_position - end_out
    gain_at = (offset >= 4 * width_loc + ffn_loc) & (offset < 5 * width_loc + ffn_loc) | (offset >= 6 * width_loc + ffn_loc) & (offset < 7 * width_loc + ffn_loc)
    center = jnp.where(gain_at, 1.0, 0.0)
    spread = jnp.where(token_position < end_up, MODEL_WIDTH ** (-0.5), jnp.where(token_position < end_down, FF ** (-0.5), jnp.where(token_position < end_qkv, MODEL_WIDTH ** (-0.5), jnp.where(token_position < end_out, 4.0 * MODEL_WIDTH ** (-0.5), 0.1))))
    leading_tokens = math.sqrt(N_DP * REPLICA_ROWS * PACKED_ROW_LENGTH)
    grad_scale = leading_tokens * jnp.where(token_position < end_up, 0.1, jnp.where(token_position < end_down, 0.2, jnp.where(token_position < end_qkv, 0.05, jnp.where(token_position < end_out, 0.1, 0.5))))
    return (center[None], spread[None], grad_scale[None])


def row_layout(key):
    key_length_total, key_cut, key_pick = jax.random.split(key, 3)
    row_index = jnp.arange(TOTAL_PACKED_ROWS, dtype=jnp.int32)
    real_token_length = jax.random.randint(key_length_total, (TOTAL_PACKED_ROWS,), 5 * PACKED_ROW_LENGTH // 8, PACKED_ROW_LENGTH + 1)
    longest_length = jax.random.randint(jax.random.fold_in(key_length_total, 1), (TOTAL_PACKED_ROWS,), 7 * PACKED_ROW_LENGTH // 8, PACKED_ROW_LENGTH + 1)
    chosen = jax.random.randint(key_pick, (N_DP,), 0, REPLICA_ROWS)
    long_row = row_index % REPLICA_ROWS == chosen[row_index // REPLICA_ROWS]
    real_token_length = jnp.where(long_row, longest_length, real_token_length)
    cut_points = jax.random.randint(key_cut, (TOTAL_PACKED_ROWS, SMAX - 1), 1, real_token_length[:, None])
    cut_points = jnp.where(long_row[:, None], real_token_length[:, None], cut_points)
    token_position = jnp.arange(PACKED_ROW_LENGTH, dtype=jnp.int32)
    sentence_labels = jnp.sum((token_position[None, :, None] >= cut_points[:, None, :]).astype(jnp.int32), axis=-1)
    real_token_flags = (token_position[None, :] < real_token_length[:, None]).astype(jnp.int32)
    return (sentence_labels.astype(jnp.int32), real_token_flags)


def draw_sentence_index_row(key, part):
    sentence_labels, real_token_flags = row_layout(key)
    return sentence_labels


def draw_padding_mask(key, part):
    sentence_labels, real_token_flags = row_layout(key)
    return real_token_flags


def draw_owner_rank(key, part):
    return owner_list(key)


def draw_master_state(key, part):
    block_of = slot_layout(key)
    key = jax.random.fold_in(key, 11)
    center, spread, grad_scale = entry_tables(block_of)
    shape = (N_TENSOR, N_DP * CAP, BLK)
    normal_draw = jax.random.truncated_normal(key, -3.0, 3.0, shape, jnp.float32)
    return (center + spread * normal_draw).astype(jnp.float32)


def draw_first_moment(key, part):
    block_of = slot_layout(key)
    key = jax.random.fold_in(key, 12)
    center, spread, grad_scale = entry_tables(block_of)
    shape = (N_TENSOR, N_DP * CAP, BLK)
    normal_draw = jax.random.truncated_normal(key, -3.0, 3.0, shape, jnp.float32)
    return ((1.0 - BETA_ONE) / BETA_ONE * grad_scale * normal_draw).astype(jnp.float32)


def draw_second_moment(key, part):
    block_of = slot_layout(key)
    key = jax.random.fold_in(key, 13)
    center, spread, grad_scale = entry_tables(block_of)
    shape = (N_TENSOR, N_DP * CAP, BLK)
    factor = jnp.exp(jax.random.uniform(key, shape, jnp.float32, math.log(0.5), math.log(2.0)))
    return (2.0 * (1.0 - BETA_TWO) / BETA_TWO * grad_scale * grad_scale * factor).astype(jnp.float32)


def shard_levels(own_key, dims, cuts, low, largest):
    factor_of, own = 1.0, jax.random.fold_in(own_key, 6)
    for dim, blocks in cuts:
        steps = jnp.exp(jax.random.uniform(jax.random.fold_in(own, dim), (blocks,), jnp.float32, low / len(cuts), largest / len(cuts)))
        factor_of = factor_of * jnp.repeat(steps, dims[dim] // blocks).reshape([-1 if axis == dim else 1 for axis in range(len(dims))])
    return factor_of


def normal_values(key, dims, scale, bound, cuts=(), kind=jnp.bfloat16):
    array = scale * jax.random.normal(key, dims, jnp.float32)
    if cuts:
        array = array * shard_levels(key, dims, cuts, -0.22, 0.18)
    return jnp.clip(array, -bound, bound).astype(kind)


def setup_inputs(seed: int = 0) -> dict:
    splits = jax.random.split(jax.random.key(seed), 9)
    layer_input_rows = normal_values(splits[0], (PACKED_ROW_LENGTH, TOTAL_PACKED_ROWS, MODEL_WIDTH), 1.0, 6.0, ((0, 4), (1, 8)))
    sentence_index_row = draw_sentence_index_row(jax.random.fold_in(splits[8], 71), 0)
    padding_mask = draw_padding_mask(jax.random.fold_in(splits[8], 71), 0)
    output_gradient = normal_values(splits[3], (PACKED_ROW_LENGTH, TOTAL_PACKED_ROWS, MODEL_WIDTH), 1.0, 6.0, ((0, 4), (1, 8)))
    owner_rank = draw_owner_rank(jax.random.fold_in(splits[8], 71), 0)
    master_state = draw_master_state(jax.random.fold_in(splits[8], 71), 0)
    first_moment = draw_first_moment(jax.random.fold_in(splits[8], 71), 0)
    second_moment = draw_second_moment(jax.random.fold_in(splits[8], 71), 0)
    return {"layer_input_rows": layer_input_rows, "sentence_index_row": sentence_index_row, "padding_mask": padding_mask, "output_gradient": output_gradient, "owner_rank": owner_rank, "master_state": master_state, "first_moment": first_moment, "second_moment": second_moment}


NORM_EPS = 1e-05
ADAM_EPS = 1e-08
BETA_ONE = 0.9
BETA_TWO = 0.999
DECAY_RATE = 0.01
MASKED = -1e+30
exact_precision = lax.Precision.HIGHEST

@jax.custom_vjp
def low(v):
    return lax.optimization_barrier(v.astype(jnp.bfloat16)).astype(jnp.float32)

@jax.custom_vjp
def low_back(v):
    return v

def low_keep(v):
    return (low(v), None)

def low_pass(kept, grad):
    return (grad,)

def back_keep(v):
    return (v, None)

def back_low(kept, grad):
    return (low(grad),)
low.defvjp(low_keep, low_pass)
low_back.defvjp(back_keep, back_low)

def slot_tables(owner_rank, per_owner):
    ordinal = jnp.arange(owner_rank.shape[0], dtype=jnp.int32)
    same_owner = owner_rank[:, None] == owner_rank[None, :]
    earlier = ordinal[None, :] < ordinal[:, None]
    ranking = lax.optimization_barrier(jnp.sum((same_owner & earlier).astype(jnp.int32), axis=1))
    return (owner_rank * per_owner + ranking).astype(jnp.int32)

def slot_blocks(slot_of, wanted):
    matches = slot_of[None, :] == wanted[:, None]
    filled = jnp.any(matches, axis=1)
    ordinal = jnp.arange(slot_of.shape[0], dtype=jnp.int32)
    block_of = lax.optimization_barrier(jnp.sum(jnp.where(matches, ordinal[None, :], 0), axis=1)).astype(jnp.int32)
    return (block_of, filled)

def step_rates(token_position, width, hidden, tensor_size):
    width_loc = width // tensor_size
    ffn_loc = hidden // tensor_size
    end_up = width * ffn_loc
    end_down = end_up + ffn_loc * width
    end_qkv = end_down + width * 3 * width_loc
    end_out = end_qkv + width_loc * width
    offset = token_position - end_out
    first_gain = (offset >= 4 * width_loc + ffn_loc) & (offset < 5 * width_loc + ffn_loc)
    second_gain = (offset >= 6 * width_loc + ffn_loc) & (offset < 7 * width_loc + ffn_loc)
    small_rate = jnp.where(first_gain | second_gain, 0.2, 0.1)
    step_rate = jnp.where(token_position < end_up, width ** (-0.5), jnp.where(token_position < end_down, hidden ** (-0.5), jnp.where(token_position < end_qkv, width ** (-0.5), jnp.where(token_position < end_out, 4.0 * width ** (-0.5), small_rate))))
    decay_on = (token_position < end_out).astype(jnp.float32)
    return (step_rate.astype(jnp.float32), decay_on)

def adamw(gradient, moment, square, weight, step_rate, decay_on, filled):
    new_moment = BETA_ONE * moment + (1.0 - BETA_ONE) * gradient
    new_square = BETA_TWO * square + (1.0 - BETA_TWO) * gradient * gradient
    unbiased = new_moment / (1.0 - BETA_ONE ** STEP)
    divisor = jnp.sqrt(new_square / (1.0 - BETA_TWO ** STEP)) + ADAM_EPS
    new_weight = weight - step_rate * (unbiased / divisor + DECAY_RATE * decay_on * weight)
    zeroed = jnp.zeros_like(weight)
    return (jnp.where(filled, new_weight, zeroed), jnp.where(filled, new_moment, zeroed), jnp.where(filled, new_square, zeroed))

def normalize(values):
    centred = values - lax.optimization_barrier(jnp.mean(values, axis=-1, keepdims=True))
    inv_dev = lax.rsqrt(lax.optimization_barrier(jnp.mean(centred * centred, axis=-1, keepdims=True)) + NORM_EPS)
    return (centred * inv_dev, inv_dev)

def allowed_pairs(sentence_labels, real_token_flags):
    row_len = sentence_labels.shape[-1]
    same_sent = sentence_labels[:, :, None] == sentence_labels[:, None, :]
    live = (real_token_flags[:, :, None] == 1) & (real_token_flags[:, None, :] == 1)
    diagonal = jnp.eye(row_len, dtype=bool)[None]
    return same_sent & live | diagonal

def unpack_all(flat_all):
    tensor_size = flat_all.shape[0]
    width_loc = MODEL_WIDTH // tensor_size
    ffn_loc = FF // tensor_size
    end_up = MODEL_WIDTH * ffn_loc
    end_down = end_up + ffn_loc * MODEL_WIDTH
    end_qkv = end_down + MODEL_WIDTH * 3 * width_loc
    end_out = end_qkv + width_loc * MODEL_WIDTH
    up_weight = flat_all[:, :end_up].reshape(tensor_size, MODEL_WIDTH, ffn_loc).transpose(1, 0, 2).reshape(MODEL_WIDTH, FF)
    down_weight = flat_all[:, end_up:end_down].reshape(FF, MODEL_WIDTH)
    w_qkv = flat_all[:, end_down:end_qkv].reshape(tensor_size, MODEL_WIDTH, 3, width_loc).transpose(1, 2, 0, 3).reshape(MODEL_WIDTH, 3, MODEL_WIDTH)
    w_out = flat_all[:, end_qkv:end_out].reshape(MODEL_WIDTH, MODEL_WIDTH)
    small_part = flat_all[:, end_out:]
    bias_q = small_part[:, :width_loc].reshape(MODEL_WIDTH)
    bias_v = small_part[:, width_loc:2 * width_loc].reshape(MODEL_WIDTH)
    expand_bias = small_part[:, 2 * width_loc:2 * width_loc + ffn_loc].reshape(FF)
    norm_all = small_part[:, 2 * width_loc + ffn_loc:].reshape(tensor_size, 6, width_loc).transpose(1, 0, 2).reshape(6, MODEL_WIDTH)
    return (up_weight, down_weight, w_qkv, w_out, bias_q, bias_v, expand_bias, norm_all)

def forward(flat_all, token_rows, sentence_labels, real_token_flags):
    up_weight, down_weight, w_qkv, w_out, bias_q, bias_v, expand_bias, norm_all = unpack_all(low(flat_all))
    sentence_group_width, row_len = sentence_labels.shape
    qkv_lin = low_back(jnp.einsum('gld,dce->glce', token_rows, w_qkv, precision=exact_precision))
    bias_qkv = jnp.stack([bias_q, jnp.zeros_like(bias_q), bias_v])
    qkv = low(qkv_lin + bias_qkv)
    queries = qkv[:, :, 0].reshape(sentence_group_width, row_len, HEADS, HEAD_DIM)
    key_rows = qkv[:, :, 1].reshape(sentence_group_width, row_len, HEADS, HEAD_DIM)
    values = qkv[:, :, 2].reshape(sentence_group_width, row_len, HEADS, HEAD_DIM)
    scaling = HEAD_DIM ** (-0.5)
    allowed = allowed_pairs(sentence_labels, real_token_flags)
    scores = low_back(scaling * jnp.einsum('gqhe,gkhe->ghqk', queries, key_rows, precision=exact_precision))
    scores = jnp.where(allowed[:, None], scores, MASKED)
    attn_prob = jax.nn.softmax(scores, axis=-1)
    attended = low(low_back(jnp.einsum('ghqk,gkhe->gqhe', low(attn_prob), values, precision=exact_precision)))
    attended = attended.reshape(sentence_group_width, row_len, MODEL_WIDTH)
    z_one = token_rows + low_back(jnp.einsum('gld,de->gle', attended, w_out, precision=exact_precision)) + norm_all[0]
    h_one = normalize(z_one)[0] * norm_all[2] + norm_all[3]
    h_low = low(h_one)
    up_pre = low_back(jnp.einsum('gld,df->glf', h_low, up_weight, precision=exact_precision)) + expand_bias
    activation_narrow = low(jax.nn.gelu(up_pre, approximate=False))
    z_two = h_one + low_back(jnp.einsum('glf,fd->gld', activation_narrow, down_weight, precision=exact_precision)) + norm_all[1]
    return normalize(z_two)[0] * norm_all[4] + norm_all[5]

def reference(layer_input_rows, sentence_index_row, padding_mask, output_gradient, owner_rank, master_state, first_moment, second_moment):
    tensor_size = master_state.shape[0]
    slot_of = slot_tables(owner_rank, CAP)
    flat_all = master_state[:, slot_of, :].reshape(tensor_size, NBLK * BLK)
    sentence_group_width = math.gcd(TOTAL_PACKED_ROWS, 8)
    sentence_group_count = TOTAL_PACKED_ROWS // sentence_group_width
    token_rows = layer_input_rows.astype(jnp.float32).transpose(1, 0, 2).reshape(sentence_group_count, sentence_group_width, PACKED_ROW_LENGTH, MODEL_WIDTH)
    live = padding_mask.astype(jnp.float32)
    output_adjoint = output_gradient.astype(jnp.float32).transpose(1, 0, 2) * live[:, :, None]
    output_adjoint = output_adjoint.reshape(sentence_group_count, sentence_group_width, PACKED_ROW_LENGTH, MODEL_WIDTH)
    sentence_labels = sentence_index_row.reshape(sentence_group_count, sentence_group_width, PACKED_ROW_LENGTH)
    real_token_flags = padding_mask.reshape(sentence_group_count, sentence_group_width, PACKED_ROW_LENGTH)

    def one_group(totals, inputs):
        tokens_g, segments_g, valid_g, cotangent_g = inputs
        outputs, pullback = jax.vjp(lambda flat_arg, token_arg: forward(flat_arg, token_arg, segments_g, valid_g), flat_all, tokens_g)
        grad_flat, grad_tokens = pullback(cotangent_g)
        return (totals + grad_flat, (outputs, grad_tokens))
    totals, (layer_everything, gradient_everything) = lax.scan(one_group, jnp.zeros_like(flat_all), (token_rows, sentence_labels, real_token_flags, output_adjoint))
    layer_row_list = layer_everything.reshape(TOTAL_PACKED_ROWS, PACKED_ROW_LENGTH, MODEL_WIDTH)
    gradient_row_list = gradient_everything.reshape(TOTAL_PACKED_ROWS, PACKED_ROW_LENGTH, MODEL_WIDTH)
    sentence_indicator = ((sentence_index_row[:, :, None] == jnp.arange(SMAX, dtype=jnp.int32)[None, None, :]) & (padding_mask[:, :, None] == 1)).astype(jnp.float32)
    sentence_sums = jnp.einsum('kpr,kpv->krv', sentence_indicator, layer_row_list, precision=exact_precision)
    counts = lax.optimization_barrier(jnp.sum(sentence_indicator, axis=1))
    pooled_mean = sentence_sums / jnp.maximum(counts, 1.0)[:, :, None]
    width_loc = MODEL_WIDTH // tensor_size
    ffn_loc = FF // tensor_size
    shared_start = 2 * MODEL_WIDTH * ffn_loc + 4 * MODEL_WIDTH * width_loc + 2 * width_loc + ffn_loc
    norm_grads = totals[:, shared_start:shared_start + 6 * width_loc].reshape(tensor_size, 6, width_loc)
    norm_grads = norm_grads.transpose(1, 0, 2).reshape(6, MODEL_WIDTH)
    wanted = jnp.arange(N_DP * CAP, dtype=jnp.int32)
    block_of, filled = slot_blocks(slot_of, wanted)
    gradient = totals.reshape(tensor_size, NBLK, BLK)[:, block_of, :]
    token_position = block_of[:, None] * BLK + jnp.arange(BLK, dtype=jnp.int32)[None, :]
    step_rate, decay_on = step_rates(token_position, MODEL_WIDTH, FF, tensor_size)
    new_master, new_first, new_second = adamw(gradient, first_moment, second_moment, master_state, step_rate[None], decay_on[None], filled[None, :, None])
    return (layer_row_list.transpose(1, 0, 2), pooled_mean, gradient_row_list.transpose(1, 0, 2), new_master, new_first, new_second, norm_grads)
```

```python
import jax
import functools
import jax.numpy as jnp
from jax import lax
from jax.experimental import pallas as pl
from jax.experimental.pallas import tpu as pltpu
from jax.sharding import PartitionSpec as P

MODEL_WIDTH = 768
HEAD_DIM = 64
FF = 3072
SMAX = 8
STEP = 10


NORM_EPS = 1e-05
ADAM_EPS = 1e-08
BETA_ONE = 0.9
BETA_TWO = 0.999
DECAY_RATE = 0.01
MASKED = -1e30
exact_precision = lax.Precision.HIGHEST


def slot_tables(owner_rank, per_owner):
    ordinal = jnp.arange(owner_rank.shape[0], dtype=jnp.int32)
    same_owner = owner_rank[:, None] == owner_rank[None, :]
    earlier = ordinal[None, :] < ordinal[:, None]
    ranking = jnp.sum((same_owner & earlier).astype(jnp.int32), axis=1)
    return owner_rank * per_owner + ranking


def slot_blocks(slot_of, wanted):
    matches = slot_of[None, :] == wanted[:, None]
    filled = jnp.any(matches, axis=1)
    ordinal = jnp.arange(slot_of.shape[0], dtype=jnp.int32)
    block_of = jnp.sum(jnp.where(matches, ordinal[None, :], 0), axis=1)
    return (block_of, filled)


def step_rates(token_position, width, hidden, tensor_size):
    width_loc = width // tensor_size
    ffn_loc = hidden // tensor_size
    end_up = width * ffn_loc
    end_down = end_up + ffn_loc * width
    end_qkv = end_down + width * 3 * width_loc
    end_out = end_qkv + width_loc * width
    offset = token_position - end_out
    first_gain = (offset >= 4 * width_loc + ffn_loc) & (offset < 5 * width_loc + ffn_loc)
    second_gain = (offset >= 6 * width_loc + ffn_loc) & (offset < 7 * width_loc + ffn_loc)
    small_rate = jnp.where(first_gain | second_gain, 0.2, 0.1)
    step_rate = jnp.where(
        token_position < end_up,
        width ** (-0.5),
        jnp.where(
            token_position < end_down,
            hidden ** (-0.5),
            jnp.where(
                token_position < end_qkv,
                width ** (-0.5),
                jnp.where(token_position < end_out, 4.0 * width ** (-0.5), small_rate),
            ),
        ),
    )
    decay_on = (token_position < end_out).astype(jnp.float32)
    return (step_rate.astype(jnp.float32), decay_on)


def adamw(gradient, moment, square, weight, step_rate, decay_on, filled):
    new_moment = BETA_ONE * moment + (1.0 - BETA_ONE) * gradient
    new_square = BETA_TWO * square + (1.0 - BETA_TWO) * gradient * gradient
    unbiased = new_moment / (1.0 - BETA_ONE**STEP)
    divisor = jnp.sqrt(new_square / (1.0 - BETA_TWO**STEP)) + ADAM_EPS
    new_weight = weight - step_rate * (unbiased / divisor + DECAY_RATE * decay_on * weight)
    zeroed = jnp.zeros_like(weight)
    return (
        jnp.where(filled, new_weight, zeroed),
        jnp.where(filled, new_moment, zeroed),
        jnp.where(filled, new_square, zeroed),
    )


def normalize(values):
    centred = values - jnp.mean(values, axis=-1, keepdims=True)
    inv_dev = lax.rsqrt(jnp.mean(centred * centred, axis=-1, keepdims=True) + NORM_EPS)
    return (centred * inv_dev, inv_dev)


def norm_back(grad_scaled, normed, inv_dev):
    first_mean = jnp.mean(grad_scaled, axis=-1, keepdims=True)
    second_mean = jnp.mean(grad_scaled * normed, axis=-1, keepdims=True)
    return inv_dev * (grad_scaled - first_mean - normed * second_mean)


def allowed_pairs(sentence_labels, real_token_flags):
    row_len = sentence_labels.shape[-1]
    same_sent = sentence_labels[:, :, None] == sentence_labels[:, None, :]
    live = (real_token_flags[:, :, None] == 1) & (real_token_flags[:, None, :] == 1)
    diagonal = jnp.eye(row_len, dtype=bool)[None]
    return same_sent & live | diagonal


def masked_scores(queries, key_rows, allowed, scaling):
    scores = (
        jnp.einsum("qshe,kshe->shqk", queries, key_rows, preferred_element_type=jnp.float32)
        * scaling
    )
    return jnp.where(allowed[:, None], scores, MASKED)


def split_flat(flat_all, width_loc, ffn_loc):
    end_up = MODEL_WIDTH * ffn_loc
    end_down = end_up + ffn_loc * MODEL_WIDTH
    end_qkv = end_down + MODEL_WIDTH * 3 * width_loc
    end_out = end_qkv + width_loc * MODEL_WIDTH
    return (
        flat_all[:end_up].reshape(MODEL_WIDTH, ffn_loc),
        flat_all[end_up:end_down].reshape(ffn_loc, MODEL_WIDTH),
        flat_all[end_down:end_qkv].reshape(MODEL_WIDTH, 3 * width_loc),
        flat_all[end_qkv:end_out].reshape(width_loc, MODEL_WIDTH),
        flat_all[end_out:],
    )


def local_general(
    layer_input_rows,
    sentence_index_row,
    padding_mask,
    output_gradient,
    owner_rank,
    master_state,
    first_moment,
    second_moment,
):
    tensor_size = lax.axis_size("tensor")
    tensor_at = lax.axis_index("tensor")
    data_size = lax.axis_size("dp")
    data_at = lax.axis_index("dp")
    width_loc = MODEL_WIDTH // tensor_size
    ffn_loc = FF // tensor_size
    heads_loc = width_loc // HEAD_DIM
    quarter = layer_input_rows.shape[0]
    seq_count = layer_input_rows.shape[1]
    row_len = quarter * tensor_size
    per_owner = master_state.shape[1]
    block_len = master_state.shape[2]
    nblocks = owner_rank.shape[0]
    slot_of = slot_tables(owner_rank, per_owner)
    gathered = lax.all_gather(master_state.astype(jnp.bfloat16), "dp", axis=1, tiled=True)[0]
    flat_weights = gathered[slot_of].reshape(nblocks * block_len)
    up_weight, down_weight, w_qkv, w_out, small_part = split_flat(flat_weights, width_loc, ffn_loc)
    bias_q = small_part[:width_loc].astype(jnp.float32)
    bias_v = small_part[width_loc : 2 * width_loc].astype(jnp.float32)
    expand_bias = small_part[2 * width_loc : 2 * width_loc + ffn_loc].astype(jnp.float32)
    norm_parts = small_part[2 * width_loc + ffn_loc :].reshape(6, width_loc)
    full_rows, norm_whole = (
        lax.all_gather(layer_input_rows, "tensor", axis=0, tiled=True),
        lax.all_gather(norm_parts, "tensor", axis=1, tiled=True),
    )
    norm_all = norm_whole.astype(jnp.float32)
    bias_out, bias_down = (norm_all[0], norm_all[1])
    gain_one, shift_one, gain_two, shift_two = (norm_all[2], norm_all[3], norm_all[4], norm_all[5])
    qkv_lin = jnp.einsum("lsd,de->lse", full_rows, w_qkv, preferred_element_type=jnp.float32)
    bias_qkv = jnp.concatenate([bias_q, jnp.zeros((width_loc,), jnp.float32), bias_v])
    qkv = (qkv_lin + bias_qkv).astype(jnp.bfloat16)
    queries = qkv[:, :, :width_loc].reshape(row_len, seq_count, heads_loc, HEAD_DIM)
    key_rows = qkv[:, :, width_loc : 2 * width_loc].reshape(row_len, seq_count, heads_loc, HEAD_DIM)
    values = qkv[:, :, 2 * width_loc :].reshape(row_len, seq_count, heads_loc, HEAD_DIM)
    scaling = HEAD_DIM ** (-0.5)
    allowed = allowed_pairs(sentence_index_row, padding_mask)
    scores = masked_scores(queries, key_rows, allowed, scaling)
    row_peak = jnp.max(scores, axis=-1, keepdims=True)
    log_total = row_peak + jnp.log(jnp.sum(jnp.exp(scores - row_peak), axis=-1, keepdims=True))
    prob_low = jnp.exp(scores - log_total).astype(jnp.bfloat16)
    attended = jnp.einsum("shqk,kshe->qshe", prob_low, values, preferred_element_type=jnp.float32)
    attended = attended.astype(jnp.bfloat16).reshape(row_len, seq_count, width_loc)
    portion_rows = attended
    attn_rows = lax.psum_scatter(
        jnp.einsum("lse,ed->lsd", portion_rows, w_out, preferred_element_type=jnp.float32).astype(
            jnp.bfloat16
        ),
        "tensor",
        scatter_dimension=0,
        tiled=True,
    ).astype(jnp.float32)
    z_one = layer_input_rows.astype(jnp.float32) + attn_rows + bias_out
    normed_one, inv_one = normalize(z_one)
    h_mine = normed_one * gain_one + shift_one
    hidden_narrow_whole = lax.all_gather(h_mine.astype(jnp.bfloat16), "tensor", axis=0, tiled=True)
    up_pre = (
        jnp.einsum(
            "wer,rb->web", hidden_narrow_whole, up_weight, preferred_element_type=jnp.float32
        )
        + expand_bias
    )
    activation_narrow = jax.nn.gelu(up_pre, approximate=False).astype(jnp.bfloat16)
    portion_rows = activation_narrow
    down_rows = lax.psum_scatter(
        jnp.einsum(
            "aij,jb->aib", portion_rows, down_weight, preferred_element_type=jnp.float32
        ).astype(jnp.bfloat16),
        "tensor",
        scatter_dimension=0,
        tiled=True,
    ).astype(jnp.float32)
    z_two = h_mine + down_rows + bias_down
    normed_two, inv_two = normalize(z_two)
    layer_out = normed_two * gain_two + shift_two
    seg_mine = lax.dynamic_slice_in_dim(sentence_index_row, tensor_at * quarter, quarter, 1)
    valid_mine = lax.dynamic_slice_in_dim(padding_mask, tensor_at * quarter, quarter, 1)
    sent_ids = jnp.arange(SMAX, dtype=jnp.int32)
    onehot_mine = (
        (seg_mine[:, :, None] == sent_ids[None, None, :]) & (valid_mine[:, :, None] == 1)
    ).astype(jnp.float32)
    pool_part = jnp.einsum("slc,lsd->scd", onehot_mine, layer_out, precision=exact_precision)
    onehot_full = (
        (sentence_index_row[:, :, None] == sent_ids[None, None, :])
        & (padding_mask[:, :, None] == 1)
    ).astype(jnp.float32)
    counts = jnp.sum(onehot_full, axis=1)
    grad_out = output_gradient.astype(jnp.float32) * valid_mine.T[:, :, None].astype(jnp.float32)
    d_gain_two = jnp.sum(grad_out * normed_two, axis=(0, 1))
    d_shift_two = jnp.sum(grad_out, axis=(0, 1))
    dz_two = norm_back(grad_out * gain_two, normed_two, inv_two)
    d_bias_down = jnp.sum(dz_two, axis=(0, 1))
    second_sum_gradient_wide = lax.all_gather(
        dz_two.astype(jnp.bfloat16), "tensor", axis=0, tiled=True
    )
    down_weight_gradient = jnp.einsum(
        "ipo,ipr->or",
        activation_narrow,
        second_sum_gradient_wide,
        preferred_element_type=jnp.float32,
    )
    activation_gradient = jnp.einsum(
        "ugp,jp->ugj", second_sum_gradient_wide, down_weight, preferred_element_type=jnp.float32
    )
    gelu_pull = jax.vjp(lambda pre_act: jax.nn.gelu(pre_act, approximate=False), up_pre)[1]
    d_up = gelu_pull(activation_gradient)[0]
    d_bias_up = jnp.sum(d_up, axis=(0, 1))
    expand_gradient_narrow = d_up.astype(jnp.bfloat16)
    up_weight_gradient = jnp.einsum(
        "iux,iuy->xy",
        hidden_narrow_whole,
        expand_gradient_narrow,
        preferred_element_type=jnp.float32,
    )
    portion_rows = expand_gradient_narrow
    dh_rows = lax.psum_scatter(
        jnp.einsum(
            "uih,vh->uiv", portion_rows, up_weight, preferred_element_type=jnp.float32
        ).astype(jnp.bfloat16),
        "tensor",
        scatter_dimension=0,
        tiled=True,
    ).astype(jnp.float32)
    dh_mine = dz_two + dh_rows
    d_gain_one = jnp.sum(dh_mine * normed_one, axis=(0, 1))
    d_shift_one = jnp.sum(dh_mine, axis=(0, 1))
    dz_one = norm_back(dh_mine * gain_one, normed_one, inv_one)
    d_bias_out = jnp.sum(dz_one, axis=(0, 1))
    dz_one_full = lax.all_gather(dz_one.astype(jnp.bfloat16), "tensor", axis=0, tiled=True)
    d_w_out = jnp.einsum("lse,lsd->ed", attended, dz_one_full, preferred_element_type=jnp.float32)
    d_attended = jnp.einsum("lsd,ed->lse", dz_one_full, w_out, preferred_element_type=jnp.float32)
    d_attended = d_attended.astype(jnp.bfloat16).reshape(row_len, seq_count, heads_loc, HEAD_DIM)
    scores_again = masked_scores(queries, key_rows, allowed, scaling)
    attn_prob = jnp.exp(scores_again - log_total)
    prob_again = attn_prob.astype(jnp.bfloat16)
    d_prob = jnp.einsum("qshe,kshe->shqk", d_attended, values, preferred_element_type=jnp.float32)
    d_values = jnp.einsum(
        "shqk,qshe->kshe", prob_again, d_attended, preferred_element_type=jnp.float32
    )
    inner = jnp.sum(d_prob * attn_prob, axis=-1, keepdims=True)
    d_scores = (attn_prob * (d_prob - inner)).astype(jnp.bfloat16)
    d_queries = (
        jnp.einsum("shqk,kshe->qshe", d_scores, key_rows, preferred_element_type=jnp.float32)
        * scaling
    )
    d_keys = (
        jnp.einsum("shqk,qshe->kshe", d_scores, queries, preferred_element_type=jnp.float32)
        * scaling
    )
    d_bias_q = jnp.sum(d_queries, axis=(0, 1)).reshape(width_loc)
    d_bias_v = jnp.sum(d_values, axis=(0, 1)).reshape(width_loc)
    d_qkv_low = jnp.concatenate(
        [
            d_queries.reshape(row_len, seq_count, width_loc),
            d_keys.reshape(row_len, seq_count, width_loc),
            d_values.reshape(row_len, seq_count, width_loc),
        ],
        axis=2,
    ).astype(jnp.bfloat16)
    d_w_qkv = jnp.einsum("lsd,lse->de", full_rows, d_qkv_low, preferred_element_type=jnp.float32)
    portion_rows = d_qkv_low
    dx_rows = lax.psum_scatter(
        jnp.einsum("lse,de->lsd", portion_rows, w_qkv, preferred_element_type=jnp.float32).astype(
            jnp.bfloat16
        ),
        "tensor",
        scatter_dimension=0,
        tiled=True,
    ).astype(jnp.float32)
    input_grad = dz_one + dx_rows
    shared_grads = jnp.stack(
        [d_bias_out, d_bias_down, d_gain_one, d_shift_one, d_gain_two, d_shift_two]
    )[None]
    pool_sum, shared_sum = (
        lax.psum_scatter(
            pool_part.astype(jnp.bfloat16), "tensor", scatter_dimension=2, tiled=True
        ).astype(jnp.float32),
        lax.psum_scatter(
            shared_grads.astype(jnp.bfloat16), "tensor", scatter_dimension=2, tiled=True
        ).astype(jnp.float32),
    )
    pooled_mean = pool_sum / jnp.maximum(counts, 1.0)[:, :, None]
    flat_grads = jnp.concatenate(
        [
            up_weight_gradient.reshape(-1),
            down_weight_gradient.reshape(-1),
            d_w_qkv.reshape(-1),
            d_w_out.reshape(-1),
            d_bias_q,
            d_bias_v,
            d_bias_up,
            shared_sum.reshape(-1),
        ]
    )
    grad_blocks = flat_grads.reshape(nblocks, block_len)
    wanted = data_at * per_owner + jnp.arange(per_owner, dtype=jnp.int32)
    block_of, filled = slot_blocks(slot_of, wanted)
    slot_grads = (
        jnp.zeros((data_size * per_owner, block_len), jnp.float32).at[slot_of].set(grad_blocks)
    )
    owned_grads = lax.psum_scatter(slot_grads, "dp", scatter_dimension=0, tiled=True)
    norm_grads = lax.psum(shared_sum[0], "dp")
    token_position = block_of[:, None] * block_len + jnp.arange(block_len, dtype=jnp.int32)[None, :]
    step_rate, decay_on = step_rates(token_position, MODEL_WIDTH, FF, tensor_size)
    new_master, new_first, new_second = adamw(
        owned_grads,
        first_moment[0],
        second_moment[0],
        master_state[0],
        step_rate,
        decay_on,
        filled[:, None],
    )
    return (
        layer_out,
        pooled_mean,
        input_grad,
        new_master[None],
        new_first[None],
        new_second[None],
        norm_grads,
    )


MESH = pl.DeviceIdType.MESH
BF = jnp.bfloat16
F32 = jnp.float32
WEIGHTS = ((576, 96), (768, 32), (768, 96), (768, 96))
MIB = 2**20


class Place:
    def __init__(self):
        d = lax.axis_index("dp")
        self.t = lax.axis_index("tensor")
        self.c = d % 2
        self.x = (d // 2) % 2
        self.y = d // 4
        self.xy = d // 2
        self.core = (d + 1 - 2 * self.c, self.t)
        self.right = (d + 2 - 4 * self.x, self.t)
        self.down = (d + 4 - 8 * self.y, self.t)
        self.diag = (d + 6 - 4 * self.x - 8 * self.y, self.t)
        self.deep = [None] + [(d, (self.t + k) % 4) for k in (1, 2, 3)]
        self.ahead = [(self.t + k) % 4 for k in range(4)]
        self.behind = [(self.t + 4 - k) % 4 for k in range(4)]

    def greet(self):
        barrier = pltpu.get_barrier_semaphore()
        peers = [self.core, self.right, self.down, self.diag] + self.deep[1:]
        for peer in peers:
            pl.semaphore_signal(barrier, inc=1, device_id=peer, device_id_type=MESH)
        pl.semaphore_wait(barrier, len(peers))


class Sender:
    def __init__(self, send_sems, recv_sems, local_sems):
        self.sems = (send_sems, recv_sems, local_sems)
        self.used = 0
        self.used_local = 0
        self.open = []

    def send(self, src, dst, peer):
        i = self.used
        self.used += 1
        copy = pltpu.make_async_remote_copy(
            src_ref=src,
            dst_ref=dst,
            send_sem=self.sems[0].at[i],
            recv_sem=self.sems[1].at[i],
            device_id=peer,
            device_id_type=MESH,
        )
        copy.start()
        self.open.append(copy)
        return copy

    def copy(self, src, dst):
        i = self.used_local
        self.used_local += 1
        copy = pltpu.make_async_copy(src, dst, self.sems[2].at[i])
        copy.start()
        return copy

    def finish(self):
        for copy in self.open:
            copy.wait_send()


def rows_of(place, rows, at=None):
    at = place.xy if at is None else at
    return pl.ds(pl.multiple_of(place.c * (4 * rows) + at * rows, 32), rows)


def half_of(place, rows):
    return pl.ds(pl.multiple_of(place.c * (4 * rows), 128), 4 * rows)


def interleave(size, parts):
    group = size // parts
    out_row = lax.broadcasted_iota(jnp.int32, (size, size), 0)
    col = lax.broadcasted_iota(jnp.int32, (size, size), 1)
    part = jnp.zeros((size, size), jnp.int32)
    for k in range(1, parts):
        part = part + (col >= k * group).astype(jnp.int32)
    return jnp.where(out_row == parts * (col - group * part) + part, 1.0, 0.0).astype(BF)


def interleave_out():
    out_row = lax.broadcasted_iota(jnp.int32, (32, 32), 0)
    col = lax.broadcasted_iota(jnp.int32, (32, 32), 1)
    part = (col >= 8).astype(jnp.int32) + (col >= 16).astype(jnp.int32)
    keep = (out_row == 3 * (col - 8 * part) + part) & (col < 24)
    return jnp.where(keep, 1.0, 0.0).astype(BF)


def dot_f32(a, b):
    return jnp.dot(a, b, preferred_element_type=F32)


def gather_kernel(
    master,
    slot_col,
    small_slot,
    x_in,
    gy_in,
    w_qkv,
    w_out,
    w_up,
    w_down,
    small_out,
    x_row,
    gy_row,
    slots,
    canon,
    land,
    share,
    p_qkv,
    p_out,
    p_up,
    p_down,
    small_mine,
    small_land,
    small_total,
    send_sems,
    recv_sems,
    local_sems,
):
    place = Place()
    link = Sender(send_sems, recv_sems, local_sems)
    place.greet()
    whole = (w_qkv, w_out, w_up, w_down)
    piece = (p_qkv, p_out, p_up, p_down)
    peers = (place.right, place.down, place.diag)
    mine_rows = pl.ds(pl.multiple_of(place.t * 128, 128), 128)

    slots[place.c] = master[...].astype(BF)
    core_slots = link.send(slots.at[place.c], slots.at[place.c], place.core)
    x_moves = [
        link.send(x_in.at[place.ahead[k]], x_row.at[mine_rows], place.deep[k]) for k in (1, 2, 3)
    ]
    stay = [link.copy(x_in.at[place.t], x_row.at[mine_rows]), link.copy(gy_in.at[place.t], gy_row.at[mine_rows])]
    core_slots.wait_recv()

    pair_slots = slots[...].reshape(384, 2304)
    slot_id = lax.broadcasted_iota(jnp.int32, (96, 384), 1) + place.xy * 384
    shares = []
    order = [(1, place.right), (2, place.down), (3, place.diag), (0, None)]
    pick_small = jnp.where(small_slot[...] == slot_id[:8], 1.0, 0.0).astype(BF)
    small_mine[...] = dot_f32(pick_small, pair_slots)
    small_moves = [
        link.send(small_mine, small_land.at[j], peer) for j, peer in enumerate(peers)
    ]
    for j, peer in order:
        at = place.xy if peer is None else peer[0] // 2
        wanted = slot_col[pl.ds(pl.multiple_of(at * 96, 96), 96), :]
        pick = jnp.where(wanted == slot_id, 1.0, 0.0).astype(BF)
        canon[j] = dot_f32(pick, pair_slots).astype(BF)
        if peer is not None:
            shares.append(link.send(canon.at[j], land.at[j - 1], peer))
    for move in shares + small_moves:
        move.wait_recv()
    share[...] = (
        canon[0].astype(F32) + land[0].astype(F32) + land[1].astype(F32) + land[2].astype(F32)
    )
    small_total[...] = small_mine[...] + small_land[0] + small_land[1] + small_land[2]

    three = interleave(96, 3)
    p_qkv[...] = dot_f32(
        interleave(96, 4),
        jnp.concatenate([share[64:88, 576 * r : 576 * r + 576] for r in range(4)], axis=0).astype(BF),
    ).astype(BF)
    out_parts = [share[88:96, 768 * k : 768 * k + 768] for k in range(3)]
    out_parts = out_parts + [jnp.zeros((8, 768), F32)]
    p_out[...] = dot_f32(interleave_out(), jnp.concatenate(out_parts, axis=0).astype(BF)).astype(BF)
    for at, ref in ((0, p_up), (32, p_down)):
        parts = [share[at : at + 32, 768 * k : 768 * k + 768] for k in range(3)]
        ref[...] = dot_f32(three, jnp.concatenate(parts, axis=0).astype(BF)).astype(BF)

    deep_moves, right_moves, down_moves, own_copies = {}, {}, {}, {}
    late = []

    def deep_send(w):
        spot = whole[w].at[place.t, rows_of(place, WEIGHTS[w][1])]
        own_copies[w] = link.copy(piece[w], spot)
        deep_moves[w] = [link.send(piece[w], spot, place.deep[k]) for k in (1, 2, 3)]

    def plane_send(w, k):
        rows = WEIGHTS[w][1]
        spot = whole[w].at[place.behind[k], rows_of(place, rows)]
        src = piece[w] if k == 0 else spot
        if k:
            deep_moves[w][k - 1].wait_recv()
        right_moves[w, k] = link.send(src, spot, place.right)
        down_moves[w, k] = link.send(src, spot, place.down)

    def plane_pass(w, k):
        rows = WEIGHTS[w][1]
        half = rows // 2
        right_moves[w, k].wait_recv()
        down_moves[w, k].wait_recv()
        t = place.behind[k]
        right_at = place.c * (4 * rows) + (place.right[0] // 2) * rows
        down_at = place.c * (4 * rows) + (place.down[0] // 2) * rows
        first = whole[w].at[t, pl.ds(pl.multiple_of(right_at, 16), half)]
        second = whole[w].at[t, pl.ds(pl.multiple_of(down_at + half, 16), half)]
        right_moves[w, k, 1] = link.send(second, second, place.right)
        down_moves[w, k, 1] = link.send(first, first, place.down)

    def core_pass(w, k):
        if k == 0:
            own_copies[w].wait()
        right_moves[w, k, 1].wait_recv()
        down_moves[w, k, 1].wait_recv()
        spot = whole[w].at[place.behind[k], half_of(place, WEIGHTS[w][1])]
        late.append(link.send(spot, spot, place.core))

    deep_send(0)
    deep_send(1)
    own_small = link.copy(small_total, small_out.at[place.t])
    small_deep = [link.send(small_total, small_out.at[place.t], place.deep[k]) for k in (1, 2, 3)]
    plane_send(0, 0)
    plane_send(1, 0)
    plane_send(2, 0)
    plane_send(3, 0)
    for k in (1, 2, 3):
        plane_send(0, k)
    deep_send(2)
    for k in range(4):
        plane_pass(0, k)
    for k in (1, 2, 3):
        plane_send(1, k)
    for k in range(4):
        core_pass(0, k)
    for k in range(4):
        plane_pass(1, k)
    for k in (1, 2, 3):
        plane_send(2, k)
    deep_send(3)
    gy_moves = [
        link.send(gy_in.at[place.ahead[k]], gy_row.at[mine_rows], place.deep[k]) for k in (1, 2, 3)
    ]
    for k in range(4):
        plane_pass(2, k)
        core_pass(1, k)
    for k in (1, 2, 3):
        plane_send(3, k)
    for k in range(4):
        core_pass(2, k)
        plane_pass(3, k)
    for k in range(4):
        core_pass(3, k)
    for move in late + x_moves + gy_moves + small_deep:
        move.wait_recv()
    for copy in stay + [own_small]:
        copy.wait()
    link.finish()


def gather_call(master, slot_col, small_slot, x_in, gy_in):
    anywhere = pl.BlockSpec(memory_space=pl.ANY)
    vmem = pl.BlockSpec(memory_space=pltpu.VMEM)
    shape = jax.ShapeDtypeStruct
    return pl.pallas_call(
        gather_kernel,
        out_shape=[
            shape((4, 768, 576), BF),
            shape((4, 256, 768), BF),
            shape((4, 768, 768), BF),
            shape((4, 768, 768), BF),
            shape((4, 8, 2304), F32),
            shape((512, 768), BF),
            shape((512, 768), BF),
        ],
        in_specs=[vmem, vmem, vmem, anywhere, anywhere],
        out_specs=[anywhere] * 7,
        scratch_shapes=[
            pltpu.VMEM((2, 192, 2304), BF),
            pltpu.VMEM((4, 96, 2304), BF),
            pltpu.VMEM((3, 96, 2304), BF),
            pltpu.VMEM((96, 2304), F32),
            pltpu.VMEM((96, 576), BF),
            pltpu.VMEM((32, 768), BF),
            pltpu.VMEM((96, 768), BF),
            pltpu.VMEM((96, 768), BF),
            pltpu.VMEM((8, 2304), F32),
            pltpu.VMEM((3, 8, 2304), F32),
            pltpu.VMEM((8, 2304), F32),
            pltpu.SemaphoreType.DMA((112,)),
            pltpu.SemaphoreType.DMA((112,)),
            pltpu.SemaphoreType.DMA((8,)),
        ],
        compiler_params=pltpu.CompilerParams(
            collective_id=0, has_side_effects=True, vmem_limit_bytes=48 * MIB
        ),
        name="gather_weights",
    )(master, slot_col, small_slot, x_in, gy_in)


def add_into(total, other, rows, step):
    groups = other.shape[0]

    @pl.loop(0, groups * (rows // step))
    def _(i):
        g = i // (rows // step)
        at = pl.ds(pl.multiple_of((i % (rows // step)) * step, step), step)
        total[g, at, :] = total[g, at, :] + other[g, at, :]


def reduce_kernel(
    g_qkv,
    g_out,
    g_up,
    g_down,
    small_in,
    out_row,
    dx_row,
    pool_in,
    blocks,
    small_out,
    out_mine,
    dx_mine,
    pool_out,
    *scratch,
):
    sums, cores, lefts, tops, lefts_two, tops_two, deeps = (scratch[4 * i : 4 * i + 4] for i in range(7))
    share, share_low, small_sum, small_land, send_sems, recv_sems, local_sems = scratch[28:]
    place = Place()
    link = Sender(send_sems, recv_sems, local_sems)
    grads = (g_qkv, g_out, g_up, g_down)
    loads = {}
    order = (3, 2, 1, 0)
    for w in order:
        rows = WEIGHTS[w][1]
        loads[w] = link.copy(grads[w].at[:, half_of(place, rows)], sums[w])
    place.greet()
    t, x, y = place.t, place.x, place.y
    core_moves = {}
    for w in order:
        rows = WEIGHTS[w][1]
        other = pl.ds(pl.multiple_of((1 - place.c) * (4 * rows), 128), 4 * rows)
        core_moves[w] = link.send(grads[w].at[:, other], cores[w], place.core)
    moves = []
    stay = [link.copy(small_in.at[t], small_sum.at[pl.ds(0, 1)])]
    small_moves = [link.send(small_in.at[place.ahead[k]], small_land.at[k - 1], place.deep[k]) for k in (1, 2, 3)]
    for src, dst in ((out_row, out_mine), (dx_row, dx_mine)):
        stay.append(link.copy(src.at[pl.ds(pl.multiple_of(t * 128, 128), 128)], dst.at[t]))
        for k in (1, 2, 3):
            part = src.at[pl.ds(pl.multiple_of(place.ahead[k] * 128, 128), 128)]
            moves.append(link.send(part, dst.at[t], place.deep[k]))
    stay.append(link.copy(pool_in, pool_out.at[t]))
    for k in (1, 2, 3):
        moves.append(link.send(pool_in, pool_out.at[t], place.deep[k]))

    first, second, third = {}, {}, {}

    def chip_row(w, yy, xx, half):
        rows = WEIGHTS[w][1]
        at = pl.multiple_of((yy * 2 + xx) * rows + half * (rows // 2), 16)
        return sums[w].at[:, pl.ds(at, rows // 2)]

    def add(total, other):
        groups, rows, _ = other.shape
        add_into(total, other, rows, 16)

    def stage_core(w):
        loads[w].wait()
        core_moves[w].wait_recv()
        add_into(sums[w], cores[w], 4 * WEIGHTS[w][1], 32)
        first[w] = []
        for i in (0, 1):
            first[w].append(link.send(chip_row(w, i, 1 - x, 0), lefts[w].at[i], place.right))
            first[w].append(link.send(chip_row(w, 1 - y, i, 1), tops[w].at[i], place.down))

    def stage_plane(w):
        for move in first[w]:
            move.wait_recv()
        add(chip_row(w, 1 - y, x, 0), lefts[w].at[1 - y])
        add(chip_row(w, y, 1 - x, 1), tops[w].at[1 - x])
        second[w] = [
            link.send(chip_row(w, 1 - y, x, 0), lefts_two[w], place.down),
            link.send(chip_row(w, y, 1 - x, 1), tops_two[w], place.right),
        ]
        add(chip_row(w, y, x, 0), lefts[w].at[y])
        add(chip_row(w, y, x, 1), tops[w].at[x])

    def stage_deep(w):
        for move in second[w]:
            move.wait_recv()
        add(chip_row(w, y, x, 0), lefts_two[w])
        add(chip_row(w, y, x, 1), tops_two[w])
        rows = WEIGHTS[w][1]
        spot = pl.ds(pl.multiple_of(place.xy * rows, 16), rows)
        third[w] = [
            link.send(sums[w].at[place.ahead[k], spot], deeps[w].at[k - 1], place.deep[k])
            for k in (1, 2, 3)
        ]

    def stage_end(w):
        for move in third[w]:
            move.wait_recv()
        rows = WEIGHTS[w][1]
        spot = pl.ds(pl.multiple_of(place.xy * rows, 16), rows)
        total = sums[w][t, spot, :].astype(F32)
        for k in range(3):
            total = total + deeps[w][k].astype(F32)
        total = total.astype(BF)
        turned = (((0,), (0,)), ((), ()))
        if w == 0:
            parts = lax.dot_general(interleave(96, 4), total, turned, preferred_element_type=F32)
            share[64:88, :] = jnp.concatenate([parts[24 * r : 24 * r + 24] for r in range(4)], axis=1)
        elif w == 1:
            parts = lax.dot_general(interleave_out(), total, turned, preferred_element_type=F32)
            for k in range(3):
                share[88:96, 768 * k : 768 * k + 768] = parts[8 * k : 8 * k + 8]
        else:
            at = 0 if w == 2 else 32
            parts = lax.dot_general(interleave(96, 3), total, turned, preferred_element_type=F32)
            for k in range(3):
                share[at : at + 32, 768 * k : 768 * k + 768] = parts[32 * k : 32 * k + 32]

    stage_core(3)
    stage_core(2)
    stage_plane(3)
    stage_core(1)
    stage_core(0)
    stage_deep(3)
    stage_plane(2)
    stage_plane(1)
    stage_deep(2)
    stage_plane(0)
    stage_end(3)
    stage_deep(1)

    stay[0].wait()
    for move in small_moves:
        move.wait_recv()
    small_sum[0] = (
        small_sum[0] + small_land[0, 0] + small_land[1, 0] + small_land[2, 0]
    )
    stage_end(2)
    stage_deep(0)
    stage_end(1)
    for i, peer in enumerate((place.core, place.right, place.down)):
        move = link.send(
            small_sum.at[pl.ds(i, 1)], small_land.at[3 + i], peer
        )
        move.wait_recv()
        small_sum[i + 1] = small_sum[i] + small_land[3 + i, 0]
    stage_end(0)
    small_out[...] = small_sum[3]

    share_low[...] = share[...].astype(BF)
    dest = pl.ds(pl.multiple_of((place.c * 4 + place.xy) * 96, 96), 96)
    keep = link.copy(share_low, blocks.at[dest])
    last = [link.send(share_low, blocks.at[dest], peer) for peer in (place.diag, place.right, place.down)]
    keep.wait()
    for move in last:
        move.wait_recv()
    half = pl.ds(pl.multiple_of(place.c * 384, 384), 384)
    across = link.send(blocks.at[half], blocks.at[half], place.core)
    across.wait_recv()
    for move in moves:
        move.wait_recv()
    for copy in stay[1:]:
        copy.wait()
    link.finish()


def reduce_call(g_qkv, g_out, g_up, g_down, small_in, out_row, dx_row, pool_in):
    anywhere = pl.BlockSpec(memory_space=pl.ANY)
    vmem = pl.BlockSpec(memory_space=pltpu.VMEM)
    shape = jax.ShapeDtypeStruct
    sums = [pltpu.VMEM((4, 4 * rows, cols), BF) for cols, rows in WEIGHTS]
    halves = [pltpu.VMEM((2, 4, rows // 2, cols), BF) for cols, rows in WEIGHTS]
    singles = [pltpu.VMEM((4, rows // 2, cols), BF) for cols, rows in WEIGHTS]
    deeps = [pltpu.VMEM((3, rows, cols), BF) for cols, rows in WEIGHTS]
    return pl.pallas_call(
        reduce_kernel,
        out_shape=[
            shape((768, 2304), BF),
            shape((24, 128), F32),
            shape((4, 128, 768), BF),
            shape((4, 128, 768), BF),
            shape((4, 8, 768), F32),
        ],
        in_specs=[anywhere] * 8,
        out_specs=[anywhere, vmem, anywhere, anywhere, anywhere],
        scratch_shapes=sums
        + sums
        + halves
        + halves
        + singles
        + singles
        + deeps
        + [
            pltpu.VMEM((96, 2304), F32),
            pltpu.VMEM((96, 2304), BF),
            pltpu.VMEM((4, 24, 128), F32),
            pltpu.VMEM((6, 1, 24, 128), F32),
            pltpu.SemaphoreType.DMA((80,)),
            pltpu.SemaphoreType.DMA((80,)),
            pltpu.SemaphoreType.DMA((12,)),
        ],
        compiler_params=pltpu.CompilerParams(
            collective_id=1, has_side_effects=True, vmem_limit_bytes=56 * MIB
        ),
        name="reduce_gradients",
    )(g_qkv, g_out, g_up, g_down, small_in, out_row, dx_row, pool_in)


def local_rows(
    layer_input_rows,
    sentence_index_row,
    padding_mask,
    output_gradient,
    owner_rank,
    master_state,
    first_moment,
    second_moment,
):
    tensor_at = lax.axis_index("tensor")
    data_at = lax.axis_index("dp")
    per_owner = master_state.shape[1]
    block_len = master_state.shape[2]
    slot_of = slot_tables(owner_rank, per_owner)
    slot_order = jnp.concatenate(
        [
            slot_of[:256].reshape(2, 4, 32),
            slot_of[256:512].reshape(2, 4, 32),
            slot_of[512:704].reshape(2, 4, 24),
            slot_of[704:768].reshape(2, 4, 8),
        ],
        axis=2,
    ).reshape(768)
    core_order = lax.dynamic_slice_in_dim(slot_order, (data_at % 2) * 384, 384, 0)[:, None]
    small_slot = jnp.broadcast_to(slot_of[768], (8, 1))

    w_qkv, w_out_padded, w_up, w_down, small_all, x_row, gy_row = gather_call(
        master_state[0],
        core_order,
        small_slot,
        jnp.transpose(layer_input_rows, (1, 0, 2)),
        jnp.transpose(output_gradient, (1, 0, 2)),
    )
    w_out = w_out_padded.reshape(4, 8, 32, 768)[:, :, :24].reshape(768, 768)
    small_all = small_all[:, 0]
    bias_q = small_all[:, :192]
    bias_v = small_all[:, 192:384]
    expand_bias = small_all[:, 384:1152]
    norm_all = small_all[:, 1152:].reshape(4, 6, 192).transpose(1, 0, 2).reshape(6, 768)
    bias_out, bias_down, gain_one, shift_one, gain_two, shift_two = (norm_all[i] for i in range(6))

    labels = lax.dynamic_index_in_dim(sentence_index_row, tensor_at, 0, keepdims=False)
    flags = lax.dynamic_index_in_dim(padding_mask, tensor_at, 0, keepdims=False)
    x_wide = x_row.astype(F32)
    qkv_lin = jnp.einsum("ld,tde->tle", x_row, w_qkv, preferred_element_type=F32)
    bias_qkv = jnp.concatenate([bias_q, jnp.zeros((4, 192), F32), bias_v], axis=1)
    qkv = (qkv_lin + bias_qkv[:, None]).astype(BF).reshape(4, 512, 3, 3, HEAD_DIM)
    queries, keys, values = (qkv[:, :, i] for i in range(3))
    scaling = HEAD_DIM ** (-0.5)
    allowed = allowed_pairs(labels[None], flags[None])[0]
    scores = jnp.einsum("tqhe,tkhe->thqk", queries, keys, preferred_element_type=F32) * scaling
    scores = jnp.where(allowed, scores, MASKED)
    peak = jnp.max(scores, axis=-1, keepdims=True)
    log_total = peak + jnp.log(jnp.sum(jnp.exp(scores - peak), axis=-1, keepdims=True))
    attn_prob = jnp.exp(scores - log_total)
    prob_low = attn_prob.astype(BF)
    attended = jnp.einsum("thqk,tkhe->qthe", prob_low, values, preferred_element_type=F32)
    attended = attended.astype(BF).reshape(512, 768)
    z_one = x_wide + dot_f32(attended, w_out) + bias_out
    normed_one, inv_one = normalize(z_one)
    h_wide = normed_one * gain_one + shift_one
    h_low = h_wide.astype(BF)
    up_pre = (
        jnp.einsum("ld,tdf->tlf", h_low, w_up, preferred_element_type=F32) + expand_bias[:, None]
    )
    act = jax.nn.gelu(up_pre, approximate=False).astype(BF)
    z_two = h_wide + jnp.einsum("tlf,tfd->ld", act, w_down, preferred_element_type=F32) + bias_down
    normed_two, inv_two = normalize(z_two)
    layer_out = normed_two * gain_two + shift_two

    sent_ids = jnp.arange(SMAX, dtype=jnp.int32)
    onehot = ((labels[None, :] == sent_ids[:, None]) & (flags[None, :] == 1)).astype(F32)
    pool_sum = jnp.dot(onehot, layer_out, precision=exact_precision)
    pool_mean = pool_sum / jnp.maximum(jnp.sum(onehot, axis=1), 1.0)[:, None]

    grad_out = gy_row.astype(F32) * flags[:, None].astype(F32)
    d_gain_two = jnp.sum(grad_out * normed_two, axis=0)
    d_shift_two = jnp.sum(grad_out, axis=0)
    dz_two = norm_back(grad_out * gain_two, normed_two, inv_two)
    d_bias_down = jnp.sum(dz_two, axis=0)
    dz_two_low = dz_two.astype(BF)
    g_down = jnp.einsum("tlf,ld->tfd", act, dz_two_low, preferred_element_type=F32).astype(BF)
    d_act = jnp.einsum("ld,tfd->tlf", dz_two_low, w_down, preferred_element_type=F32)
    d_up = jax.vjp(lambda pre: jax.nn.gelu(pre, approximate=False), up_pre)[1](d_act)[0]
    d_bias_up = jnp.sum(d_up, axis=1)
    d_up_low = d_up.astype(BF)
    g_up = jnp.einsum("ld,tlf->tdf", h_low, d_up_low, preferred_element_type=F32).astype(BF)
    dh = dz_two + jnp.einsum("tlf,tdf->ld", d_up_low, w_up, preferred_element_type=F32)
    d_gain_one = jnp.sum(dh * normed_one, axis=0)
    d_shift_one = jnp.sum(dh, axis=0)
    dz_one = norm_back(dh * gain_one, normed_one, inv_one)
    d_bias_out = jnp.sum(dz_one, axis=0)
    dz_one_low = dz_one.astype(BF)
    g_out = jnp.einsum("le,ld->ed", attended, dz_one_low, preferred_element_type=F32).astype(BF)
    g_out = jnp.pad(g_out.reshape(4, 8, 24, 768), ((0, 0), (0, 0), (0, 8), (0, 0))).reshape(4, 256, 768)
    d_att = jnp.einsum("ld,ed->le", dz_one_low, w_out, preferred_element_type=F32).astype(BF)
    d_att = d_att.reshape(512, 4, 3, HEAD_DIM)
    d_prob = jnp.einsum("qthe,tkhe->thqk", d_att, values, preferred_element_type=F32)
    d_values = jnp.einsum("thqk,qthe->tkhe", prob_low, d_att, preferred_element_type=F32)
    inner = jnp.sum(d_prob * attn_prob, axis=-1, keepdims=True)
    d_scores = (attn_prob * (d_prob - inner)).astype(BF)
    d_queries = jnp.einsum("thqk,tkhe->tqhe", d_scores, keys, preferred_element_type=F32) * scaling
    d_keys = jnp.einsum("thqk,tqhe->tkhe", d_scores, queries, preferred_element_type=F32) * scaling
    d_bias_q = jnp.sum(d_queries, axis=1).reshape(4, 192)
    d_bias_v = jnp.sum(d_values, axis=1).reshape(4, 192)
    d_qkv = jnp.stack([d_queries, d_keys, d_values], axis=2).astype(BF).reshape(4, 512, 576)
    g_qkv = jnp.einsum("ld,tle->tde", x_row, d_qkv, preferred_element_type=F32).astype(BF)
    input_grad = dz_one + jnp.einsum("tle,tde->ld", d_qkv, w_qkv, preferred_element_type=F32)

    shared = jnp.stack([d_bias_out, d_bias_down, d_gain_one, d_shift_one, d_gain_two, d_shift_two])
    shared = shared.reshape(6, 4, 192).transpose(1, 0, 2).reshape(4, 1152)
    small_grads = jnp.concatenate([d_bias_q, d_bias_v, d_bias_up, shared], axis=1)
    small_grads = jnp.pad(small_grads.reshape(4, 1, 18, 128), ((0, 0), (0, 0), (0, 6), (0, 0)))
    blocks, small_sum, out_mine, dx_mine, pool_all = reduce_call(
        g_qkv,
        g_out,
        g_up,
        g_down,
        small_grads,
        layer_out.astype(BF),
        input_grad.astype(BF),
        pool_mean,
    )
    small_row = small_sum[:18].reshape(block_len)
    norm_grads = small_row[1152:].reshape(6, 192)
    pooled = lax.dynamic_slice_in_dim(pool_all, tensor_at * 192, 192, 2)

    wanted = data_at * per_owner + jnp.arange(per_owner, dtype=jnp.int32)
    block_of, filled = slot_blocks(slot_of, wanted)
    pick = (slot_order[None, :] == wanted[:, None]).astype(BF)
    owned = dot_f32(pick, blocks)
    owned = jnp.where((wanted == slot_of[768])[:, None], small_row[None], owned)
    token_position = block_of[:, None] * block_len + jnp.arange(block_len, dtype=jnp.int32)[None, :]
    step_rate, decay_on = step_rates(token_position, MODEL_WIDTH, FF, 4)
    new_master, new_first, new_second = adamw(
        owned,
        first_moment[0],
        second_moment[0],
        master_state[0],
        step_rate,
        decay_on,
        filled[:, None],
    )
    return (
        jnp.transpose(out_mine, (1, 0, 2)).astype(F32),
        pooled,
        jnp.transpose(dx_mine, (1, 0, 2)).astype(F32),
        new_master[None],
        new_first[None],
        new_second[None],
        norm_grads,
    )


def solution(mesh):
    in_specs = (
        P("tensor", "dp", None),
        P("dp", None),
        P("dp", None),
        P("tensor", "dp", None),
        P(),
        P("tensor", "dp", None),
        P("tensor", "dp", None),
        P("tensor", "dp", None),
    )
    out_specs = (
        P("tensor", "dp", None),
        P("dp", None, "tensor"),
        P("tensor", "dp", None),
        P("tensor", "dp", None),
        P("tensor", "dp", None),
        P("tensor", "dp", None),
        P(None, "tensor"),
    )
    plain = mesh.shape["dp"] != 8 or mesh.shape["tensor"] != 4
    body = local_general if plain else local_rows
    return jax.shard_map(body, mesh=mesh, in_specs=in_specs, out_specs=out_specs, check_vma=False)
```

```python
import jax
import functools
import jax.numpy as jnp
from jax import lax
from jax.experimental import pallas as pl
from jax.experimental.pallas import tpu as pltpu
from jax.sharding import PartitionSpec as P

MODEL_WIDTH = 768
HEAD_DIM = 64
FF = 3072
SMAX = 8
STEP = 10


NORM_EPS = 1e-05
ADAM_EPS = 1e-08
BETA_ONE = 0.9
BETA_TWO = 0.999
DECAY_RATE = 0.01
MASKED = -1e30
exact_precision = lax.Precision.HIGHEST


def slot_tables(owner_rank, per_owner):
    ordinal = jnp.arange(owner_rank.shape[0], dtype=jnp.int32)
    same_owner = owner_rank[:, None] == owner_rank[None, :]
    earlier = ordinal[None, :] < ordinal[:, None]
    ranking = jnp.sum((same_owner & earlier).astype(jnp.int32), axis=1)
    return owner_rank * per_owner + ranking


def slot_blocks(slot_of, wanted):
    matches = slot_of[None, :] == wanted[:, None]
    filled = jnp.any(matches, axis=1)
    ordinal = jnp.arange(slot_of.shape[0], dtype=jnp.int32)
    block_of = jnp.sum(jnp.where(matches, ordinal[None, :], 0), axis=1)
    return (block_of, filled)


def step_rates(token_position, width, hidden, tensor_size):
    width_loc = width // tensor_size
    ffn_loc = hidden // tensor_size
    end_up = width * ffn_loc
    end_down = end_up + ffn_loc * width
    end_qkv = end_down + width * 3 * width_loc
    end_out = end_qkv + width_loc * width
    offset = token_position - end_out
    first_gain = (offset >= 4 * width_loc + ffn_loc) & (offset < 5 * width_loc + ffn_loc)
    second_gain = (offset >= 6 * width_loc + ffn_loc) & (offset < 7 * width_loc + ffn_loc)
    small_rate = jnp.where(first_gain | second_gain, 0.2, 0.1)
    step_rate = jnp.where(
        token_position < end_up,
        width ** (-0.5),
        jnp.where(
            token_position < end_down,
            hidden ** (-0.5),
            jnp.where(
                token_position < end_qkv,
                width ** (-0.5),
                jnp.where(token_position < end_out, 4.0 * width ** (-0.5), small_rate),
            ),
        ),
    )
    decay_on = (token_position < end_out).astype(jnp.float32)
    return (step_rate.astype(jnp.float32), decay_on)


def adamw(gradient, moment, square, weight, step_rate, decay_on, filled):
    new_moment = BETA_ONE * moment + (1.0 - BETA_ONE) * gradient
    new_square = BETA_TWO * square + (1.0 - BETA_TWO) * gradient * gradient
    unbiased = new_moment / (1.0 - BETA_ONE**STEP)
    divisor = jnp.sqrt(new_square / (1.0 - BETA_TWO**STEP)) + ADAM_EPS
    new_weight = weight - step_rate * (unbiased / divisor + DECAY_RATE * decay_on * weight)
    zeroed = jnp.zeros_like(weight)
    return (
        jnp.where(filled, new_weight, zeroed),
        jnp.where(filled, new_moment, zeroed),
        jnp.where(filled, new_square, zeroed),
    )


def normalize(values):
    centred = values - jnp.mean(values, axis=-1, keepdims=True)
    inv_dev = lax.rsqrt(jnp.mean(centred * centred, axis=-1, keepdims=True) + NORM_EPS)
    return (centred * inv_dev, inv_dev)


def norm_back(grad_scaled, normed, inv_dev):
    first_mean = jnp.mean(grad_scaled, axis=-1, keepdims=True)
    second_mean = jnp.mean(grad_scaled * normed, axis=-1, keepdims=True)
    return inv_dev * (grad_scaled - first_mean - normed * second_mean)


def allowed_pairs(sentence_labels, real_token_flags):
    row_len = sentence_labels.shape[-1]
    same_sent = sentence_labels[:, :, None] == sentence_labels[:, None, :]
    live = (real_token_flags[:, :, None] == 1) & (real_token_flags[:, None, :] == 1)
    diagonal = jnp.eye(row_len, dtype=bool)[None]
    return same_sent & live | diagonal


def masked_scores(queries, key_rows, allowed, scaling):
    scores = (
        jnp.einsum("qshe,kshe->shqk", queries, key_rows, preferred_element_type=jnp.float32)
        * scaling
    )
    return jnp.where(allowed[:, None], scores, MASKED)


def split_flat(flat_all, width_loc, ffn_loc):
    end_up = MODEL_WIDTH * ffn_loc
    end_down = end_up + ffn_loc * MODEL_WIDTH
    end_qkv = end_down + MODEL_WIDTH * 3 * width_loc
    end_out = end_qkv + width_loc * MODEL_WIDTH
    return (
        flat_all[:end_up].reshape(MODEL_WIDTH, ffn_loc),
        flat_all[end_up:end_down].reshape(ffn_loc, MODEL_WIDTH),
        flat_all[end_down:end_qkv].reshape(MODEL_WIDTH, 3 * width_loc),
        flat_all[end_qkv:end_out].reshape(width_loc, MODEL_WIDTH),
        flat_all[end_out:],
    )


def local_general(
    layer_input_rows,
    sentence_index_row,
    padding_mask,
    output_gradient,
    owner_rank,
    master_state,
    first_moment,
    second_moment,
):
    tensor_size = lax.axis_size("tensor")
    tensor_at = lax.axis_index("tensor")
    data_size = lax.axis_size("dp")
    data_at = lax.axis_index("dp")
    width_loc = MODEL_WIDTH // tensor_size
    ffn_loc = FF // tensor_size
    heads_loc = width_loc // HEAD_DIM
    quarter = layer_input_rows.shape[0]
    seq_count = layer_input_rows.shape[1]
    row_len = quarter * tensor_size
    per_owner = master_state.shape[1]
    block_len = master_state.shape[2]
    nblocks = owner_rank.shape[0]
    slot_of = slot_tables(owner_rank, per_owner)
    gathered = lax.all_gather(master_state.astype(jnp.bfloat16), "dp", axis=1, tiled=True)[0]
    flat_weights = gathered[slot_of].reshape(nblocks * block_len)
    up_weight, down_weight, w_qkv, w_out, small_part = split_flat(flat_weights, width_loc, ffn_loc)
    bias_q = small_part[:width_loc].astype(jnp.float32)
    bias_v = small_part[width_loc : 2 * width_loc].astype(jnp.float32)
    expand_bias = small_part[2 * width_loc : 2 * width_loc + ffn_loc].astype(jnp.float32)
    norm_parts = small_part[2 * width_loc + ffn_loc :].reshape(6, width_loc)
    full_rows, norm_whole = (
        lax.all_gather(layer_input_rows, "tensor", axis=0, tiled=True),
        lax.all_gather(norm_parts, "tensor", axis=1, tiled=True),
    )
    norm_all = norm_whole.astype(jnp.float32)
    bias_out, bias_down = (norm_all[0], norm_all[1])
    gain_one, shift_one, gain_two, shift_two = (norm_all[2], norm_all[3], norm_all[4], norm_all[5])
    qkv_lin = jnp.einsum("lsd,de->lse", full_rows, w_qkv, preferred_element_type=jnp.float32)
    bias_qkv = jnp.concatenate([bias_q, jnp.zeros((width_loc,), jnp.float32), bias_v])
    qkv = (qkv_lin + bias_qkv).astype(jnp.bfloat16)
    queries = qkv[:, :, :width_loc].reshape(row_len, seq_count, heads_loc, HEAD_DIM)
    key_rows = qkv[:, :, width_loc : 2 * width_loc].reshape(row_len, seq_count, heads_loc, HEAD_DIM)
    values = qkv[:, :, 2 * width_loc :].reshape(row_len, seq_count, heads_loc, HEAD_DIM)
    scaling = HEAD_DIM ** (-0.5)
    allowed = allowed_pairs(sentence_index_row, padding_mask)
    scores = masked_scores(queries, key_rows, allowed, scaling)
    row_peak = jnp.max(scores, axis=-1, keepdims=True)
    log_total = row_peak + jnp.log(jnp.sum(jnp.exp(scores - row_peak), axis=-1, keepdims=True))
    prob_low = jnp.exp(scores - log_total).astype(jnp.bfloat16)
    attended = jnp.einsum("shqk,kshe->qshe", prob_low, values, preferred_element_type=jnp.float32)
    attended = attended.astype(jnp.bfloat16).reshape(row_len, seq_count, width_loc)
    portion_rows = attended
    attn_rows = lax.psum_scatter(
        jnp.einsum("lse,ed->lsd", portion_rows, w_out, preferred_element_type=jnp.float32).astype(
            jnp.bfloat16
        ),
        "tensor",
        scatter_dimension=0,
        tiled=True,
    ).astype(jnp.float32)
    z_one = layer_input_rows.astype(jnp.float32) + attn_rows + bias_out
    normed_one, inv_one = normalize(z_one)
    h_mine = normed_one * gain_one + shift_one
    hidden_narrow_whole = lax.all_gather(h_mine.astype(jnp.bfloat16), "tensor", axis=0, tiled=True)
    up_pre = (
        jnp.einsum(
            "wer,rb->web", hidden_narrow_whole, up_weight, preferred_element_type=jnp.float32
        )
        + expand_bias
    )
    activation_narrow = jax.nn.gelu(up_pre, approximate=False).astype(jnp.bfloat16)
    portion_rows = activation_narrow
    down_rows = lax.psum_scatter(
        jnp.einsum(
            "aij,jb->aib", portion_rows, down_weight, preferred_element_type=jnp.float32
        ).astype(jnp.bfloat16),
        "tensor",
        scatter_dimension=0,
        tiled=True,
    ).astype(jnp.float32)
    z_two = h_mine + down_rows + bias_down
    normed_two, inv_two = normalize(z_two)
    layer_out = normed_two * gain_two + shift_two
    seg_mine = lax.dynamic_slice_in_dim(sentence_index_row, tensor_at * quarter, quarter, 1)
    valid_mine = lax.dynamic_slice_in_dim(padding_mask, tensor_at * quarter, quarter, 1)
    sent_ids = jnp.arange(SMAX, dtype=jnp.int32)
    onehot_mine = (
        (seg_mine[:, :, None] == sent_ids[None, None, :]) & (valid_mine[:, :, None] == 1)
    ).astype(jnp.float32)
    pool_part = jnp.einsum("slc,lsd->scd", onehot_mine, layer_out, precision=exact_precision)
    onehot_full = (
        (sentence_index_row[:, :, None] == sent_ids[None, None, :])
        & (padding_mask[:, :, None] == 1)
    ).astype(jnp.float32)
    counts = jnp.sum(onehot_full, axis=1)
    grad_out = output_gradient.astype(jnp.float32) * valid_mine.T[:, :, None].astype(jnp.float32)
    d_gain_two = jnp.sum(grad_out * normed_two, axis=(0, 1))
    d_shift_two = jnp.sum(grad_out, axis=(0, 1))
    dz_two = norm_back(grad_out * gain_two, normed_two, inv_two)
    d_bias_down = jnp.sum(dz_two, axis=(0, 1))
    second_sum_gradient_wide = lax.all_gather(
        dz_two.astype(jnp.bfloat16), "tensor", axis=0, tiled=True
    )
    down_weight_gradient = jnp.einsum(
        "ipo,ipr->or",
        activation_narrow,
        second_sum_gradient_wide,
        preferred_element_type=jnp.float32,
    )
    activation_gradient = jnp.einsum(
        "ugp,jp->ugj", second_sum_gradient_wide, down_weight, preferred_element_type=jnp.float32
    )
    gelu_pull = jax.vjp(lambda pre_act: jax.nn.gelu(pre_act, approximate=False), up_pre)[1]
    d_up = gelu_pull(activation_gradient)[0]
    d_bias_up = jnp.sum(d_up, axis=(0, 1))
    expand_gradient_narrow = d_up.astype(jnp.bfloat16)
    up_weight_gradient = jnp.einsum(
        "iux,iuy->xy",
        hidden_narrow_whole,
        expand_gradient_narrow,
        preferred_element_type=jnp.float32,
    )
    portion_rows = expand_gradient_narrow
    dh_rows = lax.psum_scatter(
        jnp.einsum(
            "uih,vh->uiv", portion_rows, up_weight, preferred_element_type=jnp.float32
        ).astype(jnp.bfloat16),
        "tensor",
        scatter_dimension=0,
        tiled=True,
    ).astype(jnp.float32)
    dh_mine = dz_two + dh_rows
    d_gain_one = jnp.sum(dh_mine * normed_one, axis=(0, 1))
    d_shift_one = jnp.sum(dh_mine, axis=(0, 1))
    dz_one = norm_back(dh_mine * gain_one, normed_one, inv_one)
    d_bias_out = jnp.sum(dz_one, axis=(0, 1))
    dz_one_full = lax.all_gather(dz_one.astype(jnp.bfloat16), "tensor", axis=0, tiled=True)
    d_w_out = jnp.einsum("lse,lsd->ed", attended, dz_one_full, preferred_element_type=jnp.float32)
    d_attended = jnp.einsum("lsd,ed->lse", dz_one_full, w_out, preferred_element_type=jnp.float32)
    d_attended = d_attended.astype(jnp.bfloat16).reshape(row_len, seq_count, heads_loc, HEAD_DIM)
    scores_again = masked_scores(queries, key_rows, allowed, scaling)
    attn_prob = jnp.exp(scores_again - log_total)
    prob_again = attn_prob.astype(jnp.bfloat16)
    d_prob = jnp.einsum("qshe,kshe->shqk", d_attended, values, preferred_element_type=jnp.float32)
    d_values = jnp.einsum(
        "shqk,qshe->kshe", prob_again, d_attended, preferred_element_type=jnp.float32
    )
    inner = jnp.sum(d_prob * attn_prob, axis=-1, keepdims=True)
    d_scores = (attn_prob * (d_prob - inner)).astype(jnp.bfloat16)
    d_queries = (
        jnp.einsum("shqk,kshe->qshe", d_scores, key_rows, preferred_element_type=jnp.float32)
        * scaling
    )
    d_keys = (
        jnp.einsum("shqk,qshe->kshe", d_scores, queries, preferred_element_type=jnp.float32)
        * scaling
    )
    d_bias_q = jnp.sum(d_queries, axis=(0, 1)).reshape(width_loc)
    d_bias_v = jnp.sum(d_values, axis=(0, 1)).reshape(width_loc)
    d_qkv_low = jnp.concatenate(
        [
            d_queries.reshape(row_len, seq_count, width_loc),
            d_keys.reshape(row_len, seq_count, width_loc),
            d_values.reshape(row_len, seq_count, width_loc),
        ],
        axis=2,
    ).astype(jnp.bfloat16)
    d_w_qkv = jnp.einsum("lsd,lse->de", full_rows, d_qkv_low, preferred_element_type=jnp.float32)
    portion_rows = d_qkv_low
    dx_rows = lax.psum_scatter(
        jnp.einsum("lse,de->lsd", portion_rows, w_qkv, preferred_element_type=jnp.float32).astype(
            jnp.bfloat16
        ),
        "tensor",
        scatter_dimension=0,
        tiled=True,
    ).astype(jnp.float32)
    input_grad = dz_one + dx_rows
    shared_grads = jnp.stack(
        [d_bias_out, d_bias_down, d_gain_one, d_shift_one, d_gain_two, d_shift_two]
    )[None]
    pool_sum, shared_sum = (
        lax.psum_scatter(
            pool_part.astype(jnp.bfloat16), "tensor", scatter_dimension=2, tiled=True
        ).astype(jnp.float32),
        lax.psum_scatter(
            shared_grads.astype(jnp.bfloat16), "tensor", scatter_dimension=2, tiled=True
        ).astype(jnp.float32),
    )
    pooled_mean = pool_sum / jnp.maximum(counts, 1.0)[:, :, None]
    flat_grads = jnp.concatenate(
        [
            up_weight_gradient.reshape(-1),
            down_weight_gradient.reshape(-1),
            d_w_qkv.reshape(-1),
            d_w_out.reshape(-1),
            d_bias_q,
            d_bias_v,
            d_bias_up,
            shared_sum.reshape(-1),
        ]
    )
    grad_blocks = flat_grads.reshape(nblocks, block_len)
    wanted = data_at * per_owner + jnp.arange(per_owner, dtype=jnp.int32)
    block_of, filled = slot_blocks(slot_of, wanted)
    slot_grads = (
        jnp.zeros((data_size * per_owner, block_len), jnp.float32).at[slot_of].set(grad_blocks)
    )
    owned_grads = lax.psum_scatter(slot_grads, "dp", scatter_dimension=0, tiled=True)
    norm_grads = lax.psum(shared_sum[0], "dp")
    token_position = block_of[:, None] * block_len + jnp.arange(block_len, dtype=jnp.int32)[None, :]
    step_rate, decay_on = step_rates(token_position, MODEL_WIDTH, FF, tensor_size)
    new_master, new_first, new_second = adamw(
        owned_grads,
        first_moment[0],
        second_moment[0],
        master_state[0],
        step_rate,
        decay_on,
        filled[:, None],
    )
    return (
        layer_out,
        pooled_mean,
        input_grad,
        new_master[None],
        new_first[None],
        new_second[None],
        norm_grads,
    )


MESH = pl.DeviceIdType.MESH
BF = jnp.bfloat16
F32 = jnp.float32
WEIGHTS = ((576, 96), (768, 32), (768, 96), (768, 96))
MIB = 2**20


class Place:
    def __init__(self):
        d = lax.axis_index("dp")
        self.t = lax.axis_index("tensor")
        self.c = d % 2
        self.x = (d // 2) % 2
        self.y = d // 4
        self.xy = d // 2
        self.core = (d + 1 - 2 * self.c, self.t)
        self.right = (d + 2 - 4 * self.x, self.t)
        self.down = (d + 4 - 8 * self.y, self.t)
        self.diag = (d + 6 - 4 * self.x - 8 * self.y, self.t)
        self.deep = [None] + [(d, (self.t + k) % 4) for k in (1, 2, 3)]
        self.ahead = [(self.t + k) % 4 for k in range(4)]
        self.behind = [(self.t + 4 - k) % 4 for k in range(4)]

    def greet(self):
        barrier = pltpu.get_barrier_semaphore()
        peers = [self.core, self.right, self.down, self.diag] + self.deep[1:]
        for peer in peers:
            pl.semaphore_signal(barrier, inc=1, device_id=peer, device_id_type=MESH)
        pl.semaphore_wait(barrier, len(peers))


class Sender:
    def __init__(self, send_sems, recv_sems, local_sems):
        self.sems = (send_sems, recv_sems, local_sems)
        self.used = 0
        self.used_local = 0
        self.open = []

    def send(self, src, dst, peer):
        i = self.used
        self.used += 1
        copy = pltpu.make_async_remote_copy(
            src_ref=src,
            dst_ref=dst,
            send_sem=self.sems[0].at[i],
            recv_sem=self.sems[1].at[i],
            device_id=peer,
            device_id_type=MESH,
        )
        copy.start()
        self.open.append(copy)
        return copy

    def copy(self, src, dst):
        i = self.used_local
        self.used_local += 1
        copy = pltpu.make_async_copy(src, dst, self.sems[2].at[i])
        copy.start()
        return copy

    def finish(self):
        for copy in self.open:
            copy.wait_send()


def rows_of(place, rows, at=None):
    at = place.xy if at is None else at
    return pl.ds(pl.multiple_of(place.c * (4 * rows) + at * rows, 32), rows)


def half_of(place, rows):
    return pl.ds(pl.multiple_of(place.c * (4 * rows), 128), 4 * rows)


def interleave(size, parts):
    group = size // parts
    out_row = lax.broadcasted_iota(jnp.int32, (size, size), 0)
    col = lax.broadcasted_iota(jnp.int32, (size, size), 1)
    part = jnp.zeros((size, size), jnp.int32)
    for k in range(1, parts):
        part = part + (col >= k * group).astype(jnp.int32)
    return jnp.where(out_row == parts * (col - group * part) + part, 1.0, 0.0).astype(BF)


def interleave_out():
    out_row = lax.broadcasted_iota(jnp.int32, (32, 32), 0)
    col = lax.broadcasted_iota(jnp.int32, (32, 32), 1)
    part = (col >= 8).astype(jnp.int32) + (col >= 16).astype(jnp.int32)
    keep = (out_row == 3 * (col - 8 * part) + part) & (col < 24)
    return jnp.where(keep, 1.0, 0.0).astype(BF)


def dot_f32(a, b):
    return jnp.dot(a, b, preferred_element_type=F32)


def compact_out():
    out_row = lax.broadcasted_iota(jnp.int32, (192, 256), 0)
    col = lax.broadcasted_iota(jnp.int32, (192, 256), 1)
    group = jnp.zeros((192, 256), jnp.int32)
    for i in range(1, 8):
        group = group + (out_row >= 24 * i).astype(jnp.int32)
    return jnp.where(col == out_row + 8 * group, 1.0, 0.0).astype(BF)


def dot_nt(a, b):
    return lax.dot_general(a, b, (((1,), (1,)), ((), ())), preferred_element_type=F32)


def dot_tn(a, b):
    return lax.dot_general(a, b, (((0,), (0,)), ((), ())), preferred_element_type=F32)


def norm_vectors(small, norm):
    for i in range(6):
        at = 1152 + 192 * i
        norm[i : i + 1, :] = jnp.concatenate([small[t, 0:1, at : at + 192] for t in range(4)], axis=1)


def row_loop(body, step=128):
    @pl.loop(0, 512 // step)
    def _(i):
        body(pl.ds(pl.multiple_of(i * step, step), step))


def forward_kernel(
    master,
    slot_col,
    small_slot,
    id_col,
    id_row,
    x_in,
    gy_in,
    w_qkv,
    w_out,
    w_up,
    w_down,
    out_compact,
    small_out,
    x_out,
    gy_row,
    qkv_out,
    prob_out,
    att_out,
    n_one_out,
    h_out,
    act_out,
    pull_out,
    n_two_out,
    inv_out,
    row_out,
    pool_out,
    slots,
    canon,
    land,
    share,
    p_qkv,
    p_out,
    p_up,
    p_down,
    small_mine,
    small_land,
    small_total,
    small,
    norm,
    bias_qkv,
    v_qkv,
    v_out,
    v_compact,
    v_up,
    v_down,
    x_row,
    qkv,
    prob,
    att,
    n_one,
    h_wide,
    h_low,
    act,
    pull,
    total,
    inv,
    row_low,
    pool,
    send_sems,
    recv_sems,
    local_sems,
):
    place = Place()
    link = Sender(send_sems, recv_sems, local_sems)
    place.greet()
    whole = (w_qkv, w_out, w_up, w_down)
    held = (v_qkv, v_out, v_up, v_down)
    piece = (p_qkv, p_out, p_up, p_down)
    peers = (place.right, place.down, place.diag)
    mine_rows = pl.ds(pl.multiple_of(place.t * 128, 128), 128)
    tidy = []

    slots[place.c] = master[...].astype(BF)
    core_slots = link.send(slots.at[place.c], slots.at[place.c], place.core)
    x_moves = [
        link.send(x_in.at[place.ahead[k]], x_row.at[mine_rows], place.deep[k]) for k in (1, 2, 3)
    ]
    x_stay = link.copy(x_in.at[place.t], x_row.at[mine_rows])
    tidy.append(link.copy(gy_in.at[place.t], gy_row.at[mine_rows]))
    core_slots.wait_recv()

    pair_slots = slots[...].reshape(384, 2304)
    slot_id = lax.broadcasted_iota(jnp.int32, (96, 384), 1) + place.xy * 384
    shares = []
    order = [(1, place.right), (2, place.down), (3, place.diag), (0, None)]
    pick_small = jnp.where(small_slot[...] == slot_id[:8], 1.0, 0.0).astype(BF)
    small_mine[...] = dot_f32(pick_small, pair_slots)
    small_moves = [link.send(small_mine, small_land.at[j], peer) for j, peer in enumerate(peers)]
    for j, peer in order:
        at = place.xy if peer is None else peer[0] // 2
        wanted = slot_col[pl.ds(pl.multiple_of(at * 96, 96), 96), :]
        pick = jnp.where(wanted == slot_id, 1.0, 0.0).astype(BF)
        canon[j] = dot_f32(pick, pair_slots).astype(BF)
        if peer is not None:
            shares.append(link.send(canon.at[j], land.at[j - 1], peer))
    for move in shares + small_moves:
        move.wait_recv()
    share[...] = (
        canon[0].astype(F32) + land[0].astype(F32) + land[1].astype(F32) + land[2].astype(F32)
    )
    small_total[...] = small_mine[...] + small_land[0] + small_land[1] + small_land[2]

    three = interleave(96, 3)
    p_qkv[...] = dot_f32(
        interleave(96, 4),
        jnp.concatenate([share[64:88, 576 * r : 576 * r + 576] for r in range(4)], axis=0).astype(BF),
    ).astype(BF)
    out_parts = [share[88:96, 768 * k : 768 * k + 768] for k in range(3)]
    out_parts = out_parts + [jnp.zeros((8, 768), F32)]
    p_out[...] = dot_f32(interleave_out(), jnp.concatenate(out_parts, axis=0).astype(BF)).astype(BF)

    def spread_ffn():
        for at, ref in ((0, p_up), (32, p_down)):
            parts = [share[at : at + 32, 768 * k : 768 * k + 768] for k in range(3)]
            ref[...] = dot_f32(three, jnp.concatenate(parts, axis=0).astype(BF)).astype(BF)

    deep_moves, right_moves, down_moves, own_copies, core_moves, loads = {}, {}, {}, {}, {}, {}

    def deep_send(w):
        spot = whole[w].at[place.t, rows_of(place, WEIGHTS[w][1])]
        own_copies[w] = link.copy(piece[w], spot)
        deep_moves[w] = [link.send(piece[w], spot, place.deep[k]) for k in (1, 2, 3)]

    def plane_send(w, k):
        rows = WEIGHTS[w][1]
        spot = whole[w].at[place.behind[k], rows_of(place, rows)]
        src = piece[w] if k == 0 else spot
        if k:
            deep_moves[w][k - 1].wait_recv()
        right_moves[w, k] = link.send(src, spot, place.right)
        down_moves[w, k] = link.send(src, spot, place.down)

    def plane_pass(w, k):
        rows = WEIGHTS[w][1]
        half = rows // 2
        right_moves[w, k].wait_recv()
        down_moves[w, k].wait_recv()
        t = place.behind[k]
        right_at = place.c * (4 * rows) + (place.right[0] // 2) * rows
        down_at = place.c * (4 * rows) + (place.down[0] // 2) * rows
        first = whole[w].at[t, pl.ds(pl.multiple_of(right_at, 16), half)]
        second = whole[w].at[t, pl.ds(pl.multiple_of(down_at + half, 16), half)]
        right_moves[w, k, 1] = link.send(second, second, place.right)
        down_moves[w, k, 1] = link.send(first, first, place.down)

    def core_pass(w, k):
        if k == 0:
            own_copies[w].wait()
        right_moves[w, k, 1].wait_recv()
        down_moves[w, k, 1].wait_recv()
        spot = whole[w].at[place.behind[k], half_of(place, WEIGHTS[w][1])]
        core_moves[w, k] = link.send(spot, spot, place.core)

    def load(w, k):
        core_moves[w, k].wait_recv()
        t = place.behind[k]
        loads[w, k] = link.copy(whole[w].at[t], held[w].at[t])

    def qkv_step(k):
        loads[0, k].wait()
        t = place.behind[k]

        def body(rows):
            lin = dot_f32(x_row[rows, :], v_qkv[t]) + bias_qkv[t]
            qkv[t, rows, :] = lin.astype(BF)

        row_loop(body)

    def attention(t):
        def body(rows):
            allowed = id_col[rows, :] == id_row[...]
            parts = []
            for i in range(3):
                at = 64 * i
                scores = dot_nt(qkv[t, rows, at : at + 64], qkv[t, :, 192 + at : 256 + at]) * 0.125
                scores = jnp.where(allowed, scores, MASKED)
                weight = jnp.exp(scores - jnp.max(scores, axis=1, keepdims=True))
                weight = weight * (1.0 / jnp.sum(weight, axis=1, keepdims=True))
                low = weight.astype(BF)
                prob[3 * t + i, rows, :] = low
                parts.append(dot_f32(low, qkv[t, :, 384 + at : 448 + at]))
            att[t, rows, :] = jnp.concatenate(parts, axis=1).astype(BF)

        row_loop(body)
        tidy.append(link.copy(qkv.at[t], qkv_out.at[t]))
        tidy.append(link.copy(att.at[t], att_out.at[t]))
        tidy.append(link.copy(prob.at[pl.ds(3 * t, 3)], prob_out.at[pl.ds(3 * t, 3)]))

    def out_step():
        pick = compact_out()
        for k in range(4):
            loads[1, k].wait()
        for t in range(4):
            v_compact[t] = dot_f32(pick, v_out[t]).astype(BF)
        tidy.append(link.copy(v_compact, out_compact))

        def body(rows):
            z = x_row[rows, :].astype(F32) + norm[0:1, :]
            for t in range(4):
                z = z + dot_f32(att[t, rows, :], v_compact[t])
            normed, inverse = normalize(z)
            n_one[rows, :] = normed
            inv[0, rows, :] = inverse
            h = normed * norm[2:3, :] + norm[3:4, :]
            h_low[rows, :] = h.astype(BF)
            h_wide[rows, :] = h
            total[rows, :] = h + norm[1:2, :]

        row_loop(body)
        tidy.append(link.copy(n_one, n_one_out))
        tidy.append(link.copy(h_low, h_out))

    def up_step(k):
        loads[2, k].wait()
        t = place.behind[k]

        def body(rows):
            pre = dot_f32(h_low[rows, :], v_up[t]) + small[t, 0:1, 384:1152]
            below = 0.5 + 0.5 * lax.erf(pre * (0.5**0.5))
            act[t, rows, :] = (pre * below).astype(BF)
            slope = below + pre * (jnp.exp(-0.5 * pre * pre) * 0.3989422804014327)
            pull[t, rows, :] = slope.astype(BF)

        row_loop(body)
        tidy.append(link.copy(act.at[t], act_out.at[t]))
        tidy.append(link.copy(pull.at[t], pull_out.at[t]))

    def down_step(k):
        loads[3, k].wait()
        t = place.behind[k]

        def body(rows):
            total[rows, :] += dot_f32(act[t, rows, :], v_down[t])

        row_loop(body)

    def end_step():
        ids = lax.broadcasted_iota(jnp.int32, (SMAX, 512), 0)
        member = jnp.where(ids == id_row[...], 1.0, 0.0)
        count = jnp.maximum(jnp.sum(member, axis=1, keepdims=True), 1.0)

        def body(rows):
            normed, inverse = normalize(total[rows, :])
            inv[1, rows, :] = inverse
            out = normed * norm[4:5, :] + norm[5:6, :]
            total[rows, :] = normed
            h_wide[rows, :] = out
            row_low[rows, :] = out.astype(BF)

        row_loop(body)
        pool[...] = jnp.dot(member, h_wide[...], precision=exact_precision, preferred_element_type=F32) / count
        tidy.append(link.copy(total, n_two_out))
        tidy.append(link.copy(row_low, row_out))
        tidy.append(link.copy(pool, pool_out))
        tidy.append(link.copy(inv, inv_out))

    every = range(4)
    deep_send(0)
    deep_send(1)
    tidy.append(link.copy(small_total, small.at[place.t]))
    small_deep = [link.send(small_total, small.at[place.t], place.deep[k]) for k in (1, 2, 3)]
    plane_send(0, 0)
    plane_send(1, 0)
    spread_ffn()
    plane_send(2, 0)
    for k in (1, 2, 3):
        plane_send(0, k)
    deep_send(2)
    plane_send(3, 0)
    for k in every:
        plane_pass(0, k)
    for k in (1, 2, 3):
        plane_send(1, k)
    for move in small_deep:
        move.wait_recv()
    tidy.pop().wait()
    norm_vectors(small, norm)
    for t in every:
        bias_qkv[t] = jnp.concatenate(
            [small[t, 0:1, :192], jnp.zeros((1, 192), F32), small[t, 0:1, 192:384]], axis=1
        )
    tidy.append(link.copy(small, small_out))
    x_stay.wait()
    for move in x_moves:
        move.wait_recv()
    tidy.append(link.copy(x_row, x_out))
    for k in every:
        core_pass(0, k)
    for k in every:
        plane_pass(1, k)
    for k in every:
        load(0, k)
    for k in (1, 2, 3):
        plane_send(2, k)
    deep_send(3)
    gy_moves = [
        link.send(gy_in.at[place.ahead[k]], gy_row.at[mine_rows], place.deep[k]) for k in (1, 2, 3)
    ]
    for k in every:
        qkv_step(k)
    for k in every:
        core_pass(1, k)
    plane_pass(2, 0)
    plane_pass(2, 1)
    for k in every:
        load(1, k)
    attention(0)
    plane_pass(2, 2)
    plane_pass(2, 3)
    for k in (1, 2, 3):
        plane_send(3, k)
    attention(1)
    for k in every:
        core_pass(2, k)
    attention(2)
    for k in every:
        load(2, k)
    plane_pass(3, 0)
    attention(3)
    plane_pass(3, 1)
    out_step()
    plane_pass(3, 2)
    plane_pass(3, 3)
    core_pass(3, 0)
    up_step(0)
    core_pass(3, 1)
    load(3, 0)
    up_step(1)
    core_pass(3, 2)
    core_pass(3, 3)
    up_step(2)
    load(3, 1)
    up_step(3)
    load(3, 2)
    load(3, 3)
    for k in every:
        down_step(k)
    end_step()
    for move in gy_moves:
        move.wait_recv()
    for copy in tidy:
        copy.wait()
    link.finish()


def forward_call(master, slot_col, small_slot, id_col, id_row, x_in, gy_in):
    anywhere = pl.BlockSpec(memory_space=pl.ANY)
    vmem = pl.BlockSpec(memory_space=pltpu.VMEM)
    shape = jax.ShapeDtypeStruct
    outs = [
        ((4, 768, 576), BF),
        ((4, 256, 768), BF),
        ((4, 768, 768), BF),
        ((4, 768, 768), BF),
        ((4, 192, 768), BF),
        ((4, 8, 2304), F32),
        ((512, 768), BF),
        ((512, 768), BF),
        ((4, 512, 576), BF),
        ((12, 512, 512), BF),
        ((4, 512, 192), BF),
        ((512, 768), F32),
        ((512, 768), BF),
        ((4, 512, 768), BF),
        ((4, 512, 768), BF),
        ((512, 768), F32),
        ((2, 512, 1), F32),
        ((512, 768), BF),
        ((8, 768), F32),
    ]
    scratch = [
        ((2, 192, 2304), BF),
        ((4, 96, 2304), BF),
        ((3, 96, 2304), BF),
        ((96, 2304), F32),
        ((96, 576), BF),
        ((32, 768), BF),
        ((96, 768), BF),
        ((96, 768), BF),
        ((8, 2304), F32),
        ((3, 8, 2304), F32),
        ((8, 2304), F32),
        ((4, 8, 2304), F32),
        ((8, 768), F32),
        ((4, 1, 576), F32),
        ((4, 768, 576), BF),
        ((4, 256, 768), BF),
        ((4, 192, 768), BF),
        ((4, 768, 768), BF),
        ((4, 768, 768), BF),
        ((512, 768), BF),
        ((4, 512, 576), BF),
        ((12, 512, 512), BF),
        ((4, 512, 192), BF),
        ((512, 768), F32),
        ((512, 768), F32),
        ((512, 768), BF),
        ((4, 512, 768), BF),
        ((4, 512, 768), BF),
        ((512, 768), F32),
        ((2, 512, 1), F32),
        ((512, 768), BF),
        ((8, 768), F32),
    ]
    return pl.pallas_call(
        forward_kernel,
        out_shape=[shape(*o) for o in outs],
        in_specs=[vmem] * 5 + [anywhere] * 2,
        out_specs=[anywhere] * len(outs),
        scratch_shapes=[pltpu.VMEM(*s) for s in scratch]
        + [
            pltpu.SemaphoreType.DMA((112,)),
            pltpu.SemaphoreType.DMA((112,)),
            pltpu.SemaphoreType.DMA((64,)),
        ],
        compiler_params=pltpu.CompilerParams(
            collective_id=0, has_side_effects=True, vmem_limit_bytes=60 * MIB
        ),
        name="gather_and_forward",
    )(master, slot_col, small_slot, id_col, id_row, x_in, gy_in)


def add_into(total, other, rows, step):
    groups = other.shape[0]

    @pl.loop(0, groups * (rows // step))
    def _(i):
        g = i // (rows // step)
        at = pl.ds(pl.multiple_of((i % (rows // step)) * step, step), step)
        total[g, at, :] = total[g, at, :] + other[g, at, :]


def reduce_kernel(
    g_qkv,
    g_out,
    g_up,
    g_down,
    small_in,
    out_row,
    dx_row,
    pool_in,
    blocks,
    small_out,
    out_mine,
    dx_mine,
    pool_out,
    *scratch,
):
    sums, cores, lefts, tops, lefts_two, tops_two, deeps = (scratch[4 * i : 4 * i + 4] for i in range(7))
    share, share_low, small_sum, small_land, send_sems, recv_sems, local_sems = scratch[28:]
    place = Place()
    link = Sender(send_sems, recv_sems, local_sems)
    grads = (g_qkv, g_out, g_up, g_down)
    loads = {}
    order = (3, 2, 1, 0)
    for w in order:
        rows = WEIGHTS[w][1]
        loads[w] = link.copy(grads[w].at[:, half_of(place, rows)], sums[w])
    place.greet()
    t, x, y = place.t, place.x, place.y
    core_moves = {}
    for w in order:
        rows = WEIGHTS[w][1]
        other = pl.ds(pl.multiple_of((1 - place.c) * (4 * rows), 128), 4 * rows)
        core_moves[w] = link.send(grads[w].at[:, other], cores[w], place.core)
    moves = []
    stay = [link.copy(small_in.at[t], small_sum.at[pl.ds(0, 1)])]
    small_moves = [link.send(small_in.at[place.ahead[k]], small_land.at[k - 1], place.deep[k]) for k in (1, 2, 3)]
    for src, dst in ((out_row, out_mine), (dx_row, dx_mine)):
        stay.append(link.copy(src.at[pl.ds(pl.multiple_of(t * 128, 128), 128)], dst.at[t]))
        for k in (1, 2, 3):
            part = src.at[pl.ds(pl.multiple_of(place.ahead[k] * 128, 128), 128)]
            moves.append(link.send(part, dst.at[t], place.deep[k]))
    stay.append(link.copy(pool_in, pool_out.at[t]))
    for k in (1, 2, 3):
        moves.append(link.send(pool_in, pool_out.at[t], place.deep[k]))

    first, second, third = {}, {}, {}

    def chip_row(w, yy, xx, half):
        rows = WEIGHTS[w][1]
        at = pl.multiple_of((yy * 2 + xx) * rows + half * (rows // 2), 16)
        return sums[w].at[:, pl.ds(at, rows // 2)]

    def add(total, other):
        groups, rows, _ = other.shape
        add_into(total, other, rows, 16)

    def stage_core(w):
        loads[w].wait()
        core_moves[w].wait_recv()
        add_into(sums[w], cores[w], 4 * WEIGHTS[w][1], 32)
        first[w] = []
        for i in (0, 1):
            first[w].append(link.send(chip_row(w, i, 1 - x, 0), lefts[w].at[i], place.right))
            first[w].append(link.send(chip_row(w, 1 - y, i, 1), tops[w].at[i], place.down))

    def stage_plane(w):
        for move in first[w]:
            move.wait_recv()
        add(chip_row(w, 1 - y, x, 0), lefts[w].at[1 - y])
        add(chip_row(w, y, 1 - x, 1), tops[w].at[1 - x])
        second[w] = [
            link.send(chip_row(w, 1 - y, x, 0), lefts_two[w], place.down),
            link.send(chip_row(w, y, 1 - x, 1), tops_two[w], place.right),
        ]
        add(chip_row(w, y, x, 0), lefts[w].at[y])
        add(chip_row(w, y, x, 1), tops[w].at[x])

    def stage_deep(w):
        for move in second[w]:
            move.wait_recv()
        add(chip_row(w, y, x, 0), lefts_two[w])
        add(chip_row(w, y, x, 1), tops_two[w])
        rows = WEIGHTS[w][1]
        spot = pl.ds(pl.multiple_of(place.xy * rows, 16), rows)
        third[w] = [
            link.send(sums[w].at[place.ahead[k], spot], deeps[w].at[k - 1], place.deep[k])
            for k in (1, 2, 3)
        ]

    def stage_end(w):
        for move in third[w]:
            move.wait_recv()
        rows = WEIGHTS[w][1]
        spot = pl.ds(pl.multiple_of(place.xy * rows, 16), rows)
        total = sums[w][t, spot, :].astype(F32)
        for k in range(3):
            total = total + deeps[w][k].astype(F32)
        total = total.astype(BF)
        turned = (((0,), (0,)), ((), ()))
        if w == 0:
            parts = lax.dot_general(interleave(96, 4), total, turned, preferred_element_type=F32)
            share[64:88, :] = jnp.concatenate([parts[24 * r : 24 * r + 24] for r in range(4)], axis=1)
        elif w == 1:
            parts = lax.dot_general(interleave_out(), total, turned, preferred_element_type=F32)
            for k in range(3):
                share[88:96, 768 * k : 768 * k + 768] = parts[8 * k : 8 * k + 8]
        else:
            at = 0 if w == 2 else 32
            parts = lax.dot_general(interleave(96, 3), total, turned, preferred_element_type=F32)
            for k in range(3):
                share[at : at + 32, 768 * k : 768 * k + 768] = parts[32 * k : 32 * k + 32]

    stage_core(3)
    stage_core(2)
    stage_plane(3)
    stage_core(1)
    stage_core(0)
    stage_deep(3)
    stage_plane(2)
    stage_plane(1)
    stage_deep(2)
    stage_plane(0)
    stage_end(3)
    stage_deep(1)

    stay[0].wait()
    for move in small_moves:
        move.wait_recv()
    small_sum[0] = (
        small_sum[0] + small_land[0, 0] + small_land[1, 0] + small_land[2, 0]
    )
    stage_end(2)
    stage_deep(0)
    stage_end(1)
    for i, peer in enumerate((place.core, place.right, place.down)):
        move = link.send(
            small_sum.at[pl.ds(i, 1)], small_land.at[3 + i], peer
        )
        move.wait_recv()
        small_sum[i + 1] = small_sum[i] + small_land[3 + i, 0]
    stage_end(0)
    small_out[...] = small_sum[3]

    share_low[...] = share[...].astype(BF)
    dest = pl.ds(pl.multiple_of((place.c * 4 + place.xy) * 96, 96), 96)
    keep = link.copy(share_low, blocks.at[dest])
    last = [link.send(share_low, blocks.at[dest], peer) for peer in (place.diag, place.right, place.down)]
    keep.wait()
    for move in last:
        move.wait_recv()
    half = pl.ds(pl.multiple_of(place.c * 384, 384), 384)
    across = link.send(blocks.at[half], blocks.at[half], place.core)
    across.wait_recv()
    for move in moves:
        move.wait_recv()
    for copy in stay[1:]:
        copy.wait()
    link.finish()


def reduce_call(g_qkv, g_out, g_up, g_down, small_in, out_row, dx_row, pool_in):
    anywhere = pl.BlockSpec(memory_space=pl.ANY)
    vmem = pl.BlockSpec(memory_space=pltpu.VMEM)
    shape = jax.ShapeDtypeStruct
    sums = [pltpu.VMEM((4, 4 * rows, cols), BF) for cols, rows in WEIGHTS]
    halves = [pltpu.VMEM((2, 4, rows // 2, cols), BF) for cols, rows in WEIGHTS]
    singles = [pltpu.VMEM((4, rows // 2, cols), BF) for cols, rows in WEIGHTS]
    deeps = [pltpu.VMEM((3, rows, cols), BF) for cols, rows in WEIGHTS]
    return pl.pallas_call(
        reduce_kernel,
        out_shape=[
            shape((768, 2304), BF),
            shape((24, 128), F32),
            shape((4, 128, 768), BF),
            shape((4, 128, 768), BF),
            shape((4, 8, 768), F32),
        ],
        in_specs=[anywhere] * 8,
        out_specs=[anywhere, vmem, anywhere, anywhere, anywhere],
        scratch_shapes=sums
        + sums
        + halves
        + halves
        + singles
        + singles
        + deeps
        + [
            pltpu.VMEM((96, 2304), F32),
            pltpu.VMEM((96, 2304), BF),
            pltpu.VMEM((4, 24, 128), F32),
            pltpu.VMEM((6, 1, 24, 128), F32),
            pltpu.SemaphoreType.DMA((80,)),
            pltpu.SemaphoreType.DMA((80,)),
            pltpu.SemaphoreType.DMA((12,)),
        ],
        compiler_params=pltpu.CompilerParams(
            collective_id=1, has_side_effects=True, vmem_limit_bytes=56 * MIB
        ),
        name="reduce_gradients",
    )(g_qkv, g_out, g_up, g_down, small_in, out_row, dx_row, pool_in)


def local_rows(
    layer_input_rows,
    sentence_index_row,
    padding_mask,
    output_gradient,
    owner_rank,
    master_state,
    first_moment,
    second_moment,
):
    tensor_at = lax.axis_index("tensor")
    data_at = lax.axis_index("dp")
    per_owner = master_state.shape[1]
    block_len = master_state.shape[2]
    slot_of = slot_tables(owner_rank, per_owner)
    slot_order = jnp.concatenate(
        [
            slot_of[:256].reshape(2, 4, 32),
            slot_of[256:512].reshape(2, 4, 32),
            slot_of[512:704].reshape(2, 4, 24),
            slot_of[704:768].reshape(2, 4, 8),
        ],
        axis=2,
    ).reshape(768)
    core_order = lax.dynamic_slice_in_dim(slot_order, (data_at % 2) * 384, 384, 0)[:, None]
    small_slot = jnp.broadcast_to(slot_of[768], (8, 1))

    labels = lax.dynamic_index_in_dim(sentence_index_row, tensor_at, 0, keepdims=False)
    flags = lax.dynamic_index_in_dim(padding_mask, tensor_at, 0, keepdims=False)
    ids = jnp.where(flags == 1, labels, -1 - jnp.arange(flags.shape[0], dtype=jnp.int32))
    (
        w_qkv,
        _,
        w_up,
        w_down,
        w_out,
        small_all,
        x_row,
        gy_row,
        qkv,
        prob_low,
        attended,
        normed_one,
        h_low,
        act,
        pull,
        normed_two,
        inverse,
        out_row,
        pool_mean,
    ) = forward_call(
        master_state[0],
        core_order,
        small_slot,
        ids[:, None],
        ids[None],
        jnp.transpose(layer_input_rows, (1, 0, 2)),
        jnp.transpose(output_gradient, (1, 0, 2)),
    )
    norm_all = small_all[:, 0, 1152:].reshape(4, 6, 192).transpose(1, 0, 2).reshape(6, 768)
    gain_one, gain_two = norm_all[2], norm_all[4]
    qkv = qkv.reshape(4, 512, 3, 3, HEAD_DIM)
    queries, keys, values = (qkv[:, :, i] for i in range(3))
    scaling = HEAD_DIM ** (-0.5)
    prob_low = prob_low.reshape(4, 3, 512, 512)
    attn_prob = prob_low.astype(F32)
    inv_one, inv_two = inverse[0], inverse[1]
    w_out = w_out.reshape(768, 768)
    attended = attended.transpose(1, 0, 2).reshape(512, 768)

    grad_out = gy_row.astype(F32) * flags[:, None].astype(F32)
    d_gain_two = jnp.sum(grad_out * normed_two, axis=0)
    d_shift_two = jnp.sum(grad_out, axis=0)
    dz_two = norm_back(grad_out * gain_two, normed_two, inv_two)
    d_bias_down = jnp.sum(dz_two, axis=0)
    dz_two_low = dz_two.astype(BF)
    g_down = jnp.einsum("tlf,ld->tfd", act, dz_two_low, preferred_element_type=F32).astype(BF)
    d_act = jnp.einsum("ld,tfd->tlf", dz_two_low, w_down, preferred_element_type=F32)
    d_up = d_act * pull.astype(F32)
    d_bias_up = jnp.sum(d_up, axis=1)
    d_up_low = d_up.astype(BF)
    g_up = jnp.einsum("ld,tlf->tdf", h_low, d_up_low, preferred_element_type=F32).astype(BF)
    dh = dz_two + jnp.einsum("tlf,tdf->ld", d_up_low, w_up, preferred_element_type=F32)
    d_gain_one = jnp.sum(dh * normed_one, axis=0)
    d_shift_one = jnp.sum(dh, axis=0)
    dz_one = norm_back(dh * gain_one, normed_one, inv_one)
    d_bias_out = jnp.sum(dz_one, axis=0)
    dz_one_low = dz_one.astype(BF)
    g_out = jnp.einsum("le,ld->ed", attended, dz_one_low, preferred_element_type=F32).astype(BF)
    g_out = jnp.pad(g_out.reshape(4, 8, 24, 768), ((0, 0), (0, 0), (0, 8), (0, 0))).reshape(4, 256, 768)
    d_att = jnp.einsum("ld,ed->le", dz_one_low, w_out, preferred_element_type=F32).astype(BF)
    d_att = d_att.reshape(512, 4, 3, HEAD_DIM)
    d_prob = jnp.einsum("qthe,tkhe->thqk", d_att, values, preferred_element_type=F32)
    d_values = jnp.einsum("thqk,qthe->tkhe", prob_low, d_att, preferred_element_type=F32)
    inner = jnp.sum(d_prob * attn_prob, axis=-1, keepdims=True)
    d_scores = (attn_prob * (d_prob - inner)).astype(BF)
    d_queries = jnp.einsum("thqk,tkhe->tqhe", d_scores, keys, preferred_element_type=F32) * scaling
    d_keys = jnp.einsum("thqk,tqhe->tkhe", d_scores, queries, preferred_element_type=F32) * scaling
    d_bias_q = jnp.sum(d_queries, axis=1).reshape(4, 192)
    d_bias_v = jnp.sum(d_values, axis=1).reshape(4, 192)
    d_qkv = jnp.stack([d_queries, d_keys, d_values], axis=2).astype(BF).reshape(4, 512, 576)
    g_qkv = jnp.einsum("ld,tle->tde", x_row, d_qkv, preferred_element_type=F32).astype(BF)
    input_grad = dz_one + jnp.einsum("tle,tde->ld", d_qkv, w_qkv, preferred_element_type=F32)

    shared = jnp.stack([d_bias_out, d_bias_down, d_gain_one, d_shift_one, d_gain_two, d_shift_two])
    shared = shared.reshape(6, 4, 192).transpose(1, 0, 2).reshape(4, 1152)
    small_grads = jnp.concatenate([d_bias_q, d_bias_v, d_bias_up, shared], axis=1)
    small_grads = jnp.pad(small_grads.reshape(4, 1, 18, 128), ((0, 0), (0, 0), (0, 6), (0, 0)))
    blocks, small_sum, out_mine, dx_mine, pool_all = reduce_call(
        g_qkv,
        g_out,
        g_up,
        g_down,
        small_grads,
        out_row,
        input_grad.astype(BF),
        pool_mean,
    )
    small_row = small_sum[:18].reshape(block_len)
    norm_grads = small_row[1152:].reshape(6, 192)
    pooled = lax.dynamic_slice_in_dim(pool_all, tensor_at * 192, 192, 2)

    wanted = data_at * per_owner + jnp.arange(per_owner, dtype=jnp.int32)
    block_of, filled = slot_blocks(slot_of, wanted)
    pick = (slot_order[None, :] == wanted[:, None]).astype(BF)
    owned = dot_f32(pick, blocks)
    owned = jnp.where((wanted == slot_of[768])[:, None], small_row[None], owned)
    token_position = block_of[:, None] * block_len + jnp.arange(block_len, dtype=jnp.int32)[None, :]
    step_rate, decay_on = step_rates(token_position, MODEL_WIDTH, FF, 4)
    new_master, new_first, new_second = adamw(
        owned,
        first_moment[0],
        second_moment[0],
        master_state[0],
        step_rate,
        decay_on,
        filled[:, None],
    )
    return (
        jnp.transpose(out_mine, (1, 0, 2)).astype(F32),
        pooled,
        jnp.transpose(dx_mine, (1, 0, 2)).astype(F32),
        new_master[None],
        new_first[None],
        new_second[None],
        norm_grads,
    )


def solution(mesh):
    in_specs = (
        P("tensor", "dp", None),
        P("dp", None),
        P("dp", None),
        P("tensor", "dp", None),
        P(),
        P("tensor", "dp", None),
        P("tensor", "dp", None),
        P("tensor", "dp", None),
    )
    out_specs = (
        P("tensor", "dp", None),
        P("dp", None, "tensor"),
        P("tensor", "dp", None),
        P("tensor", "dp", None),
        P("tensor", "dp", None),
        P("tensor", "dp", None),
        P(None, "tensor"),
    )
    plain = mesh.shape["dp"] != 8 or mesh.shape["tensor"] != 4
    body = local_general if plain else local_rows
    return jax.shard_map(body, mesh=mesh, in_specs=in_specs, out_specs=out_specs, check_vma=False)
```

```python
import jax
import functools
import jax.numpy as jnp
from jax import lax
from jax.experimental import pallas as pl
from jax.experimental.pallas import tpu as pltpu
from jax.sharding import PartitionSpec as P

MODEL_WIDTH = 768
HEAD_DIM = 64
FF = 3072
SMAX = 8
STEP = 10


NORM_EPS = 1e-05
ADAM_EPS = 1e-08
BETA_ONE = 0.9
BETA_TWO = 0.999
DECAY_RATE = 0.01
MASKED = -1e30
exact_precision = lax.Precision.HIGHEST


def slot_tables(owner_rank, per_owner):
    ordinal = jnp.arange(owner_rank.shape[0], dtype=jnp.int32)
    same_owner = owner_rank[:, None] == owner_rank[None, :]
    earlier = ordinal[None, :] < ordinal[:, None]
    ranking = jnp.sum((same_owner & earlier).astype(jnp.int32), axis=1)
    return owner_rank * per_owner + ranking


def slot_blocks(slot_of, wanted):
    matches = slot_of[None, :] == wanted[:, None]
    filled = jnp.any(matches, axis=1)
    ordinal = jnp.arange(slot_of.shape[0], dtype=jnp.int32)
    block_of = jnp.sum(jnp.where(matches, ordinal[None, :], 0), axis=1)
    return (block_of, filled)


def step_rates(token_position, width, hidden, tensor_size):
    width_loc = width // tensor_size
    ffn_loc = hidden // tensor_size
    end_up = width * ffn_loc
    end_down = end_up + ffn_loc * width
    end_qkv = end_down + width * 3 * width_loc
    end_out = end_qkv + width_loc * width
    offset = token_position - end_out
    first_gain = (offset >= 4 * width_loc + ffn_loc) & (offset < 5 * width_loc + ffn_loc)
    second_gain = (offset >= 6 * width_loc + ffn_loc) & (offset < 7 * width_loc + ffn_loc)
    small_rate = jnp.where(first_gain | second_gain, 0.2, 0.1)
    step_rate = jnp.where(
        token_position < end_up,
        width ** (-0.5),
        jnp.where(
            token_position < end_down,
            hidden ** (-0.5),
            jnp.where(
                token_position < end_qkv,
                width ** (-0.5),
                jnp.where(token_position < end_out, 4.0 * width ** (-0.5), small_rate),
            ),
        ),
    )
    decay_on = (token_position < end_out).astype(jnp.float32)
    return (step_rate.astype(jnp.float32), decay_on)


def adamw(gradient, moment, square, weight, step_rate, decay_on, filled):
    new_moment = BETA_ONE * moment + (1.0 - BETA_ONE) * gradient
    new_square = BETA_TWO * square + (1.0 - BETA_TWO) * gradient * gradient
    unbiased = new_moment / (1.0 - BETA_ONE**STEP)
    divisor = jnp.sqrt(new_square / (1.0 - BETA_TWO**STEP)) + ADAM_EPS
    new_weight = weight - step_rate * (unbiased / divisor + DECAY_RATE * decay_on * weight)
    zeroed = jnp.zeros_like(weight)
    return (
        jnp.where(filled, new_weight, zeroed),
        jnp.where(filled, new_moment, zeroed),
        jnp.where(filled, new_square, zeroed),
    )


def normalize(values):
    centred = values - jnp.mean(values, axis=-1, keepdims=True)
    inv_dev = lax.rsqrt(jnp.mean(centred * centred, axis=-1, keepdims=True) + NORM_EPS)
    return (centred * inv_dev, inv_dev)


def norm_back(grad_scaled, normed, inv_dev):
    first_mean = jnp.mean(grad_scaled, axis=-1, keepdims=True)
    second_mean = jnp.mean(grad_scaled * normed, axis=-1, keepdims=True)
    return inv_dev * (grad_scaled - first_mean - normed * second_mean)


def allowed_pairs(sentence_labels, real_token_flags):
    row_len = sentence_labels.shape[-1]
    same_sent = sentence_labels[:, :, None] == sentence_labels[:, None, :]
    live = (real_token_flags[:, :, None] == 1) & (real_token_flags[:, None, :] == 1)
    diagonal = jnp.eye(row_len, dtype=bool)[None]
    return same_sent & live | diagonal


def masked_scores(queries, key_rows, allowed, scaling):
    scores = (
        jnp.einsum("qshe,kshe->shqk", queries, key_rows, preferred_element_type=jnp.float32)
        * scaling
    )
    return jnp.where(allowed[:, None], scores, MASKED)


def split_flat(flat_all, width_loc, ffn_loc):
    end_up = MODEL_WIDTH * ffn_loc
    end_down = end_up + ffn_loc * MODEL_WIDTH
    end_qkv = end_down + MODEL_WIDTH * 3 * width_loc
    end_out = end_qkv + width_loc * MODEL_WIDTH
    return (
        flat_all[:end_up].reshape(MODEL_WIDTH, ffn_loc),
        flat_all[end_up:end_down].reshape(ffn_loc, MODEL_WIDTH),
        flat_all[end_down:end_qkv].reshape(MODEL_WIDTH, 3 * width_loc),
        flat_all[end_qkv:end_out].reshape(width_loc, MODEL_WIDTH),
        flat_all[end_out:],
    )


def local_general(
    layer_input_rows,
    sentence_index_row,
    padding_mask,
    output_gradient,
    owner_rank,
    master_state,
    first_moment,
    second_moment,
):
    tensor_size = lax.axis_size("tensor")
    tensor_at = lax.axis_index("tensor")
    data_size = lax.axis_size("dp")
    data_at = lax.axis_index("dp")
    width_loc = MODEL_WIDTH // tensor_size
    ffn_loc = FF // tensor_size
    heads_loc = width_loc // HEAD_DIM
    quarter = layer_input_rows.shape[0]
    seq_count = layer_input_rows.shape[1]
    row_len = quarter * tensor_size
    per_owner = master_state.shape[1]
    block_len = master_state.shape[2]
    nblocks = owner_rank.shape[0]
    slot_of = slot_tables(owner_rank, per_owner)
    gathered = lax.all_gather(master_state.astype(jnp.bfloat16), "dp", axis=1, tiled=True)[0]
    flat_weights = gathered[slot_of].reshape(nblocks * block_len)
    up_weight, down_weight, w_qkv, w_out, small_part = split_flat(flat_weights, width_loc, ffn_loc)
    bias_q = small_part[:width_loc].astype(jnp.float32)
    bias_v = small_part[width_loc : 2 * width_loc].astype(jnp.float32)
    expand_bias = small_part[2 * width_loc : 2 * width_loc + ffn_loc].astype(jnp.float32)
    norm_parts = small_part[2 * width_loc + ffn_loc :].reshape(6, width_loc)
    full_rows, norm_whole = (
        lax.all_gather(layer_input_rows, "tensor", axis=0, tiled=True),
        lax.all_gather(norm_parts, "tensor", axis=1, tiled=True),
    )
    norm_all = norm_whole.astype(jnp.float32)
    bias_out, bias_down = (norm_all[0], norm_all[1])
    gain_one, shift_one, gain_two, shift_two = (norm_all[2], norm_all[3], norm_all[4], norm_all[5])
    qkv_lin = jnp.einsum("lsd,de->lse", full_rows, w_qkv, preferred_element_type=jnp.float32)
    bias_qkv = jnp.concatenate([bias_q, jnp.zeros((width_loc,), jnp.float32), bias_v])
    qkv = (qkv_lin + bias_qkv).astype(jnp.bfloat16)
    queries = qkv[:, :, :width_loc].reshape(row_len, seq_count, heads_loc, HEAD_DIM)
    key_rows = qkv[:, :, width_loc : 2 * width_loc].reshape(row_len, seq_count, heads_loc, HEAD_DIM)
    values = qkv[:, :, 2 * width_loc :].reshape(row_len, seq_count, heads_loc, HEAD_DIM)
    scaling = HEAD_DIM ** (-0.5)
    allowed = allowed_pairs(sentence_index_row, padding_mask)
    scores = masked_scores(queries, key_rows, allowed, scaling)
    row_peak = jnp.max(scores, axis=-1, keepdims=True)
    log_total = row_peak + jnp.log(jnp.sum(jnp.exp(scores - row_peak), axis=-1, keepdims=True))
    prob_low = jnp.exp(scores - log_total).astype(jnp.bfloat16)
    attended = jnp.einsum("shqk,kshe->qshe", prob_low, values, preferred_element_type=jnp.float32)
    attended = attended.astype(jnp.bfloat16).reshape(row_len, seq_count, width_loc)
    portion_rows = attended
    attn_rows = lax.psum_scatter(
        jnp.einsum("lse,ed->lsd", portion_rows, w_out, preferred_element_type=jnp.float32).astype(
            jnp.bfloat16
        ),
        "tensor",
        scatter_dimension=0,
        tiled=True,
    ).astype(jnp.float32)
    z_one = layer_input_rows.astype(jnp.float32) + attn_rows + bias_out
    normed_one, inv_one = normalize(z_one)
    h_mine = normed_one * gain_one + shift_one
    hidden_narrow_whole = lax.all_gather(h_mine.astype(jnp.bfloat16), "tensor", axis=0, tiled=True)
    up_pre = (
        jnp.einsum(
            "wer,rb->web", hidden_narrow_whole, up_weight, preferred_element_type=jnp.float32
        )
        + expand_bias
    )
    activation_narrow = jax.nn.gelu(up_pre, approximate=False).astype(jnp.bfloat16)
    portion_rows = activation_narrow
    down_rows = lax.psum_scatter(
        jnp.einsum(
            "aij,jb->aib", portion_rows, down_weight, preferred_element_type=jnp.float32
        ).astype(jnp.bfloat16),
        "tensor",
        scatter_dimension=0,
        tiled=True,
    ).astype(jnp.float32)
    z_two = h_mine + down_rows + bias_down
    normed_two, inv_two = normalize(z_two)
    layer_out = normed_two * gain_two + shift_two
    seg_mine = lax.dynamic_slice_in_dim(sentence_index_row, tensor_at * quarter, quarter, 1)
    valid_mine = lax.dynamic_slice_in_dim(padding_mask, tensor_at * quarter, quarter, 1)
    sent_ids = jnp.arange(SMAX, dtype=jnp.int32)
    onehot_mine = (
        (seg_mine[:, :, None] == sent_ids[None, None, :]) & (valid_mine[:, :, None] == 1)
    ).astype(jnp.float32)
    pool_part = jnp.einsum("slc,lsd->scd", onehot_mine, layer_out, precision=exact_precision)
    onehot_full = (
        (sentence_index_row[:, :, None] == sent_ids[None, None, :])
        & (padding_mask[:, :, None] == 1)
    ).astype(jnp.float32)
    counts = jnp.sum(onehot_full, axis=1)
    grad_out = output_gradient.astype(jnp.float32) * valid_mine.T[:, :, None].astype(jnp.float32)
    d_gain_two = jnp.sum(grad_out * normed_two, axis=(0, 1))
    d_shift_two = jnp.sum(grad_out, axis=(0, 1))
    dz_two = norm_back(grad_out * gain_two, normed_two, inv_two)
    d_bias_down = jnp.sum(dz_two, axis=(0, 1))
    second_sum_gradient_wide = lax.all_gather(
        dz_two.astype(jnp.bfloat16), "tensor", axis=0, tiled=True
    )
    down_weight_gradient = jnp.einsum(
        "ipo,ipr->or",
        activation_narrow,
        second_sum_gradient_wide,
        preferred_element_type=jnp.float32,
    )
    activation_gradient = jnp.einsum(
        "ugp,jp->ugj", second_sum_gradient_wide, down_weight, preferred_element_type=jnp.float32
    )
    gelu_pull = jax.vjp(lambda pre_act: jax.nn.gelu(pre_act, approximate=False), up_pre)[1]
    d_up = gelu_pull(activation_gradient)[0]
    d_bias_up = jnp.sum(d_up, axis=(0, 1))
    expand_gradient_narrow = d_up.astype(jnp.bfloat16)
    up_weight_gradient = jnp.einsum(
        "iux,iuy->xy",
        hidden_narrow_whole,
        expand_gradient_narrow,
        preferred_element_type=jnp.float32,
    )
    portion_rows = expand_gradient_narrow
    dh_rows = lax.psum_scatter(
        jnp.einsum(
            "uih,vh->uiv", portion_rows, up_weight, preferred_element_type=jnp.float32
        ).astype(jnp.bfloat16),
        "tensor",
        scatter_dimension=0,
        tiled=True,
    ).astype(jnp.float32)
    dh_mine = dz_two + dh_rows
    d_gain_one = jnp.sum(dh_mine * normed_one, axis=(0, 1))
    d_shift_one = jnp.sum(dh_mine, axis=(0, 1))
    dz_one = norm_back(dh_mine * gain_one, normed_one, inv_one)
    d_bias_out = jnp.sum(dz_one, axis=(0, 1))
    dz_one_full = lax.all_gather(dz_one.astype(jnp.bfloat16), "tensor", axis=0, tiled=True)
    d_w_out = jnp.einsum("lse,lsd->ed", attended, dz_one_full, preferred_element_type=jnp.float32)
    d_attended = jnp.einsum("lsd,ed->lse", dz_one_full, w_out, preferred_element_type=jnp.float32)
    d_attended = d_attended.astype(jnp.bfloat16).reshape(row_len, seq_count, heads_loc, HEAD_DIM)
    scores_again = masked_scores(queries, key_rows, allowed, scaling)
    attn_prob = jnp.exp(scores_again - log_total)
    prob_again = attn_prob.astype(jnp.bfloat16)
    d_prob = jnp.einsum("qshe,kshe->shqk", d_attended, values, preferred_element_type=jnp.float32)
    d_values = jnp.einsum(
        "shqk,qshe->kshe", prob_again, d_attended, preferred_element_type=jnp.float32
    )
    inner = jnp.sum(d_prob * attn_prob, axis=-1, keepdims=True)
    d_scores = (attn_prob * (d_prob - inner)).astype(jnp.bfloat16)
    d_queries = (
        jnp.einsum("shqk,kshe->qshe", d_scores, key_rows, preferred_element_type=jnp.float32)
        * scaling
    )
    d_keys = (
        jnp.einsum("shqk,qshe->kshe", d_scores, queries, preferred_element_type=jnp.float32)
        * scaling
    )
    d_bias_q = jnp.sum(d_queries, axis=(0, 1)).reshape(width_loc)
    d_bias_v = jnp.sum(d_values, axis=(0, 1)).reshape(width_loc)
    d_qkv_low = jnp.concatenate(
        [
            d_queries.reshape(row_len, seq_count, width_loc),
            d_keys.reshape(row_len, seq_count, width_loc),
            d_values.reshape(row_len, seq_count, width_loc),
        ],
        axis=2,
    ).astype(jnp.bfloat16)
    d_w_qkv = jnp.einsum("lsd,lse->de", full_rows, d_qkv_low, preferred_element_type=jnp.float32)
    portion_rows = d_qkv_low
    dx_rows = lax.psum_scatter(
        jnp.einsum("lse,de->lsd", portion_rows, w_qkv, preferred_element_type=jnp.float32).astype(
            jnp.bfloat16
        ),
        "tensor",
        scatter_dimension=0,
        tiled=True,
    ).astype(jnp.float32)
    input_grad = dz_one + dx_rows
    shared_grads = jnp.stack(
        [d_bias_out, d_bias_down, d_gain_one, d_shift_one, d_gain_two, d_shift_two]
    )[None]
    pool_sum, shared_sum = (
        lax.psum_scatter(
            pool_part.astype(jnp.bfloat16), "tensor", scatter_dimension=2, tiled=True
        ).astype(jnp.float32),
        lax.psum_scatter(
            shared_grads.astype(jnp.bfloat16), "tensor", scatter_dimension=2, tiled=True
        ).astype(jnp.float32),
    )
    pooled_mean = pool_sum / jnp.maximum(counts, 1.0)[:, :, None]
    flat_grads = jnp.concatenate(
        [
            up_weight_gradient.reshape(-1),
            down_weight_gradient.reshape(-1),
            d_w_qkv.reshape(-1),
            d_w_out.reshape(-1),
            d_bias_q,
            d_bias_v,
            d_bias_up,
            shared_sum.reshape(-1),
        ]
    )
    grad_blocks = flat_grads.reshape(nblocks, block_len)
    wanted = data_at * per_owner + jnp.arange(per_owner, dtype=jnp.int32)
    block_of, filled = slot_blocks(slot_of, wanted)
    slot_grads = (
        jnp.zeros((data_size * per_owner, block_len), jnp.float32).at[slot_of].set(grad_blocks)
    )
    owned_grads = lax.psum_scatter(slot_grads, "dp", scatter_dimension=0, tiled=True)
    norm_grads = lax.psum(shared_sum[0], "dp")
    token_position = block_of[:, None] * block_len + jnp.arange(block_len, dtype=jnp.int32)[None, :]
    step_rate, decay_on = step_rates(token_position, MODEL_WIDTH, FF, tensor_size)
    new_master, new_first, new_second = adamw(
        owned_grads,
        first_moment[0],
        second_moment[0],
        master_state[0],
        step_rate,
        decay_on,
        filled[:, None],
    )
    return (
        layer_out,
        pooled_mean,
        input_grad,
        new_master[None],
        new_first[None],
        new_second[None],
        norm_grads,
    )


MESH = pl.DeviceIdType.MESH
BF = jnp.bfloat16
F32 = jnp.float32
WEIGHTS = ((576, 96), (768, 32), (768, 96), (768, 96))
MIB = 2**20


class Place:
    def __init__(self):
        d = lax.axis_index("dp")
        self.t = lax.axis_index("tensor")
        self.c = d % 2
        self.x = (d // 2) % 2
        self.y = d // 4
        self.xy = d // 2
        self.core = (d + 1 - 2 * self.c, self.t)
        self.right = (d + 2 - 4 * self.x, self.t)
        self.down = (d + 4 - 8 * self.y, self.t)
        self.diag = (d + 6 - 4 * self.x - 8 * self.y, self.t)
        self.deep = [None] + [(d, (self.t + k) % 4) for k in (1, 2, 3)]
        self.ahead = [(self.t + k) % 4 for k in range(4)]
        self.behind = [(self.t + 4 - k) % 4 for k in range(4)]

    def greet(self):
        barrier = pltpu.get_barrier_semaphore()
        peers = [self.core, self.right, self.down, self.diag] + self.deep[1:]
        for peer in peers:
            pl.semaphore_signal(barrier, inc=1, device_id=peer, device_id_type=MESH)
        pl.semaphore_wait(barrier, len(peers))


class Sender:
    def __init__(self, send_sems, recv_sems, local_sems):
        self.sems = (send_sems, recv_sems, local_sems)
        self.used = 0
        self.used_local = 0
        self.open = []

    def send(self, src, dst, peer):
        i = self.used
        self.used += 1
        copy = pltpu.make_async_remote_copy(
            src_ref=src,
            dst_ref=dst,
            send_sem=self.sems[0].at[i],
            recv_sem=self.sems[1].at[i],
            device_id=peer,
            device_id_type=MESH,
        )
        copy.start()
        self.open.append(copy)
        return copy

    def copy(self, src, dst):
        i = self.used_local
        self.used_local += 1
        copy = pltpu.make_async_copy(src, dst, self.sems[2].at[i])
        copy.start()
        return copy

    def sent(self, copy):
        copy.wait_send()
        self.open = [other for other in self.open if other is not copy]

    def finish(self):
        for copy in self.open:
            copy.wait_send()


def rows_of(place, rows, at=None):
    at = place.xy if at is None else at
    return pl.ds(pl.multiple_of(place.c * (4 * rows) + at * rows, 32), rows)


def half_of(place, rows):
    return pl.ds(pl.multiple_of(place.c * (4 * rows), 128), 4 * rows)


def interleave(size, parts):
    group = size // parts
    out_row = lax.broadcasted_iota(jnp.int32, (size, size), 0)
    col = lax.broadcasted_iota(jnp.int32, (size, size), 1)
    part = jnp.zeros((size, size), jnp.int32)
    for k in range(1, parts):
        part = part + (col >= k * group).astype(jnp.int32)
    return jnp.where(out_row == parts * (col - group * part) + part, 1.0, 0.0).astype(BF)


def interleave_out():
    out_row = lax.broadcasted_iota(jnp.int32, (32, 32), 0)
    col = lax.broadcasted_iota(jnp.int32, (32, 32), 1)
    part = (col >= 8).astype(jnp.int32) + (col >= 16).astype(jnp.int32)
    keep = (out_row == 3 * (col - 8 * part) + part) & (col < 24)
    return jnp.where(keep, 1.0, 0.0).astype(BF)


def dot_f32(a, b):
    return jnp.dot(a, b, preferred_element_type=F32)


def compact_out():
    out_row = lax.broadcasted_iota(jnp.int32, (192, 256), 0)
    col = lax.broadcasted_iota(jnp.int32, (192, 256), 1)
    group = jnp.zeros((192, 256), jnp.int32)
    for i in range(1, 8):
        group = group + (out_row >= 24 * i).astype(jnp.int32)
    return jnp.where(col == out_row + 8 * group, 1.0, 0.0).astype(BF)


def dot_nt(a, b):
    return lax.dot_general(a, b, (((1,), (1,)), ((), ())), preferred_element_type=F32)


def dot_tn(a, b):
    return lax.dot_general(a, b, (((0,), (0,)), ((), ())), preferred_element_type=F32)


def norm_vectors(small, norm):
    for i in range(6):
        at = 1152 + 192 * i
        norm[i : i + 1, :] = jnp.concatenate([small[t, 0:1, at : at + 192] for t in range(4)], axis=1)


def row_loop(body, step=128):
    @pl.loop(0, 512 // step)
    def _(i):
        body(pl.ds(pl.multiple_of(i * step, step), step))


def forward_kernel(
    master,
    slot_col,
    small_slot,
    id_col,
    id_row,
    x_in,
    gy_in,
    w_qkv,
    w_out,
    w_up,
    w_down,
    out_compact,
    small_out,
    x_out,
    gy_row,
    qkv_out,
    prob_out,
    att_out,
    n_one_out,
    h_out,
    act_out,
    pull_out,
    n_two_out,
    inv_out,
    row_out,
    pool_out,
    slots,
    canon,
    land,
    share,
    p_qkv,
    p_out,
    p_up,
    p_down,
    small_mine,
    small_land,
    small_total,
    small,
    norm,
    bias_qkv,
    v_qkv,
    v_out,
    v_compact,
    v_up,
    v_down,
    x_row,
    qkv,
    prob,
    att,
    n_one,
    h_wide,
    h_low,
    act,
    pull,
    total,
    inv,
    row_low,
    pool,
    send_sems,
    recv_sems,
    local_sems,
):
    place = Place()
    link = Sender(send_sems, recv_sems, local_sems)
    place.greet()
    whole = (w_qkv, w_out, w_up, w_down)
    held = (v_qkv, v_out, v_up, v_down)
    piece = (p_qkv, p_out, p_up, p_down)
    peers = (place.right, place.down, place.diag)
    mine_rows = pl.ds(pl.multiple_of(place.t * 128, 128), 128)
    tidy = []

    slots[place.c] = master[...].astype(BF)
    core_slots = link.send(slots.at[place.c], slots.at[place.c], place.core)
    x_moves = [
        link.send(x_in.at[place.ahead[k]], x_row.at[mine_rows], place.deep[k]) for k in (1, 2, 3)
    ]
    x_stay = link.copy(x_in.at[place.t], x_row.at[mine_rows])
    tidy.append(link.copy(gy_in.at[place.t], gy_row.at[mine_rows]))
    core_slots.wait_recv()

    pair_slots = slots[...].reshape(384, 2304)
    slot_id = lax.broadcasted_iota(jnp.int32, (96, 384), 1) + place.xy * 384
    shares = []
    order = [(1, place.right), (2, place.down), (3, place.diag), (0, None)]
    pick_small = jnp.where(small_slot[...] == slot_id[:8], 1.0, 0.0).astype(BF)
    small_mine[...] = dot_f32(pick_small, pair_slots)
    small_moves = [link.send(small_mine, small_land.at[j], peer) for j, peer in enumerate(peers)]
    for j, peer in order:
        at = place.xy if peer is None else peer[0] // 2
        wanted = slot_col[pl.ds(pl.multiple_of(at * 96, 96), 96), :]
        pick = jnp.where(wanted == slot_id, 1.0, 0.0).astype(BF)
        canon[j] = dot_f32(pick, pair_slots).astype(BF)
        if peer is not None:
            shares.append(link.send(canon.at[j], land.at[j - 1], peer))
    for move in shares + small_moves:
        move.wait_recv()
    share[...] = (
        canon[0].astype(F32) + land[0].astype(F32) + land[1].astype(F32) + land[2].astype(F32)
    )
    small_total[...] = small_mine[...] + small_land[0] + small_land[1] + small_land[2]

    three = interleave(96, 3)
    p_qkv[...] = dot_f32(
        interleave(96, 4),
        jnp.concatenate([share[64:88, 576 * r : 576 * r + 576] for r in range(4)], axis=0).astype(BF),
    ).astype(BF)
    out_parts = [share[88:96, 768 * k : 768 * k + 768] for k in range(3)]
    out_parts = out_parts + [jnp.zeros((8, 768), F32)]
    p_out[...] = dot_f32(interleave_out(), jnp.concatenate(out_parts, axis=0).astype(BF)).astype(BF)

    def spread_ffn():
        for at, ref in ((0, p_up), (32, p_down)):
            parts = [share[at : at + 32, 768 * k : 768 * k + 768] for k in range(3)]
            ref[...] = dot_f32(three, jnp.concatenate(parts, axis=0).astype(BF)).astype(BF)

    deep_moves, right_moves, down_moves, own_copies, core_moves, loads = {}, {}, {}, {}, {}, {}

    def deep_send(w):
        spot = whole[w].at[place.t, rows_of(place, WEIGHTS[w][1])]
        own_copies[w] = link.copy(piece[w], spot)
        deep_moves[w] = [link.send(piece[w], spot, place.deep[k]) for k in (1, 2, 3)]

    def plane_send(w, k):
        rows = WEIGHTS[w][1]
        spot = whole[w].at[place.behind[k], rows_of(place, rows)]
        src = piece[w] if k == 0 else spot
        if k:
            deep_moves[w][k - 1].wait_recv()
        right_moves[w, k] = link.send(src, spot, place.right)
        down_moves[w, k] = link.send(src, spot, place.down)

    def plane_pass(w, k):
        rows = WEIGHTS[w][1]
        half = rows // 2
        right_moves[w, k].wait_recv()
        down_moves[w, k].wait_recv()
        t = place.behind[k]
        right_at = place.c * (4 * rows) + (place.right[0] // 2) * rows
        down_at = place.c * (4 * rows) + (place.down[0] // 2) * rows
        first = whole[w].at[t, pl.ds(pl.multiple_of(right_at, 16), half)]
        second = whole[w].at[t, pl.ds(pl.multiple_of(down_at + half, 16), half)]
        right_moves[w, k, 1] = link.send(second, second, place.right)
        down_moves[w, k, 1] = link.send(first, first, place.down)

    def core_pass(w, k):
        if k == 0:
            own_copies[w].wait()
        right_moves[w, k, 1].wait_recv()
        down_moves[w, k, 1].wait_recv()
        spot = whole[w].at[place.behind[k], half_of(place, WEIGHTS[w][1])]
        core_moves[w, k] = link.send(spot, spot, place.core)

    def load(w, k):
        core_moves[w, k].wait_recv()
        t = place.behind[k]
        loads[w, k] = link.copy(whole[w].at[t], held[w].at[t])

    def qkv_step(k):
        loads[0, k].wait()
        t = place.behind[k]

        def body(rows):
            lin = dot_f32(x_row[rows, :], v_qkv[t]) + bias_qkv[t]
            qkv[t, rows, :] = lin.astype(BF)

        row_loop(body)

    def attention(t):
        def body(rows):
            allowed = id_col[rows, :] == id_row[...]
            parts = []
            for i in range(3):
                at = 64 * i
                scores = dot_nt(qkv[t, rows, at : at + 64], qkv[t, :, 192 + at : 256 + at]) * 0.125
                scores = jnp.where(allowed, scores, MASKED)
                weight = jnp.exp(scores - jnp.max(scores, axis=1, keepdims=True))
                weight = weight * (1.0 / jnp.sum(weight, axis=1, keepdims=True))
                low = weight.astype(BF)
                prob[3 * t + i, rows, :] = low
                parts.append(dot_f32(low, qkv[t, :, 384 + at : 448 + at]))
            att[t, rows, :] = jnp.concatenate(parts, axis=1).astype(BF)

        row_loop(body)
        tidy.append(link.copy(qkv.at[t], qkv_out.at[t]))
        tidy.append(link.copy(att.at[t], att_out.at[t]))
        tidy.append(link.copy(prob.at[pl.ds(3 * t, 3)], prob_out.at[pl.ds(3 * t, 3)]))

    def out_step():
        pick = compact_out()
        for k in range(4):
            loads[1, k].wait()
        for t in range(4):
            v_compact[t] = dot_f32(pick, v_out[t]).astype(BF)
        tidy.append(link.copy(v_compact, out_compact))

        def body(rows):
            z = x_row[rows, :].astype(F32) + norm[0:1, :]
            for t in range(4):
                z = z + dot_f32(att[t, rows, :], v_compact[t])
            normed, inverse = normalize(z)
            n_one[rows, :] = normed
            inv[0, rows, :] = inverse
            h = normed * norm[2:3, :] + norm[3:4, :]
            h_low[rows, :] = h.astype(BF)
            h_wide[rows, :] = h
            total[rows, :] = h + norm[1:2, :]

        row_loop(body)
        tidy.append(link.copy(n_one, n_one_out))
        tidy.append(link.copy(h_low, h_out))

    def up_step(k):
        loads[2, k].wait()
        t = place.behind[k]

        def body(rows):
            pre = dot_f32(h_low[rows, :], v_up[t]) + small[t, 0:1, 384:1152]
            below = 0.5 + 0.5 * lax.erf(pre * (0.5**0.5))
            act[t, rows, :] = (pre * below).astype(BF)
            slope = below + pre * (jnp.exp(-0.5 * pre * pre) * 0.3989422804014327)
            pull[t, rows, :] = slope.astype(BF)

        row_loop(body)
        tidy.append(link.copy(act.at[t], act_out.at[t]))
        tidy.append(link.copy(pull.at[t], pull_out.at[t]))

    def down_step(k):
        loads[3, k].wait()
        t = place.behind[k]

        def body(rows):
            total[rows, :] += dot_f32(act[t, rows, :], v_down[t])

        row_loop(body)

    def end_step():
        ids = lax.broadcasted_iota(jnp.int32, (SMAX, 512), 0)
        member = jnp.where(ids == id_row[...], 1.0, 0.0)
        count = jnp.maximum(jnp.sum(member, axis=1, keepdims=True), 1.0)

        def body(rows):
            normed, inverse = normalize(total[rows, :])
            inv[1, rows, :] = inverse
            out = normed * norm[4:5, :] + norm[5:6, :]
            total[rows, :] = normed
            h_wide[rows, :] = out
            row_low[rows, :] = out.astype(BF)

        row_loop(body)
        pool[...] = jnp.dot(member, h_wide[...], precision=exact_precision, preferred_element_type=F32) / count
        tidy.append(link.copy(total, n_two_out))
        tidy.append(link.copy(row_low, row_out))
        tidy.append(link.copy(pool, pool_out))
        tidy.append(link.copy(inv, inv_out))

    every = range(4)
    deep_send(0)
    deep_send(1)
    tidy.append(link.copy(small_total, small.at[place.t]))
    small_deep = [link.send(small_total, small.at[place.t], place.deep[k]) for k in (1, 2, 3)]
    plane_send(0, 0)
    plane_send(1, 0)
    spread_ffn()
    plane_send(2, 0)
    for k in (1, 2, 3):
        plane_send(0, k)
    deep_send(2)
    plane_send(3, 0)
    for k in every:
        plane_pass(0, k)
    for k in (1, 2, 3):
        plane_send(1, k)
    for move in small_deep:
        move.wait_recv()
    tidy.pop().wait()
    norm_vectors(small, norm)
    for t in every:
        bias_qkv[t] = jnp.concatenate(
            [small[t, 0:1, :192], jnp.zeros((1, 192), F32), small[t, 0:1, 192:384]], axis=1
        )
    tidy.append(link.copy(small, small_out))
    x_stay.wait()
    for move in x_moves:
        move.wait_recv()
    tidy.append(link.copy(x_row, x_out))
    for k in every:
        core_pass(0, k)
    for k in every:
        plane_pass(1, k)
    for k in every:
        load(0, k)
    for k in (1, 2, 3):
        plane_send(2, k)
    deep_send(3)
    gy_moves = [
        link.send(gy_in.at[place.ahead[k]], gy_row.at[mine_rows], place.deep[k]) for k in (1, 2, 3)
    ]
    for k in every:
        qkv_step(k)
    for k in every:
        core_pass(1, k)
    plane_pass(2, 0)
    plane_pass(2, 1)
    for k in every:
        load(1, k)
    attention(0)
    plane_pass(2, 2)
    plane_pass(2, 3)
    for k in (1, 2, 3):
        plane_send(3, k)
    attention(1)
    for k in every:
        core_pass(2, k)
    attention(2)
    for k in every:
        load(2, k)
    plane_pass(3, 0)
    attention(3)
    plane_pass(3, 1)
    out_step()
    plane_pass(3, 2)
    plane_pass(3, 3)
    core_pass(3, 0)
    up_step(0)
    core_pass(3, 1)
    load(3, 0)
    up_step(1)
    core_pass(3, 2)
    core_pass(3, 3)
    up_step(2)
    load(3, 1)
    up_step(3)
    load(3, 2)
    load(3, 3)
    for k in every:
        down_step(k)
    end_step()
    for move in gy_moves:
        move.wait_recv()
    for copy in tidy:
        copy.wait()
    link.finish()


def forward_call(master, slot_col, small_slot, id_col, id_row, x_in, gy_in):
    anywhere = pl.BlockSpec(memory_space=pl.ANY)
    vmem = pl.BlockSpec(memory_space=pltpu.VMEM)
    shape = jax.ShapeDtypeStruct
    outs = [
        ((4, 768, 576), BF),
        ((4, 256, 768), BF),
        ((4, 768, 768), BF),
        ((4, 768, 768), BF),
        ((4, 192, 768), BF),
        ((4, 8, 2304), F32),
        ((512, 768), BF),
        ((512, 768), BF),
        ((4, 512, 576), BF),
        ((12, 512, 512), BF),
        ((4, 512, 192), BF),
        ((512, 768), F32),
        ((512, 768), BF),
        ((4, 512, 768), BF),
        ((4, 512, 768), BF),
        ((512, 768), F32),
        ((2, 512, 1), F32),
        ((512, 768), BF),
        ((8, 768), F32),
    ]
    scratch = [
        ((2, 192, 2304), BF),
        ((4, 96, 2304), BF),
        ((3, 96, 2304), BF),
        ((96, 2304), F32),
        ((96, 576), BF),
        ((32, 768), BF),
        ((96, 768), BF),
        ((96, 768), BF),
        ((8, 2304), F32),
        ((3, 8, 2304), F32),
        ((8, 2304), F32),
        ((4, 8, 2304), F32),
        ((8, 768), F32),
        ((4, 1, 576), F32),
        ((4, 768, 576), BF),
        ((4, 256, 768), BF),
        ((4, 192, 768), BF),
        ((4, 768, 768), BF),
        ((4, 768, 768), BF),
        ((512, 768), BF),
        ((4, 512, 576), BF),
        ((12, 512, 512), BF),
        ((4, 512, 192), BF),
        ((512, 768), F32),
        ((512, 768), F32),
        ((512, 768), BF),
        ((4, 512, 768), BF),
        ((4, 512, 768), BF),
        ((512, 768), F32),
        ((2, 512, 1), F32),
        ((512, 768), BF),
        ((8, 768), F32),
    ]
    return pl.pallas_call(
        forward_kernel,
        out_shape=[shape(*o) for o in outs],
        in_specs=[vmem] * 5 + [anywhere] * 2,
        out_specs=[anywhere] * len(outs),
        scratch_shapes=[pltpu.VMEM(*s) for s in scratch]
        + [
            pltpu.SemaphoreType.DMA((112,)),
            pltpu.SemaphoreType.DMA((112,)),
            pltpu.SemaphoreType.DMA((64,)),
        ],
        compiler_params=pltpu.CompilerParams(
            collective_id=0, has_side_effects=True, vmem_limit_bytes=60 * MIB
        ),
        name="gather_and_forward",
    )(master, slot_col, small_slot, id_col, id_row, x_in, gy_in)


def backward_kernel(
    flag_col,
    out_row,
    pool_in,
    gy_in,
    n_two_in,
    inv_in,
    small_in,
    act_in,
    pull_in,
    w_down,
    w_up,
    h_in,
    n_one_in,
    att_in,
    w_out,
    qkv_in,
    prob_in,
    w_qkv,
    x_in,
    blocks,
    small_out,
    out_mine,
    dx_mine,
    pool_out,
    *scratch,
):
    sums, cores, lefts, tops, lefts_two, tops_two, deeps = (scratch[4 * i : 4 * i + 4] for i in range(7))
    (
        ring,
        ring_narrow,
        share,
        share_low,
        small_grad,
        small_land,
        small,
        norm,
        gy,
        normed,
        inv,
        act,
        pull,
        v_down,
        v_up,
        h_low,
        att,
        v_out,
        qkv,
        prob,
        v_qkv,
        x_row,
        wide,
        low,
        total,
        d_up,
        d_att,
        d_qkv,
        turned,
        go,
        reds,
        red_up,
        red_qv,
        send_sems,
        recv_sems,
        local_sems,
    ) = scratch[28:]
    place = Place()
    link = Sender(send_sems, recv_sems, local_sems)
    t_of = place.ahead
    steps = (1, 2, 3, 0)
    got = {}

    def load(name, src, dst):
        got[name] = link.copy(src, dst)

    load("small", small_in, small)
    load("normed", n_two_in, normed)
    load("gy", gy_in, gy)
    load("inv", inv_in, inv)

    def load_ffn(i):
        t, slot = t_of[steps[i]], i % 2
        load(("act", i), act_in.at[t], act.at[slot])
        load(("down", i), w_down.at[t], v_down.at[slot])
        load(("pull", i), pull_in.at[t], pull.at[slot])
        load(("up", i), w_up.at[t], v_up.at[slot])

    def load_att(i):
        t, slot = t_of[steps[i]], i % 2
        load(("prob", i), prob_in.at[pl.ds(3 * t, 3)], prob.at[slot])
        load(("qkv", i), w_qkv.at[t], v_qkv.at[slot])

    load_ffn(0)
    load("h", h_in, h_low)
    load_ffn(1)
    load("att", att_in, att)
    load("wout", w_out, v_out)
    load("qkvs", qkv_in, qkv)
    load("x", x_in, x_row)
    load_att(0)
    load_att(1)
    place.greet()
    t, x, y, c = place.t, place.x, place.y, place.c

    moves, stay = [], []
    stay.append(link.copy(out_row.at[pl.ds(pl.multiple_of(t * 128, 128), 128)], out_mine.at[t]))
    stay.append(link.copy(pool_in, pool_out.at[t]))
    for k in (1, 2, 3):
        part = out_row.at[pl.ds(pl.multiple_of(t_of[k] * 128, 128), 128)]
        moves.append(link.send(part, out_mine.at[t], place.deep[k]))
        moves.append(link.send(pool_in, pool_out.at[t], place.deep[k]))

    core_moves, first, second, third = {}, {}, {}, {}
    ring_open = [None] * 5
    ring_at = [0, 0]

    def chip_row(w, k, yy, xx, half):
        rows = WEIGHTS[w][1]
        at = pl.multiple_of((yy * 2 + xx) * rows + half * (rows // 2), 16)
        return sums[w].at[t_of[k], pl.ds(at, rows // 2)]

    def produce(w, k, make):
        narrow = w == 0
        slot = 3 + ring_at[1] % 2 if narrow else ring_at[0] % 3
        ring_at[narrow] += 1
        if ring_open[slot] is not None:
            link.sent(ring_open[slot])
        cols, rows = WEIGHTS[w]
        away = ring_narrow.at[slot - 3] if narrow else ring.at[slot, pl.ds(0, 4 * rows)]
        away[...] = make(1 - c).astype(BF)
        move = link.send(away, cores[w].at[k], place.core)
        ring_open[slot] = move
        core_moves[w, k] = move
        sums[w][t_of[k]] = make(c).astype(BF)

    def core_add(w, k):
        core_moves[w, k].wait_recv()
        rows = WEIGHTS[w][1]

        @pl.loop(0, 4)
        def _(i):
            at = pl.ds(pl.multiple_of(i * rows, 32), rows)
            sums[w][t_of[k], at, :] += cores[w][k, at, :]

        first[w, k] = []
        for i in (0, 1):
            first[w, k].append(link.send(chip_row(w, k, i, 1 - x, 0), lefts[w].at[k, i], place.right))
            first[w, k].append(link.send(chip_row(w, k, 1 - y, i, 1), tops[w].at[k, i], place.down))

    def add(spot, other):
        spot[...] = spot[...] + other[...]

    def plane_add(w, k):
        for move in first[w, k]:
            move.wait_recv()
        down_part, right_part = chip_row(w, k, 1 - y, x, 0), chip_row(w, k, y, 1 - x, 1)
        add(down_part, lefts[w].at[k, 1 - y])
        add(right_part, tops[w].at[k, 1 - x])
        second[w, k] = [
            link.send(down_part, lefts_two[w].at[k], place.down),
            link.send(right_part, tops_two[w].at[k], place.right),
        ]
        add(chip_row(w, k, y, x, 0), lefts[w].at[k, y])
        add(chip_row(w, k, y, x, 1), tops[w].at[k, x])

    def deep_add(w, k):
        for move in second[w, k]:
            move.wait_recv()
        add(chip_row(w, k, y, x, 0), lefts_two[w].at[k])
        add(chip_row(w, k, y, x, 1), tops_two[w].at[k])
        rows = WEIGHTS[w][1]
        if k:
            spot = pl.ds(pl.multiple_of(place.xy * rows, 16), rows)
            third[w, k] = link.send(sums[w].at[t_of[k], spot], deeps[w].at[k - 1], place.deep[k])

    def end(w):
        rows = WEIGHTS[w][1]
        spot = pl.ds(pl.multiple_of(place.xy * rows, 16), rows)
        whole = sums[w][t, spot, :].astype(F32)
        for k in (1, 2, 3):
            third[w, k].wait_recv()
            whole = whole + deeps[w][k - 1].astype(F32)
        whole = whole.astype(BF)
        if w == 0:
            parts = dot_tn(interleave(96, 4), whole)
            share[64:88, :] = jnp.concatenate([parts[24 * r : 24 * r + 24] for r in range(4)], axis=1)
        elif w == 1:
            parts = dot_tn(interleave_out(), whole)
            for k in range(3):
                share[88:96, 768 * k : 768 * k + 768] = parts[8 * k : 8 * k + 8]
        else:
            at = 0 if w == 2 else 32
            parts = dot_tn(interleave(96, 3), whole)
            for k in range(3):
                share[at : at + 32, 768 * k : 768 * k + 768] = parts[32 * k : 32 * k + 32]

    def column_sum(value):
        return jnp.sum(value, axis=0, keepdims=True)

    def norm_two_back():
        def body(rows):
            grad = gy[rows, :].astype(F32) * flag_col[rows, :]
            n = normed[rows, :]
            dz = norm_back(grad * norm[4:5, :], n, inv[1, rows, :])
            wide[rows, :] = dz
            total[rows, :] = dz
            low[rows, :] = dz.astype(BF)
            reds[4:5, :] += column_sum(grad * n)
            reds[5:6, :] += column_sum(grad)
            reds[1:2, :] += column_sum(dz)

        row_loop(body)

    def lanes(which):
        return pl.ds(pl.multiple_of(which * 384, 128), 384)

    def down_piece(i):
        k, slot = steps[i], i % 2
        got["act", i].wait()
        produce(3, k, lambda which: dot_tn(act[slot, :, lanes(which)], low[...]))

    def up_piece(i):
        k, slot = steps[i], i % 2
        got["down", i].wait()
        got["pull", i].wait()

        def body(rows):
            grad = dot_nt(low[rows, :], v_down[slot]) * pull[slot, rows, :].astype(F32)
            red_up[t_of[k]] += column_sum(grad)
            d_up[rows, :] = grad.astype(BF)

        row_loop(body, 256)
        if i == 0:
            got["h"].wait()
        produce(2, k, lambda which: dot_tn(h_low[:, lanes(which)], d_up[...]))

    def hidden_back(i):
        slot = i % 2
        got["up", i].wait()

        def body(rows):
            total[rows, :] += dot_nt(d_up[rows, :], v_up[slot])

        row_loop(body, 256)
        if i + 2 < 4:
            load_ffn(i + 2)
        if i == 1:
            load("n_one", n_one_in, normed)

    def norm_one_back():
        got["n_one"].wait()

        def body(rows):
            dh = total[rows, :]
            n = normed[rows, :]
            dz = norm_back(dh * norm[2:3, :], n, inv[0, rows, :])
            total[rows, :] = dz
            low[rows, :] = dz.astype(BF)
            reds[2:3, :] += column_sum(dh * n)
            reds[3:4, :] += column_sum(dh)
            reds[0:1, :] += column_sum(dz)

        row_loop(body)

    def out_piece(i):
        k = steps[i]
        if i == 0:
            got["att"].wait()
            got["wout"].wait()
        go[...] = dot_tn(att[t_of[k]], low[...])

        def make(which):
            part = go[pl.ds(pl.multiple_of(which * 96, 96), 96), :]
            pad = jnp.zeros((8, 768), F32)
            parts = []
            for j in range(4):
                parts += [part[24 * j : 24 * j + 24], pad]
            return jnp.concatenate(parts, axis=0)

        produce(1, k, make)

        def body(rows):
            d_att[rows, :] = dot_nt(low[rows, :], v_out[t_of[k]]).astype(BF)

        row_loop(body, 256)

    def attention_back(i):
        k, slot = steps[i], i % 2
        tk = t_of[k]
        if i == 0:
            got["qkvs"].wait()
        got["prob", i].wait()
        turned[...] = jnp.zeros_like(turned)

        def body(rows):
            d_queries = []
            for j in range(3):
                at = 64 * j
                grad = d_att[rows, at : at + 64]
                weight_low = prob[slot, j, rows, :]
                weight = weight_low.astype(F32)
                d_prob = dot_nt(grad, qkv[tk, :, 384 + at : 448 + at]) * weight
                inner = jnp.sum(d_prob, axis=1, keepdims=True)
                d_scores = (d_prob - weight * inner).astype(BF)
                d_queries.append(dot_f32(d_scores, qkv[tk, :, 192 + at : 256 + at]))
                turned[at : at + 64, :] += dot_tn(qkv[tk, rows, at : at + 64], d_scores)
                turned[192 + at : 256 + at, :] += dot_tn(grad, weight_low)
            dq = jnp.concatenate(d_queries, axis=1) * 0.125
            red_qv[tk, :, :192] += column_sum(dq)
            d_qkv[rows, :192] = dq.astype(BF)

        row_loop(body, 256)
        dk = jnp.transpose(turned[:192, :]) * 0.125
        dv = jnp.transpose(turned[192:, :])
        red_qv[tk, :, 192:] += column_sum(dv)
        d_qkv[:, 192:] = jnp.concatenate([dk, dv], axis=1).astype(BF)

    def qkv_piece(i):
        k, slot = steps[i], i % 2
        if i == 0:
            got["x"].wait()
        produce(0, k, lambda which: dot_tn(x_row[:, lanes(which)], d_qkv[...]))
        got["qkv", i].wait()

        def body(rows):
            total[rows, :] += dot_nt(d_qkv[rows, :], v_qkv[slot])

        row_loop(body, 256)
        if i + 2 < 4:
            load_att(i + 2)

    got["small"].wait()
    norm_vectors(small, norm)
    reds[...] = jnp.zeros_like(reds)
    red_up[...] = jnp.zeros_like(red_up)
    red_qv[...] = jnp.zeros_like(red_qv)
    small_grad[...] = jnp.zeros_like(small_grad)
    for name in ("normed", "gy", "inv"):
        got[name].wait()
    norm_two_back()
    a, b, d, e = ((3, k) for k in steps)
    f, g, h, j = ((2, k) for k in steps)
    down_piece(0)
    up_piece(0)
    core_add(*a)
    hidden_back(0)
    core_add(*f)
    down_piece(1)
    plane_add(*a)
    up_piece(1)
    core_add(*b)
    hidden_back(1)
    core_add(*g)
    plane_add(*f)
    down_piece(2)
    deep_add(*a)
    core_add(*d)
    up_piece(2)
    plane_add(*b)
    deep_add(*f)
    hidden_back(2)
    core_add(*h)
    down_piece(3)
    core_add(*e)
    up_piece(3)
    plane_add(*g)
    deep_add(*b)
    hidden_back(3)
    core_add(*j)
    norm_one_back()
    plane_add(*d)
    deep_add(*g)
    out_piece(0)
    attention_back(0)
    plane_add(*h)
    deep_add(*d)
    core_add(1, 1)
    qkv_piece(0)
    plane_add(*e)
    deep_add(*h)
    core_add(0, 1)
    out_piece(1)
    attention_back(1)
    core_add(1, 2)
    qkv_piece(1)
    plane_add(*j)
    deep_add(*e)
    core_add(0, 2)
    out_piece(2)
    attention_back(2)
    core_add(1, 3)
    deep_add(*j)
    plane_add(1, 1)
    qkv_piece(2)
    core_add(0, 3)
    plane_add(0, 1)
    deep_add(1, 1)
    out_piece(3)
    attention_back(3)
    core_add(1, 0)
    qkv_piece(3)
    core_add(0, 0)

    def dx_body(rows):
        low[rows, :] = total[rows, :].astype(BF)

    row_loop(dx_body)
    own_rows = pl.ds(pl.multiple_of(t * 128, 128), 128)
    stay.append(link.copy(low.at[own_rows], dx_mine.at[t]))
    for k in (1, 2, 3):
        part = low.at[pl.ds(pl.multiple_of(t_of[k] * 128, 128), 128)]
        moves.append(link.send(part, dx_mine.at[t], place.deep[k]))
    for q in range(4):
        at = slice(192 * q, 192 * q + 192)
        small_grad[q, 0:1, :] = jnp.concatenate(
            [red_qv[q], red_up[q]] + [reds[i : i + 1, at] for i in range(6)], axis=1
        )
    small_sum = small_land.at[6]
    small_keep = link.copy(small_grad.at[t], small_sum)
    small_moves = [link.send(small_grad.at[t_of[k]], small_land.at[k - 1], place.deep[k]) for k in (1, 2, 3)]
    plane_add(1, 2)
    deep_add(0, 1)
    plane_add(0, 2)
    deep_add(1, 2)
    plane_add(1, 3)
    deep_add(0, 2)
    plane_add(0, 3)
    deep_add(1, 3)
    end(3)
    end(2)
    plane_add(1, 0)
    plane_add(0, 0)
    deep_add(0, 3)
    deep_add(1, 0)
    deep_add(0, 0)
    end(1)
    small_keep.wait()
    for move in small_moves:
        move.wait_recv()
    small_land[7] = small_land[6] + small_land[0] + small_land[1] + small_land[2]
    for i, peer in enumerate((place.core, place.right, place.down)):
        move = link.send(small_land.at[7 + i], small_land.at[3 + i], peer)
        if i == 1:
            end(0)
            share_low[...] = share[...].astype(BF)
            dest = pl.ds(pl.multiple_of((c * 4 + place.xy) * 96, 96), 96)
            kept = link.copy(share_low, blocks.at[dest])
            last = [
                link.send(share_low, blocks.at[dest], to)
                for to in (place.diag, place.right, place.down)
            ]
        move.wait_recv()
        small_land[8 + i] = small_land[7 + i] + small_land[3 + i]
    small_out[...] = small_land[10]
    kept.wait()
    for move in last:
        move.wait_recv()
    half = pl.ds(pl.multiple_of(c * 384, 384), 384)
    across = link.send(blocks.at[half], blocks.at[half], place.core)
    across.wait_recv()
    for move in moves:
        move.wait_recv()
    for copy in stay:
        copy.wait()
    link.finish()


def backward_call(*args):
    anywhere = pl.BlockSpec(memory_space=pl.ANY)
    vmem = pl.BlockSpec(memory_space=pltpu.VMEM)
    shape = jax.ShapeDtypeStruct
    sums = [((4, 4 * rows, cols), BF) for cols, rows in WEIGHTS]
    halves = [((4, 2, rows // 2, cols), BF) for cols, rows in WEIGHTS]
    singles = [((4, rows // 2, cols), BF) for cols, rows in WEIGHTS]
    deeps = [((3, rows, cols), BF) for cols, rows in WEIGHTS]
    rest = [
        ((3, 384, 768), BF),
        ((2, 384, 576), BF),
        ((96, 2304), F32),
        ((96, 2304), BF),
        ((4, 8, 2304), F32),
        ((11, 8, 2304), F32),
        ((4, 8, 2304), F32),
        ((8, 768), F32),
        ((512, 768), BF),
        ((512, 768), F32),
        ((2, 512, 1), F32),
        ((2, 512, 768), BF),
        ((2, 512, 768), BF),
        ((2, 768, 768), BF),
        ((2, 768, 768), BF),
        ((512, 768), BF),
        ((4, 512, 192), BF),
        ((4, 192, 768), BF),
        ((4, 512, 576), BF),
        ((2, 3, 512, 512), BF),
        ((2, 768, 576), BF),
        ((512, 768), BF),
        ((512, 768), F32),
        ((512, 768), BF),
        ((512, 768), F32),
        ((512, 768), BF),
        ((512, 192), BF),
        ((512, 576), BF),
        ((384, 512), F32),
        ((192, 768), F32),
        ((8, 768), F32),
        ((4, 1, 768), F32),
        ((4, 1, 384), F32),
    ]
    scratch = sums + sums + halves + halves + singles + singles + deeps + rest
    return pl.pallas_call(
        backward_kernel,
        out_shape=[
            shape((768, 2304), BF),
            shape((8, 2304), F32),
            shape((4, 128, 768), BF),
            shape((4, 128, 768), BF),
            shape((4, 8, 768), F32),
        ],
        in_specs=[vmem] + [anywhere] * 18,
        out_specs=[anywhere, vmem, anywhere, anywhere, anywhere],
        scratch_shapes=[pltpu.VMEM(*s) for s in scratch]
        + [
            pltpu.SemaphoreType.DMA((160,)),
            pltpu.SemaphoreType.DMA((160,)),
            pltpu.SemaphoreType.DMA((64,)),
        ],
        compiler_params=pltpu.CompilerParams(
            collective_id=1, has_side_effects=True, vmem_limit_bytes=62 * MIB
        ),
        name="backward_and_reduce",
    )(*args)


def local_rows(
    layer_input_rows,
    sentence_index_row,
    padding_mask,
    output_gradient,
    owner_rank,
    master_state,
    first_moment,
    second_moment,
):
    tensor_at = lax.axis_index("tensor")
    data_at = lax.axis_index("dp")
    per_owner = master_state.shape[1]
    block_len = master_state.shape[2]
    slot_of = slot_tables(owner_rank, per_owner)
    slot_order = jnp.concatenate(
        [
            slot_of[:256].reshape(2, 4, 32),
            slot_of[256:512].reshape(2, 4, 32),
            slot_of[512:704].reshape(2, 4, 24),
            slot_of[704:768].reshape(2, 4, 8),
        ],
        axis=2,
    ).reshape(768)
    core_order = lax.dynamic_slice_in_dim(slot_order, (data_at % 2) * 384, 384, 0)[:, None]
    small_slot = jnp.broadcast_to(slot_of[768], (8, 1))

    labels = lax.dynamic_index_in_dim(sentence_index_row, tensor_at, 0, keepdims=False)
    flags = lax.dynamic_index_in_dim(padding_mask, tensor_at, 0, keepdims=False)
    ids = jnp.where(flags == 1, labels, -1 - jnp.arange(flags.shape[0], dtype=jnp.int32))
    (
        w_qkv,
        _,
        w_up,
        w_down,
        w_out,
        small_all,
        x_row,
        gy_row,
        qkv,
        prob_low,
        attended,
        normed_one,
        h_low,
        act,
        pull,
        normed_two,
        inverse,
        out_row,
        pool_mean,
    ) = forward_call(
        master_state[0],
        core_order,
        small_slot,
        ids[:, None],
        ids[None],
        jnp.transpose(layer_input_rows, (1, 0, 2)),
        jnp.transpose(output_gradient, (1, 0, 2)),
    )
    blocks, small_sum, out_mine, dx_mine, pool_all = backward_call(
        flags.astype(F32)[:, None],
        out_row,
        pool_mean,
        gy_row,
        normed_two,
        inverse,
        small_all,
        act,
        pull,
        w_down,
        w_up,
        h_low,
        normed_one,
        attended,
        w_out,
        qkv,
        prob_low,
        w_qkv,
        x_row,
    )
    small_row = small_sum[0]
    norm_grads = small_row[1152:].reshape(6, 192)
    pooled = lax.dynamic_slice_in_dim(pool_all, tensor_at * 192, 192, 2)

    wanted = data_at * per_owner + jnp.arange(per_owner, dtype=jnp.int32)
    block_of, filled = slot_blocks(slot_of, wanted)
    pick = (slot_order[None, :] == wanted[:, None]).astype(BF)
    owned = dot_f32(pick, blocks)
    owned = jnp.where((wanted == slot_of[768])[:, None], small_row[None], owned)
    token_position = block_of[:, None] * block_len + jnp.arange(block_len, dtype=jnp.int32)[None, :]
    step_rate, decay_on = step_rates(token_position, MODEL_WIDTH, FF, 4)
    new_master, new_first, new_second = adamw(
        owned,
        first_moment[0],
        second_moment[0],
        master_state[0],
        step_rate,
        decay_on,
        filled[:, None],
    )
    return (
        jnp.transpose(out_mine, (1, 0, 2)).astype(F32),
        pooled,
        jnp.transpose(dx_mine, (1, 0, 2)).astype(F32),
        new_master[None],
        new_first[None],
        new_second[None],
        norm_grads,
    )


def solution(mesh):
    in_specs = (
        P("tensor", "dp", None),
        P("dp", None),
        P("dp", None),
        P("tensor", "dp", None),
        P(),
        P("tensor", "dp", None),
        P("tensor", "dp", None),
        P("tensor", "dp", None),
    )
    out_specs = (
        P("tensor", "dp", None),
        P("dp", None, "tensor"),
        P("tensor", "dp", None),
        P("tensor", "dp", None),
        P("tensor", "dp", None),
        P("tensor", "dp", None),
        P(None, "tensor"),
    )
    plain = mesh.shape["dp"] != 8 or mesh.shape["tensor"] != 4
    body = local_general if plain else local_rows
    return jax.shard_map(body, mesh=mesh, in_specs=in_specs, out_specs=out_specs, check_vma=False)
```

```python
import jax
import functools
import jax.numpy as jnp
from jax import lax
from jax.experimental import pallas as pl
from jax.experimental.pallas import tpu as pltpu
from jax.sharding import PartitionSpec as P

MODEL_WIDTH = 768
HEAD_DIM = 64
FF = 3072
SMAX = 8
STEP = 10


NORM_EPS = 1e-05
ADAM_EPS = 1e-08
BETA_ONE = 0.9
BETA_TWO = 0.999
DECAY_RATE = 0.01
MASKED = -1e30
exact_precision = lax.Precision.HIGHEST


def slot_tables(owner_rank, per_owner):
    ordinal = jnp.arange(owner_rank.shape[0], dtype=jnp.int32)
    same_owner = owner_rank[:, None] == owner_rank[None, :]
    earlier = ordinal[None, :] < ordinal[:, None]
    ranking = jnp.sum((same_owner & earlier).astype(jnp.int32), axis=1)
    return owner_rank * per_owner + ranking


def slot_blocks(slot_of, wanted):
    matches = slot_of[None, :] == wanted[:, None]
    filled = jnp.any(matches, axis=1)
    ordinal = jnp.arange(slot_of.shape[0], dtype=jnp.int32)
    block_of = jnp.sum(jnp.where(matches, ordinal[None, :], 0), axis=1)
    return (block_of, filled)


def step_rates(token_position, width, hidden, tensor_size):
    width_loc = width // tensor_size
    ffn_loc = hidden // tensor_size
    end_up = width * ffn_loc
    end_down = end_up + ffn_loc * width
    end_qkv = end_down + width * 3 * width_loc
    end_out = end_qkv + width_loc * width
    offset = token_position - end_out
    first_gain = (offset >= 4 * width_loc + ffn_loc) & (offset < 5 * width_loc + ffn_loc)
    second_gain = (offset >= 6 * width_loc + ffn_loc) & (offset < 7 * width_loc + ffn_loc)
    small_rate = jnp.where(first_gain | second_gain, 0.2, 0.1)
    step_rate = jnp.where(
        token_position < end_up,
        width ** (-0.5),
        jnp.where(
            token_position < end_down,
            hidden ** (-0.5),
            jnp.where(
                token_position < end_qkv,
                width ** (-0.5),
                jnp.where(token_position < end_out, 4.0 * width ** (-0.5), small_rate),
            ),
        ),
    )
    decay_on = (token_position < end_out).astype(jnp.float32)
    return (step_rate.astype(jnp.float32), decay_on)


def adamw(gradient, moment, square, weight, step_rate, decay_on, filled):
    new_moment = BETA_ONE * moment + (1.0 - BETA_ONE) * gradient
    new_square = BETA_TWO * square + (1.0 - BETA_TWO) * gradient * gradient
    unbiased = new_moment / (1.0 - BETA_ONE**STEP)
    divisor = jnp.sqrt(new_square / (1.0 - BETA_TWO**STEP)) + ADAM_EPS
    new_weight = weight - step_rate * (unbiased / divisor + DECAY_RATE * decay_on * weight)
    zeroed = jnp.zeros_like(weight)
    return (
        jnp.where(filled, new_weight, zeroed),
        jnp.where(filled, new_moment, zeroed),
        jnp.where(filled, new_square, zeroed),
    )


def normalize(values):
    centred = values - jnp.mean(values, axis=-1, keepdims=True)
    inv_dev = lax.rsqrt(jnp.mean(centred * centred, axis=-1, keepdims=True) + NORM_EPS)
    return (centred * inv_dev, inv_dev)


def norm_back(grad_scaled, normed, inv_dev):
    first_mean = jnp.mean(grad_scaled, axis=-1, keepdims=True)
    second_mean = jnp.mean(grad_scaled * normed, axis=-1, keepdims=True)
    return inv_dev * (grad_scaled - first_mean - normed * second_mean)


def allowed_pairs(sentence_labels, real_token_flags):
    row_len = sentence_labels.shape[-1]
    same_sent = sentence_labels[:, :, None] == sentence_labels[:, None, :]
    live = (real_token_flags[:, :, None] == 1) & (real_token_flags[:, None, :] == 1)
    diagonal = jnp.eye(row_len, dtype=bool)[None]
    return same_sent & live | diagonal


def masked_scores(queries, key_rows, allowed, scaling):
    scores = (
        jnp.einsum("qshe,kshe->shqk", queries, key_rows, preferred_element_type=jnp.float32)
        * scaling
    )
    return jnp.where(allowed[:, None], scores, MASKED)


def split_flat(flat_all, width_loc, ffn_loc):
    end_up = MODEL_WIDTH * ffn_loc
    end_down = end_up + ffn_loc * MODEL_WIDTH
    end_qkv = end_down + MODEL_WIDTH * 3 * width_loc
    end_out = end_qkv + width_loc * MODEL_WIDTH
    return (
        flat_all[:end_up].reshape(MODEL_WIDTH, ffn_loc),
        flat_all[end_up:end_down].reshape(ffn_loc, MODEL_WIDTH),
        flat_all[end_down:end_qkv].reshape(MODEL_WIDTH, 3 * width_loc),
        flat_all[end_qkv:end_out].reshape(width_loc, MODEL_WIDTH),
        flat_all[end_out:],
    )


def local_general(
    layer_input_rows,
    sentence_index_row,
    padding_mask,
    output_gradient,
    owner_rank,
    master_state,
    first_moment,
    second_moment,
):
    tensor_size = lax.axis_size("tensor")
    tensor_at = lax.axis_index("tensor")
    data_size = lax.axis_size("dp")
    data_at = lax.axis_index("dp")
    width_loc = MODEL_WIDTH // tensor_size
    ffn_loc = FF // tensor_size
    heads_loc = width_loc // HEAD_DIM
    quarter = layer_input_rows.shape[0]
    seq_count = layer_input_rows.shape[1]
    row_len = quarter * tensor_size
    per_owner = master_state.shape[1]
    block_len = master_state.shape[2]
    nblocks = owner_rank.shape[0]
    slot_of = slot_tables(owner_rank, per_owner)
    gathered = lax.all_gather(master_state.astype(jnp.bfloat16), "dp", axis=1, tiled=True)[0]
    flat_weights = gathered[slot_of].reshape(nblocks * block_len)
    up_weight, down_weight, w_qkv, w_out, small_part = split_flat(flat_weights, width_loc, ffn_loc)
    bias_q = small_part[:width_loc].astype(jnp.float32)
    bias_v = small_part[width_loc : 2 * width_loc].astype(jnp.float32)
    expand_bias = small_part[2 * width_loc : 2 * width_loc + ffn_loc].astype(jnp.float32)
    norm_parts = small_part[2 * width_loc + ffn_loc :].reshape(6, width_loc)
    full_rows, norm_whole = (
        lax.all_gather(layer_input_rows, "tensor", axis=0, tiled=True),
        lax.all_gather(norm_parts, "tensor", axis=1, tiled=True),
    )
    norm_all = norm_whole.astype(jnp.float32)
    bias_out, bias_down = (norm_all[0], norm_all[1])
    gain_one, shift_one, gain_two, shift_two = (norm_all[2], norm_all[3], norm_all[4], norm_all[5])
    qkv_lin = jnp.einsum("lsd,de->lse", full_rows, w_qkv, preferred_element_type=jnp.float32)
    bias_qkv = jnp.concatenate([bias_q, jnp.zeros((width_loc,), jnp.float32), bias_v])
    qkv = (qkv_lin + bias_qkv).astype(jnp.bfloat16)
    queries = qkv[:, :, :width_loc].reshape(row_len, seq_count, heads_loc, HEAD_DIM)
    key_rows = qkv[:, :, width_loc : 2 * width_loc].reshape(row_len, seq_count, heads_loc, HEAD_DIM)
    values = qkv[:, :, 2 * width_loc :].reshape(row_len, seq_count, heads_loc, HEAD_DIM)
    scaling = HEAD_DIM ** (-0.5)
    allowed = allowed_pairs(sentence_index_row, padding_mask)
    scores = masked_scores(queries, key_rows, allowed, scaling)
    row_peak = jnp.max(scores, axis=-1, keepdims=True)
    log_total = row_peak + jnp.log(jnp.sum(jnp.exp(scores - row_peak), axis=-1, keepdims=True))
    prob_low = jnp.exp(scores - log_total).astype(jnp.bfloat16)
    attended = jnp.einsum("shqk,kshe->qshe", prob_low, values, preferred_element_type=jnp.float32)
    attended = attended.astype(jnp.bfloat16).reshape(row_len, seq_count, width_loc)
    portion_rows = attended
    attn_rows = lax.psum_scatter(
        jnp.einsum("lse,ed->lsd", portion_rows, w_out, preferred_element_type=jnp.float32).astype(
            jnp.bfloat16
        ),
        "tensor",
        scatter_dimension=0,
        tiled=True,
    ).astype(jnp.float32)
    z_one = layer_input_rows.astype(jnp.float32) + attn_rows + bias_out
    normed_one, inv_one = normalize(z_one)
    h_mine = normed_one * gain_one + shift_one
    hidden_narrow_whole = lax.all_gather(h_mine.astype(jnp.bfloat16), "tensor", axis=0, tiled=True)
    up_pre = (
        jnp.einsum(
            "wer,rb->web", hidden_narrow_whole, up_weight, preferred_element_type=jnp.float32
        )
        + expand_bias
    )
    activation_narrow = jax.nn.gelu(up_pre, approximate=False).astype(jnp.bfloat16)
    portion_rows = activation_narrow
    down_rows = lax.psum_scatter(
        jnp.einsum(
            "aij,jb->aib", portion_rows, down_weight, preferred_element_type=jnp.float32
        ).astype(jnp.bfloat16),
        "tensor",
        scatter_dimension=0,
        tiled=True,
    ).astype(jnp.float32)
    z_two = h_mine + down_rows + bias_down
    normed_two, inv_two = normalize(z_two)
    layer_out = normed_two * gain_two + shift_two
    seg_mine = lax.dynamic_slice_in_dim(sentence_index_row, tensor_at * quarter, quarter, 1)
    valid_mine = lax.dynamic_slice_in_dim(padding_mask, tensor_at * quarter, quarter, 1)
    sent_ids = jnp.arange(SMAX, dtype=jnp.int32)
    onehot_mine = (
        (seg_mine[:, :, None] == sent_ids[None, None, :]) & (valid_mine[:, :, None] == 1)
    ).astype(jnp.float32)
    pool_part = jnp.einsum("slc,lsd->scd", onehot_mine, layer_out, precision=exact_precision)
    onehot_full = (
        (sentence_index_row[:, :, None] == sent_ids[None, None, :])
        & (padding_mask[:, :, None] == 1)
    ).astype(jnp.float32)
    counts = jnp.sum(onehot_full, axis=1)
    grad_out = output_gradient.astype(jnp.float32) * valid_mine.T[:, :, None].astype(jnp.float32)
    d_gain_two = jnp.sum(grad_out * normed_two, axis=(0, 1))
    d_shift_two = jnp.sum(grad_out, axis=(0, 1))
    dz_two = norm_back(grad_out * gain_two, normed_two, inv_two)
    d_bias_down = jnp.sum(dz_two, axis=(0, 1))
    second_sum_gradient_wide = lax.all_gather(
        dz_two.astype(jnp.bfloat16), "tensor", axis=0, tiled=True
    )
    down_weight_gradient = jnp.einsum(
        "ipo,ipr->or",
        activation_narrow,
        second_sum_gradient_wide,
        preferred_element_type=jnp.float32,
    )
    activation_gradient = jnp.einsum(
        "ugp,jp->ugj", second_sum_gradient_wide, down_weight, preferred_element_type=jnp.float32
    )
    gelu_pull = jax.vjp(lambda pre_act: jax.nn.gelu(pre_act, approximate=False), up_pre)[1]
    d_up = gelu_pull(activation_gradient)[0]
    d_bias_up = jnp.sum(d_up, axis=(0, 1))
    expand_gradient_narrow = d_up.astype(jnp.bfloat16)
    up_weight_gradient = jnp.einsum(
        "iux,iuy->xy",
        hidden_narrow_whole,
        expand_gradient_narrow,
        preferred_element_type=jnp.float32,
    )
    portion_rows = expand_gradient_narrow
    dh_rows = lax.psum_scatter(
        jnp.einsum(
            "uih,vh->uiv", portion_rows, up_weight, preferred_element_type=jnp.float32
        ).astype(jnp.bfloat16),
        "tensor",
        scatter_dimension=0,
        tiled=True,
    ).astype(jnp.float32)
    dh_mine = dz_two + dh_rows
    d_gain_one = jnp.sum(dh_mine * normed_one, axis=(0, 1))
    d_shift_one = jnp.sum(dh_mine, axis=(0, 1))
    dz_one = norm_back(dh_mine * gain_one, normed_one, inv_one)
    d_bias_out = jnp.sum(dz_one, axis=(0, 1))
    dz_one_full = lax.all_gather(dz_one.astype(jnp.bfloat16), "tensor", axis=0, tiled=True)
    d_w_out = jnp.einsum("lse,lsd->ed", attended, dz_one_full, preferred_element_type=jnp.float32)
    d_attended = jnp.einsum("lsd,ed->lse", dz_one_full, w_out, preferred_element_type=jnp.float32)
    d_attended = d_attended.astype(jnp.bfloat16).reshape(row_len, seq_count, heads_loc, HEAD_DIM)
    scores_again = masked_scores(queries, key_rows, allowed, scaling)
    attn_prob = jnp.exp(scores_again - log_total)
    prob_again = attn_prob.astype(jnp.bfloat16)
    d_prob = jnp.einsum("qshe,kshe->shqk", d_attended, values, preferred_element_type=jnp.float32)
    d_values = jnp.einsum(
        "shqk,qshe->kshe", prob_again, d_attended, preferred_element_type=jnp.float32
    )
    inner = jnp.sum(d_prob * attn_prob, axis=-1, keepdims=True)
    d_scores = (attn_prob * (d_prob - inner)).astype(jnp.bfloat16)
    d_queries = (
        jnp.einsum("shqk,kshe->qshe", d_scores, key_rows, preferred_element_type=jnp.float32)
        * scaling
    )
    d_keys = (
        jnp.einsum("shqk,qshe->kshe", d_scores, queries, preferred_element_type=jnp.float32)
        * scaling
    )
    d_bias_q = jnp.sum(d_queries, axis=(0, 1)).reshape(width_loc)
    d_bias_v = jnp.sum(d_values, axis=(0, 1)).reshape(width_loc)
    d_qkv_low = jnp.concatenate(
        [
            d_queries.reshape(row_len, seq_count, width_loc),
            d_keys.reshape(row_len, seq_count, width_loc),
            d_values.reshape(row_len, seq_count, width_loc),
        ],
        axis=2,
    ).astype(jnp.bfloat16)
    d_w_qkv = jnp.einsum("lsd,lse->de", full_rows, d_qkv_low, preferred_element_type=jnp.float32)
    portion_rows = d_qkv_low
    dx_rows = lax.psum_scatter(
        jnp.einsum("lse,de->lsd", portion_rows, w_qkv, preferred_element_type=jnp.float32).astype(
            jnp.bfloat16
        ),
        "tensor",
        scatter_dimension=0,
        tiled=True,
    ).astype(jnp.float32)
    input_grad = dz_one + dx_rows
    shared_grads = jnp.stack(
        [d_bias_out, d_bias_down, d_gain_one, d_shift_one, d_gain_two, d_shift_two]
    )[None]
    pool_sum, shared_sum = (
        lax.psum_scatter(
            pool_part.astype(jnp.bfloat16), "tensor", scatter_dimension=2, tiled=True
        ).astype(jnp.float32),
        lax.psum_scatter(
            shared_grads.astype(jnp.bfloat16), "tensor", scatter_dimension=2, tiled=True
        ).astype(jnp.float32),
    )
    pooled_mean = pool_sum / jnp.maximum(counts, 1.0)[:, :, None]
    flat_grads = jnp.concatenate(
        [
            up_weight_gradient.reshape(-1),
            down_weight_gradient.reshape(-1),
            d_w_qkv.reshape(-1),
            d_w_out.reshape(-1),
            d_bias_q,
            d_bias_v,
            d_bias_up,
            shared_sum.reshape(-1),
        ]
    )
    grad_blocks = flat_grads.reshape(nblocks, block_len)
    wanted = data_at * per_owner + jnp.arange(per_owner, dtype=jnp.int32)
    block_of, filled = slot_blocks(slot_of, wanted)
    slot_grads = (
        jnp.zeros((data_size * per_owner, block_len), jnp.float32).at[slot_of].set(grad_blocks)
    )
    owned_grads = lax.psum_scatter(slot_grads, "dp", scatter_dimension=0, tiled=True)
    norm_grads = lax.psum(shared_sum[0], "dp")
    token_position = block_of[:, None] * block_len + jnp.arange(block_len, dtype=jnp.int32)[None, :]
    step_rate, decay_on = step_rates(token_position, MODEL_WIDTH, FF, tensor_size)
    new_master, new_first, new_second = adamw(
        owned_grads,
        first_moment[0],
        second_moment[0],
        master_state[0],
        step_rate,
        decay_on,
        filled[:, None],
    )
    return (
        layer_out,
        pooled_mean,
        input_grad,
        new_master[None],
        new_first[None],
        new_second[None],
        norm_grads,
    )


MESH = pl.DeviceIdType.MESH
BF = jnp.bfloat16
F32 = jnp.float32
WEIGHTS = ((576, 96), (768, 32), (768, 96), (768, 96))
MIB = 2**20


class Place:
    def __init__(self):
        d = lax.axis_index("dp")
        self.t = lax.axis_index("tensor")
        self.c = d % 2
        self.x = (d // 2) % 2
        self.y = d // 4
        self.xy = d // 2
        self.core = (d + 1 - 2 * self.c, self.t)
        self.right = (d + 2 - 4 * self.x, self.t)
        self.down = (d + 4 - 8 * self.y, self.t)
        self.diag = (d + 6 - 4 * self.x - 8 * self.y, self.t)
        self.deep = [None] + [(d, (self.t + k) % 4) for k in (1, 2, 3)]
        self.ahead = [(self.t + k) % 4 for k in range(4)]
        self.behind = [(self.t + 4 - k) % 4 for k in range(4)]

    def greet(self):
        barrier = pltpu.get_barrier_semaphore()
        peers = [self.core, self.right, self.down, self.diag] + self.deep[1:]
        for peer in peers:
            pl.semaphore_signal(barrier, inc=1, device_id=peer, device_id_type=MESH)
        pl.semaphore_wait(barrier, len(peers))


class Sender:
    def __init__(self, send_sems, recv_sems, local_sems):
        self.sems = (send_sems, recv_sems, local_sems)
        self.used = 0
        self.used_local = 0
        self.open = []

    def send(self, src, dst, peer):
        i = self.used
        self.used += 1
        copy = pltpu.make_async_remote_copy(
            src_ref=src,
            dst_ref=dst,
            send_sem=self.sems[0].at[i],
            recv_sem=self.sems[1].at[i],
            device_id=peer,
            device_id_type=MESH,
        )
        copy.start()
        self.open.append(copy)
        return copy

    def copy(self, src, dst):
        i = self.used_local
        self.used_local += 1
        copy = pltpu.make_async_copy(src, dst, self.sems[2].at[i])
        copy.start()
        return copy

    def sent(self, copy):
        copy.wait_send()
        self.open = [other for other in self.open if other is not copy]

    def finish(self):
        for copy in self.open:
            copy.wait_send()


def rows_of(place, rows, at=None):
    at = place.xy if at is None else at
    return pl.ds(pl.multiple_of(place.c * (4 * rows) + at * rows, 32), rows)


def half_of(place, rows):
    return pl.ds(pl.multiple_of(place.c * (4 * rows), 128), 4 * rows)


def interleave(size, parts):
    group = size // parts
    out_row = lax.broadcasted_iota(jnp.int32, (size, size), 0)
    col = lax.broadcasted_iota(jnp.int32, (size, size), 1)
    part = jnp.zeros((size, size), jnp.int32)
    for k in range(1, parts):
        part = part + (col >= k * group).astype(jnp.int32)
    return jnp.where(out_row == parts * (col - group * part) + part, 1.0, 0.0).astype(BF)


def interleave_out():
    out_row = lax.broadcasted_iota(jnp.int32, (32, 32), 0)
    col = lax.broadcasted_iota(jnp.int32, (32, 32), 1)
    part = (col >= 8).astype(jnp.int32) + (col >= 16).astype(jnp.int32)
    keep = (out_row == 3 * (col - 8 * part) + part) & (col < 24)
    return jnp.where(keep, 1.0, 0.0).astype(BF)


def dot_f32(a, b):
    return jnp.dot(a, b, preferred_element_type=F32)


def compact_out():
    out_row = lax.broadcasted_iota(jnp.int32, (192, 256), 0)
    col = lax.broadcasted_iota(jnp.int32, (192, 256), 1)
    group = jnp.zeros((192, 256), jnp.int32)
    for i in range(1, 8):
        group = group + (out_row >= 24 * i).astype(jnp.int32)
    return jnp.where(col == out_row + 8 * group, 1.0, 0.0).astype(BF)


def dot_nt(a, b):
    return lax.dot_general(a, b, (((1,), (1,)), ((), ())), preferred_element_type=F32)


def dot_tn(a, b):
    return lax.dot_general(a, b, (((0,), (0,)), ((), ())), preferred_element_type=F32)


def norm_vectors(small, norm):
    for i in range(6):
        at = 1152 + 192 * i
        norm[i : i + 1, :] = jnp.concatenate([small[t, 0:1, at : at + 192] for t in range(4)], axis=1)


def row_loop(body, step=128):
    @pl.loop(0, 512 // step)
    def _(i):
        body(pl.ds(pl.multiple_of(i * step, step), step))


def forward_kernel(
    master,
    slot_col,
    small_slot,
    id_col,
    id_row,
    x_in,
    gy_in,
    w_qkv,
    w_out,
    w_up,
    w_down,
    out_compact,
    small_out,
    x_out,
    gy_row,
    qkv_out,
    prob_out,
    att_out,
    n_one_out,
    h_out,
    act_out,
    pull_out,
    n_two_out,
    inv_out,
    row_out,
    pool_out,
    slots,
    canon_att,
    canon_ffn,
    land_att,
    land_ffn,
    share,
    p_qkv,
    p_out,
    p_up,
    p_down,
    small_mine,
    small_land,
    small_total,
    small,
    norm,
    bias_qkv,
    v_qkv,
    v_out,
    v_compact,
    v_up,
    v_down,
    x_row,
    qkv,
    prob,
    att,
    n_one,
    h_wide,
    h_low,
    act,
    pull,
    total,
    inv,
    row_low,
    pool,
    send_sems,
    recv_sems,
    local_sems,
):
    place = Place()
    link = Sender(send_sems, recv_sems, local_sems)
    slots[place.c] = master[...].astype(BF)
    place.greet()
    whole = (w_qkv, w_out, w_up, w_down)
    held = (v_qkv, v_out, v_up, v_down)
    piece = (p_qkv, p_out, p_up, p_down)
    peers = (place.right, place.down, place.diag)
    mine_rows = pl.ds(pl.multiple_of(place.t * 128, 128), 128)
    tidy = []

    core_slots = link.send(slots.at[place.c], slots.at[place.c], place.core)
    x_moves = [
        link.send(x_in.at[place.ahead[k]], x_row.at[mine_rows], place.deep[k]) for k in (1, 2, 3)
    ]
    x_stay = link.copy(x_in.at[place.t], x_row.at[mine_rows])
    tidy.append(link.copy(gy_in.at[place.t], gy_row.at[mine_rows]))
    core_slots.wait_recv()

    pair_slots = slots[...].reshape(384, 2304)
    slot_id = lax.broadcasted_iota(jnp.int32, (64, 384), 1) + place.xy * 384
    order = [(3, place.diag), (1, place.right), (2, place.down), (0, None)]

    def spread(lo, rows, canon, land):
        sent = []
        for j, peer in order:
            at = place.xy if peer is None else peer[0] // 2
            wanted = slot_col[pl.ds(pl.multiple_of(at * 96 + lo, 32), rows), :]
            pick = jnp.where(wanted == slot_id[:rows], 1.0, 0.0).astype(BF)
            canon[j] = dot_f32(pick, pair_slots).astype(BF)
            if peer is not None:
                sent.append(link.send(canon.at[j], land.at[j - 1], peer))
        return sent

    def collect(sent, lo, rows, canon, land):
        for move in sent:
            move.wait_recv()
        share[lo : lo + rows, :] = (
            canon[0].astype(F32) + land[0].astype(F32) + land[1].astype(F32) + land[2].astype(F32)
        )

    att_sent = spread(64, 32, canon_att, land_att)
    pick_small = jnp.where(small_slot[...] == slot_id[:8], 1.0, 0.0).astype(BF)
    small_mine[...] = dot_f32(pick_small, pair_slots)
    small_moves = [link.send(small_mine, small_land.at[j], peer) for j, peer in enumerate(peers)]
    att_sent[0].wait_recv()
    ffn_sent = spread(0, 64, canon_ffn, land_ffn)
    collect(att_sent[1:], 64, 32, canon_att, land_att)

    p_qkv[...] = dot_f32(
        interleave(96, 4),
        jnp.concatenate([share[64:88, 576 * r : 576 * r + 576] for r in range(4)], axis=0).astype(BF),
    ).astype(BF)

    def spread_out():
        parts = [share[88:96, 768 * k : 768 * k + 768] for k in range(3)]
        parts = parts + [jnp.zeros((8, 768), F32)]
        p_out[...] = dot_f32(interleave_out(), jnp.concatenate(parts, axis=0).astype(BF)).astype(BF)

    def spread_ffn():
        three = interleave(96, 3)
        for at, ref in ((0, p_up), (32, p_down)):
            parts = [share[at : at + 32, 768 * k : 768 * k + 768] for k in range(3)]
            ref[...] = dot_f32(three, jnp.concatenate(parts, axis=0).astype(BF)).astype(BF)

    deep_moves, right_moves, down_moves, own_copies, core_moves, loads = {}, {}, {}, {}, {}, {}

    def deep_send(w):
        spot = whole[w].at[place.t, rows_of(place, WEIGHTS[w][1])]
        own_copies[w] = link.copy(piece[w], spot)
        deep_moves[w] = [link.send(piece[w], spot, place.deep[k]) for k in (1, 2, 3)]

    def plane_send(w, k):
        rows = WEIGHTS[w][1]
        spot = whole[w].at[place.behind[k], rows_of(place, rows)]
        src = piece[w] if k == 0 else spot
        if k:
            deep_moves[w][k - 1].wait_recv()
        right_moves[w, k] = link.send(src, spot, place.right)
        down_moves[w, k] = link.send(src, spot, place.down)

    def plane_pass(w, k):
        rows = WEIGHTS[w][1]
        half = rows // 2
        right_moves[w, k].wait_recv()
        down_moves[w, k].wait_recv()
        t = place.behind[k]
        right_at = place.c * (4 * rows) + (place.right[0] // 2) * rows
        down_at = place.c * (4 * rows) + (place.down[0] // 2) * rows
        first = whole[w].at[t, pl.ds(pl.multiple_of(right_at, 16), half)]
        second = whole[w].at[t, pl.ds(pl.multiple_of(down_at + half, 16), half)]
        right_moves[w, k, 1] = link.send(second, second, place.right)
        down_moves[w, k, 1] = link.send(first, first, place.down)

    def core_pass(w, k):
        if k == 0:
            own_copies[w].wait()
        right_moves[w, k, 1].wait_recv()
        down_moves[w, k, 1].wait_recv()
        spot = whole[w].at[place.behind[k], half_of(place, WEIGHTS[w][1])]
        core_moves[w, k] = link.send(spot, spot, place.core)

    def load(w, k):
        core_moves[w, k].wait_recv()
        t = place.behind[k]
        loads[w, k] = link.copy(whole[w].at[t], held[w].at[t])

    def qkv_step(k):
        loads[0, k].wait()
        t = place.behind[k]

        def body(rows):
            lin = dot_f32(x_row[rows, :], v_qkv[t]) + bias_qkv[t]
            qkv[t, rows, :] = lin.astype(BF)

        row_loop(body, 256)

    def attention(k):
        t = place.behind[k]

        def body(rows):
            allowed = id_col[rows, :] == id_row[...]
            parts = []
            for i in range(3):
                at = 64 * i
                scores = dot_nt(qkv[t, rows, at : at + 64], qkv[t, :, 192 + at : 256 + at]) * 0.125
                scores = jnp.where(allowed, scores, MASKED)
                weight = jnp.exp(scores - jnp.max(scores, axis=1, keepdims=True))
                weight = weight * (1.0 / jnp.sum(weight, axis=1, keepdims=True))
                low = weight.astype(BF)
                prob[3 * t + i, rows, :] = low
                parts.append(dot_f32(low, qkv[t, :, 384 + at : 448 + at]))
            att[t, rows, :] = jnp.concatenate(parts, axis=1).astype(BF)

        row_loop(body, 256)
        tidy.append(link.copy(qkv.at[t], qkv_out.at[t]))
        tidy.append(link.copy(att.at[t], att_out.at[t]))
        tidy.append(link.copy(prob.at[pl.ds(3 * t, 3)], prob_out.at[pl.ds(3 * t, 3)]))

    def out_step():
        pick = compact_out()
        for k in range(4):
            loads[1, k].wait()
        for t in range(4):
            v_compact[t] = dot_f32(pick, v_out[t]).astype(BF)
        tidy.append(link.copy(v_compact, out_compact))

        def body(rows):
            z = x_row[rows, :].astype(F32) + norm[0:1, :]
            for t in range(4):
                z = z + dot_f32(att[t, rows, :], v_compact[t])
            normed, inverse = normalize(z)
            n_one[rows, :] = normed
            inv[0, rows, :] = inverse
            h = normed * norm[2:3, :] + norm[3:4, :]
            h_low[rows, :] = h.astype(BF)
            h_wide[rows, :] = h
            total[rows, :] = h + norm[1:2, :]

        row_loop(body, 256)
        tidy.append(link.copy(n_one, n_one_out))
        tidy.append(link.copy(h_low, h_out))

    def up_step(k):
        loads[2, k].wait()
        t = place.behind[k]

        def body(rows):
            pre = dot_f32(h_low[rows, :], v_up[t]) + small[t, 0:1, 384:1152]
            below = 0.5 + 0.5 * lax.erf(pre * (0.5**0.5))
            act[t, rows, :] = (pre * below).astype(BF)
            slope = below + pre * (jnp.exp(-0.5 * pre * pre) * 0.3989422804014327)
            pull[t, rows, :] = slope.astype(BF)

        row_loop(body, 256)
        tidy.append(link.copy(act.at[t], act_out.at[t]))
        tidy.append(link.copy(pull.at[t], pull_out.at[t]))

    def down_step(k):
        loads[3, k].wait()
        t = place.behind[k]

        def body(rows):
            total[rows, :] += dot_f32(act[t, rows, :], v_down[t])

        row_loop(body, 256)

    def end_step():
        ids = lax.broadcasted_iota(jnp.int32, (SMAX, 512), 0)
        member = jnp.where(ids == id_row[...], 1.0, 0.0)
        count = jnp.maximum(jnp.sum(member, axis=1, keepdims=True), 1.0)

        def body(rows):
            normed, inverse = normalize(total[rows, :])
            inv[1, rows, :] = inverse
            out = normed * norm[4:5, :] + norm[5:6, :]
            total[rows, :] = normed
            h_wide[rows, :] = out
            row_low[rows, :] = out.astype(BF)

        row_loop(body, 256)
        pool[...] = jnp.dot(member, h_wide[...], precision=exact_precision, preferred_element_type=F32) / count
        tidy.append(link.copy(total, n_two_out))
        tidy.append(link.copy(row_low, row_out))
        tidy.append(link.copy(pool, pool_out))
        tidy.append(link.copy(inv, inv_out))

    every = range(4)
    others = (1, 2, 3)
    deep_send(0)
    plane_send(0, 0)
    spread_out()
    deep_send(1)
    plane_send(1, 0)
    collect(ffn_sent, 0, 64, canon_ffn, land_ffn)
    spread_ffn()
    plane_send(2, 0)
    plane_pass(0, 0)
    for k in others:
        plane_send(0, k)
    deep_send(2)
    for move in small_moves:
        move.wait_recv()
    small_total[...] = small_mine[...] + small_land[0] + small_land[1] + small_land[2]
    small_stay = link.copy(small_total, small.at[place.t])
    small_deep = [link.send(small_total, small.at[place.t], place.deep[k]) for k in others]
    x_stay.wait()
    for move in x_moves:
        move.wait_recv()
    tidy.append(link.copy(x_row, x_out))
    plane_pass(1, 0)
    for k in others:
        plane_send(1, k)
    core_pass(0, 0)
    plane_send(3, 0)
    for k in others:
        plane_pass(0, k)
    small_stay.wait()
    for move in small_deep:
        move.wait_recv()
    norm_vectors(small, norm)
    for t in every:
        bias_qkv[t] = jnp.concatenate(
            [small[t, 0:1, :192], jnp.zeros((1, 192), F32), small[t, 0:1, 192:384]], axis=1
        )
    tidy.append(link.copy(small, small_out))
    load(0, 0)
    qkv_step(0)
    attention(0)
    for k in others:
        plane_send(2, k)
    deep_send(3)
    for k in others:
        plane_pass(1, k)
        core_pass(0, k)
    plane_pass(2, 0)
    for k in others:
        load(0, k)
    qkv_step(1)
    attention(1)
    plane_pass(3, 0)
    for k in every:
        core_pass(1, k)
    plane_pass(2, 1)
    qkv_step(2)
    attention(2)
    plane_pass(2, 2)
    core_pass(2, 0)
    for k in every:
        load(1, k)
    qkv_step(3)
    plane_pass(2, 3)
    core_pass(2, 1)
    attention(3)
    load(2, 0)
    plane_send(3, 1)
    plane_send(3, 2)
    plane_send(3, 3)
    gy_moves = [
        link.send(gy_in.at[place.ahead[k]], gy_row.at[mine_rows], place.deep[k]) for k in others
    ]
    core_pass(2, 2)
    core_pass(3, 0)
    out_step()
    load(2, 1)
    load(2, 2)
    load(3, 0)
    core_pass(2, 3)
    plane_pass(3, 1)
    up_step(0)
    up_step(1)
    plane_pass(3, 2)
    core_pass(3, 1)
    load(2, 3)
    load(3, 1)
    up_step(2)
    plane_pass(3, 3)
    core_pass(3, 2)
    up_step(3)
    down_step(0)
    core_pass(3, 3)
    down_step(1)
    load(3, 2)
    down_step(2)
    load(3, 3)
    down_step(3)
    end_step()
    for move in gy_moves:
        move.wait_recv()
    for copy in tidy:
        copy.wait()
    link.finish()


def forward_call(master, slot_col, small_slot, id_col, id_row, x_in, gy_in):
    anywhere = pl.BlockSpec(memory_space=pl.ANY)
    vmem = pl.BlockSpec(memory_space=pltpu.VMEM)
    shape = jax.ShapeDtypeStruct
    outs = [
        ((4, 768, 576), BF),
        ((4, 256, 768), BF),
        ((4, 768, 768), BF),
        ((4, 768, 768), BF),
        ((4, 192, 768), BF),
        ((4, 8, 2304), F32),
        ((512, 768), BF),
        ((512, 768), BF),
        ((4, 512, 576), BF),
        ((12, 512, 512), BF),
        ((4, 512, 192), BF),
        ((512, 768), F32),
        ((512, 768), BF),
        ((4, 512, 768), BF),
        ((4, 512, 768), BF),
        ((512, 768), F32),
        ((2, 512, 1), F32),
        ((512, 768), BF),
        ((8, 768), F32),
    ]
    scratch = [
        ((2, 192, 2304), BF),
        ((4, 32, 2304), BF),
        ((4, 64, 2304), BF),
        ((3, 32, 2304), BF),
        ((3, 64, 2304), BF),
        ((96, 2304), F32),
        ((96, 576), BF),
        ((32, 768), BF),
        ((96, 768), BF),
        ((96, 768), BF),
        ((8, 2304), F32),
        ((3, 8, 2304), F32),
        ((8, 2304), F32),
        ((4, 8, 2304), F32),
        ((8, 768), F32),
        ((4, 1, 576), F32),
        ((4, 768, 576), BF),
        ((4, 256, 768), BF),
        ((4, 192, 768), BF),
        ((4, 768, 768), BF),
        ((4, 768, 768), BF),
        ((512, 768), BF),
        ((4, 512, 576), BF),
        ((12, 512, 512), BF),
        ((4, 512, 192), BF),
        ((512, 768), F32),
        ((512, 768), F32),
        ((512, 768), BF),
        ((4, 512, 768), BF),
        ((4, 512, 768), BF),
        ((512, 768), F32),
        ((2, 512, 1), F32),
        ((512, 768), BF),
        ((8, 768), F32),
    ]
    return pl.pallas_call(
        forward_kernel,
        out_shape=[shape(*o) for o in outs],
        in_specs=[vmem] * 5 + [anywhere] * 2,
        out_specs=[anywhere] * len(outs),
        scratch_shapes=[pltpu.VMEM(*s) for s in scratch]
        + [
            pltpu.SemaphoreType.DMA((112,)),
            pltpu.SemaphoreType.DMA((112,)),
            pltpu.SemaphoreType.DMA((64,)),
        ],
        compiler_params=pltpu.CompilerParams(
            collective_id=0, has_side_effects=True, vmem_limit_bytes=60 * MIB
        ),
        name="gather_and_forward",
    )(master, slot_col, small_slot, id_col, id_row, x_in, gy_in)


def backward_kernel(
    flag_col,
    out_row,
    pool_in,
    gy_in,
    n_two_in,
    inv_in,
    small_in,
    act_in,
    pull_in,
    w_down,
    w_up,
    h_in,
    n_one_in,
    att_in,
    w_out,
    qkv_in,
    prob_in,
    w_qkv,
    x_in,
    blocks,
    small_out,
    out_mine,
    dx_mine,
    pool_out,
    *scratch,
):
    sums, cores, lefts, tops, lefts_two, tops_two, deeps = (scratch[4 * i : 4 * i + 4] for i in range(7))
    (
        ring,
        ring_narrow,
        share,
        share_low,
        small_grad,
        small_land,
        small,
        norm,
        gy,
        normed,
        inv,
        act,
        pull,
        v_down,
        v_up,
        h_low,
        att,
        v_out,
        qkv,
        prob,
        v_qkv,
        x_row,
        wide,
        low,
        total,
        d_up,
        d_att,
        d_qkv,
        turned,
        go,
        reds,
        red_up,
        red_qv,
        send_sems,
        recv_sems,
        local_sems,
    ) = scratch[28:]
    place = Place()
    link = Sender(send_sems, recv_sems, local_sems)
    t_of = place.ahead
    steps = (1, 2, 3, 0)
    got = {}

    def load(name, src, dst):
        got[name] = link.copy(src, dst)

    load("small", small_in, small)
    load("normed", n_two_in, normed)
    load("gy", gy_in, gy)
    load("inv", inv_in, inv)

    def load_ffn(i):
        t, slot = t_of[steps[i]], i % 2
        load(("act", i), act_in.at[t], act.at[slot])
        load(("down", i), w_down.at[t], v_down.at[slot])
        load(("pull", i), pull_in.at[t], pull.at[slot])
        load(("up", i), w_up.at[t], v_up.at[slot])

    def load_att(i):
        t, slot = t_of[steps[i]], i % 2
        load(("prob", i), prob_in.at[pl.ds(3 * t, 3)], prob.at[slot])
        load(("qkv", i), w_qkv.at[t], v_qkv.at[slot])

    load_ffn(0)
    load("h", h_in, h_low)
    load_ffn(1)
    load("att", att_in, att)
    load("wout", w_out, v_out)
    load("qkvs", qkv_in, qkv)
    load("x", x_in, x_row)
    load_att(0)
    load_att(1)
    place.greet()
    t, x, y, c = place.t, place.x, place.y, place.c

    moves, stay = [], []
    stay.append(link.copy(out_row.at[pl.ds(pl.multiple_of(t * 128, 128), 128)], out_mine.at[t]))
    stay.append(link.copy(pool_in, pool_out.at[t]))
    for k in (1, 2, 3):
        part = out_row.at[pl.ds(pl.multiple_of(t_of[k] * 128, 128), 128)]
        moves.append(link.send(part, out_mine.at[t], place.deep[k]))
        moves.append(link.send(pool_in, pool_out.at[t], place.deep[k]))

    core_moves, first, second, third = {}, {}, {}, {}
    ring_open = [None] * 5
    ring_at = [0, 0]

    def chip_row(w, k, yy, xx, half):
        rows = WEIGHTS[w][1]
        at = pl.multiple_of((yy * 2 + xx) * rows + half * (rows // 2), 16)
        return sums[w].at[t_of[k], pl.ds(at, rows // 2)]

    def produce(w, k, make):
        narrow = w == 0
        slot = 3 + ring_at[1] % 2 if narrow else ring_at[0] % 3
        ring_at[narrow] += 1
        if ring_open[slot] is not None:
            link.sent(ring_open[slot])
        cols, rows = WEIGHTS[w]
        away = ring_narrow.at[slot - 3] if narrow else ring.at[slot, pl.ds(0, 4 * rows)]
        away[...] = make(1 - c).astype(BF)
        move = link.send(away, cores[w].at[k], place.core)
        ring_open[slot] = move
        core_moves[w, k] = move
        sums[w][t_of[k]] = make(c).astype(BF)

    def core_add(w, k):
        core_moves[w, k].wait_recv()
        rows = WEIGHTS[w][1]

        @pl.loop(0, 4)
        def _(i):
            at = pl.ds(pl.multiple_of(i * rows, 32), rows)
            sums[w][t_of[k], at, :] += cores[w][k, at, :]

        first[w, k] = []
        for i in (0, 1):
            first[w, k].append(link.send(chip_row(w, k, i, 1 - x, 0), lefts[w].at[k, i], place.right))
            first[w, k].append(link.send(chip_row(w, k, 1 - y, i, 1), tops[w].at[k, i], place.down))

    def add(spot, other):
        spot[...] = spot[...] + other[...]

    def plane_add(w, k):
        for move in first[w, k]:
            move.wait_recv()
        down_part, right_part = chip_row(w, k, 1 - y, x, 0), chip_row(w, k, y, 1 - x, 1)
        add(down_part, lefts[w].at[k, 1 - y])
        add(right_part, tops[w].at[k, 1 - x])
        second[w, k] = [
            link.send(down_part, lefts_two[w].at[k], place.down),
            link.send(right_part, tops_two[w].at[k], place.right),
        ]
        add(chip_row(w, k, y, x, 0), lefts[w].at[k, y])
        add(chip_row(w, k, y, x, 1), tops[w].at[k, x])

    def deep_add(w, k):
        for move in second[w, k]:
            move.wait_recv()
        add(chip_row(w, k, y, x, 0), lefts_two[w].at[k])
        add(chip_row(w, k, y, x, 1), tops_two[w].at[k])
        rows = WEIGHTS[w][1]
        if k:
            spot = pl.ds(pl.multiple_of(place.xy * rows, 16), rows)
            third[w, k] = link.send(sums[w].at[t_of[k], spot], deeps[w].at[k - 1], place.deep[k])

    def end(w):
        rows = WEIGHTS[w][1]
        spot = pl.ds(pl.multiple_of(place.xy * rows, 16), rows)
        whole = sums[w][t, spot, :].astype(F32)
        for k in (1, 2, 3):
            third[w, k].wait_recv()
            whole = whole + deeps[w][k - 1].astype(F32)
        whole = whole.astype(BF)
        if w == 0:
            parts = dot_tn(interleave(96, 4), whole)
            share[64:88, :] = jnp.concatenate([parts[24 * r : 24 * r + 24] for r in range(4)], axis=1)
        elif w == 1:
            parts = dot_tn(interleave_out(), whole)
            for k in range(3):
                share[88:96, 768 * k : 768 * k + 768] = parts[8 * k : 8 * k + 8]
        else:
            at = 0 if w == 2 else 32
            parts = dot_tn(interleave(96, 3), whole)
            for k in range(3):
                share[at : at + 32, 768 * k : 768 * k + 768] = parts[32 * k : 32 * k + 32]

    def column_sum(value):
        return jnp.sum(value, axis=0, keepdims=True)

    def norm_two_back():
        def body(rows):
            grad = gy[rows, :].astype(F32) * flag_col[rows, :]
            n = normed[rows, :]
            dz = norm_back(grad * norm[4:5, :], n, inv[1, rows, :])
            wide[rows, :] = dz
            total[rows, :] = dz
            low[rows, :] = dz.astype(BF)
            reds[4:5, :] += column_sum(grad * n)
            reds[5:6, :] += column_sum(grad)
            reds[1:2, :] += column_sum(dz)

        row_loop(body)

    def lanes(which):
        return pl.ds(pl.multiple_of(which * 384, 128), 384)

    def down_piece(i):
        k, slot = steps[i], i % 2
        got["act", i].wait()
        produce(3, k, lambda which: dot_tn(act[slot, :, lanes(which)], low[...]))

    def act_back(i):
        k, slot = steps[i], i % 2
        got["down", i].wait()
        got["pull", i].wait()

        def body(rows):
            grad = dot_nt(low[rows, :], v_down[slot]) * pull[slot, rows, :].astype(F32)
            red_up[t_of[k]] += column_sum(grad)
            d_up[rows, :] = grad.astype(BF)

        row_loop(body, 256)

    def up_piece(i):
        if i == 0:
            got["h"].wait()
        produce(2, steps[i], lambda which: dot_tn(h_low[:, lanes(which)], d_up[...]))

    def hidden_back(i):
        slot = i % 2
        got["up", i].wait()

        def body(rows):
            total[rows, :] += dot_nt(d_up[rows, :], v_up[slot])

        row_loop(body, 256)
        if i + 2 < 4:
            load_ffn(i + 2)
        if i == 1:
            load("n_one", n_one_in, normed)

    def norm_one_back():
        got["n_one"].wait()

        def body(rows):
            dh = total[rows, :]
            n = normed[rows, :]
            dz = norm_back(dh * norm[2:3, :], n, inv[0, rows, :])
            total[rows, :] = dz
            low[rows, :] = dz.astype(BF)
            reds[2:3, :] += column_sum(dh * n)
            reds[3:4, :] += column_sum(dh)
            reds[0:1, :] += column_sum(dz)

        row_loop(body)

    def out_piece(i):
        k = steps[i]
        if i == 0:
            got["att"].wait()
            got["wout"].wait()
        go[...] = dot_tn(att[t_of[k]], low[...])

        def make(which):
            part = go[pl.ds(pl.multiple_of(which * 96, 96), 96), :]
            pad = jnp.zeros((8, 768), F32)
            parts = []
            for j in range(4):
                parts += [part[24 * j : 24 * j + 24], pad]
            return jnp.concatenate(parts, axis=0)

        produce(1, k, make)

        def body(rows):
            d_att[rows, :] = dot_nt(low[rows, :], v_out[t_of[k]]).astype(BF)

        row_loop(body, 256)

    def attention_back(i):
        k, slot = steps[i], i % 2
        tk = t_of[k]
        if i == 0:
            got["qkvs"].wait()
        got["prob", i].wait()
        turned[...] = jnp.zeros_like(turned)

        def body(rows):
            d_queries = []
            for j in range(3):
                at = 64 * j
                grad = d_att[rows, at : at + 64]
                weight_low = prob[slot, j, rows, :]
                weight = weight_low.astype(F32)
                d_prob = dot_nt(grad, qkv[tk, :, 384 + at : 448 + at]) * weight
                inner = jnp.sum(d_prob, axis=1, keepdims=True)
                d_scores = (d_prob - weight * inner).astype(BF)
                d_queries.append(dot_f32(d_scores, qkv[tk, :, 192 + at : 256 + at]))
                turned[at : at + 64, :] += dot_tn(qkv[tk, rows, at : at + 64], d_scores)
                turned[192 + at : 256 + at, :] += dot_tn(grad, weight_low)
            dq = jnp.concatenate(d_queries, axis=1) * 0.125
            red_qv[tk, :, :192] += column_sum(dq)
            d_qkv[rows, :192] = dq.astype(BF)

        row_loop(body, 256)
        dk = jnp.transpose(turned[:192, :]) * 0.125
        dv = jnp.transpose(turned[192:, :])
        red_qv[tk, :, 192:] += column_sum(dv)
        d_qkv[:, 192:] = jnp.concatenate([dk, dv], axis=1).astype(BF)

    def qkv_piece(i):
        k, slot = steps[i], i % 2
        if i == 0:
            got["x"].wait()
        produce(0, k, lambda which: dot_tn(x_row[:, lanes(which)], d_qkv[...]))
        got["qkv", i].wait()

        def body(rows):
            total[rows, :] += dot_nt(d_qkv[rows, :], v_qkv[slot])

        row_loop(body, 256)
        if i + 2 < 4:
            load_att(i + 2)

    def share_send(lo, hi):
        share_low[lo:hi, :] = share[lo:hi, :].astype(BF)
        mine = c * 4 + place.xy
        rows = pl.ds(lo, hi - lo)
        return (
            link.copy(share_low.at[rows], blocks.at[mine, rows]),
            link.send(share_low.at[rows], blocks.at[mine, rows], place.right),
            link.send(share_low.at[rows], blocks.at[mine, rows], place.down),
        )

    def share_pass(sent, lo, hi):
        half = (hi - lo) // 2
        sent[1].wait_recv()
        sent[2].wait_recv()
        one = blocks.at[c * 4 + place.right[0] // 2, pl.ds(lo, half)]
        two = blocks.at[c * 4 + place.down[0] // 2, pl.ds(lo + half, half)]
        return link.send(one, one, place.down), link.send(two, two, place.right)

    def share_across(sent, passed, lo, hi):
        sent[0].wait()
        passed[0].wait_recv()
        passed[1].wait_recv()
        spot = blocks.at[pl.ds(c * 4, 4), pl.ds(lo, hi - lo)]
        return link.send(spot, spot, place.core)

    got["small"].wait()
    norm_vectors(small, norm)
    reds[...] = jnp.zeros_like(reds)
    red_up[...] = jnp.zeros_like(red_up)
    red_qv[...] = jnp.zeros_like(red_qv)
    small_grad[...] = jnp.zeros_like(small_grad)
    for name in ("normed", "gy", "inv"):
        got[name].wait()
    norm_two_back()
    down = [(3, k) for k in steps]
    up = [(2, k) for k in steps]
    out = [(1, k) for k in steps]
    att_in_w = [(0, k) for k in steps]
    down_piece(0)
    act_back(0)
    core_add(*down[0])
    up_piece(0)
    hidden_back(0)
    core_add(*up[0])
    plane_add(*down[0])
    down_piece(1)
    act_back(1)
    core_add(*down[1])
    plane_add(*up[0])
    up_piece(1)
    deep_add(*down[0])
    hidden_back(1)
    core_add(*up[1])
    plane_add(*down[1])
    down_piece(2)
    deep_add(*up[0])
    act_back(2)
    core_add(*down[2])
    up_piece(2)
    plane_add(*up[1])
    deep_add(*down[1])
    hidden_back(2)
    core_add(*up[2])
    down_piece(3)
    plane_add(*down[2])
    deep_add(*up[1])
    act_back(3)
    core_add(*down[3])
    up_piece(3)
    deep_add(*down[2])
    hidden_back(3)
    core_add(*up[3])
    plane_add(*up[2])
    norm_one_back()
    out_piece(0)
    plane_add(*down[3])
    deep_add(*up[2])
    attention_back(0)
    core_add(*out[0])
    plane_add(*up[3])
    deep_add(*down[3])
    qkv_piece(0)
    out_piece(1)
    deep_add(*up[3])
    core_add(*att_in_w[0])
    attention_back(1)
    core_add(*out[1])
    plane_add(*out[0])
    end(3)
    end(2)
    ffn_sent = share_send(0, 64)
    qkv_piece(1)
    plane_add(*att_in_w[0])
    deep_add(*out[0])
    out_piece(2)
    core_add(*att_in_w[1])
    attention_back(2)
    core_add(*out[2])
    plane_add(*out[1])
    deep_add(*att_in_w[0])
    ffn_passed = share_pass(ffn_sent, 0, 64)
    qkv_piece(2)
    plane_add(*att_in_w[1])
    out_piece(3)
    core_add(*att_in_w[2])
    deep_add(*out[1])
    attention_back(3)
    core_add(*out[3])
    plane_add(*out[2])
    deep_add(*att_in_w[1])
    qkv_piece(3)
    plane_add(*att_in_w[2])
    plane_add(*out[3])
    core_add(*att_in_w[3])

    def dx_body(rows):
        low[rows, :] = total[rows, :].astype(BF)

    row_loop(dx_body)
    for q in range(4):
        at = slice(192 * q, 192 * q + 192)
        small_grad[q, 0:1, :] = jnp.concatenate(
            [red_qv[q], red_up[q]] + [reds[i : i + 1, at] for i in range(6)], axis=1
        )
    small_sum = small_land.at[6]
    small_keep = link.copy(small_grad.at[t], small_sum)
    small_moves = [link.send(small_grad.at[t_of[k]], small_land.at[k - 1], place.deep[k]) for k in (1, 2, 3)]

    deep_add(*out[2])
    deep_add(*att_in_w[2])
    own_rows = pl.ds(pl.multiple_of(t * 128, 128), 128)
    stay.append(link.copy(low.at[own_rows], dx_mine.at[t]))
    for k in (1, 2, 3):
        part = low.at[pl.ds(pl.multiple_of(t_of[k] * 128, 128), 128)]
        moves.append(link.send(part, dx_mine.at[t], place.deep[k]))
    small_keep.wait()
    for move in small_moves:
        move.wait_recv()
    small_land[7] = small_land[6] + small_land[0] + small_land[1] + small_land[2]
    doubling = [link.send(small_land.at[7], small_land.at[3], place.core)]
    deep_add(*out[3])
    plane_add(*att_in_w[3])
    ffn_across = share_across(ffn_sent, ffn_passed, 0, 64)
    deep_add(*att_in_w[3])
    end(1)
    doubling[0].wait_recv()
    small_land[8] = small_land[7] + small_land[3]
    doubling.append(link.send(small_land.at[8], small_land.at[4], place.right))
    end(0)
    att_sent = share_send(64, 96)
    doubling[1].wait_recv()
    small_land[9] = small_land[8] + small_land[4]
    doubling.append(link.send(small_land.at[9], small_land.at[5], place.down))
    att_passed = share_pass(att_sent, 64, 96)
    doubling[2].wait_recv()
    small_out[...] = small_land[9] + small_land[5]
    att_across = share_across(att_sent, att_passed, 64, 96)
    ffn_across.wait_recv()
    att_across.wait_recv()
    for move in moves:
        move.wait_recv()
    for copy in stay:
        copy.wait()
    link.finish()


def backward_call(*args):
    anywhere = pl.BlockSpec(memory_space=pl.ANY)
    vmem = pl.BlockSpec(memory_space=pltpu.VMEM)
    shape = jax.ShapeDtypeStruct
    sums = [((4, 4 * rows, cols), BF) for cols, rows in WEIGHTS]
    halves = [((4, 2, rows // 2, cols), BF) for cols, rows in WEIGHTS]
    singles = [((4, rows // 2, cols), BF) for cols, rows in WEIGHTS]
    deeps = [((3, rows, cols), BF) for cols, rows in WEIGHTS]
    rest = [
        ((3, 384, 768), BF),
        ((2, 384, 576), BF),
        ((96, 2304), F32),
        ((96, 2304), BF),
        ((4, 8, 2304), F32),
        ((11, 8, 2304), F32),
        ((4, 8, 2304), F32),
        ((8, 768), F32),
        ((512, 768), BF),
        ((512, 768), F32),
        ((2, 512, 1), F32),
        ((2, 512, 768), BF),
        ((2, 512, 768), BF),
        ((2, 768, 768), BF),
        ((2, 768, 768), BF),
        ((512, 768), BF),
        ((4, 512, 192), BF),
        ((4, 192, 768), BF),
        ((4, 512, 576), BF),
        ((2, 3, 512, 512), BF),
        ((2, 768, 576), BF),
        ((512, 768), BF),
        ((512, 768), F32),
        ((512, 768), BF),
        ((512, 768), F32),
        ((512, 768), BF),
        ((512, 192), BF),
        ((512, 576), BF),
        ((384, 512), F32),
        ((192, 768), F32),
        ((8, 768), F32),
        ((4, 1, 768), F32),
        ((4, 1, 384), F32),
    ]
    scratch = sums + sums + halves + halves + singles + singles + deeps + rest
    return pl.pallas_call(
        backward_kernel,
        out_shape=[
            shape((8, 96, 2304), BF),
            shape((8, 2304), F32),
            shape((4, 128, 768), BF),
            shape((4, 128, 768), BF),
            shape((4, 8, 768), F32),
        ],
        in_specs=[vmem] + [anywhere] * 18,
        out_specs=[anywhere, vmem, anywhere, anywhere, anywhere],
        scratch_shapes=[pltpu.VMEM(*s) for s in scratch]
        + [
            pltpu.SemaphoreType.DMA((160,)),
            pltpu.SemaphoreType.DMA((160,)),
            pltpu.SemaphoreType.DMA((64,)),
        ],
        compiler_params=pltpu.CompilerParams(
            collective_id=1, has_side_effects=True, vmem_limit_bytes=62 * MIB
        ),
        name="backward_and_reduce",
    )(*args)


def local_rows(
    layer_input_rows,
    sentence_index_row,
    padding_mask,
    output_gradient,
    owner_rank,
    master_state,
    first_moment,
    second_moment,
):
    tensor_at = lax.axis_index("tensor")
    data_at = lax.axis_index("dp")
    per_owner = master_state.shape[1]
    block_len = master_state.shape[2]
    slot_of = slot_tables(owner_rank, per_owner)
    slot_order = jnp.concatenate(
        [
            slot_of[:256].reshape(2, 4, 32),
            slot_of[256:512].reshape(2, 4, 32),
            slot_of[512:704].reshape(2, 4, 24),
            slot_of[704:768].reshape(2, 4, 8),
        ],
        axis=2,
    ).reshape(768)
    core_order = lax.dynamic_slice_in_dim(slot_order, (data_at % 2) * 384, 384, 0)[:, None]
    small_slot = jnp.broadcast_to(slot_of[768], (8, 1))

    labels = lax.dynamic_index_in_dim(sentence_index_row, tensor_at, 0, keepdims=False)
    flags = lax.dynamic_index_in_dim(padding_mask, tensor_at, 0, keepdims=False)
    ids = jnp.where(flags == 1, labels, -1 - jnp.arange(flags.shape[0], dtype=jnp.int32))
    (
        w_qkv,
        _,
        w_up,
        w_down,
        w_out,
        small_all,
        x_row,
        gy_row,
        qkv,
        prob_low,
        attended,
        normed_one,
        h_low,
        act,
        pull,
        normed_two,
        inverse,
        out_row,
        pool_mean,
    ) = forward_call(
        master_state[0],
        core_order,
        small_slot,
        ids[:, None],
        ids[None],
        jnp.transpose(layer_input_rows, (1, 0, 2)),
        jnp.transpose(output_gradient, (1, 0, 2)),
    )
    blocks, small_sum, out_mine, dx_mine, pool_all = backward_call(
        flags.astype(F32)[:, None],
        out_row,
        pool_mean,
        gy_row,
        normed_two,
        inverse,
        small_all,
        act,
        pull,
        w_down,
        w_up,
        h_low,
        normed_one,
        attended,
        w_out,
        qkv,
        prob_low,
        w_qkv,
        x_row,
    )
    small_row = small_sum[0]
    norm_grads = small_row[1152:].reshape(6, 192)
    pooled = lax.dynamic_slice_in_dim(pool_all, tensor_at * 192, 192, 2)

    wanted = data_at * per_owner + jnp.arange(per_owner, dtype=jnp.int32)
    block_of, filled = slot_blocks(slot_of, wanted)
    pick = (slot_order[None, :] == wanted[:, None]).astype(BF)
    owned = dot_f32(pick, blocks.reshape(768, block_len))
    owned = jnp.where((wanted == slot_of[768])[:, None], small_row[None], owned)
    token_position = block_of[:, None] * block_len + jnp.arange(block_len, dtype=jnp.int32)[None, :]
    step_rate, decay_on = step_rates(token_position, MODEL_WIDTH, FF, 4)
    new_master, new_first, new_second = adamw(
        owned,
        first_moment[0],
        second_moment[0],
        master_state[0],
        step_rate,
        decay_on,
        filled[:, None],
    )
    return (
        jnp.transpose(out_mine, (1, 0, 2)).astype(F32),
        pooled,
        jnp.transpose(dx_mine, (1, 0, 2)).astype(F32),
        new_master[None],
        new_first[None],
        new_second[None],
        norm_grads,
    )


def solution(mesh):
    in_specs = (
        P("tensor", "dp", None),
        P("dp", None),
        P("dp", None),
        P("tensor", "dp", None),
        P(),
        P("tensor", "dp", None),
        P("tensor", "dp", None),
        P("tensor", "dp", None),
    )
    out_specs = (
        P("tensor", "dp", None),
        P("dp", None, "tensor"),
        P("tensor", "dp", None),
        P("tensor", "dp", None),
        P("tensor", "dp", None),
        P("tensor", "dp", None),
        P(None, "tensor"),
    )
    plain = mesh.shape["dp"] != 8 or mesh.shape["tensor"] != 4
    body = local_general if plain else local_rows
    return jax.shard_map(body, mesh=mesh, in_specs=in_specs, out_specs=out_specs, check_vma=False)
```

```python
import jax
import numpy as np
import jax.numpy as jnp
from jax import lax
from jax.experimental import pallas as pl
from jax.experimental.pallas import tpu as pltpu
from jax.sharding import PartitionSpec as P

MODEL_WIDTH = 768
HEAD_DIM = 64
FF = 3072
SMAX = 8
STEP = 10


NORM_EPS = 1e-05
ADAM_EPS = 1e-08
BETA_ONE = 0.9
BETA_TWO = 0.999
DECAY_RATE = 0.01
MASKED = -1e30
exact_precision = lax.Precision.HIGHEST


def slot_tables(owner_rank, per_owner):
    ordinal = jnp.arange(owner_rank.shape[0], dtype=jnp.int32)
    same_owner = owner_rank[:, None] == owner_rank[None, :]
    earlier = ordinal[None, :] < ordinal[:, None]
    ranking = jnp.sum((same_owner & earlier).astype(jnp.int32), axis=1)
    return owner_rank * per_owner + ranking


def slot_blocks(slot_of, wanted):
    matches = slot_of[None, :] == wanted[:, None]
    filled = jnp.any(matches, axis=1)
    ordinal = jnp.arange(slot_of.shape[0], dtype=jnp.int32)
    block_of = jnp.sum(jnp.where(matches, ordinal[None, :], 0), axis=1)
    return (block_of, filled)


def step_rates(token_position, width, hidden, tensor_size):
    width_loc = width // tensor_size
    ffn_loc = hidden // tensor_size
    end_up = width * ffn_loc
    end_down = end_up + ffn_loc * width
    end_qkv = end_down + width * 3 * width_loc
    end_out = end_qkv + width_loc * width
    offset = token_position - end_out
    first_gain = (offset >= 4 * width_loc + ffn_loc) & (offset < 5 * width_loc + ffn_loc)
    second_gain = (offset >= 6 * width_loc + ffn_loc) & (offset < 7 * width_loc + ffn_loc)
    small_rate = jnp.where(first_gain | second_gain, 0.2, 0.1)
    step_rate = jnp.where(
        token_position < end_up,
        width ** (-0.5),
        jnp.where(
            token_position < end_down,
            hidden ** (-0.5),
            jnp.where(
                token_position < end_qkv,
                width ** (-0.5),
                jnp.where(token_position < end_out, 4.0 * width ** (-0.5), small_rate),
            ),
        ),
    )
    decay_on = (token_position < end_out).astype(jnp.float32)
    return (step_rate.astype(jnp.float32), decay_on)


def adamw(gradient, moment, square, weight, step_rate, decay_on, filled):
    new_moment = BETA_ONE * moment + (1.0 - BETA_ONE) * gradient
    new_square = BETA_TWO * square + (1.0 - BETA_TWO) * gradient * gradient
    unbiased = new_moment / (1.0 - BETA_ONE**STEP)
    divisor = jnp.sqrt(new_square / (1.0 - BETA_TWO**STEP)) + ADAM_EPS
    new_weight = weight - step_rate * (unbiased / divisor + DECAY_RATE * decay_on * weight)
    zeroed = jnp.zeros_like(weight)
    return (
        jnp.where(filled, new_weight, zeroed),
        jnp.where(filled, new_moment, zeroed),
        jnp.where(filled, new_square, zeroed),
    )


def normalize(values):
    centred = values - jnp.mean(values, axis=-1, keepdims=True)
    inv_dev = lax.rsqrt(jnp.mean(centred * centred, axis=-1, keepdims=True) + NORM_EPS)
    return (centred * inv_dev, inv_dev)


def norm_back(grad_scaled, normed, inv_dev):
    first_mean = jnp.mean(grad_scaled, axis=-1, keepdims=True)
    second_mean = jnp.mean(grad_scaled * normed, axis=-1, keepdims=True)
    return inv_dev * (grad_scaled - first_mean - normed * second_mean)


def allowed_pairs(sentence_labels, real_token_flags):
    row_len = sentence_labels.shape[-1]
    same_sent = sentence_labels[:, :, None] == sentence_labels[:, None, :]
    live = (real_token_flags[:, :, None] == 1) & (real_token_flags[:, None, :] == 1)
    diagonal = jnp.eye(row_len, dtype=bool)[None]
    return same_sent & live | diagonal


def masked_scores(queries, key_rows, allowed, scaling):
    scores = (
        jnp.einsum("qshe,kshe->shqk", queries, key_rows, preferred_element_type=jnp.float32)
        * scaling
    )
    return jnp.where(allowed[:, None], scores, MASKED)


def split_flat(flat_all, width_loc, ffn_loc):
    end_up = MODEL_WIDTH * ffn_loc
    end_down = end_up + ffn_loc * MODEL_WIDTH
    end_qkv = end_down + MODEL_WIDTH * 3 * width_loc
    end_out = end_qkv + width_loc * MODEL_WIDTH
    return (
        flat_all[:end_up].reshape(MODEL_WIDTH, ffn_loc),
        flat_all[end_up:end_down].reshape(ffn_loc, MODEL_WIDTH),
        flat_all[end_down:end_qkv].reshape(MODEL_WIDTH, 3 * width_loc),
        flat_all[end_qkv:end_out].reshape(width_loc, MODEL_WIDTH),
        flat_all[end_out:],
    )


def local_general(
    layer_input_rows,
    sentence_index_row,
    padding_mask,
    output_gradient,
    owner_rank,
    master_state,
    first_moment,
    second_moment,
):
    tensor_size = lax.axis_size("tensor")
    tensor_at = lax.axis_index("tensor")
    data_size = lax.axis_size("dp")
    data_at = lax.axis_index("dp")
    width_loc = MODEL_WIDTH // tensor_size
    ffn_loc = FF // tensor_size
    heads_loc = width_loc // HEAD_DIM
    quarter = layer_input_rows.shape[0]
    seq_count = layer_input_rows.shape[1]
    row_len = quarter * tensor_size
    per_owner = master_state.shape[1]
    block_len = master_state.shape[2]
    nblocks = owner_rank.shape[0]
    slot_of = slot_tables(owner_rank, per_owner)
    gathered = lax.all_gather(master_state.astype(jnp.bfloat16), "dp", axis=1, tiled=True)[0]
    flat_weights = gathered[slot_of].reshape(nblocks * block_len)
    up_weight, down_weight, w_qkv, w_out, small_part = split_flat(flat_weights, width_loc, ffn_loc)
    bias_q = small_part[:width_loc].astype(jnp.float32)
    bias_v = small_part[width_loc : 2 * width_loc].astype(jnp.float32)
    expand_bias = small_part[2 * width_loc : 2 * width_loc + ffn_loc].astype(jnp.float32)
    norm_parts = small_part[2 * width_loc + ffn_loc :].reshape(6, width_loc)
    full_rows, norm_whole = (
        lax.all_gather(layer_input_rows, "tensor", axis=0, tiled=True),
        lax.all_gather(norm_parts, "tensor", axis=1, tiled=True),
    )
    norm_all = norm_whole.astype(jnp.float32)
    bias_out, bias_down = (norm_all[0], norm_all[1])
    gain_one, shift_one, gain_two, shift_two = (norm_all[2], norm_all[3], norm_all[4], norm_all[5])
    qkv_lin = jnp.einsum("lsd,de->lse", full_rows, w_qkv, preferred_element_type=jnp.float32)
    bias_qkv = jnp.concatenate([bias_q, jnp.zeros((width_loc,), jnp.float32), bias_v])
    qkv = (qkv_lin + bias_qkv).astype(jnp.bfloat16)
    queries = qkv[:, :, :width_loc].reshape(row_len, seq_count, heads_loc, HEAD_DIM)
    key_rows = qkv[:, :, width_loc : 2 * width_loc].reshape(row_len, seq_count, heads_loc, HEAD_DIM)
    values = qkv[:, :, 2 * width_loc :].reshape(row_len, seq_count, heads_loc, HEAD_DIM)
    scaling = HEAD_DIM ** (-0.5)
    allowed = allowed_pairs(sentence_index_row, padding_mask)
    scores = masked_scores(queries, key_rows, allowed, scaling)
    row_peak = jnp.max(scores, axis=-1, keepdims=True)
    log_total = row_peak + jnp.log(jnp.sum(jnp.exp(scores - row_peak), axis=-1, keepdims=True))
    prob_low = jnp.exp(scores - log_total).astype(jnp.bfloat16)
    attended = jnp.einsum("shqk,kshe->qshe", prob_low, values, preferred_element_type=jnp.float32)
    attended = attended.astype(jnp.bfloat16).reshape(row_len, seq_count, width_loc)
    portion_rows = attended
    attn_rows = lax.psum_scatter(
        jnp.einsum("lse,ed->lsd", portion_rows, w_out, preferred_element_type=jnp.float32).astype(
            jnp.bfloat16
        ),
        "tensor",
        scatter_dimension=0,
        tiled=True,
    ).astype(jnp.float32)
    z_one = layer_input_rows.astype(jnp.float32) + attn_rows + bias_out
    normed_one, inv_one = normalize(z_one)
    h_mine = normed_one * gain_one + shift_one
    hidden_narrow_whole = lax.all_gather(h_mine.astype(jnp.bfloat16), "tensor", axis=0, tiled=True)
    up_pre = (
        jnp.einsum(
            "wer,rb->web", hidden_narrow_whole, up_weight, preferred_element_type=jnp.float32
        )
        + expand_bias
    )
    activation_narrow = jax.nn.gelu(up_pre, approximate=False).astype(jnp.bfloat16)
    portion_rows = activation_narrow
    down_rows = lax.psum_scatter(
        jnp.einsum(
            "aij,jb->aib", portion_rows, down_weight, preferred_element_type=jnp.float32
        ).astype(jnp.bfloat16),
        "tensor",
        scatter_dimension=0,
        tiled=True,
    ).astype(jnp.float32)
    z_two = h_mine + down_rows + bias_down
    normed_two, inv_two = normalize(z_two)
    layer_out = normed_two * gain_two + shift_two
    seg_mine = lax.dynamic_slice_in_dim(sentence_index_row, tensor_at * quarter, quarter, 1)
    valid_mine = lax.dynamic_slice_in_dim(padding_mask, tensor_at * quarter, quarter, 1)
    sent_ids = jnp.arange(SMAX, dtype=jnp.int32)
    onehot_mine = (
        (seg_mine[:, :, None] == sent_ids[None, None, :]) & (valid_mine[:, :, None] == 1)
    ).astype(jnp.float32)
    pool_part = jnp.einsum("slc,lsd->scd", onehot_mine, layer_out, precision=exact_precision)
    onehot_full = (
        (sentence_index_row[:, :, None] == sent_ids[None, None, :])
        & (padding_mask[:, :, None] == 1)
    ).astype(jnp.float32)
    counts = jnp.sum(onehot_full, axis=1)
    grad_out = output_gradient.astype(jnp.float32) * valid_mine.T[:, :, None].astype(jnp.float32)
    d_gain_two = jnp.sum(grad_out * normed_two, axis=(0, 1))
    d_shift_two = jnp.sum(grad_out, axis=(0, 1))
    dz_two = norm_back(grad_out * gain_two, normed_two, inv_two)
    d_bias_down = jnp.sum(dz_two, axis=(0, 1))
    second_sum_gradient_wide = lax.all_gather(
        dz_two.astype(jnp.bfloat16), "tensor", axis=0, tiled=True
    )
    down_weight_gradient = jnp.einsum(
        "ipo,ipr->or",
        activation_narrow,
        second_sum_gradient_wide,
        preferred_element_type=jnp.float32,
    )
    activation_gradient = jnp.einsum(
        "ugp,jp->ugj", second_sum_gradient_wide, down_weight, preferred_element_type=jnp.float32
    )
    gelu_pull = jax.vjp(lambda pre_act: jax.nn.gelu(pre_act, approximate=False), up_pre)[1]
    d_up = gelu_pull(activation_gradient)[0]
    d_bias_up = jnp.sum(d_up, axis=(0, 1))
    expand_gradient_narrow = d_up.astype(jnp.bfloat16)
    up_weight_gradient = jnp.einsum(
        "iux,iuy->xy",
        hidden_narrow_whole,
        expand_gradient_narrow,
        preferred_element_type=jnp.float32,
    )
    portion_rows = expand_gradient_narrow
    dh_rows = lax.psum_scatter(
        jnp.einsum(
            "uih,vh->uiv", portion_rows, up_weight, preferred_element_type=jnp.float32
        ).astype(jnp.bfloat16),
        "tensor",
        scatter_dimension=0,
        tiled=True,
    ).astype(jnp.float32)
    dh_mine = dz_two + dh_rows
    d_gain_one = jnp.sum(dh_mine * normed_one, axis=(0, 1))
    d_shift_one = jnp.sum(dh_mine, axis=(0, 1))
    dz_one = norm_back(dh_mine * gain_one, normed_one, inv_one)
    d_bias_out = jnp.sum(dz_one, axis=(0, 1))
    dz_one_full = lax.all_gather(dz_one.astype(jnp.bfloat16), "tensor", axis=0, tiled=True)
    d_w_out = jnp.einsum("lse,lsd->ed", attended, dz_one_full, preferred_element_type=jnp.float32)
    d_attended = jnp.einsum("lsd,ed->lse", dz_one_full, w_out, preferred_element_type=jnp.float32)
    d_attended = d_attended.astype(jnp.bfloat16).reshape(row_len, seq_count, heads_loc, HEAD_DIM)
    scores_again = masked_scores(queries, key_rows, allowed, scaling)
    attn_prob = jnp.exp(scores_again - log_total)
    prob_again = attn_prob.astype(jnp.bfloat16)
    d_prob = jnp.einsum("qshe,kshe->shqk", d_attended, values, preferred_element_type=jnp.float32)
    d_values = jnp.einsum(
        "shqk,qshe->kshe", prob_again, d_attended, preferred_element_type=jnp.float32
    )
    inner = jnp.sum(d_prob * attn_prob, axis=-1, keepdims=True)
    d_scores = (attn_prob * (d_prob - inner)).astype(jnp.bfloat16)
    d_queries = (
        jnp.einsum("shqk,kshe->qshe", d_scores, key_rows, preferred_element_type=jnp.float32)
        * scaling
    )
    d_keys = (
        jnp.einsum("shqk,qshe->kshe", d_scores, queries, preferred_element_type=jnp.float32)
        * scaling
    )
    d_bias_q = jnp.sum(d_queries, axis=(0, 1)).reshape(width_loc)
    d_bias_v = jnp.sum(d_values, axis=(0, 1)).reshape(width_loc)
    d_qkv_low = jnp.concatenate(
        [
            d_queries.reshape(row_len, seq_count, width_loc),
            d_keys.reshape(row_len, seq_count, width_loc),
            d_values.reshape(row_len, seq_count, width_loc),
        ],
        axis=2,
    ).astype(jnp.bfloat16)
    d_w_qkv = jnp.einsum("lsd,lse->de", full_rows, d_qkv_low, preferred_element_type=jnp.float32)
    portion_rows = d_qkv_low
    dx_rows = lax.psum_scatter(
        jnp.einsum("lse,de->lsd", portion_rows, w_qkv, preferred_element_type=jnp.float32).astype(
            jnp.bfloat16
        ),
        "tensor",
        scatter_dimension=0,
        tiled=True,
    ).astype(jnp.float32)
    input_grad = dz_one + dx_rows
    shared_grads = jnp.stack(
        [d_bias_out, d_bias_down, d_gain_one, d_shift_one, d_gain_two, d_shift_two]
    )[None]
    pool_sum, shared_sum = (
        lax.psum_scatter(
            pool_part.astype(jnp.bfloat16), "tensor", scatter_dimension=2, tiled=True
        ).astype(jnp.float32),
        lax.psum_scatter(
            shared_grads.astype(jnp.bfloat16), "tensor", scatter_dimension=2, tiled=True
        ).astype(jnp.float32),
    )
    pooled_mean = pool_sum / jnp.maximum(counts, 1.0)[:, :, None]
    flat_grads = jnp.concatenate(
        [
            up_weight_gradient.reshape(-1),
            down_weight_gradient.reshape(-1),
            d_w_qkv.reshape(-1),
            d_w_out.reshape(-1),
            d_bias_q,
            d_bias_v,
            d_bias_up,
            shared_sum.reshape(-1),
        ]
    )
    grad_blocks = flat_grads.reshape(nblocks, block_len)
    wanted = data_at * per_owner + jnp.arange(per_owner, dtype=jnp.int32)
    block_of, filled = slot_blocks(slot_of, wanted)
    slot_grads = (
        jnp.zeros((data_size * per_owner, block_len), jnp.float32).at[slot_of].set(grad_blocks)
    )
    owned_grads = lax.psum_scatter(slot_grads, "dp", scatter_dimension=0, tiled=True)
    norm_grads = lax.psum(shared_sum[0], "dp")
    token_position = block_of[:, None] * block_len + jnp.arange(block_len, dtype=jnp.int32)[None, :]
    step_rate, decay_on = step_rates(token_position, MODEL_WIDTH, FF, tensor_size)
    new_master, new_first, new_second = adamw(
        owned_grads,
        first_moment[0],
        second_moment[0],
        master_state[0],
        step_rate,
        decay_on,
        filled[:, None],
    )
    return (
        layer_out,
        pooled_mean,
        input_grad,
        new_master[None],
        new_first[None],
        new_second[None],
        norm_grads,
    )


MESH = pl.DeviceIdType.MESH
BF = jnp.bfloat16
F32 = jnp.float32
WEIGHTS = ((576, 96), (768, 32), (768, 96), (768, 96))
MIB = 2**20


class Place:
    def __init__(self):
        d = lax.axis_index("dp")
        self.t = lax.axis_index("tensor")
        self.c = d % 2
        self.x = (d // 2) % 2
        self.y = d // 4
        self.xy = d // 2
        self.core = (d + 1 - 2 * self.c, self.t)
        self.right = (d + 2 - 4 * self.x, self.t)
        self.down = (d + 4 - 8 * self.y, self.t)
        self.diag = (d + 6 - 4 * self.x - 8 * self.y, self.t)
        self.deep = [None] + [(d, (self.t + k) % 4) for k in (1, 2, 3)]
        self.ahead = [(self.t + k) % 4 for k in range(4)]
        self.behind = [(self.t + 4 - k) % 4 for k in range(4)]

    def greet(self):
        barrier = pltpu.get_barrier_semaphore()
        peers = [self.core, self.right, self.down, self.diag] + self.deep[1:]
        for peer in peers:
            pl.semaphore_signal(barrier, inc=1, device_id=peer, device_id_type=MESH)
        pl.semaphore_wait(barrier, len(peers))


class Sender:
    def __init__(self, send_sems, recv_sems, local_sems):
        self.sems = (send_sems, recv_sems, local_sems)
        self.used = 0
        self.used_local = 0
        self.open = []

    def send(self, src, dst, peer):
        i = self.used
        self.used += 1
        copy = pltpu.make_async_remote_copy(
            src_ref=src,
            dst_ref=dst,
            send_sem=self.sems[0].at[i],
            recv_sem=self.sems[1].at[i],
            device_id=peer,
            device_id_type=MESH,
        )
        copy.start()
        self.open.append(copy)
        return copy

    def copy(self, src, dst):
        i = self.used_local
        self.used_local += 1
        copy = pltpu.make_async_copy(src, dst, self.sems[2].at[i])
        copy.start()
        return copy

    def sent(self, copy):
        copy.wait_send()
        self.open = [other for other in self.open if other is not copy]

    def finish(self):
        for copy in self.open:
            copy.wait_send()


def rows_of(place, rows, at=None):
    at = place.xy if at is None else at
    return pl.ds(pl.multiple_of(place.c * (4 * rows) + at * rows, 32), rows)


def half_of(place, rows):
    return pl.ds(pl.multiple_of(place.c * (4 * rows), 128), 4 * rows)


def interleave(size, parts):
    group = size // parts
    out_row = lax.broadcasted_iota(jnp.int32, (size, size), 0)
    col = lax.broadcasted_iota(jnp.int32, (size, size), 1)
    part = jnp.zeros((size, size), jnp.int32)
    for k in range(1, parts):
        part = part + (col >= k * group).astype(jnp.int32)
    return jnp.where(out_row == parts * (col - group * part) + part, 1.0, 0.0).astype(BF)


def interleave_out():
    out_row = lax.broadcasted_iota(jnp.int32, (32, 32), 0)
    col = lax.broadcasted_iota(jnp.int32, (32, 32), 1)
    part = (col >= 8).astype(jnp.int32) + (col >= 16).astype(jnp.int32)
    keep = (out_row == 3 * (col - 8 * part) + part) & (col < 24)
    return jnp.where(keep, 1.0, 0.0).astype(BF)


def dot_f32(a, b):
    return jnp.dot(a, b, preferred_element_type=F32)


def compact_out():
    out_row = lax.broadcasted_iota(jnp.int32, (192, 256), 0)
    col = lax.broadcasted_iota(jnp.int32, (192, 256), 1)
    group = jnp.zeros((192, 256), jnp.int32)
    for i in range(1, 8):
        group = group + (out_row >= 24 * i).astype(jnp.int32)
    return jnp.where(col == out_row + 8 * group, 1.0, 0.0).astype(BF)


def dot_nt(a, b):
    return lax.dot_general(a, b, (((1,), (1,)), ((), ())), preferred_element_type=F32)


def dot_tn(a, b):
    return lax.dot_general(a, b, (((0,), (0,)), ((), ())), preferred_element_type=F32)


def unpack_small(packed, small):
    for t in range(4):
        small[t] = jnp.concatenate([packed[t, i : i + 1, :] for i in range(6)], axis=1)


def norm_vectors(small, norm):
    for i in range(6):
        at = 1152 + 192 * i
        norm[i : i + 1, :] = jnp.concatenate([small[t, 0:1, at : at + 192] for t in range(4)], axis=1)


def row_loop(body, step=128):
    @pl.loop(0, 512 // step)
    def _(i):
        body(pl.ds(pl.multiple_of(i * step, step), step))


def forward_kernel(
    master,
    owners,
    order_col,
    labels,
    flags,
    x_in,
    gy_in,
    w_qkv,
    w_out,
    w_up,
    w_down,
    out_compact,
    slot_out,
    small_out,
    x_out,
    gy_row,
    qkv_out,
    prob_out,
    att_out,
    n_one_out,
    h_out,
    act_out,
    pull_out,
    n_two_out,
    inv_out,
    row_out,
    pool_out,
    slot_row,
    slot_col,
    id_row,
    id_col,
    slots,
    canon_att,
    canon_ffn,
    land_att,
    land_ffn,
    pass_ffn,
    pass_land,
    share,
    p_qkv,
    p_out,
    p_up,
    p_down,
    small_mine,
    small_land,
    small_total,
    packed,
    small,
    norm,
    bias_qkv,
    v_qkv,
    v_out,
    v_compact,
    v_up,
    v_down,
    x_row,
    qkv,
    prob,
    att,
    n_one,
    h_wide,
    h_low,
    act,
    pull,
    total,
    inv,
    row_low,
    pool,
    send_sems,
    recv_sems,
    local_sems,
):
    place = Place()
    link = Sender(send_sems, recv_sems, local_sems)
    slots[place.c] = master[...].astype(BF)

    blocks = owners.shape[1]
    wide = slot_row.shape[1]
    owner = jnp.concatenate(
        [owners[...].astype(F32), jnp.full((1, wide - blocks), -1.0, F32)], axis=1
    )
    kinds = lax.broadcasted_iota(jnp.int32, (8, wide), 0).astype(F32)
    owned = jnp.where(kinds == owner, 1.0, 0.0)
    ordinal = lax.broadcasted_iota(jnp.int32, (wide, wide), 1)
    earlier = jnp.where(lax.broadcasted_iota(jnp.int32, (wide, wide), 0) < ordinal, 1.0, 0.0)
    ahead = dot_f32(owned.astype(BF), earlier.astype(BF))
    ranking = jnp.sum(owned * ahead, axis=0, keepdims=True)
    place_of = jnp.where(order_col[...] == ordinal, 1.0, 0.0).astype(BF)
    pair = jnp.where(kinds == 0.0, owner, ranking).astype(BF)
    row = dot_nt(pair, place_of)
    col = dot_nt(place_of, pair)
    per_owner = float(master.shape[0])
    slot_row[...] = jnp.broadcast_to(row[0:1, :] * per_owner + row[1:2, :], slot_row.shape)
    slot_col[...] = jnp.broadcast_to(col[:, 0:1] * per_owner + col[:, 1:2], slot_col.shape)

    own = pl.ds(place.t, 1)
    apart = -1 - lax.broadcasted_iota(jnp.int32, (1, 512), 1)
    ids = jnp.where(flags[own, :] == 1, labels[own, :], apart).astype(F32)
    id_row[...] = jnp.broadcast_to(ids, id_row.shape)
    id_col[...] = jnp.transpose(id_row[...])
    place.greet()
    whole = (w_qkv, w_out, w_up, w_down)
    held = (v_qkv, v_out, v_up, v_down)
    piece = (p_qkv, p_out, p_up, p_down)
    peers = (place.right, place.down, place.diag)
    mine_rows = pl.ds(pl.multiple_of(place.t * 128, 128), 128)
    tidy = [link.copy(slot_row, slot_out)]

    core_slots = link.send(slots.at[place.c], slots.at[place.c], place.core)
    x_moves = [
        link.send(x_in.at[place.ahead[k]], x_row.at[mine_rows], place.deep[k]) for k in (1, 2, 3)
    ]
    x_stay = link.copy(x_in.at[place.t], x_row.at[mine_rows])
    tidy.append(link.copy(gy_in.at[place.t], gy_row.at[mine_rows]))
    core_slots.wait_recv()

    pair_slots = slots[...].reshape(384, 2304)
    slot_id = (lax.broadcasted_iota(jnp.int32, (64, 384), 1) + place.xy * 384).astype(F32)
    order = [(3, place.diag), (1, place.right), (2, place.down), (0, None)]

    def spread(lo, rows, canon, land):
        sent = []
        for j, peer in order:
            at = place.xy if peer is None else peer[0] // 2
            spot = pl.ds(pl.multiple_of(place.c * 384 + at * 96 + lo, 32), rows)
            wanted = slot_col[spot, 0:1]
            pick = jnp.where(wanted == slot_id[:rows], 1.0, 0.0).astype(BF)
            canon[j] = dot_f32(pick, pair_slots).astype(BF)
            if peer is not None:
                sent.append(link.send(canon.at[j], land.at[j - 1], peer))
        return sent

    def collect(sent, lo, rows, canon, land):
        for move in sent:
            move.wait_recv()
        share[lo : lo + rows, :] = (
            canon[0].astype(F32) + land[0].astype(F32) + land[1].astype(F32) + land[2].astype(F32)
        )

    att_sent = spread(64, 32, canon_att, land_att)
    pick_small = jnp.where(slot_row[:, 768:769] == slot_id[:8], 1.0, 0.0).astype(BF)
    picked = dot_f32(pick_small, pair_slots)
    for i in range(6):
        small_mine[i : i + 1, :] = picked[0:1, 384 * i : 384 * i + 384]
    small_mine[6:8, :] = jnp.zeros((2, 384), F32)
    small_moves = [link.send(small_mine, small_land.at[j], peer) for j, peer in enumerate(peers)]
    def spread_halves():
        for j, peer in order:
            at = place.xy if peer is None else peer[0] // 2
            spot = pl.ds(pl.multiple_of(place.c * 384 + at * 96, 32), 64)
            pick = jnp.where(slot_col[spot, 0:1] == slot_id, 1.0, 0.0).astype(BF)
            canon_ffn[j] = dot_f32(pick, pair_slots).astype(BF)
            if j in (1, 3):
                half = canon_ffn.at[j, pl.ds(0, 32)]
                halves[j, 0] = link.send(half, land_ffn.at[0, j // 2], place.right)
            if j in (2, 3):
                half = canon_ffn.at[j, pl.ds(32, 32)]
                halves[j, 1] = link.send(half, land_ffn.at[1, j - 2], place.down)

    def pass_halves():
        halves[3, 0].wait_recv()
        pass_ffn[0] = canon_ffn[2, 0:32, :] + land_ffn[0, 1]
        halves["down"] = link.send(pass_ffn.at[0], pass_land.at[0], place.down)
        halves[3, 1].wait_recv()
        pass_ffn[1] = canon_ffn[1, 32:64, :] + land_ffn[1, 1]
        halves["right"] = link.send(pass_ffn.at[1], pass_land.at[1], place.right)

    def collect_halves():
        halves[1, 0].wait_recv()
        halves[2, 1].wait_recv()
        halves["down"].wait_recv()
        halves["right"].wait_recv()
        for i in range(2):
            share[32 * i : 32 * i + 32, :] = (
                canon_ffn[0, 32 * i : 32 * i + 32, :] + land_ffn[i, 0] + pass_land[i]
            ).astype(F32)

    halves = {}
    att_sent[0].wait_recv()
    spread_halves()
    collect(att_sent[1:], 64, 32, canon_att, land_att)

    p_qkv[...] = dot_f32(
        interleave(96, 4),
        jnp.concatenate([share[64:88, 576 * r : 576 * r + 576] for r in range(4)], axis=0).astype(BF),
    ).astype(BF)

    def spread_out():
        parts = [share[88:96, 768 * k : 768 * k + 768] for k in range(3)]
        parts = parts + [jnp.zeros((8, 768), F32)]
        p_out[...] = dot_f32(interleave_out(), jnp.concatenate(parts, axis=0).astype(BF)).astype(BF)

    def spread_ffn():
        three = interleave(96, 3)
        for at, ref in ((0, p_up), (32, p_down)):
            parts = [share[at : at + 32, 768 * k : 768 * k + 768] for k in range(3)]
            ref[...] = dot_f32(three, jnp.concatenate(parts, axis=0).astype(BF)).astype(BF)

    deep_moves, right_moves, down_moves, own_copies, core_moves, loads = {}, {}, {}, {}, {}, {}

    def deep_send(w):
        spot = whole[w].at[place.t, rows_of(place, WEIGHTS[w][1])]
        own_copies[w] = link.copy(piece[w], spot)
        deep_moves[w] = [link.send(piece[w], spot, place.deep[k]) for k in (1, 2, 3)]

    def plane_send(w, k):
        rows = WEIGHTS[w][1]
        spot = whole[w].at[place.behind[k], rows_of(place, rows)]
        src = piece[w] if k == 0 else spot
        if k:
            deep_moves[w][k - 1].wait_recv()
        right_moves[w, k] = link.send(src, spot, place.right)
        down_moves[w, k] = link.send(src, spot, place.down)

    def plane_pass(w, k):
        rows = WEIGHTS[w][1]
        half = rows // 2
        right_moves[w, k].wait_recv()
        down_moves[w, k].wait_recv()
        t = place.behind[k]
        right_at = place.c * (4 * rows) + (place.right[0] // 2) * rows
        down_at = place.c * (4 * rows) + (place.down[0] // 2) * rows
        first = whole[w].at[t, pl.ds(pl.multiple_of(right_at, 16), half)]
        second = whole[w].at[t, pl.ds(pl.multiple_of(down_at + half, 16), half)]
        right_moves[w, k, 1] = link.send(second, second, place.right)
        down_moves[w, k, 1] = link.send(first, first, place.down)

    def core_pass(w, k):
        if k == 0:
            own_copies[w].wait()
        right_moves[w, k, 1].wait_recv()
        down_moves[w, k, 1].wait_recv()
        spot = whole[w].at[place.behind[k], half_of(place, WEIGHTS[w][1])]
        core_moves[w, k] = link.send(spot, spot, place.core)

    def load(w, k):
        core_moves[w, k].wait_recv()
        t = place.behind[k]
        loads[w, k] = link.copy(whole[w].at[t], held[w].at[t])

    def qkv_step(k):
        loads[0, k].wait()
        t = place.behind[k]

        def body(rows):
            lin = dot_f32(x_row[rows, :], v_qkv[t]) + bias_qkv[t]
            qkv[t, rows, :] = lin.astype(BF)

        row_loop(body, 256)

    def attention(k):
        t = place.behind[k]

        def body(rows):
            allowed = id_col[rows, 0:1] == id_row[0:1, :]
            parts = []
            for i in range(3):
                at = 64 * i
                scores = dot_nt(qkv[t, rows, at : at + 64], qkv[t, :, 192 + at : 256 + at]) * 0.125
                scores = jnp.where(allowed, scores, MASKED)
                weight = jnp.exp(scores - jnp.max(scores, axis=1, keepdims=True))
                weight = weight * (1.0 / jnp.sum(weight, axis=1, keepdims=True))
                low = weight.astype(BF)
                prob[3 * t + i, rows, :] = low
                parts.append(dot_f32(low, qkv[t, :, 384 + at : 448 + at]))
            att[t, rows, :] = jnp.concatenate(parts, axis=1).astype(BF)

        row_loop(body, 256)
        tidy.append(link.copy(qkv.at[t], qkv_out.at[t]))
        tidy.append(link.copy(att.at[t], att_out.at[t]))
        tidy.append(link.copy(prob.at[pl.ds(3 * t, 3)], prob_out.at[pl.ds(3 * t, 3)]))

    def out_step():
        pick = compact_out()
        for k in range(4):
            loads[1, k].wait()
        for t in range(4):
            v_compact[t] = dot_f32(pick, v_out[t]).astype(BF)
        tidy.append(link.copy(v_compact, out_compact))

        def body(rows):
            z = x_row[rows, :].astype(F32) + norm[0:1, :]
            for t in range(4):
                z = z + dot_f32(att[t, rows, :], v_compact[t])
            normed, inverse = normalize(z)
            n_one[rows, :] = normed
            inv[0, rows, :] = inverse
            h = normed * norm[2:3, :] + norm[3:4, :]
            h_low[rows, :] = h.astype(BF)
            h_wide[rows, :] = h
            total[rows, :] = h + norm[1:2, :]

        row_loop(body, 256)
        tidy.append(link.copy(n_one, n_one_out))
        tidy.append(link.copy(h_low, h_out))

    def up_step(k):
        loads[2, k].wait()
        t = place.behind[k]

        def body(rows):
            pre = dot_f32(h_low[rows, :], v_up[t]) + small[t, 0:1, 384:1152]
            below = 0.5 + 0.5 * lax.erf(pre * (0.5**0.5))
            act[t, rows, :] = (pre * below).astype(BF)
            slope = below + pre * (jnp.exp(-0.5 * pre * pre) * 0.3989422804014327)
            pull[t, rows, :] = slope.astype(BF)

        row_loop(body, 256)
        tidy.append(link.copy(act.at[t], act_out.at[t]))
        tidy.append(link.copy(pull.at[t], pull_out.at[t]))

    def down_step(k):
        loads[3, k].wait()
        t = place.behind[k]

        def body(rows):
            total[rows, :] += dot_f32(act[t, rows, :], v_down[t])

        row_loop(body, 256)

    def end_step():
        sentence = lax.broadcasted_iota(jnp.int32, (SMAX, 512), 0).astype(F32)
        member = jnp.where(sentence == id_row[...], 1.0, 0.0)
        count = jnp.maximum(jnp.sum(member, axis=1, keepdims=True), 1.0)

        def body(rows):
            normed, inverse = normalize(total[rows, :])
            inv[1, rows, :] = inverse
            out = normed * norm[4:5, :] + norm[5:6, :]
            total[rows, :] = normed
            h_wide[rows, :] = out
            row_low[rows, :] = out.astype(BF)

        row_loop(body, 256)
        pool[...] = jnp.dot(member, h_wide[...], precision=exact_precision, preferred_element_type=F32) / count
        tidy.append(link.copy(total, n_two_out))
        tidy.append(link.copy(row_low, row_out))
        tidy.append(link.copy(pool, pool_out))
        tidy.append(link.copy(inv, inv_out))

    every = range(4)
    others = (1, 2, 3)
    deep_send(0)
    plane_send(0, 0)
    spread_out()
    deep_send(1)
    plane_send(1, 0)
    pass_halves()
    collect_halves()
    spread_ffn()
    plane_send(2, 0)
    plane_pass(0, 0)
    for k in others:
        plane_send(0, k)
    deep_send(2)
    for move in small_moves:
        move.wait_recv()
    small_total[...] = small_mine[...] + small_land[0] + small_land[1] + small_land[2]
    small_stay = link.copy(small_total, packed.at[place.t])
    small_deep = [link.send(small_total, packed.at[place.t], place.deep[k]) for k in others]
    x_stay.wait()
    for move in x_moves:
        move.wait_recv()
    tidy.append(link.copy(x_row, x_out))
    plane_pass(1, 0)
    for k in others:
        plane_send(1, k)
    core_pass(0, 0)
    plane_send(3, 0)
    for k in others:
        plane_pass(0, k)
    small_stay.wait()
    for move in small_deep:
        move.wait_recv()
    unpack_small(packed, small)
    norm_vectors(small, norm)
    for t in every:
        bias_qkv[t] = jnp.concatenate(
            [small[t, 0:1, :192], jnp.zeros((1, 192), F32), small[t, 0:1, 192:384]], axis=1
        )
    tidy.append(link.copy(packed, small_out))
    load(0, 0)
    qkv_step(0)
    attention(0)
    for k in others:
        plane_send(2, k)
    deep_send(3)
    for k in others:
        plane_pass(1, k)
        core_pass(0, k)
    plane_pass(2, 0)
    for k in others:
        load(0, k)
    qkv_step(1)
    attention(1)
    plane_pass(3, 0)
    for k in every:
        core_pass(1, k)
    plane_pass(2, 1)
    qkv_step(2)
    attention(2)
    plane_pass(2, 2)
    core_pass(2, 0)
    for k in every:
        load(1, k)
    qkv_step(3)
    plane_pass(2, 3)
    core_pass(2, 1)
    attention(3)
    load(2, 0)
    plane_send(3, 1)
    plane_send(3, 2)
    plane_send(3, 3)
    gy_moves = [
        link.send(gy_in.at[place.ahead[k]], gy_row.at[mine_rows], place.deep[k]) for k in others
    ]
    core_pass(2, 2)
    core_pass(3, 0)
    out_step()
    load(2, 1)
    load(2, 2)
    load(3, 0)
    core_pass(2, 3)
    plane_pass(3, 1)
    up_step(0)
    up_step(1)
    plane_pass(3, 2)
    core_pass(3, 1)
    load(2, 3)
    load(3, 1)
    up_step(2)
    plane_pass(3, 3)
    core_pass(3, 2)
    up_step(3)
    down_step(0)
    core_pass(3, 3)
    down_step(1)
    load(3, 2)
    down_step(2)
    load(3, 3)
    down_step(3)
    end_step()
    for move in gy_moves:
        move.wait_recv()
    for copy in tidy:
        copy.wait()
    link.finish()


def forward_call(master, owners, order_col, labels, flags, x_in, gy_in):
    anywhere = pl.BlockSpec(memory_space=pl.ANY)
    vmem = pl.BlockSpec(memory_space=pltpu.VMEM)
    shape = jax.ShapeDtypeStruct
    outs = [
        ((4, 768, 576), BF),
        ((4, 256, 768), BF),
        ((4, 768, 768), BF),
        ((4, 768, 768), BF),
        ((4, 192, 768), BF),
        ((8, 896), F32),
        ((4, 8, 384), F32),
        ((512, 768), BF),
        ((512, 768), BF),
        ((4, 512, 576), BF),
        ((12, 512, 512), BF),
        ((4, 512, 192), BF),
        ((512, 768), F32),
        ((512, 768), BF),
        ((4, 512, 768), BF),
        ((4, 512, 768), BF),
        ((512, 768), F32),
        ((2, 512, 1), F32),
        ((512, 768), BF),
        ((8, 768), F32),
    ]
    scratch = [
        ((8, 896), F32),
        ((896, 8), F32),
        ((8, 512), F32),
        ((512, 8), F32),
        ((2, 192, 2304), BF),
        ((4, 32, 2304), BF),
        ((4, 64, 2304), BF),
        ((3, 32, 2304), BF),
        ((2, 2, 32, 2304), BF),
        ((2, 32, 2304), BF),
        ((2, 32, 2304), BF),
        ((96, 2304), F32),
        ((96, 576), BF),
        ((32, 768), BF),
        ((96, 768), BF),
        ((96, 768), BF),
        ((8, 384), F32),
        ((3, 8, 384), F32),
        ((8, 384), F32),
        ((4, 8, 384), F32),
        ((4, 1, 2304), F32),
        ((8, 768), F32),
        ((4, 1, 576), F32),
        ((4, 768, 576), BF),
        ((4, 256, 768), BF),
        ((4, 192, 768), BF),
        ((4, 768, 768), BF),
        ((4, 768, 768), BF),
        ((512, 768), BF),
        ((4, 512, 576), BF),
        ((12, 512, 512), BF),
        ((4, 512, 192), BF),
        ((512, 768), F32),
        ((512, 768), F32),
        ((512, 768), BF),
        ((4, 512, 768), BF),
        ((4, 512, 768), BF),
        ((512, 768), F32),
        ((2, 512, 1), F32),
        ((512, 768), BF),
        ((8, 768), F32),
    ]
    return pl.pallas_call(
        forward_kernel,
        out_shape=[shape(*o) for o in outs],
        in_specs=[vmem] * 5 + [anywhere] * 2,
        out_specs=[anywhere] * len(outs),
        scratch_shapes=[pltpu.VMEM(*s) for s in scratch]
        + [
            pltpu.SemaphoreType.DMA((128,)),
            pltpu.SemaphoreType.DMA((128,)),
            pltpu.SemaphoreType.DMA((64,)),
        ],
        compiler_params=pltpu.CompilerParams(
            collective_id=0, has_side_effects=True, vmem_limit_bytes=60 * MIB
        ),
        name="gather_and_forward",
    )(master, owners, order_col, labels, flags, x_in, gy_in)


def backward_kernel(
    flags,
    out_row,
    pool_in,
    gy_in,
    n_two_in,
    inv_in,
    small_in,
    act_in,
    pull_in,
    w_down,
    w_up,
    h_in,
    n_one_in,
    att_in,
    w_out,
    qkv_in,
    prob_in,
    w_qkv,
    x_in,
    blocks,
    small_out,
    out_mine,
    dx_mine,
    pool_out,
    *scratch,
):
    sums, cores, lefts, tops, lefts_two, tops_two, deeps = (scratch[4 * i : 4 * i + 4] for i in range(7))
    (
        ring,
        ring_narrow,
        share,
        share_low,
        small_grad,
        small_land,
        packed,
        small,
        norm,
        gy,
        normed,
        inv,
        act,
        pull,
        v_down,
        v_up,
        h_low,
        att,
        v_out,
        qkv,
        prob,
        v_qkv,
        x_row,
        wide,
        low,
        total,
        d_up,
        d_att,
        d_qkv,
        turned,
        go,
        reds,
        red_up,
        red_qv,
        flag_col,
        send_sems,
        recv_sems,
        local_sems,
    ) = scratch[28:]
    place = Place()
    link = Sender(send_sems, recv_sems, local_sems)
    t_of = place.ahead
    steps = (1, 2, 3, 0)
    got = {}

    def load(name, src, dst):
        got[name] = link.copy(src, dst)

    load("small", small_in, packed)
    load("normed", n_two_in, normed)
    load("gy", gy_in, gy)
    load("inv", inv_in, inv)

    def load_ffn(i):
        t, slot = t_of[steps[i]], i % 2
        load(("act", i), act_in.at[t], act.at[slot])
        load(("down", i), w_down.at[t], v_down.at[slot])
        load(("pull", i), pull_in.at[t], pull.at[slot])
        load(("up", i), w_up.at[t], v_up.at[slot])

    def load_att(i):
        t, slot = t_of[steps[i]], i % 2
        load(("prob", i), prob_in.at[pl.ds(3 * t, 3)], prob.at[slot])
        load(("qkv", i), w_qkv.at[t], v_qkv.at[slot])

    own_flags = flags[pl.ds(place.t, 1), :].astype(F32)
    flag_col[...] = jnp.transpose(jnp.broadcast_to(own_flags, (8, 512)))
    place.greet()
    t, x, y, c = place.t, place.x, place.y, place.c

    moves, stay = [], []
    stay.append(link.copy(out_row.at[pl.ds(pl.multiple_of(t * 128, 128), 128)], out_mine.at[t]))
    stay.append(link.copy(pool_in, pool_out.at[t]))
    for k in (1, 2, 3):
        part = out_row.at[pl.ds(pl.multiple_of(t_of[k] * 128, 128), 128)]
        moves.append(link.send(part, out_mine.at[t], place.deep[k]))
        moves.append(link.send(pool_in, pool_out.at[t], place.deep[k]))

    core_moves, first, second, third = {}, {}, {}, {}
    ring_open = [None] * 5
    ring_at = [0, 0]

    def chip_row(w, k, yy, xx, half):
        rows = WEIGHTS[w][1]
        at = pl.multiple_of((yy * 2 + xx) * rows + half * (rows // 2), 16)
        return sums[w].at[t_of[k], pl.ds(at, rows // 2)]

    def produce(w, k, make):
        narrow = w == 0
        slot = 3 + ring_at[1] % 2 if narrow else ring_at[0] % 3
        ring_at[narrow] += 1
        if ring_open[slot] is not None:
            link.sent(ring_open[slot])
        cols, rows = WEIGHTS[w]
        away = ring_narrow.at[slot - 3] if narrow else ring.at[slot, pl.ds(0, 4 * rows)]
        away[...] = make(1 - c).astype(BF)
        move = link.send(away, cores[w].at[k], place.core)
        ring_open[slot] = move
        core_moves[w, k] = move
        sums[w][t_of[k]] = make(c).astype(BF)

    def core_add(w, k):
        core_moves[w, k].wait_recv()
        rows = WEIGHTS[w][1]

        @pl.loop(0, 4)
        def _(i):
            at = pl.ds(pl.multiple_of(i * rows, 32), rows)
            sums[w][t_of[k], at, :] += cores[w][k, at, :]

        first[w, k] = []
        for i in (0, 1):
            first[w, k].append(link.send(chip_row(w, k, i, 1 - x, 0), lefts[w].at[k, i], place.right))
            first[w, k].append(link.send(chip_row(w, k, 1 - y, i, 1), tops[w].at[k, i], place.down))

    def add(spot, other):
        spot[...] = spot[...] + other[...]

    def plane_add(w, k):
        for move in first[w, k]:
            move.wait_recv()
        down_part, right_part = chip_row(w, k, 1 - y, x, 0), chip_row(w, k, y, 1 - x, 1)
        add(down_part, lefts[w].at[k, 1 - y])
        add(right_part, tops[w].at[k, 1 - x])
        second[w, k] = [
            link.send(down_part, lefts_two[w].at[k], place.down),
            link.send(right_part, tops_two[w].at[k], place.right),
        ]
        add(chip_row(w, k, y, x, 0), lefts[w].at[k, y])
        add(chip_row(w, k, y, x, 1), tops[w].at[k, x])

    def deep_add(w, k):
        for move in second[w, k]:
            move.wait_recv()
        add(chip_row(w, k, y, x, 0), lefts_two[w].at[k])
        add(chip_row(w, k, y, x, 1), tops_two[w].at[k])
        rows = WEIGHTS[w][1]
        if k:
            spot = pl.ds(pl.multiple_of(place.xy * rows, 16), rows)
            third[w, k] = link.send(sums[w].at[t_of[k], spot], deeps[w].at[k - 1], place.deep[k])

    def end(w):
        rows = WEIGHTS[w][1]
        spot = pl.ds(pl.multiple_of(place.xy * rows, 16), rows)
        whole = sums[w][t, spot, :].astype(F32)
        for k in (1, 2, 3):
            third[w, k].wait_recv()
            whole = whole + deeps[w][k - 1].astype(F32)
        whole = whole.astype(BF)
        if w == 0:
            parts = dot_tn(interleave(96, 4), whole)
            share[64:88, :] = jnp.concatenate([parts[24 * r : 24 * r + 24] for r in range(4)], axis=1)
        elif w == 1:
            parts = dot_tn(interleave_out(), whole)
            for k in range(3):
                share[88:96, 768 * k : 768 * k + 768] = parts[8 * k : 8 * k + 8]
        else:
            at = 0 if w == 2 else 32
            parts = dot_tn(interleave(96, 3), whole)
            for k in range(3):
                share[at : at + 32, 768 * k : 768 * k + 768] = parts[32 * k : 32 * k + 32]

    def column_sum(value):
        return jnp.sum(value, axis=0, keepdims=True)

    def norm_two_back():
        def body(rows):
            grad = gy[rows, :].astype(F32) * flag_col[rows, 0:1]
            n = normed[rows, :]
            dz = norm_back(grad * norm[4:5, :], n, inv[1, rows, :])
            wide[rows, :] = dz
            total[rows, :] = dz
            low[rows, :] = dz.astype(BF)
            reds[4:5, :] += column_sum(grad * n)
            reds[5:6, :] += column_sum(grad)
            reds[1:2, :] += column_sum(dz)

        row_loop(body)

    def lanes(which):
        return pl.ds(pl.multiple_of(which * 384, 128), 384)

    def down_piece(i):
        k, slot = steps[i], i % 2
        got["act", i].wait()
        produce(3, k, lambda which: dot_tn(act[slot, :, lanes(which)], low[...]))

    def act_back(i):
        k, slot = steps[i], i % 2
        got["down", i].wait()
        got["pull", i].wait()

        def body(rows):
            grad = dot_nt(low[rows, :], v_down[slot]) * pull[slot, rows, :].astype(F32)
            red_up[t_of[k]] += column_sum(grad)
            d_up[rows, :] = grad.astype(BF)

        row_loop(body, 256)

    def up_piece(i):
        if i == 0:
            got["h"].wait()
        produce(2, steps[i], lambda which: dot_tn(h_low[:, lanes(which)], d_up[...]))

    def hidden_back(i):
        slot = i % 2
        got["up", i].wait()

        def body(rows):
            total[rows, :] += dot_nt(d_up[rows, :], v_up[slot])

        row_loop(body, 256)
        if i + 2 < 4:
            load_ffn(i + 2)
        if i == 1:
            load("n_one", n_one_in, normed)

    def norm_one_back():
        got["n_one"].wait()

        def body(rows):
            dh = total[rows, :]
            n = normed[rows, :]
            dz = norm_back(dh * norm[2:3, :], n, inv[0, rows, :])
            total[rows, :] = dz
            low[rows, :] = dz.astype(BF)
            reds[2:3, :] += column_sum(dh * n)
            reds[3:4, :] += column_sum(dh)
            reds[0:1, :] += column_sum(dz)

        row_loop(body)

    def out_piece(i):
        k = steps[i]
        if i == 0:
            got["att"].wait()
            got["wout"].wait()
        go[...] = dot_tn(att[t_of[k]], low[...])

        def make(which):
            part = go[pl.ds(pl.multiple_of(which * 96, 96), 96), :]
            pad = jnp.zeros((8, 768), F32)
            parts = []
            for j in range(4):
                parts += [part[24 * j : 24 * j + 24], pad]
            return jnp.concatenate(parts, axis=0)

        produce(1, k, make)

        def body(rows):
            d_att[rows, :] = dot_nt(low[rows, :], v_out[t_of[k]]).astype(BF)

        row_loop(body, 256)

    def attention_back(i):
        k, slot = steps[i], i % 2
        tk = t_of[k]
        if i == 0:
            got["qkvs"].wait()
        got["prob", i].wait()
        turned[...] = jnp.zeros_like(turned)

        def body(rows):
            d_queries = []
            for j in range(3):
                at = 64 * j
                grad = d_att[rows, at : at + 64]
                weight_low = prob[slot, j, rows, :]
                weight = weight_low.astype(F32)
                d_prob = dot_nt(grad, qkv[tk, :, 384 + at : 448 + at]) * weight
                inner = jnp.sum(d_prob, axis=1, keepdims=True)
                d_scores = (d_prob - weight * inner).astype(BF)
                d_queries.append(dot_f32(d_scores, qkv[tk, :, 192 + at : 256 + at]))
                turned[at : at + 64, :] += dot_tn(qkv[tk, rows, at : at + 64], d_scores)
                turned[192 + at : 256 + at, :] += dot_tn(grad, weight_low)
            dq = jnp.concatenate(d_queries, axis=1) * 0.125
            red_qv[tk, :, :192] += column_sum(dq)
            d_qkv[rows, :192] = dq.astype(BF)

        row_loop(body, 256)
        dk = jnp.transpose(turned[:192, :]) * 0.125
        dv = jnp.transpose(turned[192:, :])
        red_qv[tk, :, 192:] += column_sum(dv)
        d_qkv[:, 192:] = jnp.concatenate([dk, dv], axis=1).astype(BF)

    def qkv_piece(i):
        k, slot = steps[i], i % 2
        if i == 0:
            got["x"].wait()
        produce(0, k, lambda which: dot_tn(x_row[:, lanes(which)], d_qkv[...]))
        got["qkv", i].wait()

        def body(rows):
            total[rows, :] += dot_nt(d_qkv[rows, :], v_qkv[slot])

        row_loop(body, 256)
        if i + 2 < 4:
            load_att(i + 2)

    def share_send(lo, hi):
        share_low[lo:hi, :] = share[lo:hi, :].astype(BF)
        mine = c * 4 + place.xy
        rows = pl.ds(lo, hi - lo)
        return (
            link.copy(share_low.at[rows], blocks.at[mine, rows]),
            link.send(share_low.at[rows], blocks.at[mine, rows], place.right),
            link.send(share_low.at[rows], blocks.at[mine, rows], place.down),
        )

    def share_pass(sent, lo, hi):
        half = (hi - lo) // 2
        sent[1].wait_recv()
        sent[2].wait_recv()
        one = blocks.at[c * 4 + place.right[0] // 2, pl.ds(lo, half)]
        two = blocks.at[c * 4 + place.down[0] // 2, pl.ds(lo + half, half)]
        return link.send(one, one, place.down), link.send(two, two, place.right)

    def share_across(sent, passed, lo, hi):
        sent[0].wait()
        passed[0].wait_recv()
        passed[1].wait_recv()
        spot = blocks.at[pl.ds(c * 4, 4), pl.ds(lo, hi - lo)]
        return link.send(spot, spot, place.core)

    got["small"].wait()
    unpack_small(packed, small)
    norm_vectors(small, norm)
    reds[...] = jnp.zeros_like(reds)
    red_up[...] = jnp.zeros_like(red_up)
    red_qv[...] = jnp.zeros_like(red_qv)
    small_grad[...] = jnp.zeros_like(small_grad)
    for name in ("normed", "gy", "inv"):
        got[name].wait()
    load_ffn(0)
    load("h", h_in, h_low)
    norm_two_back()
    load_ffn(1)
    down = [(3, k) for k in steps]
    up = [(2, k) for k in steps]
    out = [(1, k) for k in steps]
    att_in_w = [(0, k) for k in steps]
    down_piece(0)
    load("att", att_in, att)
    load("wout", w_out, v_out)
    load("qkvs", qkv_in, qkv)
    act_back(0)
    load("x", x_in, x_row)
    load_att(0)
    load_att(1)
    core_add(*down[0])
    up_piece(0)
    hidden_back(0)
    core_add(*up[0])
    plane_add(*down[0])
    down_piece(1)
    act_back(1)
    core_add(*down[1])
    plane_add(*up[0])
    up_piece(1)
    deep_add(*down[0])
    hidden_back(1)
    core_add(*up[1])
    plane_add(*down[1])
    down_piece(2)
    deep_add(*up[0])
    act_back(2)
    core_add(*down[2])
    up_piece(2)
    plane_add(*up[1])
    deep_add(*down[1])
    hidden_back(2)
    core_add(*up[2])
    down_piece(3)
    plane_add(*down[2])
    deep_add(*up[1])
    act_back(3)
    core_add(*down[3])
    up_piece(3)
    deep_add(*down[2])
    hidden_back(3)
    core_add(*up[3])
    plane_add(*up[2])
    norm_one_back()
    out_piece(0)
    plane_add(*down[3])
    deep_add(*up[2])
    attention_back(0)
    core_add(*out[0])
    plane_add(*up[3])
    deep_add(*down[3])
    qkv_piece(0)
    out_piece(1)
    deep_add(*up[3])
    core_add(*att_in_w[0])
    attention_back(1)
    core_add(*out[1])
    plane_add(*out[0])
    end(3)
    end(2)
    ffn_sent = share_send(0, 64)
    qkv_piece(1)
    plane_add(*att_in_w[0])
    deep_add(*out[0])
    out_piece(2)
    core_add(*att_in_w[1])
    attention_back(2)
    core_add(*out[2])
    plane_add(*out[1])
    deep_add(*att_in_w[0])
    ffn_passed = share_pass(ffn_sent, 0, 64)
    qkv_piece(2)
    plane_add(*att_in_w[1])
    out_piece(3)
    core_add(*att_in_w[2])
    deep_add(*out[1])
    attention_back(3)
    core_add(*out[3])
    plane_add(*out[2])
    deep_add(*att_in_w[1])
    qkv_piece(3)
    plane_add(*att_in_w[2])
    plane_add(*out[3])
    core_add(*att_in_w[3])

    def dx_body(rows):
        low[rows, :] = total[rows, :].astype(BF)

    row_loop(dx_body)
    for q in range(4):
        at = slice(192 * q, 192 * q + 192)
        line = jnp.concatenate(
            [red_qv[q], red_up[q]] + [reds[i : i + 1, at] for i in range(6)], axis=1
        )
        for i in range(6):
            small_grad[q, i : i + 1, :] = line[:, 384 * i : 384 * i + 384]
    small_sum = small_land.at[6]
    small_keep = link.copy(small_grad.at[t], small_sum)
    small_moves = [link.send(small_grad.at[t_of[k]], small_land.at[k - 1], place.deep[k]) for k in (1, 2, 3)]

    deep_add(*out[2])
    deep_add(*att_in_w[2])
    own_rows = pl.ds(pl.multiple_of(t * 128, 128), 128)
    stay.append(link.copy(low.at[own_rows], dx_mine.at[t]))
    for k in (1, 2, 3):
        part = low.at[pl.ds(pl.multiple_of(t_of[k] * 128, 128), 128)]
        moves.append(link.send(part, dx_mine.at[t], place.deep[k]))
    small_keep.wait()
    for move in small_moves:
        move.wait_recv()
    small_land[7] = small_land[6] + small_land[0] + small_land[1] + small_land[2]
    doubling = [link.send(small_land.at[7], small_land.at[3], place.core)]
    deep_add(*out[3])
    plane_add(*att_in_w[3])
    ffn_across = share_across(ffn_sent, ffn_passed, 0, 64)
    deep_add(*att_in_w[3])
    end(1)
    doubling[0].wait_recv()
    small_land[8] = small_land[7] + small_land[3]
    doubling.append(link.send(small_land.at[8], small_land.at[4], place.right))
    end(0)
    att_sent = share_send(64, 96)
    doubling[1].wait_recv()
    small_land[9] = small_land[8] + small_land[4]
    doubling.append(link.send(small_land.at[9], small_land.at[5], place.down))
    att_passed = share_pass(att_sent, 64, 96)
    doubling[2].wait_recv()
    small_out[...] = small_land[9] + small_land[5]
    att_across = share_across(att_sent, att_passed, 64, 96)
    ffn_across.wait_recv()
    att_across.wait_recv()
    for move in moves:
        move.wait_recv()
    for copy in stay:
        copy.wait()
    link.finish()


def backward_call(*args):
    anywhere = pl.BlockSpec(memory_space=pl.ANY)
    vmem = pl.BlockSpec(memory_space=pltpu.VMEM)
    shape = jax.ShapeDtypeStruct
    sums = [((4, 4 * rows, cols), BF) for cols, rows in WEIGHTS]
    halves = [((4, 2, rows // 2, cols), BF) for cols, rows in WEIGHTS]
    singles = [((4, rows // 2, cols), BF) for cols, rows in WEIGHTS]
    deeps = [((3, rows, cols), BF) for cols, rows in WEIGHTS]
    rest = [
        ((3, 384, 768), BF),
        ((2, 384, 576), BF),
        ((96, 2304), F32),
        ((96, 2304), BF),
        ((4, 8, 384), F32),
        ((11, 8, 384), F32),
        ((4, 8, 384), F32),
        ((4, 1, 2304), F32),
        ((8, 768), F32),
        ((512, 768), BF),
        ((512, 768), F32),
        ((2, 512, 1), F32),
        ((2, 512, 768), BF),
        ((2, 512, 768), BF),
        ((2, 768, 768), BF),
        ((2, 768, 768), BF),
        ((512, 768), BF),
        ((4, 512, 192), BF),
        ((4, 192, 768), BF),
        ((4, 512, 576), BF),
        ((2, 3, 512, 512), BF),
        ((2, 768, 576), BF),
        ((512, 768), BF),
        ((512, 768), F32),
        ((512, 768), BF),
        ((512, 768), F32),
        ((512, 768), BF),
        ((512, 192), BF),
        ((512, 576), BF),
        ((384, 512), F32),
        ((192, 768), F32),
        ((8, 768), F32),
        ((4, 1, 768), F32),
        ((4, 1, 384), F32),
        ((512, 8), F32),
    ]
    scratch = sums + sums + halves + halves + singles + singles + deeps + rest
    return pl.pallas_call(
        backward_kernel,
        out_shape=[
            shape((8, 96, 2304), BF),
            shape((8, 384), F32),
            shape((4, 128, 768), BF),
            shape((4, 128, 768), BF),
            shape((4, 8, 768), F32),
        ],
        in_specs=[vmem] + [anywhere] * 18,
        out_specs=[anywhere, vmem, anywhere, anywhere, anywhere],
        scratch_shapes=[pltpu.VMEM(*s) for s in scratch]
        + [
            pltpu.SemaphoreType.DMA((160,)),
            pltpu.SemaphoreType.DMA((160,)),
            pltpu.SemaphoreType.DMA((64,)),
        ],
        compiler_params=pltpu.CompilerParams(
            collective_id=1, has_side_effects=True, vmem_limit_bytes=62 * MIB
        ),
        name="backward_and_reduce",
    )(*args)


def finish_kernel(
    slot_row,
    blocks,
    small,
    pool,
    master,
    first,
    second,
    out_mine,
    dx_mine,
    new_master,
    new_first,
    new_second,
    layer_out,
    input_grad,
    pooled,
    norm_grads,
):
    step = pl.program_id(0)
    rows = master.shape[0]
    t = lax.axis_index("tensor")
    start = lax.axis_index("dp") * (rows * pl.num_programs(0)) + step * rows
    wanted = (lax.broadcasted_iota(jnp.int32, (rows, 1), 0) + start).astype(F32)
    match = slot_row[0:1, :768] == wanted
    gradient = dot_f32(jnp.where(match, 1.0, 0.0).astype(BF), blocks[...])
    is_small = slot_row[0:1, 768:769] == wanted
    small_line = jnp.concatenate([small[i : i + 1, :] for i in range(6)], axis=1)
    gradient = jnp.where(is_small, small_line, gradient)

    at = lax.broadcasted_iota(jnp.int32, (1, 768), 1) % 96
    rates = jnp.where(
        at < 32,
        MODEL_WIDTH ** (-0.5),
        jnp.where(
            at < 64,
            FF ** (-0.5),
            jnp.where(at < 88, MODEL_WIDTH ** (-0.5), 4.0 * MODEL_WIDTH ** (-0.5)),
        ),
    ).astype(F32)
    rate = jnp.sum(jnp.where(match, rates, 0.0), axis=1, keepdims=True)
    filled = (rate > 0.0) | is_small
    offset = lax.broadcasted_iota(jnp.int32, (1, small_line.shape[1]), 1) - 1152
    gain = ((offset >= 384) & (offset < 576)) | ((offset >= 768) & (offset < 960))
    small_rate = jnp.where(gain, 0.2, 0.1).astype(F32)
    step_rate = jnp.where(is_small, small_rate, rate)
    decay_on = jnp.where(is_small, 0.0, 1.0)
    new_master[...], new_first[...], new_second[...] = adamw(
        gradient, first[...], second[...], master[...], step_rate, decay_on, filled
    )
    for src, dst in ((out_mine, layer_out), (dx_mine, input_grad)):
        for row in range(4):
            dst[:, row, :] = src[row].astype(F32)

    @pl.when(step == 0)
    def _():
        total = jnp.zeros((4, 8, 192), F32)
        for q in range(4):
            total = total + jnp.where(t == q, pool[:, :, 192 * q : 192 * q + 192], 0.0)
        pooled[...] = total
        norm_grads[...] = jnp.concatenate(
            [small_line[:, 1152 + 192 * i : 1344 + 192 * i] for i in range(6)], axis=0
        )


def finish_call(slot_row, blocks, small, pool, master, first, second, out_mine, dx_mine):
    steps = 4
    slots, block_len = master.shape
    shape = jax.ShapeDtypeStruct

    def whole(*dims):
        return pl.BlockSpec(dims, lambda i: (0,) * len(dims))

    state = pl.BlockSpec((slots // steps, block_len), lambda i: (i, 0))
    token_in = pl.BlockSpec((4, 128 // steps, 768), lambda i: (0, i, 0))
    token_out = pl.BlockSpec((128 // steps, 4, 768), lambda i: (i, 0, 0))
    return pl.pallas_call(
        finish_kernel,
        grid=(steps,),
        out_shape=[shape((slots, block_len), F32)] * 3
        + [shape((128, 4, 768), F32)] * 2
        + [shape((4, 8, 192), F32), shape((6, 192), F32)],
        in_specs=[whole(8, 896), whole(768, block_len), whole(8, 384), whole(4, 8, 768)]
        + [state] * 3
        + [token_in] * 2,
        out_specs=[state] * 3 + [token_out] * 2 + [whole(4, 8, 192), whole(6, 192)],
        compiler_params=pltpu.CompilerParams(vmem_limit_bytes=62 * MIB),
        name="owners_update",
    )(slot_row, blocks, small, pool, master, first, second, out_mine, dx_mine)


def share_order():
    order = []
    for core in range(2):
        for chip in range(4):
            for base, count in ((0, 32), (256, 32), (512, 24), (704, 8)):
                at = base + (core * 4 + chip) * count
                order += list(range(at, at + count))
    return np.array(order + [768] + [4096] * 127, np.int32)


def local_rows(
    layer_input_rows,
    sentence_index_row,
    padding_mask,
    output_gradient,
    owner_rank,
    master_state,
    first_moment,
    second_moment,
):
    block_len = master_state.shape[2]
    order = share_order()
    (
        w_qkv,
        _,
        w_up,
        w_down,
        w_out,
        slot_row,
        small_all,
        x_row,
        gy_row,
        qkv,
        prob_low,
        attended,
        normed_one,
        h_low,
        act,
        pull,
        normed_two,
        inverse,
        out_row,
        pool_mean,
    ) = forward_call(
        master_state[0],
        owner_rank[None],
        jnp.asarray(order[:, None]),
        sentence_index_row,
        padding_mask,
        jnp.transpose(layer_input_rows, (1, 0, 2)),
        jnp.transpose(output_gradient, (1, 0, 2)),
    )
    blocks, small_sum, out_mine, dx_mine, pool_all = backward_call(
        padding_mask,
        out_row,
        pool_mean,
        gy_row,
        normed_two,
        inverse,
        small_all,
        act,
        pull,
        w_down,
        w_up,
        h_low,
        normed_one,
        attended,
        w_out,
        qkv,
        prob_low,
        w_qkv,
        x_row,
    )
    new_master, new_first, new_second, layer_out, input_grad, pooled, norm_grads = finish_call(
        slot_row,
        blocks.reshape(768, block_len),
        small_sum,
        pool_all,
        master_state[0],
        first_moment[0],
        second_moment[0],
        out_mine,
        dx_mine,
    )
    return (
        layer_out,
        pooled,
        input_grad,
        new_master[None],
        new_first[None],
        new_second[None],
        norm_grads,
    )


def solution(mesh):
    in_specs = (
        P("tensor", "dp", None),
        P("dp", None),
        P("dp", None),
        P("tensor", "dp", None),
        P(),
        P("tensor", "dp", None),
        P("tensor", "dp", None),
        P("tensor", "dp", None),
    )
    out_specs = (
        P("tensor", "dp", None),
        P("dp", None, "tensor"),
        P("tensor", "dp", None),
        P("tensor", "dp", None),
        P("tensor", "dp", None),
        P("tensor", "dp", None),
        P(None, "tensor"),
    )
    plain = mesh.shape["dp"] != 8 or mesh.shape["tensor"] != 4
    body = local_general if plain else local_rows
    return jax.shard_map(body, mesh=mesh, in_specs=in_specs, out_specs=out_specs, check_vma=False)
```

```python
import jax
import numpy as np
import jax.numpy as jnp
from jax import lax
from jax.experimental import pallas as pl
from jax.experimental.pallas import tpu as pltpu
from jax.sharding import PartitionSpec as P

MODEL_WIDTH = 768
HEAD_DIM = 64
FF = 3072
SMAX = 8
STEP = 10


NORM_EPS = 1e-05
ADAM_EPS = 1e-08
BETA_ONE = 0.9
BETA_TWO = 0.999
DECAY_RATE = 0.01
MASKED = -1e30
exact_precision = lax.Precision.HIGHEST


def slot_tables(owner_rank, per_owner):
    ordinal = jnp.arange(owner_rank.shape[0], dtype=jnp.int32)
    same_owner = owner_rank[:, None] == owner_rank[None, :]
    earlier = ordinal[None, :] < ordinal[:, None]
    ranking = jnp.sum((same_owner & earlier).astype(jnp.int32), axis=1)
    return owner_rank * per_owner + ranking


def slot_blocks(slot_of, wanted):
    matches = slot_of[None, :] == wanted[:, None]
    filled = jnp.any(matches, axis=1)
    ordinal = jnp.arange(slot_of.shape[0], dtype=jnp.int32)
    block_of = jnp.sum(jnp.where(matches, ordinal[None, :], 0), axis=1)
    return (block_of, filled)


def step_rates(token_position, width, hidden, tensor_size):
    width_loc = width // tensor_size
    ffn_loc = hidden // tensor_size
    end_up = width * ffn_loc
    end_down = end_up + ffn_loc * width
    end_qkv = end_down + width * 3 * width_loc
    end_out = end_qkv + width_loc * width
    offset = token_position - end_out
    first_gain = (offset >= 4 * width_loc + ffn_loc) & (offset < 5 * width_loc + ffn_loc)
    second_gain = (offset >= 6 * width_loc + ffn_loc) & (offset < 7 * width_loc + ffn_loc)
    small_rate = jnp.where(first_gain | second_gain, 0.2, 0.1)
    step_rate = jnp.where(
        token_position < end_up,
        width ** (-0.5),
        jnp.where(
            token_position < end_down,
            hidden ** (-0.5),
            jnp.where(
                token_position < end_qkv,
                width ** (-0.5),
                jnp.where(token_position < end_out, 4.0 * width ** (-0.5), small_rate),
            ),
        ),
    )
    decay_on = (token_position < end_out).astype(jnp.float32)
    return (step_rate.astype(jnp.float32), decay_on)


def adamw(gradient, moment, square, weight, step_rate, decay_on, filled):
    new_moment = BETA_ONE * moment + (1.0 - BETA_ONE) * gradient
    new_square = BETA_TWO * square + (1.0 - BETA_TWO) * gradient * gradient
    unbiased = new_moment / (1.0 - BETA_ONE**STEP)
    divisor = jnp.sqrt(new_square / (1.0 - BETA_TWO**STEP)) + ADAM_EPS
    new_weight = weight - step_rate * (unbiased / divisor + DECAY_RATE * decay_on * weight)
    zeroed = jnp.zeros_like(weight)
    return (
        jnp.where(filled, new_weight, zeroed),
        jnp.where(filled, new_moment, zeroed),
        jnp.where(filled, new_square, zeroed),
    )


def normalize(values):
    centred = values - jnp.mean(values, axis=-1, keepdims=True)
    inv_dev = lax.rsqrt(jnp.mean(centred * centred, axis=-1, keepdims=True) + NORM_EPS)
    return (centred * inv_dev, inv_dev)


def norm_back(grad_scaled, normed, inv_dev):
    first_mean = jnp.mean(grad_scaled, axis=-1, keepdims=True)
    second_mean = jnp.mean(grad_scaled * normed, axis=-1, keepdims=True)
    return inv_dev * (grad_scaled - first_mean - normed * second_mean)


def allowed_pairs(sentence_labels, real_token_flags):
    row_len = sentence_labels.shape[-1]
    same_sent = sentence_labels[:, :, None] == sentence_labels[:, None, :]
    live = (real_token_flags[:, :, None] == 1) & (real_token_flags[:, None, :] == 1)
    diagonal = jnp.eye(row_len, dtype=bool)[None]
    return same_sent & live | diagonal


def masked_scores(queries, key_rows, allowed, scaling):
    scores = (
        jnp.einsum("qshe,kshe->shqk", queries, key_rows, preferred_element_type=jnp.float32)
        * scaling
    )
    return jnp.where(allowed[:, None], scores, MASKED)


def split_flat(flat_all, width_loc, ffn_loc):
    end_up = MODEL_WIDTH * ffn_loc
    end_down = end_up + ffn_loc * MODEL_WIDTH
    end_qkv = end_down + MODEL_WIDTH * 3 * width_loc
    end_out = end_qkv + width_loc * MODEL_WIDTH
    return (
        flat_all[:end_up].reshape(MODEL_WIDTH, ffn_loc),
        flat_all[end_up:end_down].reshape(ffn_loc, MODEL_WIDTH),
        flat_all[end_down:end_qkv].reshape(MODEL_WIDTH, 3 * width_loc),
        flat_all[end_qkv:end_out].reshape(width_loc, MODEL_WIDTH),
        flat_all[end_out:],
    )


def local_general(
    layer_input_rows,
    sentence_index_row,
    padding_mask,
    output_gradient,
    owner_rank,
    master_state,
    first_moment,
    second_moment,
):
    tensor_size = lax.axis_size("tensor")
    tensor_at = lax.axis_index("tensor")
    data_size = lax.axis_size("dp")
    data_at = lax.axis_index("dp")
    width_loc = MODEL_WIDTH // tensor_size
    ffn_loc = FF // tensor_size
    heads_loc = width_loc // HEAD_DIM
    quarter = layer_input_rows.shape[0]
    seq_count = layer_input_rows.shape[1]
    row_len = quarter * tensor_size
    per_owner = master_state.shape[1]
    block_len = master_state.shape[2]
    nblocks = owner_rank.shape[0]
    slot_of = slot_tables(owner_rank, per_owner)
    gathered = lax.all_gather(master_state.astype(jnp.bfloat16), "dp", axis=1, tiled=True)[0]
    flat_weights = gathered[slot_of].reshape(nblocks * block_len)
    up_weight, down_weight, w_qkv, w_out, small_part = split_flat(flat_weights, width_loc, ffn_loc)
    bias_q = small_part[:width_loc].astype(jnp.float32)
    bias_v = small_part[width_loc : 2 * width_loc].astype(jnp.float32)
    expand_bias = small_part[2 * width_loc : 2 * width_loc + ffn_loc].astype(jnp.float32)
    norm_parts = small_part[2 * width_loc + ffn_loc :].reshape(6, width_loc)
    full_rows, norm_whole = (
        lax.all_gather(layer_input_rows, "tensor", axis=0, tiled=True),
        lax.all_gather(norm_parts, "tensor", axis=1, tiled=True),
    )
    norm_all = norm_whole.astype(jnp.float32)
    bias_out, bias_down = (norm_all[0], norm_all[1])
    gain_one, shift_one, gain_two, shift_two = (norm_all[2], norm_all[3], norm_all[4], norm_all[5])
    qkv_lin = jnp.einsum("lsd,de->lse", full_rows, w_qkv, preferred_element_type=jnp.float32)
    bias_qkv = jnp.concatenate([bias_q, jnp.zeros((width_loc,), jnp.float32), bias_v])
    qkv = (qkv_lin + bias_qkv).astype(jnp.bfloat16)
    queries = qkv[:, :, :width_loc].reshape(row_len, seq_count, heads_loc, HEAD_DIM)
    key_rows = qkv[:, :, width_loc : 2 * width_loc].reshape(row_len, seq_count, heads_loc, HEAD_DIM)
    values = qkv[:, :, 2 * width_loc :].reshape(row_len, seq_count, heads_loc, HEAD_DIM)
    scaling = HEAD_DIM ** (-0.5)
    allowed = allowed_pairs(sentence_index_row, padding_mask)
    scores = masked_scores(queries, key_rows, allowed, scaling)
    row_peak = jnp.max(scores, axis=-1, keepdims=True)
    log_total = row_peak + jnp.log(jnp.sum(jnp.exp(scores - row_peak), axis=-1, keepdims=True))
    prob_low = jnp.exp(scores - log_total).astype(jnp.bfloat16)
    attended = jnp.einsum("shqk,kshe->qshe", prob_low, values, preferred_element_type=jnp.float32)
    attended = attended.astype(jnp.bfloat16).reshape(row_len, seq_count, width_loc)
    portion_rows = attended
    attn_rows = lax.psum_scatter(
        jnp.einsum("lse,ed->lsd", portion_rows, w_out, preferred_element_type=jnp.float32).astype(
            jnp.bfloat16
        ),
        "tensor",
        scatter_dimension=0,
        tiled=True,
    ).astype(jnp.float32)
    z_one = layer_input_rows.astype(jnp.float32) + attn_rows + bias_out
    normed_one, inv_one = normalize(z_one)
    h_mine = normed_one * gain_one + shift_one
    hidden_narrow_whole = lax.all_gather(h_mine.astype(jnp.bfloat16), "tensor", axis=0, tiled=True)
    up_pre = (
        jnp.einsum(
            "wer,rb->web", hidden_narrow_whole, up_weight, preferred_element_type=jnp.float32
        )
        + expand_bias
    )
    activation_narrow = jax.nn.gelu(up_pre, approximate=False).astype(jnp.bfloat16)
    portion_rows = activation_narrow
    down_rows = lax.psum_scatter(
        jnp.einsum(
            "aij,jb->aib", portion_rows, down_weight, preferred_element_type=jnp.float32
        ).astype(jnp.bfloat16),
        "tensor",
        scatter_dimension=0,
        tiled=True,
    ).astype(jnp.float32)
    z_two = h_mine + down_rows + bias_down
    normed_two, inv_two = normalize(z_two)
    layer_out = normed_two * gain_two + shift_two
    seg_mine = lax.dynamic_slice_in_dim(sentence_index_row, tensor_at * quarter, quarter, 1)
    valid_mine = lax.dynamic_slice_in_dim(padding_mask, tensor_at * quarter, quarter, 1)
    sent_ids = jnp.arange(SMAX, dtype=jnp.int32)
    onehot_mine = (
        (seg_mine[:, :, None] == sent_ids[None, None, :]) & (valid_mine[:, :, None] == 1)
    ).astype(jnp.float32)
    pool_part = jnp.einsum("slc,lsd->scd", onehot_mine, layer_out, precision=exact_precision)
    onehot_full = (
        (sentence_index_row[:, :, None] == sent_ids[None, None, :])
        & (padding_mask[:, :, None] == 1)
    ).astype(jnp.float32)
    counts = jnp.sum(onehot_full, axis=1)
    grad_out = output_gradient.astype(jnp.float32) * valid_mine.T[:, :, None].astype(jnp.float32)
    d_gain_two = jnp.sum(grad_out * normed_two, axis=(0, 1))
    d_shift_two = jnp.sum(grad_out, axis=(0, 1))
    dz_two = norm_back(grad_out * gain_two, normed_two, inv_two)
    d_bias_down = jnp.sum(dz_two, axis=(0, 1))
    second_sum_gradient_wide = lax.all_gather(
        dz_two.astype(jnp.bfloat16), "tensor", axis=0, tiled=True
    )
    down_weight_gradient = jnp.einsum(
        "ipo,ipr->or",
        activation_narrow,
        second_sum_gradient_wide,
        preferred_element_type=jnp.float32,
    )
    activation_gradient = jnp.einsum(
        "ugp,jp->ugj", second_sum_gradient_wide, down_weight, preferred_element_type=jnp.float32
    )
    gelu_pull = jax.vjp(lambda pre_act: jax.nn.gelu(pre_act, approximate=False), up_pre)[1]
    d_up = gelu_pull(activation_gradient)[0]
    d_bias_up = jnp.sum(d_up, axis=(0, 1))
    expand_gradient_narrow = d_up.astype(jnp.bfloat16)
    up_weight_gradient = jnp.einsum(
        "iux,iuy->xy",
        hidden_narrow_whole,
        expand_gradient_narrow,
        preferred_element_type=jnp.float32,
    )
    portion_rows = expand_gradient_narrow
    dh_rows = lax.psum_scatter(
        jnp.einsum(
            "uih,vh->uiv", portion_rows, up_weight, preferred_element_type=jnp.float32
        ).astype(jnp.bfloat16),
        "tensor",
        scatter_dimension=0,
        tiled=True,
    ).astype(jnp.float32)
    dh_mine = dz_two + dh_rows
    d_gain_one = jnp.sum(dh_mine * normed_one, axis=(0, 1))
    d_shift_one = jnp.sum(dh_mine, axis=(0, 1))
    dz_one = norm_back(dh_mine * gain_one, normed_one, inv_one)
    d_bias_out = jnp.sum(dz_one, axis=(0, 1))
    dz_one_full = lax.all_gather(dz_one.astype(jnp.bfloat16), "tensor", axis=0, tiled=True)
    d_w_out = jnp.einsum("lse,lsd->ed", attended, dz_one_full, preferred_element_type=jnp.float32)
    d_attended = jnp.einsum("lsd,ed->lse", dz_one_full, w_out, preferred_element_type=jnp.float32)
    d_attended = d_attended.astype(jnp.bfloat16).reshape(row_len, seq_count, heads_loc, HEAD_DIM)
    scores_again = masked_scores(queries, key_rows, allowed, scaling)
    attn_prob = jnp.exp(scores_again - log_total)
    prob_again = attn_prob.astype(jnp.bfloat16)
    d_prob = jnp.einsum("qshe,kshe->shqk", d_attended, values, preferred_element_type=jnp.float32)
    d_values = jnp.einsum(
        "shqk,qshe->kshe", prob_again, d_attended, preferred_element_type=jnp.float32
    )
    inner = jnp.sum(d_prob * attn_prob, axis=-1, keepdims=True)
    d_scores = (attn_prob * (d_prob - inner)).astype(jnp.bfloat16)
    d_queries = (
        jnp.einsum("shqk,kshe->qshe", d_scores, key_rows, preferred_element_type=jnp.float32)
        * scaling
    )
    d_keys = (
        jnp.einsum("shqk,qshe->kshe", d_scores, queries, preferred_element_type=jnp.float32)
        * scaling
    )
    d_bias_q = jnp.sum(d_queries, axis=(0, 1)).reshape(width_loc)
    d_bias_v = jnp.sum(d_values, axis=(0, 1)).reshape(width_loc)
    d_qkv_low = jnp.concatenate(
        [
            d_queries.reshape(row_len, seq_count, width_loc),
            d_keys.reshape(row_len, seq_count, width_loc),
            d_values.reshape(row_len, seq_count, width_loc),
        ],
        axis=2,
    ).astype(jnp.bfloat16)
    d_w_qkv = jnp.einsum("lsd,lse->de", full_rows, d_qkv_low, preferred_element_type=jnp.float32)
    portion_rows = d_qkv_low
    dx_rows = lax.psum_scatter(
        jnp.einsum("lse,de->lsd", portion_rows, w_qkv, preferred_element_type=jnp.float32).astype(
            jnp.bfloat16
        ),
        "tensor",
        scatter_dimension=0,
        tiled=True,
    ).astype(jnp.float32)
    input_grad = dz_one + dx_rows
    shared_grads = jnp.stack(
        [d_bias_out, d_bias_down, d_gain_one, d_shift_one, d_gain_two, d_shift_two]
    )[None]
    pool_sum, shared_sum = (
        lax.psum_scatter(
            pool_part.astype(jnp.bfloat16), "tensor", scatter_dimension=2, tiled=True
        ).astype(jnp.float32),
        lax.psum_scatter(
            shared_grads.astype(jnp.bfloat16), "tensor", scatter_dimension=2, tiled=True
        ).astype(jnp.float32),
    )
    pooled_mean = pool_sum / jnp.maximum(counts, 1.0)[:, :, None]
    flat_grads = jnp.concatenate(
        [
            up_weight_gradient.reshape(-1),
            down_weight_gradient.reshape(-1),
            d_w_qkv.reshape(-1),
            d_w_out.reshape(-1),
            d_bias_q,
            d_bias_v,
            d_bias_up,
            shared_sum.reshape(-1),
        ]
    )
    grad_blocks = flat_grads.reshape(nblocks, block_len)
    wanted = data_at * per_owner + jnp.arange(per_owner, dtype=jnp.int32)
    block_of, filled = slot_blocks(slot_of, wanted)
    slot_grads = (
        jnp.zeros((data_size * per_owner, block_len), jnp.float32).at[slot_of].set(grad_blocks)
    )
    owned_grads = lax.psum_scatter(slot_grads, "dp", scatter_dimension=0, tiled=True)
    norm_grads = lax.psum(shared_sum[0], "dp")
    token_position = block_of[:, None] * block_len + jnp.arange(block_len, dtype=jnp.int32)[None, :]
    step_rate, decay_on = step_rates(token_position, MODEL_WIDTH, FF, tensor_size)
    new_master, new_first, new_second = adamw(
        owned_grads,
        first_moment[0],
        second_moment[0],
        master_state[0],
        step_rate,
        decay_on,
        filled[:, None],
    )
    return (
        layer_out,
        pooled_mean,
        input_grad,
        new_master[None],
        new_first[None],
        new_second[None],
        norm_grads,
    )


MESH = pl.DeviceIdType.MESH
BF = jnp.bfloat16
F32 = jnp.float32
WEIGHTS = ((576, 96), (768, 32), (768, 96), (768, 96))
MIB = 2**20


class Place:
    def __init__(self):
        d = lax.axis_index("dp")
        self.t = lax.axis_index("tensor")
        self.c = d % 2
        self.x = (d // 2) % 2
        self.y = d // 4
        self.xy = d // 2
        self.core = (d + 1 - 2 * self.c, self.t)
        self.right = (d + 2 - 4 * self.x, self.t)
        self.down = (d + 4 - 8 * self.y, self.t)
        self.diag = (d + 6 - 4 * self.x - 8 * self.y, self.t)
        self.deep = [None] + [(d, (self.t + k) % 4) for k in (1, 2, 3)]
        self.ahead = [(self.t + k) % 4 for k in range(4)]
        self.behind = [(self.t + 4 - k) % 4 for k in range(4)]

    def greet(self):
        barrier = pltpu.get_barrier_semaphore()
        peers = [self.core, self.right, self.down, self.diag] + self.deep[1:]
        for peer in peers:
            pl.semaphore_signal(barrier, inc=1, device_id=peer, device_id_type=MESH)
        pl.semaphore_wait(barrier, len(peers))


class Sender:
    def __init__(self, send_sems, recv_sems, local_sems):
        self.sems = (send_sems, recv_sems, local_sems)
        self.used = 0
        self.used_local = 0
        self.open = []

    def send(self, src, dst, peer):
        i = self.used
        self.used += 1
        copy = pltpu.make_async_remote_copy(
            src_ref=src,
            dst_ref=dst,
            send_sem=self.sems[0].at[i],
            recv_sem=self.sems[1].at[i],
            device_id=peer,
            device_id_type=MESH,
        )
        copy.start()
        self.open.append(copy)
        return copy

    def copy(self, src, dst):
        i = self.used_local
        self.used_local += 1
        copy = pltpu.make_async_copy(src, dst, self.sems[2].at[i])
        copy.start()
        return copy

    def sent(self, copy):
        copy.wait_send()
        self.open = [other for other in self.open if other is not copy]

    def finish(self):
        for copy in self.open:
            copy.wait_send()


def rows_of(place, rows, at=None):
    at = place.xy if at is None else at
    return pl.ds(pl.multiple_of(place.c * (4 * rows) + at * rows, 32), rows)


def half_of(place, rows):
    return pl.ds(pl.multiple_of(place.c * (4 * rows), 128), 4 * rows)


def interleave(size, parts):
    group = size // parts
    out_row = lax.broadcasted_iota(jnp.int32, (size, size), 0)
    col = lax.broadcasted_iota(jnp.int32, (size, size), 1)
    part = jnp.zeros((size, size), jnp.int32)
    for k in range(1, parts):
        part = part + (col >= k * group).astype(jnp.int32)
    return jnp.where(out_row == parts * (col - group * part) + part, 1.0, 0.0).astype(BF)


def interleave_out():
    out_row = lax.broadcasted_iota(jnp.int32, (32, 32), 0)
    col = lax.broadcasted_iota(jnp.int32, (32, 32), 1)
    part = (col >= 8).astype(jnp.int32) + (col >= 16).astype(jnp.int32)
    keep = (out_row == 3 * (col - 8 * part) + part) & (col < 24)
    return jnp.where(keep, 1.0, 0.0).astype(BF)


def dot_f32(a, b):
    return jnp.dot(a, b, preferred_element_type=F32)


def compact_out():
    out_row = lax.broadcasted_iota(jnp.int32, (192, 256), 0)
    col = lax.broadcasted_iota(jnp.int32, (192, 256), 1)
    group = jnp.zeros((192, 256), jnp.int32)
    for i in range(1, 8):
        group = group + (out_row >= 24 * i).astype(jnp.int32)
    return jnp.where(col == out_row + 8 * group, 1.0, 0.0).astype(BF)


def dot_nt(a, b):
    return lax.dot_general(a, b, (((1,), (1,)), ((), ())), preferred_element_type=F32)


def dot_tn(a, b):
    return lax.dot_general(a, b, (((0,), (0,)), ((), ())), preferred_element_type=F32)


def unpack_small(packed, small):
    for t in range(4):
        small[t] = jnp.concatenate([packed[t, i : i + 1, :] for i in range(6)], axis=1)


def norm_vectors(small, norm):
    for i in range(6):
        at = 1152 + 192 * i
        norm[i : i + 1, :] = jnp.concatenate([small[t, 0:1, at : at + 192] for t in range(4)], axis=1)


def row_loop(body, step=128):
    @pl.loop(0, 512 // step)
    def _(i):
        body(pl.ds(pl.multiple_of(i * step, step), step))


def forward_kernel(
    master,
    owners,
    order_col,
    labels,
    flags,
    x_in,
    gy_in,
    w_qkv,
    w_out,
    w_up,
    w_down,
    out_compact,
    slot_out,
    small_out,
    x_out,
    gy_row,
    qkv_out,
    prob_out,
    att_out,
    n_one_out,
    h_out,
    act_out,
    pull_out,
    n_two_out,
    inv_out,
    row_out,
    pool_out,
    slot_row,
    slot_col,
    id_row,
    id_col,
    slots,
    canon_att,
    canon_ffn,
    land_att,
    land_ffn,
    pass_ffn,
    pass_land,
    share,
    p_qkv,
    p_out,
    p_up,
    p_down,
    small_mine,
    small_land,
    small_total,
    packed,
    small,
    norm,
    bias_qkv,
    v_qkv,
    v_out,
    v_compact,
    v_up,
    v_down,
    x_row,
    qkv,
    prob,
    att,
    n_one,
    h_wide,
    h_low,
    act,
    pull,
    total,
    inv,
    row_low,
    pool,
    send_sems,
    recv_sems,
    local_sems,
):
    place = Place()
    link = Sender(send_sems, recv_sems, local_sems)
    slots[place.c] = master[...].astype(BF)

    blocks = owners.shape[1]
    wide = slot_row.shape[1]
    owner = jnp.concatenate(
        [owners[...].astype(F32), jnp.full((1, wide - blocks), -1.0, F32)], axis=1
    )
    kinds = lax.broadcasted_iota(jnp.int32, (8, wide), 0).astype(F32)
    owned = jnp.where(kinds == owner, 1.0, 0.0)
    ordinal = lax.broadcasted_iota(jnp.int32, (wide, wide), 1)
    earlier = jnp.where(lax.broadcasted_iota(jnp.int32, (wide, wide), 0) < ordinal, 1.0, 0.0)
    ahead = dot_f32(owned.astype(BF), earlier.astype(BF))
    ranking = jnp.sum(owned * ahead, axis=0, keepdims=True)
    place_of = jnp.where(order_col[...] == ordinal, 1.0, 0.0).astype(BF)
    pair = jnp.where(kinds == 0.0, owner, ranking).astype(BF)
    row = dot_nt(pair, place_of)
    col = dot_nt(place_of, pair)
    per_owner = float(master.shape[0])
    slot_row[...] = jnp.broadcast_to(row[0:1, :] * per_owner + row[1:2, :], slot_row.shape)
    slot_col[...] = jnp.broadcast_to(col[:, 0:1] * per_owner + col[:, 1:2], slot_col.shape)

    own = pl.ds(place.t, 1)
    apart = -1 - lax.broadcasted_iota(jnp.int32, (1, 512), 1)
    ids = jnp.where(flags[own, :] == 1, labels[own, :], apart).astype(F32)
    id_row[...] = jnp.broadcast_to(ids, id_row.shape)
    id_col[...] = jnp.transpose(id_row[...])
    place.greet()
    whole = (w_qkv, w_out, w_up, w_down)
    held = (v_qkv, v_out, v_up, v_down)
    piece = (p_qkv, p_out, p_up, p_down)
    peers = (place.right, place.down, place.diag)
    mine_rows = pl.ds(pl.multiple_of(place.t * 128, 128), 128)
    tidy = [link.copy(slot_row, slot_out)]

    core_slots = link.send(slots.at[place.c], slots.at[place.c], place.core)
    x_moves = [
        link.send(x_in.at[place.ahead[k]], x_row.at[mine_rows], place.deep[k]) for k in (1, 2, 3)
    ]
    x_stay = link.copy(x_in.at[place.t], x_row.at[mine_rows])
    tidy.append(link.copy(gy_in.at[place.t], gy_row.at[mine_rows]))
    core_slots.wait_recv()

    pair_slots = slots[...].reshape(384, 2304)
    slot_id = (lax.broadcasted_iota(jnp.int32, (64, 384), 1) + place.xy * 384).astype(F32)
    order = [(3, place.diag), (1, place.right), (2, place.down), (0, None)]

    def spread(lo, rows, canon, land):
        sent = []
        for j, peer in order:
            at = place.xy if peer is None else peer[0] // 2
            spot = pl.ds(pl.multiple_of(place.c * 384 + at * 96 + lo, 32), rows)
            wanted = slot_col[spot, 0:1]
            pick = jnp.where(wanted == slot_id[:rows], 1.0, 0.0).astype(BF)
            canon[j] = dot_f32(pick, pair_slots).astype(BF)
            if peer is not None:
                sent.append(link.send(canon.at[j], land.at[j - 1], peer))
        return sent

    def collect(sent, lo, rows, canon, land):
        for move in sent:
            move.wait_recv()
        share[lo : lo + rows, :] = (
            canon[0].astype(F32) + land[0].astype(F32) + land[1].astype(F32) + land[2].astype(F32)
        )

    att_sent = spread(64, 32, canon_att, land_att)
    pick_small = jnp.where(slot_row[:, 768:769] == slot_id[:8], 1.0, 0.0).astype(BF)
    picked = dot_f32(pick_small, pair_slots)
    for i in range(6):
        small_mine[i : i + 1, :] = picked[0:1, 384 * i : 384 * i + 384]
    small_mine[6:8, :] = jnp.zeros((2, 384), F32)
    small_moves = [link.send(small_mine, small_land.at[j], peer) for j, peer in enumerate(peers)]
    def spread_halves():
        for j, peer in order:
            at = place.xy if peer is None else peer[0] // 2
            spot = pl.ds(pl.multiple_of(place.c * 384 + at * 96, 32), 64)
            pick = jnp.where(slot_col[spot, 0:1] == slot_id, 1.0, 0.0).astype(BF)
            canon_ffn[j] = dot_f32(pick, pair_slots).astype(BF)
            if j in (1, 3):
                half = canon_ffn.at[j, pl.ds(0, 32)]
                halves[j, 0] = link.send(half, land_ffn.at[0, j // 2], place.right)
            if j in (2, 3):
                half = canon_ffn.at[j, pl.ds(32, 32)]
                halves[j, 1] = link.send(half, land_ffn.at[1, j - 2], place.down)

    def pass_halves():
        halves[3, 0].wait_recv()
        pass_ffn[0] = canon_ffn[2, 0:32, :] + land_ffn[0, 1]
        halves["down"] = link.send(pass_ffn.at[0], pass_land.at[0], place.down)
        halves[3, 1].wait_recv()
        pass_ffn[1] = canon_ffn[1, 32:64, :] + land_ffn[1, 1]
        halves["right"] = link.send(pass_ffn.at[1], pass_land.at[1], place.right)

    def collect_halves():
        halves[1, 0].wait_recv()
        halves[2, 1].wait_recv()
        halves["down"].wait_recv()
        halves["right"].wait_recv()
        for i in range(2):
            share[32 * i : 32 * i + 32, :] = (
                canon_ffn[0, 32 * i : 32 * i + 32, :] + land_ffn[i, 0] + pass_land[i]
            ).astype(F32)

    halves = {}
    att_sent[0].wait_recv()
    spread_halves()
    collect(att_sent[1:], 64, 32, canon_att, land_att)

    p_qkv[...] = dot_f32(
        interleave(96, 4),
        jnp.concatenate([share[64:88, 576 * r : 576 * r + 576] for r in range(4)], axis=0).astype(BF),
    ).astype(BF)

    def spread_out():
        parts = [share[88:96, 768 * k : 768 * k + 768] for k in range(3)]
        parts = parts + [jnp.zeros((8, 768), F32)]
        p_out[...] = dot_f32(interleave_out(), jnp.concatenate(parts, axis=0).astype(BF)).astype(BF)

    def spread_ffn():
        three = interleave(96, 3)
        for at, ref in ((0, p_up), (32, p_down)):
            parts = [share[at : at + 32, 768 * k : 768 * k + 768] for k in range(3)]
            ref[...] = dot_f32(three, jnp.concatenate(parts, axis=0).astype(BF)).astype(BF)

    deep_moves, right_moves, down_moves, own_copies, core_moves, loads = {}, {}, {}, {}, {}, {}

    def deep_send(w):
        spot = whole[w].at[place.t, rows_of(place, WEIGHTS[w][1])]
        own_copies[w] = link.copy(piece[w], spot)
        deep_moves[w] = [link.send(piece[w], spot, place.deep[k]) for k in (1, 2, 3)]

    def plane_send(w, k):
        rows = WEIGHTS[w][1]
        spot = whole[w].at[place.behind[k], rows_of(place, rows)]
        src = piece[w] if k == 0 else spot
        if k:
            deep_moves[w][k - 1].wait_recv()
        right_moves[w, k] = link.send(src, spot, place.right)
        down_moves[w, k] = link.send(src, spot, place.down)

    def plane_pass(w, k):
        rows = WEIGHTS[w][1]
        half = rows // 2
        right_moves[w, k].wait_recv()
        down_moves[w, k].wait_recv()
        t = place.behind[k]
        right_at = place.c * (4 * rows) + (place.right[0] // 2) * rows
        down_at = place.c * (4 * rows) + (place.down[0] // 2) * rows
        first = whole[w].at[t, pl.ds(pl.multiple_of(right_at, 16), half)]
        second = whole[w].at[t, pl.ds(pl.multiple_of(down_at + half, 16), half)]
        right_moves[w, k, 1] = link.send(second, second, place.right)
        down_moves[w, k, 1] = link.send(first, first, place.down)

    def core_pass(w, k):
        if k == 0:
            own_copies[w].wait()
        right_moves[w, k, 1].wait_recv()
        down_moves[w, k, 1].wait_recv()
        spot = whole[w].at[place.behind[k], half_of(place, WEIGHTS[w][1])]
        core_moves[w, k] = link.send(spot, spot, place.core)

    def load(w, k):
        core_moves[w, k].wait_recv()
        t = place.behind[k]
        loads[w, k] = link.copy(whole[w].at[t], held[w].at[t])

    def qkv_step(k):
        loads[0, k].wait()
        t = place.behind[k]

        def body(rows):
            lin = dot_f32(x_row[rows, :], v_qkv[t]) + bias_qkv[t]
            qkv[t, rows, :] = lin.astype(BF)

        row_loop(body, 256)

    def attention(k):
        t = place.behind[k]

        def body(rows):
            allowed = id_col[rows, 0:1] == id_row[0:1, :]
            parts = []
            for i in range(3):
                at = 64 * i
                scores = dot_nt(qkv[t, rows, at : at + 64], qkv[t, :, 192 + at : 256 + at]) * 0.125
                scores = jnp.where(allowed, scores, MASKED)
                weight = jnp.exp(scores - jnp.max(scores, axis=1, keepdims=True))
                weight = weight * (1.0 / jnp.sum(weight, axis=1, keepdims=True))
                low = weight.astype(BF)
                prob[3 * t + i, rows, :] = low
                parts.append(dot_f32(low, qkv[t, :, 384 + at : 448 + at]))
            att[t, rows, :] = jnp.concatenate(parts, axis=1).astype(BF)

        row_loop(body, 256)
        tidy.append(link.copy(qkv.at[t], qkv_out.at[t]))
        tidy.append(link.copy(att.at[t], att_out.at[t]))
        tidy.append(link.copy(prob.at[pl.ds(3 * t, 3)], prob_out.at[pl.ds(3 * t, 3)]))

    def out_step():
        pick = compact_out()
        for k in range(4):
            loads[1, k].wait()
        for t in range(4):
            v_compact[t] = dot_f32(pick, v_out[t]).astype(BF)
        tidy.append(link.copy(v_compact, out_compact))

        def body(rows):
            z = x_row[rows, :].astype(F32) + norm[0:1, :]
            for t in range(4):
                z = z + dot_f32(att[t, rows, :], v_compact[t])
            normed, inverse = normalize(z)
            n_one[rows, :] = normed
            inv[0, rows, :] = inverse
            h = normed * norm[2:3, :] + norm[3:4, :]
            h_low[rows, :] = h.astype(BF)
            h_wide[rows, :] = h
            total[rows, :] = h + norm[1:2, :]

        row_loop(body, 256)
        tidy.append(link.copy(n_one, n_one_out))
        tidy.append(link.copy(h_low, h_out))

    def up_step(k):
        loads[2, k].wait()
        t = place.behind[k]

        def body(rows):
            pre = dot_f32(h_low[rows, :], v_up[t]) + small[t, 0:1, 384:1152]
            below = 0.5 + 0.5 * lax.erf(pre * (0.5**0.5))
            act[t, rows, :] = (pre * below).astype(BF)
            slope = below + pre * (jnp.exp(-0.5 * pre * pre) * 0.3989422804014327)
            pull[t, rows, :] = slope.astype(BF)

        row_loop(body, 256)
        tidy.append(link.copy(act.at[t], act_out.at[t]))
        tidy.append(link.copy(pull.at[t], pull_out.at[t]))

    def down_step(k):
        loads[3, k].wait()
        t = place.behind[k]

        def body(rows):
            total[rows, :] += dot_f32(act[t, rows, :], v_down[t])

        row_loop(body, 256)

    def end_step():
        sentence = lax.broadcasted_iota(jnp.int32, (SMAX, 512), 0).astype(F32)
        member = jnp.where(sentence == id_row[...], 1.0, 0.0)
        count = jnp.maximum(jnp.sum(member, axis=1, keepdims=True), 1.0)

        def body(rows):
            normed, inverse = normalize(total[rows, :])
            inv[1, rows, :] = inverse
            out = normed * norm[4:5, :] + norm[5:6, :]
            total[rows, :] = normed
            h_wide[rows, :] = out
            row_low[rows, :] = out.astype(BF)

        row_loop(body, 256)
        pool[...] = jnp.dot(member, h_wide[...], precision=exact_precision, preferred_element_type=F32) / count
        tidy.append(link.copy(total, n_two_out))
        tidy.append(link.copy(row_low, row_out))
        tidy.append(link.copy(pool, pool_out))
        tidy.append(link.copy(inv, inv_out))

    every = range(4)
    others = (1, 2, 3)
    small_state, gy_moves = {}, []

    def small_collect():
        for move in small_moves:
            move.wait_recv()
        small_total[...] = small_mine[...] + small_land[0] + small_land[1] + small_land[2]
        small_state["stay"] = link.copy(small_total, packed.at[place.t])
        small_state["deep"] = [
            link.send(small_total, packed.at[place.t], place.deep[k]) for k in others
        ]

    def small_ready():
        small_state["stay"].wait()
        for move in small_state["deep"]:
            move.wait_recv()
        unpack_small(packed, small)
        norm_vectors(small, norm)
        for t in every:
            bias_qkv[t] = jnp.concatenate(
                [small[t, 0:1, :192], jnp.zeros((1, 192), F32), small[t, 0:1, 192:384]], axis=1
            )
        tidy.append(link.copy(packed, small_out))

    def x_ready():
        x_stay.wait()
        for move in x_moves:
            move.wait_recv()
        tidy.append(link.copy(x_row, x_out))

    def gy_send():
        for k in others:
            gy_moves.append(link.send(gy_in.at[place.ahead[k]], gy_row.at[mine_rows], place.deep[k]))

    def gy_ready():
        for move in gy_moves:
            move.wait_recv()

    spread_out()
    deep_send(1)
    plane_send(0, 0)
    pass_halves()
    deep_send(0)
    plane_send(1, 0)
    plane_pass(0, 0)
    plane_send(1, 3)
    x_ready()
    collect_halves()
    spread_ffn()
    plane_send(2, 0)
    small_collect()
    plane_send(1, 2)
    plane_send(0, 1)
    plane_pass(1, 0)
    deep_send(2)
    plane_send(1, 1)
    plane_send(0, 3)
    small_ready()
    plane_pass(1, 3)
    plane_pass(0, 1)
    core_pass(0, 0)
    load(0, 0)
    core_pass(1, 0)
    plane_pass(1, 2)
    plane_pass(0, 3)
    core_pass(1, 3)
    plane_pass(2, 0)
    plane_send(0, 2)
    deep_send(3)
    core_pass(0, 1)
    qkv_step(0)
    load(0, 1)
    plane_send(2, 1)
    core_pass(0, 3)
    attention(0)
    load(0, 3)
    qkv_step(3)
    plane_send(2, 2)
    load(1, 3)
    gy_send()
    qkv_step(1)
    plane_pass(1, 1)
    plane_pass(0, 2)
    plane_send(2, 3)
    core_pass(1, 2)
    attention(3)
    core_pass(1, 1)
    plane_send(3, 0)
    core_pass(0, 2)
    core_pass(2, 0)
    load(1, 0)
    attention(1)
    plane_pass(2, 3)
    plane_pass(2, 2)
    plane_pass(2, 1)
    load(1, 2)
    plane_send(3, 2)
    load(2, 0)
    load(0, 2)
    qkv_step(2)
    load(1, 1)
    plane_pass(3, 0)
    plane_send(3, 3)
    attention(2)
    plane_send(3, 1)
    core_pass(2, 3)
    out_step()
    load(2, 3)
    core_pass(2, 1)
    up_step(0)
    load(2, 1)
    core_pass(2, 2)
    up_step(3)
    plane_pass(3, 2)
    load(2, 2)
    core_pass(3, 0)
    up_step(1)
    load(3, 0)
    plane_pass(3, 3)
    up_step(2)
    plane_pass(3, 1)
    core_pass(3, 2)
    down_step(0)
    core_pass(3, 3)
    load(3, 2)
    core_pass(3, 1)
    load(3, 3)
    down_step(2)
    gy_ready()
    load(3, 1)
    down_step(3)
    down_step(1)
    end_step()
    for copy in tidy:
        copy.wait()
    link.finish()


def forward_call(master, owners, order_col, labels, flags, x_in, gy_in):
    anywhere = pl.BlockSpec(memory_space=pl.ANY)
    vmem = pl.BlockSpec(memory_space=pltpu.VMEM)
    shape = jax.ShapeDtypeStruct
    outs = [
        ((4, 768, 576), BF),
        ((4, 256, 768), BF),
        ((4, 768, 768), BF),
        ((4, 768, 768), BF),
        ((4, 192, 768), BF),
        ((8, 896), F32),
        ((4, 8, 384), F32),
        ((512, 768), BF),
        ((512, 768), BF),
        ((4, 512, 576), BF),
        ((12, 512, 512), BF),
        ((4, 512, 192), BF),
        ((512, 768), F32),
        ((512, 768), BF),
        ((4, 512, 768), BF),
        ((4, 512, 768), BF),
        ((512, 768), F32),
        ((2, 512, 1), F32),
        ((512, 768), BF),
        ((8, 768), F32),
    ]
    scratch = [
        ((8, 896), F32),
        ((896, 8), F32),
        ((8, 512), F32),
        ((512, 8), F32),
        ((2, 192, 2304), BF),
        ((4, 32, 2304), BF),
        ((4, 64, 2304), BF),
        ((3, 32, 2304), BF),
        ((2, 2, 32, 2304), BF),
        ((2, 32, 2304), BF),
        ((2, 32, 2304), BF),
        ((96, 2304), F32),
        ((96, 576), BF),
        ((32, 768), BF),
        ((96, 768), BF),
        ((96, 768), BF),
        ((8, 384), F32),
        ((3, 8, 384), F32),
        ((8, 384), F32),
        ((4, 8, 384), F32),
        ((4, 1, 2304), F32),
        ((8, 768), F32),
        ((4, 1, 576), F32),
        ((4, 768, 576), BF),
        ((4, 256, 768), BF),
        ((4, 192, 768), BF),
        ((4, 768, 768), BF),
        ((4, 768, 768), BF),
        ((512, 768), BF),
        ((4, 512, 576), BF),
        ((12, 512, 512), BF),
        ((4, 512, 192), BF),
        ((512, 768), F32),
        ((512, 768), F32),
        ((512, 768), BF),
        ((4, 512, 768), BF),
        ((4, 512, 768), BF),
        ((512, 768), F32),
        ((2, 512, 1), F32),
        ((512, 768), BF),
        ((8, 768), F32),
    ]
    return pl.pallas_call(
        forward_kernel,
        out_shape=[shape(*o) for o in outs],
        in_specs=[vmem] * 5 + [anywhere] * 2,
        out_specs=[anywhere] * len(outs),
        scratch_shapes=[pltpu.VMEM(*s) for s in scratch]
        + [
            pltpu.SemaphoreType.DMA((128,)),
            pltpu.SemaphoreType.DMA((128,)),
            pltpu.SemaphoreType.DMA((64,)),
        ],
        compiler_params=pltpu.CompilerParams(
            collective_id=0, has_side_effects=True, vmem_limit_bytes=60 * MIB
        ),
        name="gather_and_forward",
    )(master, owners, order_col, labels, flags, x_in, gy_in)


def backward_kernel(
    flags,
    out_row,
    pool_in,
    gy_in,
    n_two_in,
    inv_in,
    small_in,
    act_in,
    pull_in,
    w_down,
    w_up,
    h_in,
    n_one_in,
    att_in,
    w_out,
    qkv_in,
    prob_in,
    w_qkv,
    x_in,
    blocks,
    small_out,
    out_mine,
    dx_mine,
    pool_out,
    *scratch,
):
    sums, cores, lefts, tops, lefts_two, tops_two, deeps = (scratch[4 * i : 4 * i + 4] for i in range(7))
    (
        ring,
        ring_narrow,
        share,
        share_low,
        small_grad,
        small_land,
        packed,
        small,
        norm,
        gy,
        normed,
        inv,
        act,
        pull,
        v_down,
        v_up,
        h_low,
        att,
        v_out,
        qkv,
        prob,
        v_qkv,
        x_row,
        wide,
        low,
        total,
        d_up,
        d_att,
        d_qkv,
        turned,
        go,
        reds,
        red_up,
        red_qv,
        flag_col,
        send_sems,
        recv_sems,
        local_sems,
    ) = scratch[28:]
    place = Place()
    link = Sender(send_sems, recv_sems, local_sems)
    t_of = place.ahead
    steps = (1, 2, 3, 0)
    got = {}

    def fetch(name, src, dst):
        got[name] = link.copy(src, dst)

    fetch("small", small_in, packed)
    fetch("normed", n_two_in, normed)
    fetch("gy", gy_in, gy)
    fetch("inv", inv_in, inv)

    def load_ffn(i):
        t, slot = t_of[steps[i]], i % 2
        fetch(("act", i), act_in.at[t], act.at[slot])
        fetch(("down", i), w_down.at[t], v_down.at[slot])
        fetch(("pull", i), pull_in.at[t], pull.at[slot])
        fetch(("up", i), w_up.at[t], v_up.at[slot])

    def load_att(i):
        t, slot = t_of[steps[i]], i % 2
        fetch(("prob", i), prob_in.at[pl.ds(3 * t, 3)], prob.at[slot])
        fetch(("qkv", i), w_qkv.at[t], v_qkv.at[slot])

    own_flags = flags[pl.ds(place.t, 1), :].astype(F32)
    flag_col[...] = jnp.transpose(jnp.broadcast_to(own_flags, (8, 512)))
    place.greet()
    t, x, y, c = place.t, place.x, place.y, place.c

    moves, stay = [], []
    stay.append(link.copy(out_row.at[pl.ds(pl.multiple_of(t * 128, 128), 128)], out_mine.at[t]))
    stay.append(link.copy(pool_in, pool_out.at[t]))
    for k in (1, 2, 3):
        part = out_row.at[pl.ds(pl.multiple_of(t_of[k] * 128, 128), 128)]
        moves.append(link.send(part, out_mine.at[t], place.deep[k]))
        moves.append(link.send(pool_in, pool_out.at[t], place.deep[k]))

    core_moves, first, second, third = {}, {}, {}, {}
    ring_open = [None] * 5
    ring_at = [0, 0]

    def chip_row(w, k, yy, xx, half):
        rows = WEIGHTS[w][1]
        at = pl.multiple_of((yy * 2 + xx) * rows + half * (rows // 2), 16)
        return sums[w].at[t_of[k], pl.ds(at, rows // 2)]

    def produce(w, k, make):
        narrow = w == 0
        slot = 3 + ring_at[1] % 2 if narrow else ring_at[0] % 3
        ring_at[narrow] += 1
        if ring_open[slot] is not None:
            link.sent(ring_open[slot])
        cols, rows = WEIGHTS[w]
        away = ring_narrow.at[slot - 3] if narrow else ring.at[slot, pl.ds(0, 4 * rows)]
        away[...] = make(1 - c).astype(BF)
        move = link.send(away, cores[w].at[k], place.core)
        ring_open[slot] = move
        core_moves[w, k] = move
        sums[w][t_of[k]] = make(c).astype(BF)

    def core_add(w, k):
        core_moves[w, k].wait_recv()
        rows = WEIGHTS[w][1]

        @pl.loop(0, 4)
        def _(i):
            at = pl.ds(pl.multiple_of(i * rows, 32), rows)
            sums[w][t_of[k], at, :] += cores[w][k, at, :]

        first[w, k] = []
        for i in (0, 1):
            first[w, k].append(link.send(chip_row(w, k, i, 1 - x, 0), lefts[w].at[k, i], place.right))
            first[w, k].append(link.send(chip_row(w, k, 1 - y, i, 1), tops[w].at[k, i], place.down))

    def add(spot, other):
        spot[...] = spot[...] + other[...]

    def plane_add(w, k):
        for move in first[w, k]:
            move.wait_recv()
        down_part, right_part = chip_row(w, k, 1 - y, x, 0), chip_row(w, k, y, 1 - x, 1)
        add(down_part, lefts[w].at[k, 1 - y])
        add(right_part, tops[w].at[k, 1 - x])
        second[w, k] = [
            link.send(down_part, lefts_two[w].at[k], place.down),
            link.send(right_part, tops_two[w].at[k], place.right),
        ]
        add(chip_row(w, k, y, x, 0), lefts[w].at[k, y])
        add(chip_row(w, k, y, x, 1), tops[w].at[k, x])

    def deep_add(w, k):
        for move in second[w, k]:
            move.wait_recv()
        add(chip_row(w, k, y, x, 0), lefts_two[w].at[k])
        add(chip_row(w, k, y, x, 1), tops_two[w].at[k])
        rows = WEIGHTS[w][1]
        if k:
            spot = pl.ds(pl.multiple_of(place.xy * rows, 16), rows)
            third[w, k] = link.send(sums[w].at[t_of[k], spot], deeps[w].at[k - 1], place.deep[k])

    def end(w):
        rows = WEIGHTS[w][1]
        spot = pl.ds(pl.multiple_of(place.xy * rows, 16), rows)
        whole = sums[w][t, spot, :].astype(F32)
        for k in (1, 2, 3):
            third[w, k].wait_recv()
            whole = whole + deeps[w][k - 1].astype(F32)
        whole = whole.astype(BF)
        if w == 0:
            parts = dot_tn(interleave(96, 4), whole)
            share[64:88, :] = jnp.concatenate([parts[24 * r : 24 * r + 24] for r in range(4)], axis=1)
        elif w == 1:
            parts = dot_tn(interleave_out(), whole)
            for k in range(3):
                share[88:96, 768 * k : 768 * k + 768] = parts[8 * k : 8 * k + 8]
        else:
            at = 0 if w == 2 else 32
            parts = dot_tn(interleave(96, 3), whole)
            for k in range(3):
                share[at : at + 32, 768 * k : 768 * k + 768] = parts[32 * k : 32 * k + 32]

    def column_sum(value):
        return jnp.sum(value, axis=0, keepdims=True)

    def norm_two_back():
        def body(rows):
            grad = gy[rows, :].astype(F32) * flag_col[rows, 0:1]
            n = normed[rows, :]
            dz = norm_back(grad * norm[4:5, :], n, inv[1, rows, :])
            wide[rows, :] = dz
            total[rows, :] = dz
            low[rows, :] = dz.astype(BF)
            reds[4:5, :] += column_sum(grad * n)
            reds[5:6, :] += column_sum(grad)
            reds[1:2, :] += column_sum(dz)

        row_loop(body)

    def lanes(which):
        return pl.ds(pl.multiple_of(which * 384, 128), 384)

    def down_piece(i):
        k, slot = steps[i], i % 2
        got["act", i].wait()
        produce(3, k, lambda which: dot_tn(act[slot, :, lanes(which)], low[...]))

    def act_back(i):
        k, slot = steps[i], i % 2
        got["down", i].wait()
        got["pull", i].wait()

        def body(rows):
            grad = dot_nt(low[rows, :], v_down[slot]) * pull[slot, rows, :].astype(F32)
            red_up[t_of[k]] += column_sum(grad)
            d_up[rows, :] = grad.astype(BF)

        row_loop(body, 256)

    def up_piece(i):
        if i == 0:
            got["h"].wait()
        produce(2, steps[i], lambda which: dot_tn(h_low[:, lanes(which)], d_up[...]))

    def hidden_back(i):
        slot = i % 2
        got["up", i].wait()

        def body(rows):
            total[rows, :] += dot_nt(d_up[rows, :], v_up[slot])

        row_loop(body, 256)
        if i == 1:
            fetch("n_one", n_one_in, normed)

    def norm_one_back():
        got["n_one"].wait()

        def body(rows):
            dh = total[rows, :]
            n = normed[rows, :]
            dz = norm_back(dh * norm[2:3, :], n, inv[0, rows, :])
            total[rows, :] = dz
            low[rows, :] = dz.astype(BF)
            reds[2:3, :] += column_sum(dh * n)
            reds[3:4, :] += column_sum(dh)
            reds[0:1, :] += column_sum(dz)

        row_loop(body)

    def out_piece(i):
        k = steps[i]
        if i == 0:
            got["att"].wait()
            got["wout"].wait()
        go[...] = dot_tn(att[t_of[k]], low[...])

        def make(which):
            part = go[pl.ds(pl.multiple_of(which * 96, 96), 96), :]
            pad = jnp.zeros((8, 768), F32)
            parts = []
            for j in range(4):
                parts += [part[24 * j : 24 * j + 24], pad]
            return jnp.concatenate(parts, axis=0)

        produce(1, k, make)

        def body(rows):
            d_att[rows, :] = dot_nt(low[rows, :], v_out[t_of[k]]).astype(BF)

        row_loop(body, 256)

    def attention_back(i):
        k, slot = steps[i], i % 2
        tk = t_of[k]
        if i == 0:
            got["qkvs"].wait()
        got["prob", i].wait()
        turned[...] = jnp.zeros_like(turned)

        def body(rows):
            d_queries = []
            for j in range(3):
                at = 64 * j
                grad = d_att[rows, at : at + 64]
                weight_low = prob[slot, j, rows, :]
                weight = weight_low.astype(F32)
                d_prob = dot_nt(grad, qkv[tk, :, 384 + at : 448 + at]) * weight
                inner = jnp.sum(d_prob, axis=1, keepdims=True)
                d_scores = (d_prob - weight * inner).astype(BF)
                d_queries.append(dot_f32(d_scores, qkv[tk, :, 192 + at : 256 + at]))
                turned[at : at + 64, :] += dot_tn(qkv[tk, rows, at : at + 64], d_scores)
                turned[192 + at : 256 + at, :] += dot_tn(grad, weight_low)
            dq = jnp.concatenate(d_queries, axis=1) * 0.125
            red_qv[tk, :, :192] += column_sum(dq)
            d_qkv[rows, :192] = dq.astype(BF)

        row_loop(body, 256)
        dk = jnp.transpose(turned[:192, :]) * 0.125
        dv = jnp.transpose(turned[192:, :])
        red_qv[tk, :, 192:] += column_sum(dv)
        d_qkv[:, 192:] = jnp.concatenate([dk, dv], axis=1).astype(BF)

    def qkv_piece(i):
        k, slot = steps[i], i % 2
        if i == 0:
            got["x"].wait()
        produce(0, k, lambda which: dot_tn(x_row[:, lanes(which)], d_qkv[...]))
        got["qkv", i].wait()

        def body(rows):
            total[rows, :] += dot_nt(d_qkv[rows, :], v_qkv[slot])

        row_loop(body, 256)

    sent, passed, across = {}, {}, {}

    def share_send(lo, hi):
        share_low[lo:hi, :] = share[lo:hi, :].astype(BF)
        mine = c * 4 + place.xy
        rows = pl.ds(lo, hi - lo)
        sent[lo] = (
            link.copy(share_low.at[rows], blocks.at[mine, rows]),
            link.send(share_low.at[rows], blocks.at[mine, rows], place.right),
            link.send(share_low.at[rows], blocks.at[mine, rows], place.down),
        )

    def share_pass(lo, hi):
        half = (hi - lo) // 2
        sent[lo][1].wait_recv()
        sent[lo][2].wait_recv()
        one = blocks.at[c * 4 + place.right[0] // 2, pl.ds(lo, half)]
        two = blocks.at[c * 4 + place.down[0] // 2, pl.ds(lo + half, half)]
        passed[lo] = link.send(one, one, place.down), link.send(two, two, place.right)

    def share_across(lo, hi):
        sent[lo][0].wait()
        passed[lo][0].wait_recv()
        passed[lo][1].wait_recv()
        spot = blocks.at[pl.ds(c * 4, 4), pl.ds(lo, hi - lo)]
        across[lo] = link.send(spot, spot, place.core)

    def share_ready(lo):
        across[lo].wait_recv()

    got["small"].wait()
    unpack_small(packed, small)
    norm_vectors(small, norm)
    reds[...] = jnp.zeros_like(reds)
    red_up[...] = jnp.zeros_like(red_up)
    red_qv[...] = jnp.zeros_like(red_qv)
    small_grad[...] = jnp.zeros_like(small_grad)
    for name in ("normed", "gy", "inv"):
        got[name].wait()
    def load_rest():
        fetch("h", h_in, h_low)
        fetch("att", att_in, att)
        fetch("wout", w_out, v_out)
        fetch("qkvs", qkv_in, qkv)
        fetch("x", x_in, x_row)

    small_state = {}

    def small_send():
        def dx_body(rows):
            low[rows, :] = total[rows, :].astype(BF)

        row_loop(dx_body)
        for q in range(4):
            at = slice(192 * q, 192 * q + 192)
            line = jnp.concatenate(
                [red_qv[q], red_up[q]] + [reds[i : i + 1, at] for i in range(6)], axis=1
            )
            for i in range(6):
                small_grad[q, i : i + 1, :] = line[:, 384 * i : 384 * i + 384]
        small_state["keep"] = link.copy(small_grad.at[t], small_land.at[6])
        small_state["deep"] = [
            link.send(small_grad.at[t_of[k]], small_land.at[k - 1], place.deep[k]) for k in (1, 2, 3)
        ]

    def dx_send():
        own_rows = pl.ds(pl.multiple_of(t * 128, 128), 128)
        stay.append(link.copy(low.at[own_rows], dx_mine.at[t]))
        for k in (1, 2, 3):
            part = low.at[pl.ds(pl.multiple_of(t_of[k] * 128, 128), 128)]
            moves.append(link.send(part, dx_mine.at[t], place.deep[k]))

    def small_core():
        small_state["keep"].wait()
        for move in small_state["deep"]:
            move.wait_recv()
        small_land[7] = small_land[6] + small_land[0] + small_land[1] + small_land[2]
        small_state["core"] = link.send(small_land.at[7], small_land.at[3], place.core)

    def small_right():
        small_state["core"].wait_recv()
        small_land[8] = small_land[7] + small_land[3]
        small_state["right"] = link.send(small_land.at[8], small_land.at[4], place.right)

    def small_down():
        small_state["right"].wait_recv()
        small_land[9] = small_land[8] + small_land[4]
        small_state["down"] = link.send(small_land.at[9], small_land.at[5], place.down)

    def small_end():
        small_state["down"].wait_recv()
        small_out[...] = small_land[9] + small_land[5]

    load_ffn(0)
    norm_two_back()
    load_ffn(1)
    down_piece(0)
    load_rest()
    act_back(0)
    core_add(3, 1)
    load_att(0)
    load_att(1)
    up_piece(0)
    hidden_back(0)
    load_ffn(2)
    core_add(2, 1)
    down_piece(1)
    act_back(1)
    core_add(3, 2)
    up_piece(1)
    hidden_back(1)
    core_add(2, 2)
    load_ffn(3)
    down_piece(2)
    act_back(2)
    plane_add(3, 2)
    plane_add(3, 1)
    up_piece(2)
    hidden_back(2)
    down_piece(3)
    plane_add(2, 2)
    core_add(2, 3)
    act_back(3)
    plane_add(2, 1)
    up_piece(3)
    deep_add(3, 2)
    hidden_back(3)
    deep_add(2, 2)
    norm_one_back()
    core_add(3, 3)
    out_piece(0)
    core_add(2, 0)
    attention_back(0)
    deep_add(2, 1)
    qkv_piece(0)
    plane_add(2, 3)
    load_att(2)
    core_add(0, 1)
    deep_add(3, 1)
    out_piece(1)
    attention_back(1)
    plane_add(3, 3)
    core_add(1, 2)
    plane_add(2, 0)
    deep_add(2, 3)
    qkv_piece(1)
    load_att(3)
    out_piece(2)
    plane_add(0, 1)
    attention_back(2)
    core_add(0, 2)
    deep_add(3, 3)
    core_add(1, 1)
    qkv_piece(2)
    deep_add(0, 1)
    out_piece(3)
    plane_add(1, 2)
    core_add(1, 3)
    core_add(0, 3)
    attention_back(3)
    deep_add(1, 2)
    plane_add(0, 2)
    plane_add(1, 3)
    core_add(1, 0)
    plane_add(1, 1)
    plane_add(0, 3)
    core_add(3, 0)
    deep_add(0, 2)
    qkv_piece(3)
    small_send()
    core_add(0, 0)
    deep_add(0, 3)
    deep_add(1, 1)
    deep_add(1, 3)
    plane_add(3, 0)
    small_core()
    deep_add(2, 0)
    end(2)
    plane_add(1, 0)
    dx_send()
    plane_add(0, 0)
    small_right()
    deep_add(3, 0)
    end(3)
    share_send(0, 64)
    deep_add(0, 0)
    end(0)
    deep_add(1, 0)
    end(1)
    share_send(64, 96)
    share_pass(0, 64)
    small_down()
    share_pass(64, 96)
    share_across(0, 64)
    share_across(64, 96)
    share_ready(0)
    share_ready(64)
    small_end()
    for move in moves:
        move.wait_recv()
    for copy in stay:
        copy.wait()
    link.finish()


def backward_call(*args):
    anywhere = pl.BlockSpec(memory_space=pl.ANY)
    vmem = pl.BlockSpec(memory_space=pltpu.VMEM)
    shape = jax.ShapeDtypeStruct
    sums = [((4, 4 * rows, cols), BF) for cols, rows in WEIGHTS]
    halves = [((4, 2, rows // 2, cols), BF) for cols, rows in WEIGHTS]
    singles = [((4, rows // 2, cols), BF) for cols, rows in WEIGHTS]
    deeps = [((3, rows, cols), BF) for cols, rows in WEIGHTS]
    rest = [
        ((3, 384, 768), BF),
        ((2, 384, 576), BF),
        ((96, 2304), F32),
        ((96, 2304), BF),
        ((4, 8, 384), F32),
        ((11, 8, 384), F32),
        ((4, 8, 384), F32),
        ((4, 1, 2304), F32),
        ((8, 768), F32),
        ((512, 768), BF),
        ((512, 768), F32),
        ((2, 512, 1), F32),
        ((2, 512, 768), BF),
        ((2, 512, 768), BF),
        ((2, 768, 768), BF),
        ((2, 768, 768), BF),
        ((512, 768), BF),
        ((4, 512, 192), BF),
        ((4, 192, 768), BF),
        ((4, 512, 576), BF),
        ((2, 3, 512, 512), BF),
        ((2, 768, 576), BF),
        ((512, 768), BF),
        ((512, 768), F32),
        ((512, 768), BF),
        ((512, 768), F32),
        ((512, 768), BF),
        ((512, 192), BF),
        ((512, 576), BF),
        ((384, 512), F32),
        ((192, 768), F32),
        ((8, 768), F32),
        ((4, 1, 768), F32),
        ((4, 1, 384), F32),
        ((512, 8), F32),
    ]
    scratch = sums + sums + halves + halves + singles + singles + deeps + rest
    return pl.pallas_call(
        backward_kernel,
        out_shape=[
            shape((8, 96, 2304), BF),
            shape((8, 384), F32),
            shape((4, 128, 768), BF),
            shape((4, 128, 768), BF),
            shape((4, 8, 768), F32),
        ],
        in_specs=[vmem] + [anywhere] * 18,
        out_specs=[anywhere, vmem, anywhere, anywhere, anywhere],
        scratch_shapes=[pltpu.VMEM(*s) for s in scratch]
        + [
            pltpu.SemaphoreType.DMA((160,)),
            pltpu.SemaphoreType.DMA((160,)),
            pltpu.SemaphoreType.DMA((64,)),
        ],
        compiler_params=pltpu.CompilerParams(
            collective_id=1, has_side_effects=True, vmem_limit_bytes=62 * MIB
        ),
        name="backward_and_reduce",
    )(*args)


def finish_kernel(
    slot_row,
    blocks,
    small,
    pool,
    master,
    first,
    second,
    out_mine,
    dx_mine,
    new_master,
    new_first,
    new_second,
    layer_out,
    input_grad,
    pooled,
    norm_grads,
):
    step = pl.program_id(0)
    rows = master.shape[0]
    t = lax.axis_index("tensor")
    start = lax.axis_index("dp") * (rows * pl.num_programs(0)) + step * rows
    wanted = (lax.broadcasted_iota(jnp.int32, (rows, 1), 0) + start).astype(F32)
    match = slot_row[0:1, :768] == wanted
    gradient = dot_f32(jnp.where(match, 1.0, 0.0).astype(BF), blocks[...])
    is_small = slot_row[0:1, 768:769] == wanted
    small_line = jnp.concatenate([small[i : i + 1, :] for i in range(6)], axis=1)
    gradient = jnp.where(is_small, small_line, gradient)

    at = lax.broadcasted_iota(jnp.int32, (1, 768), 1) % 96
    rates = jnp.where(
        at < 32,
        MODEL_WIDTH ** (-0.5),
        jnp.where(
            at < 64,
            FF ** (-0.5),
            jnp.where(at < 88, MODEL_WIDTH ** (-0.5), 4.0 * MODEL_WIDTH ** (-0.5)),
        ),
    ).astype(F32)
    rate = jnp.sum(jnp.where(match, rates, 0.0), axis=1, keepdims=True)
    filled = (rate > 0.0) | is_small
    offset = lax.broadcasted_iota(jnp.int32, (1, small_line.shape[1]), 1) - 1152
    gain = ((offset >= 384) & (offset < 576)) | ((offset >= 768) & (offset < 960))
    small_rate = jnp.where(gain, 0.2, 0.1).astype(F32)
    step_rate = jnp.where(is_small, small_rate, rate)
    decay_on = jnp.where(is_small, 0.0, 1.0)
    new_master[...], new_first[...], new_second[...] = adamw(
        gradient, first[...], second[...], master[...], step_rate, decay_on, filled
    )
    for src, dst in ((out_mine, layer_out), (dx_mine, input_grad)):
        for row in range(4):
            dst[:, row, :] = src[row].astype(F32)

    @pl.when(step == 0)
    def _():
        total = jnp.zeros((4, 8, 192), F32)
        for q in range(4):
            total = total + jnp.where(t == q, pool[:, :, 192 * q : 192 * q + 192], 0.0)
        pooled[...] = total
        norm_grads[...] = jnp.concatenate(
            [small_line[:, 1152 + 192 * i : 1344 + 192 * i] for i in range(6)], axis=0
        )


def finish_call(slot_row, blocks, small, pool, master, first, second, out_mine, dx_mine):
    steps = 4
    slots, block_len = master.shape
    shape = jax.ShapeDtypeStruct

    def whole(*dims):
        return pl.BlockSpec(dims, lambda i: (0,) * len(dims))

    state = pl.BlockSpec((slots // steps, block_len), lambda i: (i, 0))
    token_in = pl.BlockSpec((4, 128 // steps, 768), lambda i: (0, i, 0))
    token_out = pl.BlockSpec((128 // steps, 4, 768), lambda i: (i, 0, 0))
    return pl.pallas_call(
        finish_kernel,
        grid=(steps,),
        out_shape=[shape((slots, block_len), F32)] * 3
        + [shape((128, 4, 768), F32)] * 2
        + [shape((4, 8, 192), F32), shape((6, 192), F32)],
        in_specs=[whole(8, 896), whole(768, block_len), whole(8, 384), whole(4, 8, 768)]
        + [state] * 3
        + [token_in] * 2,
        out_specs=[state] * 3 + [token_out] * 2 + [whole(4, 8, 192), whole(6, 192)],
        compiler_params=pltpu.CompilerParams(vmem_limit_bytes=62 * MIB),
        name="owners_update",
    )(slot_row, blocks, small, pool, master, first, second, out_mine, dx_mine)


def share_order():
    order = []
    for core in range(2):
        for chip in range(4):
            for base, count in ((0, 32), (256, 32), (512, 24), (704, 8)):
                at = base + (core * 4 + chip) * count
                order += list(range(at, at + count))
    return np.array(order + [768] + [4096] * 127, np.int32)


def local_rows(
    layer_input_rows,
    sentence_index_row,
    padding_mask,
    output_gradient,
    owner_rank,
    master_state,
    first_moment,
    second_moment,
):
    block_len = master_state.shape[2]
    order = share_order()
    (
        w_qkv,
        _,
        w_up,
        w_down,
        w_out,
        slot_row,
        small_all,
        x_row,
        gy_row,
        qkv,
        prob_low,
        attended,
        normed_one,
        h_low,
        act,
        pull,
        normed_two,
        inverse,
        out_row,
        pool_mean,
    ) = forward_call(
        master_state[0],
        owner_rank[None],
        jnp.asarray(order[:, None]),
        sentence_index_row,
        padding_mask,
        jnp.transpose(layer_input_rows, (1, 0, 2)),
        jnp.transpose(output_gradient, (1, 0, 2)),
    )
    blocks, small_sum, out_mine, dx_mine, pool_all = backward_call(
        padding_mask,
        out_row,
        pool_mean,
        gy_row,
        normed_two,
        inverse,
        small_all,
        act,
        pull,
        w_down,
        w_up,
        h_low,
        normed_one,
        attended,
        w_out,
        qkv,
        prob_low,
        w_qkv,
        x_row,
    )
    new_master, new_first, new_second, layer_out, input_grad, pooled, norm_grads = finish_call(
        slot_row,
        blocks.reshape(768, block_len),
        small_sum,
        pool_all,
        master_state[0],
        first_moment[0],
        second_moment[0],
        out_mine,
        dx_mine,
    )
    return (
        layer_out,
        pooled,
        input_grad,
        new_master[None],
        new_first[None],
        new_second[None],
        norm_grads,
    )


def solution(mesh):
    in_specs = (
        P("tensor", "dp", None),
        P("dp", None),
        P("dp", None),
        P("tensor", "dp", None),
        P(),
        P("tensor", "dp", None),
        P("tensor", "dp", None),
        P("tensor", "dp", None),
    )
    out_specs = (
        P("tensor", "dp", None),
        P("dp", None, "tensor"),
        P("tensor", "dp", None),
        P("tensor", "dp", None),
        P("tensor", "dp", None),
        P("tensor", "dp", None),
        P(None, "tensor"),
    )
    plain = mesh.shape["dp"] != 8 or mesh.shape["tensor"] != 4
    body = local_general if plain else local_rows
    return jax.shard_map(body, mesh=mesh, in_specs=in_specs, out_specs=out_specs, check_vma=False)
```

```python
import jax
import numpy as np
import jax.numpy as jnp
from jax import lax
from jax.experimental import pallas as pl
from jax.experimental.pallas import tpu as pltpu
from jax.sharding import PartitionSpec as P

MODEL_WIDTH = 768
HEAD_DIM = 64
FF = 3072
SMAX = 8
STEP = 10


NORM_EPS = 1e-05
ADAM_EPS = 1e-08
BETA_ONE = 0.9
BETA_TWO = 0.999
DECAY_RATE = 0.01
MASKED = -1e30
exact_precision = lax.Precision.HIGHEST


def slot_tables(owner_rank, per_owner):
    ordinal = jnp.arange(owner_rank.shape[0], dtype=jnp.int32)
    same_owner = owner_rank[:, None] == owner_rank[None, :]
    earlier = ordinal[None, :] < ordinal[:, None]
    ranking = jnp.sum((same_owner & earlier).astype(jnp.int32), axis=1)
    return owner_rank * per_owner + ranking


def slot_blocks(slot_of, wanted):
    matches = slot_of[None, :] == wanted[:, None]
    filled = jnp.any(matches, axis=1)
    ordinal = jnp.arange(slot_of.shape[0], dtype=jnp.int32)
    block_of = jnp.sum(jnp.where(matches, ordinal[None, :], 0), axis=1)
    return (block_of, filled)


def step_rates(token_position, width, hidden, tensor_size):
    width_loc = width // tensor_size
    ffn_loc = hidden // tensor_size
    end_up = width * ffn_loc
    end_down = end_up + ffn_loc * width
    end_qkv = end_down + width * 3 * width_loc
    end_out = end_qkv + width_loc * width
    offset = token_position - end_out
    first_gain = (offset >= 4 * width_loc + ffn_loc) & (offset < 5 * width_loc + ffn_loc)
    second_gain = (offset >= 6 * width_loc + ffn_loc) & (offset < 7 * width_loc + ffn_loc)
    small_rate = jnp.where(first_gain | second_gain, 0.2, 0.1)
    step_rate = jnp.where(
        token_position < end_up,
        width ** (-0.5),
        jnp.where(
            token_position < end_down,
            hidden ** (-0.5),
            jnp.where(
                token_position < end_qkv,
                width ** (-0.5),
                jnp.where(token_position < end_out, 4.0 * width ** (-0.5), small_rate),
            ),
        ),
    )
    decay_on = (token_position < end_out).astype(jnp.float32)
    return (step_rate.astype(jnp.float32), decay_on)


def adamw(gradient, moment, square, weight, step_rate, decay_on, filled):
    new_moment = BETA_ONE * moment + (1.0 - BETA_ONE) * gradient
    new_square = BETA_TWO * square + (1.0 - BETA_TWO) * gradient * gradient
    unbiased = new_moment / (1.0 - BETA_ONE**STEP)
    divisor = jnp.sqrt(new_square / (1.0 - BETA_TWO**STEP)) + ADAM_EPS
    new_weight = weight - step_rate * (unbiased / divisor + DECAY_RATE * decay_on * weight)
    zeroed = jnp.zeros_like(weight)
    return (
        jnp.where(filled, new_weight, zeroed),
        jnp.where(filled, new_moment, zeroed),
        jnp.where(filled, new_square, zeroed),
    )


def normalize(values):
    centred = values - jnp.mean(values, axis=-1, keepdims=True)
    inv_dev = lax.rsqrt(jnp.mean(centred * centred, axis=-1, keepdims=True) + NORM_EPS)
    return (centred * inv_dev, inv_dev)


def norm_back(grad_scaled, normed, inv_dev):
    first_mean = jnp.mean(grad_scaled, axis=-1, keepdims=True)
    second_mean = jnp.mean(grad_scaled * normed, axis=-1, keepdims=True)
    return inv_dev * (grad_scaled - first_mean - normed * second_mean)


def allowed_pairs(sentence_labels, real_token_flags):
    row_len = sentence_labels.shape[-1]
    same_sent = sentence_labels[:, :, None] == sentence_labels[:, None, :]
    live = (real_token_flags[:, :, None] == 1) & (real_token_flags[:, None, :] == 1)
    diagonal = jnp.eye(row_len, dtype=bool)[None]
    return same_sent & live | diagonal


def masked_scores(queries, key_rows, allowed, scaling):
    scores = (
        jnp.einsum("qshe,kshe->shqk", queries, key_rows, preferred_element_type=jnp.float32)
        * scaling
    )
    return jnp.where(allowed[:, None], scores, MASKED)


def split_flat(flat_all, width_loc, ffn_loc):
    end_up = MODEL_WIDTH * ffn_loc
    end_down = end_up + ffn_loc * MODEL_WIDTH
    end_qkv = end_down + MODEL_WIDTH * 3 * width_loc
    end_out = end_qkv + width_loc * MODEL_WIDTH
    return (
        flat_all[:end_up].reshape(MODEL_WIDTH, ffn_loc),
        flat_all[end_up:end_down].reshape(ffn_loc, MODEL_WIDTH),
        flat_all[end_down:end_qkv].reshape(MODEL_WIDTH, 3 * width_loc),
        flat_all[end_qkv:end_out].reshape(width_loc, MODEL_WIDTH),
        flat_all[end_out:],
    )


def local_general(
    layer_input_rows,
    sentence_index_row,
    padding_mask,
    output_gradient,
    owner_rank,
    master_state,
    first_moment,
    second_moment,
):
    tensor_size = lax.axis_size("tensor")
    tensor_at = lax.axis_index("tensor")
    data_size = lax.axis_size("dp")
    data_at = lax.axis_index("dp")
    width_loc = MODEL_WIDTH // tensor_size
    ffn_loc = FF // tensor_size
    heads_loc = width_loc // HEAD_DIM
    quarter = layer_input_rows.shape[0]
    seq_count = layer_input_rows.shape[1]
    row_len = quarter * tensor_size
    per_owner = master_state.shape[1]
    block_len = master_state.shape[2]
    nblocks = owner_rank.shape[0]
    slot_of = slot_tables(owner_rank, per_owner)
    gathered = lax.all_gather(master_state.astype(jnp.bfloat16), "dp", axis=1, tiled=True)[0]
    flat_weights = gathered[slot_of].reshape(nblocks * block_len)
    up_weight, down_weight, w_qkv, w_out, small_part = split_flat(flat_weights, width_loc, ffn_loc)
    bias_q = small_part[:width_loc].astype(jnp.float32)
    bias_v = small_part[width_loc : 2 * width_loc].astype(jnp.float32)
    expand_bias = small_part[2 * width_loc : 2 * width_loc + ffn_loc].astype(jnp.float32)
    norm_parts = small_part[2 * width_loc + ffn_loc :].reshape(6, width_loc)
    full_rows, norm_whole = (
        lax.all_gather(layer_input_rows, "tensor", axis=0, tiled=True),
        lax.all_gather(norm_parts, "tensor", axis=1, tiled=True),
    )
    norm_all = norm_whole.astype(jnp.float32)
    bias_out, bias_down = (norm_all[0], norm_all[1])
    gain_one, shift_one, gain_two, shift_two = (norm_all[2], norm_all[3], norm_all[4], norm_all[5])
    qkv_lin = jnp.einsum("lsd,de->lse", full_rows, w_qkv, preferred_element_type=jnp.float32)
    bias_qkv = jnp.concatenate([bias_q, jnp.zeros((width_loc,), jnp.float32), bias_v])
    qkv = (qkv_lin + bias_qkv).astype(jnp.bfloat16)
    queries = qkv[:, :, :width_loc].reshape(row_len, seq_count, heads_loc, HEAD_DIM)
    key_rows = qkv[:, :, width_loc : 2 * width_loc].reshape(row_len, seq_count, heads_loc, HEAD_DIM)
    values = qkv[:, :, 2 * width_loc :].reshape(row_len, seq_count, heads_loc, HEAD_DIM)
    scaling = HEAD_DIM ** (-0.5)
    allowed = allowed_pairs(sentence_index_row, padding_mask)
    scores = masked_scores(queries, key_rows, allowed, scaling)
    row_peak = jnp.max(scores, axis=-1, keepdims=True)
    log_total = row_peak + jnp.log(jnp.sum(jnp.exp(scores - row_peak), axis=-1, keepdims=True))
    prob_low = jnp.exp(scores - log_total).astype(jnp.bfloat16)
    attended = jnp.einsum("shqk,kshe->qshe", prob_low, values, preferred_element_type=jnp.float32)
    attended = attended.astype(jnp.bfloat16).reshape(row_len, seq_count, width_loc)
    portion_rows = attended
    attn_rows = lax.psum_scatter(
        jnp.einsum("lse,ed->lsd", portion_rows, w_out, preferred_element_type=jnp.float32).astype(
            jnp.bfloat16
        ),
        "tensor",
        scatter_dimension=0,
        tiled=True,
    ).astype(jnp.float32)
    z_one = layer_input_rows.astype(jnp.float32) + attn_rows + bias_out
    normed_one, inv_one = normalize(z_one)
    h_mine = normed_one * gain_one + shift_one
    hidden_narrow_whole = lax.all_gather(h_mine.astype(jnp.bfloat16), "tensor", axis=0, tiled=True)
    up_pre = (
        jnp.einsum(
            "wer,rb->web", hidden_narrow_whole, up_weight, preferred_element_type=jnp.float32
        )
        + expand_bias
    )
    activation_narrow = jax.nn.gelu(up_pre, approximate=False).astype(jnp.bfloat16)
    portion_rows = activation_narrow
    down_rows = lax.psum_scatter(
        jnp.einsum(
            "aij,jb->aib", portion_rows, down_weight, preferred_element_type=jnp.float32
        ).astype(jnp.bfloat16),
        "tensor",
        scatter_dimension=0,
        tiled=True,
    ).astype(jnp.float32)
    z_two = h_mine + down_rows + bias_down
    normed_two, inv_two = normalize(z_two)
    layer_out = normed_two * gain_two + shift_two
    seg_mine = lax.dynamic_slice_in_dim(sentence_index_row, tensor_at * quarter, quarter, 1)
    valid_mine = lax.dynamic_slice_in_dim(padding_mask, tensor_at * quarter, quarter, 1)
    sent_ids = jnp.arange(SMAX, dtype=jnp.int32)
    onehot_mine = (
        (seg_mine[:, :, None] == sent_ids[None, None, :]) & (valid_mine[:, :, None] == 1)
    ).astype(jnp.float32)
    pool_part = jnp.einsum("slc,lsd->scd", onehot_mine, layer_out, precision=exact_precision)
    onehot_full = (
        (sentence_index_row[:, :, None] == sent_ids[None, None, :])
        & (padding_mask[:, :, None] == 1)
    ).astype(jnp.float32)
    counts = jnp.sum(onehot_full, axis=1)
    grad_out = output_gradient.astype(jnp.float32) * valid_mine.T[:, :, None].astype(jnp.float32)
    d_gain_two = jnp.sum(grad_out * normed_two, axis=(0, 1))
    d_shift_two = jnp.sum(grad_out, axis=(0, 1))
    dz_two = norm_back(grad_out * gain_two, normed_two, inv_two)
    d_bias_down = jnp.sum(dz_two, axis=(0, 1))
    second_sum_gradient_wide = lax.all_gather(
        dz_two.astype(jnp.bfloat16), "tensor", axis=0, tiled=True
    )
    down_weight_gradient = jnp.einsum(
        "ipo,ipr->or",
        activation_narrow,
        second_sum_gradient_wide,
        preferred_element_type=jnp.float32,
    )
    activation_gradient = jnp.einsum(
        "ugp,jp->ugj", second_sum_gradient_wide, down_weight, preferred_element_type=jnp.float32
    )
    gelu_pull = jax.vjp(lambda pre_act: jax.nn.gelu(pre_act, approximate=False), up_pre)[1]
    d_up = gelu_pull(activation_gradient)[0]
    d_bias_up = jnp.sum(d_up, axis=(0, 1))
    expand_gradient_narrow = d_up.astype(jnp.bfloat16)
    up_weight_gradient = jnp.einsum(
        "iux,iuy->xy",
        hidden_narrow_whole,
        expand_gradient_narrow,
        preferred_element_type=jnp.float32,
    )
    portion_rows = expand_gradient_narrow
    dh_rows = lax.psum_scatter(
        jnp.einsum(
            "uih,vh->uiv", portion_rows, up_weight, preferred_element_type=jnp.float32
        ).astype(jnp.bfloat16),
        "tensor",
        scatter_dimension=0,
        tiled=True,
    ).astype(jnp.float32)
    dh_mine = dz_two + dh_rows
    d_gain_one = jnp.sum(dh_mine * normed_one, axis=(0, 1))
    d_shift_one = jnp.sum(dh_mine, axis=(0, 1))
    dz_one = norm_back(dh_mine * gain_one, normed_one, inv_one)
    d_bias_out = jnp.sum(dz_one, axis=(0, 1))
    dz_one_full = lax.all_gather(dz_one.astype(jnp.bfloat16), "tensor", axis=0, tiled=True)
    d_w_out = jnp.einsum("lse,lsd->ed", attended, dz_one_full, preferred_element_type=jnp.float32)
    d_attended = jnp.einsum("lsd,ed->lse", dz_one_full, w_out, preferred_element_type=jnp.float32)
    d_attended = d_attended.astype(jnp.bfloat16).reshape(row_len, seq_count, heads_loc, HEAD_DIM)
    scores_again = masked_scores(queries, key_rows, allowed, scaling)
    attn_prob = jnp.exp(scores_again - log_total)
    prob_again = attn_prob.astype(jnp.bfloat16)
    d_prob = jnp.einsum("qshe,kshe->shqk", d_attended, values, preferred_element_type=jnp.float32)
    d_values = jnp.einsum(
        "shqk,qshe->kshe", prob_again, d_attended, preferred_element_type=jnp.float32
    )
    inner = jnp.sum(d_prob * attn_prob, axis=-1, keepdims=True)
    d_scores = (attn_prob * (d_prob - inner)).astype(jnp.bfloat16)
    d_queries = (
        jnp.einsum("shqk,kshe->qshe", d_scores, key_rows, preferred_element_type=jnp.float32)
        * scaling
    )
    d_keys = (
        jnp.einsum("shqk,qshe->kshe", d_scores, queries, preferred_element_type=jnp.float32)
        * scaling
    )
    d_bias_q = jnp.sum(d_queries, axis=(0, 1)).reshape(width_loc)
    d_bias_v = jnp.sum(d_values, axis=(0, 1)).reshape(width_loc)
    d_qkv_low = jnp.concatenate(
        [
            d_queries.reshape(row_len, seq_count, width_loc),
            d_keys.reshape(row_len, seq_count, width_loc),
            d_values.reshape(row_len, seq_count, width_loc),
        ],
        axis=2,
    ).astype(jnp.bfloat16)
    d_w_qkv = jnp.einsum("lsd,lse->de", full_rows, d_qkv_low, preferred_element_type=jnp.float32)
    portion_rows = d_qkv_low
    dx_rows = lax.psum_scatter(
        jnp.einsum("lse,de->lsd", portion_rows, w_qkv, preferred_element_type=jnp.float32).astype(
            jnp.bfloat16
        ),
        "tensor",
        scatter_dimension=0,
        tiled=True,
    ).astype(jnp.float32)
    input_grad = dz_one + dx_rows
    shared_grads = jnp.stack(
        [d_bias_out, d_bias_down, d_gain_one, d_shift_one, d_gain_two, d_shift_two]
    )[None]
    pool_sum, shared_sum = (
        lax.psum_scatter(
            pool_part.astype(jnp.bfloat16), "tensor", scatter_dimension=2, tiled=True
        ).astype(jnp.float32),
        lax.psum_scatter(
            shared_grads.astype(jnp.bfloat16), "tensor", scatter_dimension=2, tiled=True
        ).astype(jnp.float32),
    )
    pooled_mean = pool_sum / jnp.maximum(counts, 1.0)[:, :, None]
    flat_grads = jnp.concatenate(
        [
            up_weight_gradient.reshape(-1),
            down_weight_gradient.reshape(-1),
            d_w_qkv.reshape(-1),
            d_w_out.reshape(-1),
            d_bias_q,
            d_bias_v,
            d_bias_up,
            shared_sum.reshape(-1),
        ]
    )
    grad_blocks = flat_grads.reshape(nblocks, block_len)
    wanted = data_at * per_owner + jnp.arange(per_owner, dtype=jnp.int32)
    block_of, filled = slot_blocks(slot_of, wanted)
    slot_grads = (
        jnp.zeros((data_size * per_owner, block_len), jnp.float32).at[slot_of].set(grad_blocks)
    )
    owned_grads = lax.psum_scatter(slot_grads, "dp", scatter_dimension=0, tiled=True)
    norm_grads = lax.psum(shared_sum[0], "dp")
    token_position = block_of[:, None] * block_len + jnp.arange(block_len, dtype=jnp.int32)[None, :]
    step_rate, decay_on = step_rates(token_position, MODEL_WIDTH, FF, tensor_size)
    new_master, new_first, new_second = adamw(
        owned_grads,
        first_moment[0],
        second_moment[0],
        master_state[0],
        step_rate,
        decay_on,
        filled[:, None],
    )
    return (
        layer_out,
        pooled_mean,
        input_grad,
        new_master[None],
        new_first[None],
        new_second[None],
        norm_grads,
    )


MESH = pl.DeviceIdType.MESH
BF = jnp.bfloat16
F32 = jnp.float32
WEIGHTS = ((576, 96), (768, 32), (768, 96), (768, 96))
MIB = 2**20


class Place:
    def __init__(self):
        d = lax.axis_index("dp")
        self.t = lax.axis_index("tensor")
        self.c = d % 2
        self.x = (d // 2) % 2
        self.y = d // 4
        self.xy = d // 2
        self.core = (d + 1 - 2 * self.c, self.t)
        self.right = (d + 2 - 4 * self.x, self.t)
        self.down = (d + 4 - 8 * self.y, self.t)
        self.diag = (d + 6 - 4 * self.x - 8 * self.y, self.t)
        self.deep = [None] + [(d, (self.t + k) % 4) for k in (1, 2, 3)]
        self.ahead = [(self.t + k) % 4 for k in range(4)]
        self.behind = [(self.t + 4 - k) % 4 for k in range(4)]

    def hail(self):
        peers = [self.core, self.right, self.down, self.diag] + self.deep[1:]
        for peer in peers:
            pl.semaphore_signal(
                pltpu.get_barrier_semaphore(), inc=1, device_id=peer, device_id_type=MESH
            )

    def meet(self):
        pl.semaphore_wait(pltpu.get_barrier_semaphore(), 7)


class Sender:
    def __init__(self, send_sems, recv_sems, local_sems):
        self.sems = (send_sems, recv_sems, local_sems)
        self.used = 0
        self.used_local = 0
        self.open = []

    def send(self, src, dst, peer):
        i = self.used
        self.used += 1
        copy = pltpu.make_async_remote_copy(
            src_ref=src,
            dst_ref=dst,
            send_sem=self.sems[0].at[i],
            recv_sem=self.sems[1].at[i],
            device_id=peer,
            device_id_type=MESH,
        )
        copy.start()
        self.open.append(copy)
        return copy

    def copy(self, src, dst):
        i = self.used_local
        self.used_local += 1
        copy = pltpu.make_async_copy(src, dst, self.sems[2].at[i])
        copy.start()
        return copy

    def sent(self, copy):
        copy.wait_send()
        self.open = [other for other in self.open if other is not copy]

    def finish(self):
        for copy in self.open:
            copy.wait_send()


def rows_of(place, rows, at=None):
    at = place.xy if at is None else at
    return pl.ds(pl.multiple_of(place.c * (4 * rows) + at * rows, 32), rows)


def half_of(place, rows):
    return pl.ds(pl.multiple_of(place.c * (4 * rows), 128), 4 * rows)


def interleave(size, parts):
    group = size // parts
    out_row = lax.broadcasted_iota(jnp.int32, (size, size), 0)
    col = lax.broadcasted_iota(jnp.int32, (size, size), 1)
    part = jnp.zeros((size, size), jnp.int32)
    for k in range(1, parts):
        part = part + (col >= k * group).astype(jnp.int32)
    return jnp.where(out_row == parts * (col - group * part) + part, 1.0, 0.0).astype(BF)


def interleave_out():
    out_row = lax.broadcasted_iota(jnp.int32, (32, 32), 0)
    col = lax.broadcasted_iota(jnp.int32, (32, 32), 1)
    part = (col >= 8).astype(jnp.int32) + (col >= 16).astype(jnp.int32)
    keep = (out_row == 3 * (col - 8 * part) + part) & (col < 24)
    return jnp.where(keep, 1.0, 0.0).astype(BF)


def dot_f32(a, b):
    return jnp.dot(a, b, preferred_element_type=F32)


def compact_out():
    out_row = lax.broadcasted_iota(jnp.int32, (192, 256), 0)
    col = lax.broadcasted_iota(jnp.int32, (192, 256), 1)
    group = jnp.zeros((192, 256), jnp.int32)
    for i in range(1, 8):
        group = group + (out_row >= 24 * i).astype(jnp.int32)
    return jnp.where(col == out_row + 8 * group, 1.0, 0.0).astype(BF)


def dot_nt(a, b):
    return lax.dot_general(a, b, (((1,), (1,)), ((), ())), preferred_element_type=F32)


def dot_tn(a, b):
    return lax.dot_general(a, b, (((0,), (0,)), ((), ())), preferred_element_type=F32)


def unpack_small(packed, small):
    for t in range(4):
        small[t] = jnp.concatenate([packed[t, i : i + 1, :] for i in range(6)], axis=1)


def norm_vectors(small, norm):
    for i in range(6):
        at = 1152 + 192 * i
        norm[i : i + 1, :] = jnp.concatenate([small[t, 0:1, at : at + 192] for t in range(4)], axis=1)


def row_loop(body, step=128):
    @pl.loop(0, 512 // step)
    def _(i):
        body(pl.ds(pl.multiple_of(i * step, step), step))


def forward_kernel(
    master,
    owners,
    order_col,
    labels,
    flags,
    x_in,
    gy_in,
    w_qkv,
    w_out,
    w_up,
    w_down,
    out_compact,
    slot_out,
    small_out,
    x_out,
    gy_row,
    qkv_out,
    prob_out,
    att_out,
    n_one_out,
    h_out,
    act_out,
    pull_out,
    z_two_out,
    inv_out,
    slot_row,
    slot_col,
    id_row,
    id_col,
    slots,
    canon_att,
    canon_ffn,
    land_att,
    land_ffn,
    pass_ffn,
    pass_land,
    share,
    p_qkv,
    p_out,
    p_up,
    p_down,
    small_mine,
    small_land,
    small_total,
    packed,
    small,
    norm,
    bias_qkv,
    v_qkv,
    v_out,
    v_compact,
    v_up,
    v_down,
    x_row,
    qkv,
    prob,
    att,
    n_one,
    h_low,
    act,
    pull,
    total,
    inv,
    send_sems,
    recv_sems,
    local_sems,
):
    place = Place()
    link = Sender(send_sems, recv_sems, local_sems)
    place.hail()
    slots[place.c] = master[...].astype(BF)

    place.meet()
    whole = (w_qkv, w_out, w_up, w_down)
    held = (v_qkv, v_out, v_up, v_down)
    piece = (p_qkv, p_out, p_up, p_down)
    peers = (place.right, place.down, place.diag)
    mine_rows = pl.ds(pl.multiple_of(place.t * 128, 128), 128)
    tidy = []

    core_slots = link.send(slots.at[place.c], slots.at[place.c], place.core)
    x_moves = [
        link.send(x_in.at[place.ahead[k]], x_row.at[mine_rows], place.deep[k]) for k in (1, 2, 3)
    ]
    x_stay = link.copy(x_in.at[place.t], x_row.at[mine_rows])
    tidy.append(link.copy(gy_in.at[place.t], gy_row.at[mine_rows]))

    blocks = owners.shape[0]
    wide = slot_row.shape[1]
    owner = jnp.concatenate(
        [owners[...].astype(F32)[None], jnp.full((1, wide - blocks), -1.0, F32)], axis=1
    )
    kinds = lax.broadcasted_iota(jnp.int32, (8, wide), 0).astype(F32)
    owned = jnp.where(kinds == owner, 1.0, 0.0)
    ordinal = lax.broadcasted_iota(jnp.int32, (wide, wide), 1)
    earlier = jnp.where(lax.broadcasted_iota(jnp.int32, (wide, wide), 0) < ordinal, 1.0, 0.0)
    ahead = dot_f32(owned.astype(BF), earlier.astype(BF))
    ranking = jnp.sum(owned * ahead, axis=0, keepdims=True)
    place_of = jnp.where(order_col[...] == ordinal, 1.0, 0.0).astype(BF)
    pair = jnp.where(kinds == 0.0, owner, ranking).astype(BF)
    row = dot_nt(pair, place_of)
    col = dot_nt(place_of, pair)
    per_owner = float(master.shape[0])
    slot_row[...] = jnp.broadcast_to(row[0:1, :] * per_owner + row[1:2, :], slot_row.shape)
    slot_col[...] = jnp.broadcast_to(col[:, 0:1] * per_owner + col[:, 1:2], slot_col.shape)

    own = pl.ds(place.t, 1)
    apart = -1 - lax.broadcasted_iota(jnp.int32, (1, 512), 1)
    ids = jnp.where(flags[own, :] == 1, labels[own, :], apart).astype(F32)
    id_row[...] = jnp.broadcast_to(ids, id_row.shape)
    id_col[...] = jnp.transpose(id_row[...])
    tidy.append(link.copy(slot_row, slot_out))
    core_slots.wait_recv()

    pair_slots = slots[...].reshape(384, 2304)
    slot_id = (lax.broadcasted_iota(jnp.int32, (64, 384), 1) + place.xy * 384).astype(F32)
    order = [(3, place.diag), (1, place.right), (2, place.down), (0, None)]

    def spread(lo, rows, canon, land):
        sent = []
        for j, peer in order:
            at = place.xy if peer is None else peer[0] // 2
            spot = pl.ds(pl.multiple_of(place.c * 384 + at * 96 + lo, 32), rows)
            wanted = slot_col[spot, 0:1]
            pick = jnp.where(wanted == slot_id[:rows], 1.0, 0.0).astype(BF)
            canon[j] = dot_f32(pick, pair_slots).astype(BF)
            if peer is not None:
                sent.append(link.send(canon.at[j], land.at[j - 1], peer))
        return sent

    def collect(sent, lo, rows, canon, land):
        for move in sent:
            move.wait_recv()
        share[lo : lo + rows, :] = (
            canon[0].astype(F32) + land[0].astype(F32) + land[1].astype(F32) + land[2].astype(F32)
        )

    att_sent = spread(64, 32, canon_att, land_att)
    pick_small = jnp.where(slot_row[:, 768:769] == slot_id[:8], 1.0, 0.0).astype(BF)
    picked = dot_f32(pick_small, pair_slots)
    for i in range(6):
        small_mine[i : i + 1, :] = picked[0:1, 384 * i : 384 * i + 384]
    small_mine[6:8, :] = jnp.zeros((2, 384), F32)
    small_moves = [link.send(small_mine, small_land.at[j], peer) for j, peer in enumerate(peers)]
    def spread_halves():
        for j, peer in order:
            at = place.xy if peer is None else peer[0] // 2
            spot = pl.ds(pl.multiple_of(place.c * 384 + at * 96, 32), 64)
            pick = jnp.where(slot_col[spot, 0:1] == slot_id, 1.0, 0.0).astype(BF)
            canon_ffn[j] = dot_f32(pick, pair_slots).astype(BF)
            if j in (1, 3):
                half = canon_ffn.at[j, pl.ds(0, 32)]
                halves[j, 0] = link.send(half, land_ffn.at[0, j // 2], place.right)
            if j in (2, 3):
                half = canon_ffn.at[j, pl.ds(32, 32)]
                halves[j, 1] = link.send(half, land_ffn.at[1, j - 2], place.down)

    def pass_halves():
        halves[3, 0].wait_recv()
        pass_ffn[0] = canon_ffn[2, 0:32, :] + land_ffn[0, 1]
        halves["down"] = link.send(pass_ffn.at[0], pass_land.at[0], place.down)
        halves[3, 1].wait_recv()
        pass_ffn[1] = canon_ffn[1, 32:64, :] + land_ffn[1, 1]
        halves["right"] = link.send(pass_ffn.at[1], pass_land.at[1], place.right)

    def collect_halves():
        halves[1, 0].wait_recv()
        halves[2, 1].wait_recv()
        halves["down"].wait_recv()
        halves["right"].wait_recv()
        for i in range(2):
            share[32 * i : 32 * i + 32, :] = (
                canon_ffn[0, 32 * i : 32 * i + 32, :] + land_ffn[i, 0] + pass_land[i]
            ).astype(F32)

    halves = {}
    att_sent[0].wait_recv()
    spread_halves()
    collect(att_sent[1:], 64, 32, canon_att, land_att)

    p_qkv[...] = dot_f32(
        interleave(96, 4),
        jnp.concatenate([share[64:88, 576 * r : 576 * r + 576] for r in range(4)], axis=0).astype(BF),
    ).astype(BF)

    def spread_out():
        parts = [share[88:96, 768 * k : 768 * k + 768] for k in range(3)]
        parts = parts + [jnp.zeros((8, 768), F32)]
        p_out[...] = dot_f32(interleave_out(), jnp.concatenate(parts, axis=0).astype(BF)).astype(BF)

    def spread_ffn():
        three = interleave(96, 3)
        for at, ref in ((0, p_up), (32, p_down)):
            parts = [share[at : at + 32, 768 * k : 768 * k + 768] for k in range(3)]
            ref[...] = dot_f32(three, jnp.concatenate(parts, axis=0).astype(BF)).astype(BF)

    deep_moves, right_moves, down_moves, own_copies, core_moves, loads = {}, {}, {}, {}, {}, {}

    def deep_send(w):
        spot = whole[w].at[place.t, rows_of(place, WEIGHTS[w][1])]
        own_copies[w] = link.copy(piece[w], spot)
        deep_moves[w] = [link.send(piece[w], spot, place.deep[k]) for k in (1, 2, 3)]

    def plane_send(w, k):
        rows = WEIGHTS[w][1]
        spot = whole[w].at[place.behind[k], rows_of(place, rows)]
        src = piece[w] if k == 0 else spot
        if k:
            deep_moves[w][k - 1].wait_recv()
        right_moves[w, k] = link.send(src, spot, place.right)
        down_moves[w, k] = link.send(src, spot, place.down)

    def plane_pass(w, k):
        rows = WEIGHTS[w][1]
        half = rows // 2
        right_moves[w, k].wait_recv()
        down_moves[w, k].wait_recv()
        t = place.behind[k]
        right_at = place.c * (4 * rows) + (place.right[0] // 2) * rows
        down_at = place.c * (4 * rows) + (place.down[0] // 2) * rows
        first = whole[w].at[t, pl.ds(pl.multiple_of(right_at, 16), half)]
        second = whole[w].at[t, pl.ds(pl.multiple_of(down_at + half, 16), half)]
        right_moves[w, k, 1] = link.send(second, second, place.right)
        down_moves[w, k, 1] = link.send(first, first, place.down)

    def core_pass(w, k):
        if k == 0:
            own_copies[w].wait()
        right_moves[w, k, 1].wait_recv()
        down_moves[w, k, 1].wait_recv()
        spot = whole[w].at[place.behind[k], half_of(place, WEIGHTS[w][1])]
        core_moves[w, k] = link.send(spot, spot, place.core)

    def load(w, k):
        core_moves[w, k].wait_recv()
        t = place.behind[k]
        loads[w, k] = link.copy(whole[w].at[t], held[w].at[t])

    def qkv_step(k):
        loads[0, k].wait()
        t = place.behind[k]

        def body(rows):
            lin = dot_f32(x_row[rows, :], v_qkv[t]) + bias_qkv[t]
            qkv[t, rows, :] = lin.astype(BF)

        row_loop(body, 256)

    def attention(k):
        t = place.behind[k]

        def body(rows):
            allowed = id_col[rows, 0:1] == id_row[0:1, :]
            parts = []
            for i in range(3):
                at = 64 * i
                scores = dot_nt(qkv[t, rows, at : at + 64], qkv[t, :, 192 + at : 256 + at]) * 0.125
                scores = jnp.where(allowed, scores, MASKED)
                weight = jnp.exp(scores - jnp.max(scores, axis=1, keepdims=True))
                weight = weight * (1.0 / jnp.sum(weight, axis=1, keepdims=True))
                low = weight.astype(BF)
                prob[3 * t + i, rows, :] = low
                parts.append(dot_f32(low, qkv[t, :, 384 + at : 448 + at]))
            att[t, rows, :] = jnp.concatenate(parts, axis=1).astype(BF)

        row_loop(body, 256)
        tidy.append(link.copy(qkv.at[t], qkv_out.at[t]))
        tidy.append(link.copy(att.at[t], att_out.at[t]))
        tidy.append(link.copy(prob.at[pl.ds(3 * t, 3)], prob_out.at[pl.ds(3 * t, 3)]))

    def out_step():
        pick = compact_out()
        for k in range(4):
            loads[1, k].wait()
        for t in range(4):
            v_compact[t] = dot_f32(pick, v_out[t]).astype(BF)
        tidy.append(link.copy(v_compact, out_compact))

        def body(rows):
            z = x_row[rows, :].astype(F32) + norm[0:1, :]
            for t in range(4):
                z = z + dot_f32(att[t, rows, :], v_compact[t])
            normed, inverse = normalize(z)
            n_one[rows, :] = normed
            inv[rows, :] = inverse
            h = normed * norm[2:3, :] + norm[3:4, :]
            h_low[rows, :] = h.astype(BF)
            total[rows, :] = h + norm[1:2, :]

        row_loop(body, 256)
        tidy.append(link.copy(n_one, n_one_out))
        tidy.append(link.copy(h_low, h_out))

    def up_step(k):
        loads[2, k].wait()
        t = place.behind[k]

        def body(rows):
            pre = dot_f32(h_low[rows, :], v_up[t]) + small[t, 0:1, 384:1152]
            below = 0.5 + 0.5 * lax.erf(pre * (0.5**0.5))
            act[t, rows, :] = (pre * below).astype(BF)
            slope = below + pre * (jnp.exp(-0.5 * pre * pre) * 0.3989422804014327)
            pull[t, rows, :] = slope.astype(BF)

        row_loop(body, 256)
        tidy.append(link.copy(act.at[t], act_out.at[t]))
        tidy.append(link.copy(pull.at[t], pull_out.at[t]))

    def down_step(k):
        loads[3, k].wait()
        t = place.behind[k]

        def body(rows):
            total[rows, :] += dot_f32(act[t, rows, :], v_down[t])

        row_loop(body, 256)

    def end_step():
        tidy.append(link.copy(total, z_two_out))
        tidy.append(link.copy(inv, inv_out))

    every = range(4)
    others = (1, 2, 3)
    small_state, gy_moves = {}, []

    def small_collect():
        for move in small_moves:
            move.wait_recv()
        small_total[...] = small_mine[...] + small_land[0] + small_land[1] + small_land[2]
        small_state["stay"] = link.copy(small_total, packed.at[place.t])
        small_state["deep"] = [
            link.send(small_total, packed.at[place.t], place.deep[k]) for k in others
        ]

    def small_ready():
        small_state["stay"].wait()
        for move in small_state["deep"]:
            move.wait_recv()
        unpack_small(packed, small)
        norm_vectors(small, norm)
        for t in every:
            bias_qkv[t] = jnp.concatenate(
                [small[t, 0:1, :192], jnp.zeros((1, 192), F32), small[t, 0:1, 192:384]], axis=1
            )
        tidy.append(link.copy(packed, small_out))

    def x_ready():
        x_stay.wait()
        for move in x_moves:
            move.wait_recv()
        tidy.append(link.copy(x_row, x_out))

    def gy_send():
        for k in others:
            gy_moves.append(link.send(gy_in.at[place.ahead[k]], gy_row.at[mine_rows], place.deep[k]))

    def gy_ready():
        for move in gy_moves:
            move.wait_recv()

    spread_out()
    deep_send(1)
    plane_send(0, 0)
    pass_halves()
    deep_send(0)
    plane_send(1, 0)
    plane_pass(0, 0)
    plane_send(1, 3)
    collect_halves()
    spread_ffn()
    plane_send(2, 0)
    plane_pass(1, 3)
    small_collect()
    plane_send(1, 2)
    plane_send(0, 1)
    plane_pass(1, 0)
    deep_send(2)
    plane_send(1, 1)
    plane_send(0, 3)
    small_ready()
    plane_pass(0, 1)
    core_pass(0, 0)
    load(0, 0)
    core_pass(1, 0)
    plane_pass(1, 2)
    plane_pass(0, 3)
    core_pass(1, 3)
    plane_pass(2, 0)
    plane_send(0, 2)
    deep_send(3)
    x_ready()
    core_pass(0, 1)
    qkv_step(0)
    plane_send(2, 1)
    core_pass(0, 3)
    attention(0)
    load(0, 3)
    qkv_step(3)
    plane_send(2, 2)
    load(1, 3)
    load(0, 1)
    gy_send()
    qkv_step(1)
    plane_pass(1, 1)
    plane_pass(0, 2)
    plane_send(2, 3)
    core_pass(1, 2)
    attention(3)
    core_pass(1, 1)
    plane_send(3, 0)
    core_pass(0, 2)
    core_pass(2, 0)
    load(1, 0)
    attention(1)
    plane_pass(2, 3)
    plane_pass(2, 2)
    plane_pass(2, 1)
    load(1, 2)
    plane_send(3, 2)
    load(2, 0)
    load(0, 2)
    qkv_step(2)
    load(1, 1)
    plane_pass(3, 0)
    plane_send(3, 3)
    attention(2)
    plane_send(3, 1)
    core_pass(2, 3)
    out_step()
    load(2, 3)
    core_pass(2, 1)
    up_step(0)
    load(2, 1)
    core_pass(2, 2)
    up_step(3)
    plane_pass(3, 2)
    load(2, 2)
    core_pass(3, 0)
    up_step(1)
    load(3, 0)
    plane_pass(3, 3)
    up_step(2)
    plane_pass(3, 1)
    core_pass(3, 2)
    down_step(0)
    core_pass(3, 3)
    load(3, 2)
    core_pass(3, 1)
    load(3, 3)
    down_step(2)
    gy_ready()
    load(3, 1)
    down_step(3)
    down_step(1)
    end_step()
    for copy in tidy:
        copy.wait()
    link.finish()


def forward_call(master, owners, order_col, labels, flags, x_in, gy_in):
    anywhere = pl.BlockSpec(memory_space=pl.ANY)
    vmem = pl.BlockSpec(memory_space=pltpu.VMEM)
    shape = jax.ShapeDtypeStruct
    outs = [
        ((4, 768, 576), BF),
        ((4, 256, 768), BF),
        ((4, 768, 768), BF),
        ((4, 768, 768), BF),
        ((4, 192, 768), BF),
        ((8, 896), F32),
        ((4, 8, 384), F32),
        ((512, 768), BF),
        ((512, 768), BF),
        ((4, 512, 576), BF),
        ((12, 512, 512), BF),
        ((4, 512, 192), BF),
        ((512, 768), F32),
        ((512, 768), BF),
        ((4, 512, 768), BF),
        ((4, 512, 768), BF),
        ((512, 768), F32),
        ((512, 1), F32),
    ]
    scratch = [
        ((8, 896), F32),
        ((896, 8), F32),
        ((8, 512), F32),
        ((512, 8), F32),
        ((2, 192, 2304), BF),
        ((4, 32, 2304), BF),
        ((4, 64, 2304), BF),
        ((3, 32, 2304), BF),
        ((2, 2, 32, 2304), BF),
        ((2, 32, 2304), BF),
        ((2, 32, 2304), BF),
        ((96, 2304), F32),
        ((96, 576), BF),
        ((32, 768), BF),
        ((96, 768), BF),
        ((96, 768), BF),
        ((8, 384), F32),
        ((3, 8, 384), F32),
        ((8, 384), F32),
        ((4, 8, 384), F32),
        ((4, 1, 2304), F32),
        ((8, 768), F32),
        ((4, 1, 576), F32),
        ((4, 768, 576), BF),
        ((4, 256, 768), BF),
        ((4, 192, 768), BF),
        ((4, 768, 768), BF),
        ((4, 768, 768), BF),
        ((512, 768), BF),
        ((4, 512, 576), BF),
        ((12, 512, 512), BF),
        ((4, 512, 192), BF),
        ((512, 768), F32),
        ((512, 768), BF),
        ((4, 512, 768), BF),
        ((4, 512, 768), BF),
        ((512, 768), F32),
        ((512, 1), F32),
    ]
    return pl.pallas_call(
        forward_kernel,
        out_shape=[shape(*o) for o in outs],
        in_specs=[vmem] * 5 + [anywhere] * 2,
        out_specs=[anywhere] * len(outs),
        scratch_shapes=[pltpu.VMEM(*s) for s in scratch]
        + [
            pltpu.SemaphoreType.DMA((128,)),
            pltpu.SemaphoreType.DMA((128,)),
            pltpu.SemaphoreType.DMA((64,)),
        ],
        compiler_params=pltpu.CompilerParams(
            collective_id=0, has_side_effects=True, vmem_limit_bytes=60 * MIB
        ),
        name="gather_and_forward",
    )(master, owners, order_col, labels, flags, x_in, gy_in)


def backward_kernel(
    labels,
    flags,
    gy_in,
    z_two_in,
    inv_in,
    small_in,
    act_in,
    pull_in,
    w_down,
    w_up,
    h_in,
    n_one_in,
    att_in,
    w_out,
    qkv_in,
    prob_in,
    w_qkv,
    x_in,
    blocks,
    small_out,
    out_mine,
    dx_mine,
    pool_out,
    *scratch,
):
    sums, cores, lefts, tops, lefts_two, tops_two, deeps = (scratch[4 * i : 4 * i + 4] for i in range(7))
    (
        ring,
        ring_narrow,
        share,
        share_low,
        small_grad,
        small_land,
        packed,
        small,
        norm,
        gy,
        normed,
        inv,
        act,
        pull,
        v_down,
        v_up,
        h_low,
        att,
        v_out,
        qkv,
        prob,
        v_qkv,
        x_row,
        wide,
        low,
        total,
        d_up,
        d_att,
        d_qkv,
        turned,
        go,
        reds,
        red_up,
        red_qv,
        flag_col,
        row_low,
        pool,
        send_sems,
        recv_sems,
        local_sems,
    ) = scratch[28:]
    place = Place()
    place.hail()
    link = Sender(send_sems, recv_sems, local_sems)
    t_of = place.ahead
    steps = (1, 2, 3, 0)
    got = {}

    def fetch(name, src, dst):
        got[name] = link.copy(src, dst)

    fetch("small", small_in, packed)
    fetch("normed", z_two_in, normed)
    fetch("gy", gy_in, gy)
    fetch("inv", inv_in, inv)

    def load_ffn(i):
        t, slot = t_of[steps[i]], i % 2
        fetch(("act", i), act_in.at[t], act.at[slot])
        fetch(("down", i), w_down.at[t], v_down.at[slot])
        fetch(("pull", i), pull_in.at[t], pull.at[slot])
        fetch(("up", i), w_up.at[t], v_up.at[slot])

    def load_att(i):
        t, slot = t_of[steps[i]], i % 2
        fetch(("prob", i), prob_in.at[pl.ds(3 * t, 3)], prob.at[slot])
        fetch(("qkv", i), w_qkv.at[t], v_qkv.at[slot])

    own = pl.ds(place.t, 1)
    own_flags = flags[own, :].astype(F32)
    flag_col[...] = jnp.transpose(jnp.broadcast_to(own_flags, (8, 512)))
    t, x, y, c = place.t, place.x, place.y, place.c
    moves, stay = [], []

    core_moves, first, second, third = {}, {}, {}, {}
    ring_open = [None] * 5
    ring_at = [0, 0]

    def chip_row(w, k, yy, xx, half):
        rows = WEIGHTS[w][1]
        at = pl.multiple_of((yy * 2 + xx) * rows + half * (rows // 2), 16)
        return sums[w].at[t_of[k], pl.ds(at, rows // 2)]

    def produce(w, k, make):
        narrow = w == 0
        slot = 3 + ring_at[1] % 2 if narrow else ring_at[0] % 3
        ring_at[narrow] += 1
        if ring_open[slot] is not None:
            link.sent(ring_open[slot])
        cols, rows = WEIGHTS[w]
        away = ring_narrow.at[slot - 3] if narrow else ring.at[slot, pl.ds(0, 4 * rows)]
        away[...] = make(1 - c).astype(BF)
        move = link.send(away, cores[w].at[k], place.core)
        ring_open[slot] = move
        core_moves[w, k] = move
        sums[w][t_of[k]] = make(c).astype(BF)

    def core_add(w, k):
        core_moves[w, k].wait_recv()
        rows = WEIGHTS[w][1]

        @pl.loop(0, 4)
        def _(i):
            at = pl.ds(pl.multiple_of(i * rows, 32), rows)
            sums[w][t_of[k], at, :] += cores[w][k, at, :]

        first[w, k] = []
        for i in (0, 1):
            first[w, k].append(link.send(chip_row(w, k, i, 1 - x, 0), lefts[w].at[k, i], place.right))
            first[w, k].append(link.send(chip_row(w, k, 1 - y, i, 1), tops[w].at[k, i], place.down))

    def add(spot, other):
        spot[...] = spot[...] + other[...]

    def plane_add(w, k):
        for move in first[w, k]:
            move.wait_recv()
        down_part, right_part = chip_row(w, k, 1 - y, x, 0), chip_row(w, k, y, 1 - x, 1)
        add(down_part, lefts[w].at[k, 1 - y])
        add(right_part, tops[w].at[k, 1 - x])
        second[w, k] = [
            link.send(down_part, lefts_two[w].at[k], place.down),
            link.send(right_part, tops_two[w].at[k], place.right),
        ]
        add(chip_row(w, k, y, x, 0), lefts[w].at[k, y])
        add(chip_row(w, k, y, x, 1), tops[w].at[k, x])

    def deep_add(w, k):
        for move in second[w, k]:
            move.wait_recv()
        add(chip_row(w, k, y, x, 0), lefts_two[w].at[k])
        add(chip_row(w, k, y, x, 1), tops_two[w].at[k])
        rows = WEIGHTS[w][1]
        if k:
            spot = pl.ds(pl.multiple_of(place.xy * rows, 16), rows)
            third[w, k] = link.send(sums[w].at[t_of[k], spot], deeps[w].at[k - 1], place.deep[k])

    def end(w):
        rows = WEIGHTS[w][1]
        spot = pl.ds(pl.multiple_of(place.xy * rows, 16), rows)
        whole = sums[w][t, spot, :].astype(F32)
        for k in (1, 2, 3):
            third[w, k].wait_recv()
            whole = whole + deeps[w][k - 1].astype(F32)
        whole = whole.astype(BF)
        if w == 0:
            parts = dot_tn(interleave(96, 4), whole)
            share[64:88, :] = jnp.concatenate([parts[24 * r : 24 * r + 24] for r in range(4)], axis=1)
        elif w == 1:
            parts = dot_tn(interleave_out(), whole)
            for k in range(3):
                share[88:96, 768 * k : 768 * k + 768] = parts[8 * k : 8 * k + 8]
        else:
            at = 0 if w == 2 else 32
            parts = dot_tn(interleave(96, 3), whole)
            for k in range(3):
                share[at : at + 32, 768 * k : 768 * k + 768] = parts[32 * k : 32 * k + 32]

    def column_sum(value):
        return jnp.sum(value, axis=0, keepdims=True)

    def norm_two_back():
        def body(rows):
            grad = gy[rows, :].astype(F32) * flag_col[rows, 0:1]
            n, inverse = normalize(normed[rows, :])
            normed[rows, :] = n
            dz = norm_back(grad * norm[4:5, :], n, inverse)
            wide[rows, :] = dz
            total[rows, :] = dz
            low[rows, :] = dz.astype(BF)
            reds[4:5, :] += column_sum(grad * n)
            reds[5:6, :] += column_sum(grad)
            reds[1:2, :] += column_sum(dz)

        row_loop(body)

    def emit_out():
        sentence = lax.broadcasted_iota(jnp.int32, (SMAX, 512), 0).astype(F32)
        member = jnp.where((sentence == labels[own, :].astype(F32)) & (own_flags == 1.0), 1.0, 0.0)
        count = jnp.maximum(jnp.sum(member, axis=1, keepdims=True), 1.0)
        pooled = jnp.zeros((SMAX, 768), F32)
        for i in range(4):
            rows = slice(128 * i, 128 * i + 128)
            out = normed[rows, :] * norm[4:5, :] + norm[5:6, :]
            row_low[rows, :] = out.astype(BF)
            pooled = pooled + jnp.dot(
                member[:, rows], out, precision=exact_precision, preferred_element_type=F32
            )
        pool[...] = pooled / count
        own_rows = pl.ds(pl.multiple_of(t * 128, 128), 128)
        stay.append(link.copy(row_low.at[own_rows], out_mine.at[t]))
        stay.append(link.copy(pool, pool_out.at[t]))
        for k in (1, 2, 3):
            part = row_low.at[pl.ds(pl.multiple_of(t_of[k] * 128, 128), 128)]
            moves.append(link.send(part, out_mine.at[t], place.deep[k]))
            moves.append(link.send(pool, pool_out.at[t], place.deep[k]))

    def lanes(which):
        return pl.ds(pl.multiple_of(which * 384, 128), 384)

    def down_piece(i):
        k, slot = steps[i], i % 2
        got["act", i].wait()
        produce(3, k, lambda which: dot_tn(act[slot, :, lanes(which)], low[...]))

    def act_back(i):
        k, slot = steps[i], i % 2
        got["down", i].wait()
        got["pull", i].wait()

        def body(rows):
            grad = dot_nt(low[rows, :], v_down[slot]) * pull[slot, rows, :].astype(F32)
            red_up[t_of[k]] += column_sum(grad)
            d_up[rows, :] = grad.astype(BF)

        row_loop(body, 256)

    def up_piece(i):
        if i == 0:
            got["h"].wait()
        produce(2, steps[i], lambda which: dot_tn(h_low[:, lanes(which)], d_up[...]))

    def hidden_back(i):
        slot = i % 2
        got["up", i].wait()

        def body(rows):
            total[rows, :] += dot_nt(d_up[rows, :], v_up[slot])

        row_loop(body, 256)
        if i == 1:
            fetch("n_one", n_one_in, normed)

    def norm_one_back():
        got["n_one"].wait()

        def body(rows):
            dh = total[rows, :]
            n = normed[rows, :]
            dz = norm_back(dh * norm[2:3, :], n, inv[rows, :])
            total[rows, :] = dz
            low[rows, :] = dz.astype(BF)
            reds[2:3, :] += column_sum(dh * n)
            reds[3:4, :] += column_sum(dh)
            reds[0:1, :] += column_sum(dz)

        row_loop(body)

    def out_piece(i):
        k = steps[i]
        if i == 0:
            got["att"].wait()
            got["wout"].wait()
        go[...] = dot_tn(att[t_of[k]], low[...])

        def make(which):
            part = go[pl.ds(pl.multiple_of(which * 96, 96), 96), :]
            pad = jnp.zeros((8, 768), F32)
            parts = []
            for j in range(4):
                parts += [part[24 * j : 24 * j + 24], pad]
            return jnp.concatenate(parts, axis=0)

        produce(1, k, make)

        def body(rows):
            d_att[rows, :] = dot_nt(low[rows, :], v_out[t_of[k]]).astype(BF)

        row_loop(body, 256)

    def attention_back(i):
        k, slot = steps[i], i % 2
        tk = t_of[k]
        if i == 0:
            got["qkvs"].wait()
        got["prob", i].wait()
        turned[...] = jnp.zeros_like(turned)

        def body(rows):
            d_queries = []
            for j in range(3):
                at = 64 * j
                grad = d_att[rows, at : at + 64]
                weight_low = prob[slot, j, rows, :]
                weight = weight_low.astype(F32)
                d_prob = dot_nt(grad, qkv[tk, :, 384 + at : 448 + at]) * weight
                inner = jnp.sum(d_prob, axis=1, keepdims=True)
                d_scores = (d_prob - weight * inner).astype(BF)
                d_queries.append(dot_f32(d_scores, qkv[tk, :, 192 + at : 256 + at]))
                turned[at : at + 64, :] += dot_tn(qkv[tk, rows, at : at + 64], d_scores)
                turned[192 + at : 256 + at, :] += dot_tn(grad, weight_low)
            dq = jnp.concatenate(d_queries, axis=1) * 0.125
            red_qv[tk, :, :192] += column_sum(dq)
            d_qkv[rows, :192] = dq.astype(BF)

        row_loop(body, 256)
        dk = jnp.transpose(turned[:192, :]) * 0.125
        dv = jnp.transpose(turned[192:, :])
        red_qv[tk, :, 192:] += column_sum(dv)
        d_qkv[:, 192:] = jnp.concatenate([dk, dv], axis=1).astype(BF)

    def qkv_piece(i):
        k, slot = steps[i], i % 2
        if i == 0:
            got["x"].wait()
        produce(0, k, lambda which: dot_tn(x_row[:, lanes(which)], d_qkv[...]))
        got["qkv", i].wait()

        def body(rows):
            total[rows, :] += dot_nt(d_qkv[rows, :], v_qkv[slot])

        row_loop(body, 256)

    sent, passed, across = {}, {}, {}

    def share_send(lo, hi):
        share_low[lo:hi, :] = share[lo:hi, :].astype(BF)
        mine = c * 4 + place.xy
        rows = pl.ds(lo, hi - lo)
        sent[lo] = (
            link.copy(share_low.at[rows], blocks.at[mine, rows]),
            link.send(share_low.at[rows], blocks.at[mine, rows], place.right),
            link.send(share_low.at[rows], blocks.at[mine, rows], place.down),
        )

    def share_pass(lo, hi):
        half = (hi - lo) // 2
        sent[lo][1].wait_recv()
        sent[lo][2].wait_recv()
        one = blocks.at[c * 4 + place.right[0] // 2, pl.ds(lo, half)]
        two = blocks.at[c * 4 + place.down[0] // 2, pl.ds(lo + half, half)]
        passed[lo] = link.send(one, one, place.down), link.send(two, two, place.right)

    def share_across(lo, hi):
        sent[lo][0].wait()
        passed[lo][0].wait_recv()
        passed[lo][1].wait_recv()
        spot = blocks.at[pl.ds(c * 4, 4), pl.ds(lo, hi - lo)]
        across[lo] = link.send(spot, spot, place.core)

    def share_ready(lo):
        across[lo].wait_recv()

    got["small"].wait()
    unpack_small(packed, small)
    norm_vectors(small, norm)
    reds[...] = jnp.zeros_like(reds)
    red_up[...] = jnp.zeros_like(red_up)
    red_qv[...] = jnp.zeros_like(red_qv)
    small_grad[...] = jnp.zeros_like(small_grad)
    for name in ("normed", "gy", "inv"):
        got[name].wait()
    def load_rest():
        fetch("h", h_in, h_low)
        fetch("att", att_in, att)
        fetch("wout", w_out, v_out)
        fetch("qkvs", qkv_in, qkv)
        fetch("x", x_in, x_row)

    small_state = {}

    def meet():
        place.meet()

    def small_send():
        def dx_body(rows):
            low[rows, :] = total[rows, :].astype(BF)

        row_loop(dx_body)
        for q in range(4):
            at = slice(192 * q, 192 * q + 192)
            line = jnp.concatenate(
                [red_qv[q], red_up[q]] + [reds[i : i + 1, at] for i in range(6)], axis=1
            )
            for i in range(6):
                small_grad[q, i : i + 1, :] = line[:, 384 * i : 384 * i + 384]
        small_state["keep"] = link.copy(small_grad.at[t], small_land.at[6])
        small_state["deep"] = [
            link.send(small_grad.at[t_of[k]], small_land.at[k - 1], place.deep[k]) for k in (1, 2, 3)
        ]

    def dx_send():
        own_rows = pl.ds(pl.multiple_of(t * 128, 128), 128)
        stay.append(link.copy(low.at[own_rows], dx_mine.at[t]))
        for k in (1, 2, 3):
            part = low.at[pl.ds(pl.multiple_of(t_of[k] * 128, 128), 128)]
            moves.append(link.send(part, dx_mine.at[t], place.deep[k]))

    def small_core():
        small_state["keep"].wait()
        for move in small_state["deep"]:
            move.wait_recv()
        small_land[7] = small_land[6] + small_land[0] + small_land[1] + small_land[2]
        small_state["core"] = link.send(small_land.at[7], small_land.at[3], place.core)

    def small_right():
        small_state["core"].wait_recv()
        small_land[8] = small_land[7] + small_land[3]
        small_state["right"] = link.send(small_land.at[8], small_land.at[4], place.right)

    def small_down():
        small_state["right"].wait_recv()
        small_land[9] = small_land[8] + small_land[4]
        small_state["down"] = link.send(small_land.at[9], small_land.at[5], place.down)

    def small_end():
        small_state["down"].wait_recv()
        small_out[...] = small_land[9] + small_land[5]

    load_ffn(0)
    norm_two_back()
    meet()
    load_ffn(1)
    down_piece(0)
    load_rest()
    act_back(0)
    emit_out()
    core_add(3, 1)
    load_att(0)
    load_att(1)
    up_piece(0)
    hidden_back(0)
    load_ffn(2)
    core_add(2, 1)
    down_piece(1)
    act_back(1)
    core_add(3, 2)
    up_piece(1)
    hidden_back(1)
    core_add(2, 2)
    load_ffn(3)
    down_piece(2)
    act_back(2)
    plane_add(3, 2)
    up_piece(2)
    hidden_back(2)
    plane_add(3, 1)
    down_piece(3)
    plane_add(2, 2)
    core_add(2, 3)
    act_back(3)
    deep_add(3, 2)
    up_piece(3)
    plane_add(2, 1)
    hidden_back(3)
    deep_add(2, 2)
    norm_one_back()
    core_add(3, 3)
    out_piece(0)
    core_add(2, 0)
    attention_back(0)
    deep_add(2, 1)
    qkv_piece(0)
    load_att(2)
    plane_add(2, 3)
    core_add(0, 1)
    deep_add(3, 1)
    out_piece(1)
    attention_back(1)
    plane_add(3, 3)
    core_add(1, 2)
    plane_add(2, 0)
    deep_add(2, 3)
    qkv_piece(1)
    load_att(3)
    plane_add(0, 1)
    out_piece(2)
    core_add(0, 2)
    attention_back(2)
    deep_add(3, 3)
    core_add(1, 1)
    qkv_piece(2)
    deep_add(0, 1)
    core_add(1, 3)
    out_piece(3)
    plane_add(1, 2)
    core_add(0, 3)
    attention_back(3)
    deep_add(1, 2)
    plane_add(0, 2)
    plane_add(1, 3)
    plane_add(1, 1)
    plane_add(0, 3)
    core_add(3, 0)
    core_add(1, 0)
    deep_add(0, 2)
    qkv_piece(3)
    small_send()
    deep_add(0, 3)
    deep_add(1, 1)
    core_add(0, 0)
    deep_add(1, 3)
    plane_add(3, 0)
    small_core()
    deep_add(2, 0)
    plane_add(1, 0)
    plane_add(0, 0)
    dx_send()
    end(2)
    small_right()
    deep_add(3, 0)
    end(3)
    share_send(0, 64)
    deep_add(1, 0)
    deep_add(0, 0)
    end(0)
    end(1)
    share_send(64, 96)
    share_pass(0, 64)
    small_down()
    share_pass(64, 96)
    share_across(0, 64)
    share_across(64, 96)
    share_ready(0)
    share_ready(64)
    small_end()
    for move in moves:
        move.wait_recv()
    for copy in stay:
        copy.wait()
    link.finish()


def backward_call(*args):
    anywhere = pl.BlockSpec(memory_space=pl.ANY)
    vmem = pl.BlockSpec(memory_space=pltpu.VMEM)
    shape = jax.ShapeDtypeStruct
    sums = [((4, 4 * rows, cols), BF) for cols, rows in WEIGHTS]
    halves = [((4, 2, rows // 2, cols), BF) for cols, rows in WEIGHTS]
    singles = [((4, rows // 2, cols), BF) for cols, rows in WEIGHTS]
    deeps = [((3, rows, cols), BF) for cols, rows in WEIGHTS]
    rest = [
        ((3, 384, 768), BF),
        ((2, 384, 576), BF),
        ((96, 2304), F32),
        ((96, 2304), BF),
        ((4, 8, 384), F32),
        ((11, 8, 384), F32),
        ((4, 8, 384), F32),
        ((4, 1, 2304), F32),
        ((8, 768), F32),
        ((512, 768), BF),
        ((512, 768), F32),
        ((512, 1), F32),
        ((2, 512, 768), BF),
        ((2, 512, 768), BF),
        ((2, 768, 768), BF),
        ((2, 768, 768), BF),
        ((512, 768), BF),
        ((4, 512, 192), BF),
        ((4, 192, 768), BF),
        ((4, 512, 576), BF),
        ((2, 3, 512, 512), BF),
        ((2, 768, 576), BF),
        ((512, 768), BF),
        ((512, 768), F32),
        ((512, 768), BF),
        ((512, 768), F32),
        ((512, 768), BF),
        ((512, 192), BF),
        ((512, 576), BF),
        ((384, 512), F32),
        ((192, 768), F32),
        ((8, 768), F32),
        ((4, 1, 768), F32),
        ((4, 1, 384), F32),
        ((512, 8), F32),
        ((512, 768), BF),
        ((8, 768), F32),
    ]
    scratch = sums + sums + halves + halves + singles + singles + deeps + rest
    return pl.pallas_call(
        backward_kernel,
        out_shape=[
            shape((8, 96, 2304), BF),
            shape((8, 384), F32),
            shape((4, 128, 768), BF),
            shape((4, 128, 768), BF),
            shape((4, 8, 768), F32),
        ],
        in_specs=[vmem] * 2 + [anywhere] * 16,
        out_specs=[anywhere, vmem, anywhere, anywhere, anywhere],
        scratch_shapes=[pltpu.VMEM(*s) for s in scratch]
        + [
            pltpu.SemaphoreType.DMA((160,)),
            pltpu.SemaphoreType.DMA((160,)),
            pltpu.SemaphoreType.DMA((64,)),
        ],
        compiler_params=pltpu.CompilerParams(
            collective_id=1, has_side_effects=True, vmem_limit_bytes=62 * MIB
        ),
        name="backward_and_reduce",
    )(*args)


def finish_kernel(
    slot_row,
    blocks,
    small,
    pool,
    master,
    first,
    second,
    out_mine,
    dx_mine,
    new_master,
    new_first,
    new_second,
    layer_out,
    input_grad,
    pooled,
    norm_grads,
):
    step = pl.program_id(0)
    rows = master.shape[0]
    t = lax.axis_index("tensor")
    start = lax.axis_index("dp") * (rows * pl.num_programs(0)) + step * rows
    wanted = (lax.broadcasted_iota(jnp.int32, (rows, 1), 0) + start).astype(F32)
    match = slot_row[0:1, :768] == wanted
    gradient = dot_f32(jnp.where(match, 1.0, 0.0).astype(BF), blocks[...])
    is_small = slot_row[0:1, 768:769] == wanted
    small_line = jnp.concatenate([small[i : i + 1, :] for i in range(6)], axis=1)
    gradient = jnp.where(is_small, small_line, gradient)

    at = lax.broadcasted_iota(jnp.int32, (1, 768), 1) % 96
    rates = jnp.where(
        at < 32,
        MODEL_WIDTH ** (-0.5),
        jnp.where(
            at < 64,
            FF ** (-0.5),
            jnp.where(at < 88, MODEL_WIDTH ** (-0.5), 4.0 * MODEL_WIDTH ** (-0.5)),
        ),
    ).astype(F32)
    rate = jnp.sum(jnp.where(match, rates, 0.0), axis=1, keepdims=True)
    filled = (rate > 0.0) | is_small
    offset = lax.broadcasted_iota(jnp.int32, (1, small_line.shape[1]), 1) - 1152
    gain = ((offset >= 384) & (offset < 576)) | ((offset >= 768) & (offset < 960))
    small_rate = jnp.where(gain, 0.2, 0.1).astype(F32)
    step_rate = jnp.where(is_small, small_rate, rate)
    decay_on = jnp.where(is_small, 0.0, 1.0)
    new_master[...], new_first[...], new_second[...] = adamw(
        gradient, first[...], second[...], master[...], step_rate, decay_on, filled
    )
    for src, dst in ((out_mine, layer_out), (dx_mine, input_grad)):
        for row in range(4):
            dst[:, row, :] = src[row].astype(F32)

    @pl.when(step == 0)
    def _():
        total = jnp.zeros((4, 8, 192), F32)
        for q in range(4):
            total = total + jnp.where(t == q, pool[:, :, 192 * q : 192 * q + 192], 0.0)
        pooled[...] = total
        norm_grads[...] = jnp.concatenate(
            [small_line[:, 1152 + 192 * i : 1344 + 192 * i] for i in range(6)], axis=0
        )


def finish_call(slot_row, blocks, small, pool, master, first, second, out_mine, dx_mine):
    steps = 2
    slots, block_len = master.shape
    shape = jax.ShapeDtypeStruct

    def whole(*dims):
        return pl.BlockSpec(dims, lambda i: (0,) * len(dims))

    state = pl.BlockSpec((slots // steps, block_len), lambda i: (i, 0))
    token_in = pl.BlockSpec((4, 128 // steps, 768), lambda i: (0, i, 0))
    token_out = pl.BlockSpec((128 // steps, 4, 768), lambda i: (i, 0, 0))
    return pl.pallas_call(
        finish_kernel,
        grid=(steps,),
        out_shape=[shape((slots, block_len), F32)] * 3
        + [shape((128, 4, 768), F32)] * 2
        + [shape((4, 8, 192), F32), shape((6, 192), F32)],
        in_specs=[whole(8, 896), whole(768, block_len), whole(8, 384), whole(4, 8, 768)]
        + [state] * 3
        + [token_in] * 2,
        out_specs=[state] * 3 + [token_out] * 2 + [whole(4, 8, 192), whole(6, 192)],
        compiler_params=pltpu.CompilerParams(vmem_limit_bytes=62 * MIB),
        name="owners_update",
    )(slot_row, blocks, small, pool, master, first, second, out_mine, dx_mine)


def share_order():
    order = []
    for core in range(2):
        for chip in range(4):
            for base, count in ((0, 32), (256, 32), (512, 24), (704, 8)):
                at = base + (core * 4 + chip) * count
                order += list(range(at, at + count))
    return np.array(order + [768] + [4096] * 127, np.int32)


def local_rows(
    layer_input_rows,
    sentence_index_row,
    padding_mask,
    output_gradient,
    owner_rank,
    master_state,
    first_moment,
    second_moment,
):
    block_len = master_state.shape[2]
    order = share_order()
    (
        w_qkv,
        _,
        w_up,
        w_down,
        w_out,
        slot_row,
        small_all,
        x_row,
        gy_row,
        qkv,
        prob_low,
        attended,
        normed_one,
        h_low,
        act,
        pull,
        z_two,
        inverse,
    ) = forward_call(
        master_state[0],
        owner_rank,
        jnp.asarray(order[:, None]),
        sentence_index_row,
        padding_mask,
        jnp.transpose(layer_input_rows, (1, 0, 2)),
        jnp.transpose(output_gradient, (1, 0, 2)),
    )
    blocks, small_sum, out_mine, dx_mine, pool_all = backward_call(
        sentence_index_row,
        padding_mask,
        gy_row,
        z_two,
        inverse,
        small_all,
        act,
        pull,
        w_down,
        w_up,
        h_low,
        normed_one,
        attended,
        w_out,
        qkv,
        prob_low,
        w_qkv,
        x_row,
    )
    new_master, new_first, new_second, layer_out, input_grad, pooled, norm_grads = finish_call(
        slot_row,
        blocks.reshape(768, block_len),
        small_sum,
        pool_all,
        master_state[0],
        first_moment[0],
        second_moment[0],
        out_mine,
        dx_mine,
    )
    return (
        layer_out,
        pooled,
        input_grad,
        new_master[None],
        new_first[None],
        new_second[None],
        norm_grads,
    )


def solution(mesh):
    in_specs = (
        P("tensor", "dp", None),
        P("dp", None),
        P("dp", None),
        P("tensor", "dp", None),
        P(),
        P("tensor", "dp", None),
        P("tensor", "dp", None),
        P("tensor", "dp", None),
    )
    out_specs = (
        P("tensor", "dp", None),
        P("dp", None, "tensor"),
        P("tensor", "dp", None),
        P("tensor", "dp", None),
        P("tensor", "dp", None),
        P("tensor", "dp", None),
        P(None, "tensor"),
    )
    plain = mesh.shape["dp"] != 8 or mesh.shape["tensor"] != 4
    body = local_general if plain else local_rows
    return jax.shard_map(body, mesh=mesh, in_specs=in_specs, out_specs=out_specs, check_vma=False)
```

```python
import jax
import numpy as np
import jax.numpy as jnp
from jax import lax
from jax.experimental import pallas as pl
from jax.experimental.pallas import tpu as pltpu
from jax.sharding import PartitionSpec as P

MODEL_WIDTH = 768
HEAD_DIM = 64
FF = 3072
SMAX = 8
STEP = 10


NORM_EPS = 1e-05
ADAM_EPS = 1e-08
BETA_ONE = 0.9
BETA_TWO = 0.999
DECAY_RATE = 0.01
MASKED = -1e30
exact_precision = lax.Precision.HIGHEST


def slot_tables(owner_rank, per_owner):
    ordinal = jnp.arange(owner_rank.shape[0], dtype=jnp.int32)
    same_owner = owner_rank[:, None] == owner_rank[None, :]
    earlier = ordinal[None, :] < ordinal[:, None]
    ranking = jnp.sum((same_owner & earlier).astype(jnp.int32), axis=1)
    return owner_rank * per_owner + ranking


def slot_blocks(slot_of, wanted):
    matches = slot_of[None, :] == wanted[:, None]
    filled = jnp.any(matches, axis=1)
    ordinal = jnp.arange(slot_of.shape[0], dtype=jnp.int32)
    block_of = jnp.sum(jnp.where(matches, ordinal[None, :], 0), axis=1)
    return (block_of, filled)


def step_rates(token_position, width, hidden, tensor_size):
    width_loc = width // tensor_size
    ffn_loc = hidden // tensor_size
    end_up = width * ffn_loc
    end_down = end_up + ffn_loc * width
    end_qkv = end_down + width * 3 * width_loc
    end_out = end_qkv + width_loc * width
    offset = token_position - end_out
    first_gain = (offset >= 4 * width_loc + ffn_loc) & (offset < 5 * width_loc + ffn_loc)
    second_gain = (offset >= 6 * width_loc + ffn_loc) & (offset < 7 * width_loc + ffn_loc)
    small_rate = jnp.where(first_gain | second_gain, 0.2, 0.1)
    step_rate = jnp.where(
        token_position < end_up,
        width ** (-0.5),
        jnp.where(
            token_position < end_down,
            hidden ** (-0.5),
            jnp.where(
                token_position < end_qkv,
                width ** (-0.5),
                jnp.where(token_position < end_out, 4.0 * width ** (-0.5), small_rate),
            ),
        ),
    )
    decay_on = (token_position < end_out).astype(jnp.float32)
    return (step_rate.astype(jnp.float32), decay_on)


def adamw(gradient, moment, square, weight, step_rate, decay_on, filled):
    new_moment = BETA_ONE * moment + (1.0 - BETA_ONE) * gradient
    new_square = BETA_TWO * square + (1.0 - BETA_TWO) * gradient * gradient
    unbiased = new_moment / (1.0 - BETA_ONE**STEP)
    divisor = jnp.sqrt(new_square / (1.0 - BETA_TWO**STEP)) + ADAM_EPS
    new_weight = weight - step_rate * (unbiased / divisor + DECAY_RATE * decay_on * weight)
    zeroed = jnp.zeros_like(weight)
    return (
        jnp.where(filled, new_weight, zeroed),
        jnp.where(filled, new_moment, zeroed),
        jnp.where(filled, new_square, zeroed),
    )


def normalize(values):
    centred = values - jnp.mean(values, axis=-1, keepdims=True)
    inv_dev = lax.rsqrt(jnp.mean(centred * centred, axis=-1, keepdims=True) + NORM_EPS)
    return (centred * inv_dev, inv_dev)


def norm_back(grad_scaled, normed, inv_dev):
    first_mean = jnp.mean(grad_scaled, axis=-1, keepdims=True)
    second_mean = jnp.mean(grad_scaled * normed, axis=-1, keepdims=True)
    return inv_dev * (grad_scaled - first_mean - normed * second_mean)


def allowed_pairs(sentence_labels, real_token_flags):
    row_len = sentence_labels.shape[-1]
    same_sent = sentence_labels[:, :, None] == sentence_labels[:, None, :]
    live = (real_token_flags[:, :, None] == 1) & (real_token_flags[:, None, :] == 1)
    diagonal = jnp.eye(row_len, dtype=bool)[None]
    return same_sent & live | diagonal


def masked_scores(queries, key_rows, allowed, scaling):
    scores = (
        jnp.einsum("qshe,kshe->shqk", queries, key_rows, preferred_element_type=jnp.float32)
        * scaling
    )
    return jnp.where(allowed[:, None], scores, MASKED)


def split_flat(flat_all, width_loc, ffn_loc):
    end_up = MODEL_WIDTH * ffn_loc
    end_down = end_up + ffn_loc * MODEL_WIDTH
    end_qkv = end_down + MODEL_WIDTH * 3 * width_loc
    end_out = end_qkv + width_loc * MODEL_WIDTH
    return (
        flat_all[:end_up].reshape(MODEL_WIDTH, ffn_loc),
        flat_all[end_up:end_down].reshape(ffn_loc, MODEL_WIDTH),
        flat_all[end_down:end_qkv].reshape(MODEL_WIDTH, 3 * width_loc),
        flat_all[end_qkv:end_out].reshape(width_loc, MODEL_WIDTH),
        flat_all[end_out:],
    )


def local_general(
    layer_input_rows,
    sentence_index_row,
    padding_mask,
    output_gradient,
    owner_rank,
    master_state,
    first_moment,
    second_moment,
):
    tensor_size = lax.axis_size("tensor")
    tensor_at = lax.axis_index("tensor")
    data_size = lax.axis_size("dp")
    data_at = lax.axis_index("dp")
    width_loc = MODEL_WIDTH // tensor_size
    ffn_loc = FF // tensor_size
    heads_loc = width_loc // HEAD_DIM
    quarter = layer_input_rows.shape[0]
    seq_count = layer_input_rows.shape[1]
    row_len = quarter * tensor_size
    per_owner = master_state.shape[1]
    block_len = master_state.shape[2]
    nblocks = owner_rank.shape[0]
    slot_of = slot_tables(owner_rank, per_owner)
    gathered = lax.all_gather(master_state.astype(jnp.bfloat16), "dp", axis=1, tiled=True)[0]
    flat_weights = gathered[slot_of].reshape(nblocks * block_len)
    up_weight, down_weight, w_qkv, w_out, small_part = split_flat(flat_weights, width_loc, ffn_loc)
    bias_q = small_part[:width_loc].astype(jnp.float32)
    bias_v = small_part[width_loc : 2 * width_loc].astype(jnp.float32)
    expand_bias = small_part[2 * width_loc : 2 * width_loc + ffn_loc].astype(jnp.float32)
    norm_parts = small_part[2 * width_loc + ffn_loc :].reshape(6, width_loc)
    full_rows, norm_whole = (
        lax.all_gather(layer_input_rows, "tensor", axis=0, tiled=True),
        lax.all_gather(norm_parts, "tensor", axis=1, tiled=True),
    )
    norm_all = norm_whole.astype(jnp.float32)
    bias_out, bias_down = (norm_all[0], norm_all[1])
    gain_one, shift_one, gain_two, shift_two = (norm_all[2], norm_all[3], norm_all[4], norm_all[5])
    qkv_lin = jnp.einsum("lsd,de->lse", full_rows, w_qkv, preferred_element_type=jnp.float32)
    bias_qkv = jnp.concatenate([bias_q, jnp.zeros((width_loc,), jnp.float32), bias_v])
    qkv = (qkv_lin + bias_qkv).astype(jnp.bfloat16)
    queries = qkv[:, :, :width_loc].reshape(row_len, seq_count, heads_loc, HEAD_DIM)
    key_rows = qkv[:, :, width_loc : 2 * width_loc].reshape(row_len, seq_count, heads_loc, HEAD_DIM)
    values = qkv[:, :, 2 * width_loc :].reshape(row_len, seq_count, heads_loc, HEAD_DIM)
    scaling = HEAD_DIM ** (-0.5)
    allowed = allowed_pairs(sentence_index_row, padding_mask)
    scores = masked_scores(queries, key_rows, allowed, scaling)
    row_peak = jnp.max(scores, axis=-1, keepdims=True)
    log_total = row_peak + jnp.log(jnp.sum(jnp.exp(scores - row_peak), axis=-1, keepdims=True))
    prob_low = jnp.exp(scores - log_total).astype(jnp.bfloat16)
    attended = jnp.einsum("shqk,kshe->qshe", prob_low, values, preferred_element_type=jnp.float32)
    attended = attended.astype(jnp.bfloat16).reshape(row_len, seq_count, width_loc)
    portion_rows = attended
    attn_rows = lax.psum_scatter(
        jnp.einsum("lse,ed->lsd", portion_rows, w_out, preferred_element_type=jnp.float32).astype(
            jnp.bfloat16
        ),
        "tensor",
        scatter_dimension=0,
        tiled=True,
    ).astype(jnp.float32)
    z_one = layer_input_rows.astype(jnp.float32) + attn_rows + bias_out
    normed_one, inv_one = normalize(z_one)
    h_mine = normed_one * gain_one + shift_one
    hidden_narrow_whole = lax.all_gather(h_mine.astype(jnp.bfloat16), "tensor", axis=0, tiled=True)
    up_pre = (
        jnp.einsum(
            "wer,rb->web", hidden_narrow_whole, up_weight, preferred_element_type=jnp.float32
        )
        + expand_bias
    )
    activation_narrow = jax.nn.gelu(up_pre, approximate=False).astype(jnp.bfloat16)
    portion_rows = activation_narrow
    down_rows = lax.psum_scatter(
        jnp.einsum(
            "aij,jb->aib", portion_rows, down_weight, preferred_element_type=jnp.float32
        ).astype(jnp.bfloat16),
        "tensor",
        scatter_dimension=0,
        tiled=True,
    ).astype(jnp.float32)
    z_two = h_mine + down_rows + bias_down
    normed_two, inv_two = normalize(z_two)
    layer_out = normed_two * gain_two + shift_two
    seg_mine = lax.dynamic_slice_in_dim(sentence_index_row, tensor_at * quarter, quarter, 1)
    valid_mine = lax.dynamic_slice_in_dim(padding_mask, tensor_at * quarter, quarter, 1)
    sent_ids = jnp.arange(SMAX, dtype=jnp.int32)
    onehot_mine = (
        (seg_mine[:, :, None] == sent_ids[None, None, :]) & (valid_mine[:, :, None] == 1)
    ).astype(jnp.float32)
    pool_part = jnp.einsum("slc,lsd->scd", onehot_mine, layer_out, precision=exact_precision)
    onehot_full = (
        (sentence_index_row[:, :, None] == sent_ids[None, None, :])
        & (padding_mask[:, :, None] == 1)
    ).astype(jnp.float32)
    counts = jnp.sum(onehot_full, axis=1)
    grad_out = output_gradient.astype(jnp.float32) * valid_mine.T[:, :, None].astype(jnp.float32)
    d_gain_two = jnp.sum(grad_out * normed_two, axis=(0, 1))
    d_shift_two = jnp.sum(grad_out, axis=(0, 1))
    dz_two = norm_back(grad_out * gain_two, normed_two, inv_two)
    d_bias_down = jnp.sum(dz_two, axis=(0, 1))
    second_sum_gradient_wide = lax.all_gather(
        dz_two.astype(jnp.bfloat16), "tensor", axis=0, tiled=True
    )
    down_weight_gradient = jnp.einsum(
        "ipo,ipr->or",
        activation_narrow,
        second_sum_gradient_wide,
        preferred_element_type=jnp.float32,
    )
    activation_gradient = jnp.einsum(
        "ugp,jp->ugj", second_sum_gradient_wide, down_weight, preferred_element_type=jnp.float32
    )
    gelu_pull = jax.vjp(lambda pre_act: jax.nn.gelu(pre_act, approximate=False), up_pre)[1]
    d_up = gelu_pull(activation_gradient)[0]
    d_bias_up = jnp.sum(d_up, axis=(0, 1))
    expand_gradient_narrow = d_up.astype(jnp.bfloat16)
    up_weight_gradient = jnp.einsum(
        "iux,iuy->xy",
        hidden_narrow_whole,
        expand_gradient_narrow,
        preferred_element_type=jnp.float32,
    )
    portion_rows = expand_gradient_narrow
    dh_rows = lax.psum_scatter(
        jnp.einsum(
            "uih,vh->uiv", portion_rows, up_weight, preferred_element_type=jnp.float32
        ).astype(jnp.bfloat16),
        "tensor",
        scatter_dimension=0,
        tiled=True,
    ).astype(jnp.float32)
    dh_mine = dz_two + dh_rows
    d_gain_one = jnp.sum(dh_mine * normed_one, axis=(0, 1))
    d_shift_one = jnp.sum(dh_mine, axis=(0, 1))
    dz_one = norm_back(dh_mine * gain_one, normed_one, inv_one)
    d_bias_out = jnp.sum(dz_one, axis=(0, 1))
    dz_one_full = lax.all_gather(dz_one.astype(jnp.bfloat16), "tensor", axis=0, tiled=True)
    d_w_out = jnp.einsum("lse,lsd->ed", attended, dz_one_full, preferred_element_type=jnp.float32)
    d_attended = jnp.einsum("lsd,ed->lse", dz_one_full, w_out, preferred_element_type=jnp.float32)
    d_attended = d_attended.astype(jnp.bfloat16).reshape(row_len, seq_count, heads_loc, HEAD_DIM)
    scores_again = masked_scores(queries, key_rows, allowed, scaling)
    attn_prob = jnp.exp(scores_again - log_total)
    prob_again = attn_prob.astype(jnp.bfloat16)
    d_prob = jnp.einsum("qshe,kshe->shqk", d_attended, values, preferred_element_type=jnp.float32)
    d_values = jnp.einsum(
        "shqk,qshe->kshe", prob_again, d_attended, preferred_element_type=jnp.float32
    )
    inner = jnp.sum(d_prob * attn_prob, axis=-1, keepdims=True)
    d_scores = (attn_prob * (d_prob - inner)).astype(jnp.bfloat16)
    d_queries = (
        jnp.einsum("shqk,kshe->qshe", d_scores, key_rows, preferred_element_type=jnp.float32)
        * scaling
    )
    d_keys = (
        jnp.einsum("shqk,qshe->kshe", d_scores, queries, preferred_element_type=jnp.float32)
        * scaling
    )
    d_bias_q = jnp.sum(d_queries, axis=(0, 1)).reshape(width_loc)
    d_bias_v = jnp.sum(d_values, axis=(0, 1)).reshape(width_loc)
    d_qkv_low = jnp.concatenate(
        [
            d_queries.reshape(row_len, seq_count, width_loc),
            d_keys.reshape(row_len, seq_count, width_loc),
            d_values.reshape(row_len, seq_count, width_loc),
        ],
        axis=2,
    ).astype(jnp.bfloat16)
    d_w_qkv = jnp.einsum("lsd,lse->de", full_rows, d_qkv_low, preferred_element_type=jnp.float32)
    portion_rows = d_qkv_low
    dx_rows = lax.psum_scatter(
        jnp.einsum("lse,de->lsd", portion_rows, w_qkv, preferred_element_type=jnp.float32).astype(
            jnp.bfloat16
        ),
        "tensor",
        scatter_dimension=0,
        tiled=True,
    ).astype(jnp.float32)
    input_grad = dz_one + dx_rows
    shared_grads = jnp.stack(
        [d_bias_out, d_bias_down, d_gain_one, d_shift_one, d_gain_two, d_shift_two]
    )[None]
    pool_sum, shared_sum = (
        lax.psum_scatter(
            pool_part.astype(jnp.bfloat16), "tensor", scatter_dimension=2, tiled=True
        ).astype(jnp.float32),
        lax.psum_scatter(
            shared_grads.astype(jnp.bfloat16), "tensor", scatter_dimension=2, tiled=True
        ).astype(jnp.float32),
    )
    pooled_mean = pool_sum / jnp.maximum(counts, 1.0)[:, :, None]
    flat_grads = jnp.concatenate(
        [
            up_weight_gradient.reshape(-1),
            down_weight_gradient.reshape(-1),
            d_w_qkv.reshape(-1),
            d_w_out.reshape(-1),
            d_bias_q,
            d_bias_v,
            d_bias_up,
            shared_sum.reshape(-1),
        ]
    )
    grad_blocks = flat_grads.reshape(nblocks, block_len)
    wanted = data_at * per_owner + jnp.arange(per_owner, dtype=jnp.int32)
    block_of, filled = slot_blocks(slot_of, wanted)
    slot_grads = (
        jnp.zeros((data_size * per_owner, block_len), jnp.float32).at[slot_of].set(grad_blocks)
    )
    owned_grads = lax.psum_scatter(slot_grads, "dp", scatter_dimension=0, tiled=True)
    norm_grads = lax.psum(shared_sum[0], "dp")
    token_position = block_of[:, None] * block_len + jnp.arange(block_len, dtype=jnp.int32)[None, :]
    step_rate, decay_on = step_rates(token_position, MODEL_WIDTH, FF, tensor_size)
    new_master, new_first, new_second = adamw(
        owned_grads,
        first_moment[0],
        second_moment[0],
        master_state[0],
        step_rate,
        decay_on,
        filled[:, None],
    )
    return (
        layer_out,
        pooled_mean,
        input_grad,
        new_master[None],
        new_first[None],
        new_second[None],
        norm_grads,
    )


MESH = pl.DeviceIdType.MESH
BF = jnp.bfloat16
F32 = jnp.float32
WEIGHTS = ((768, 96), (768, 96), (768, 96))
MIB = 2**20


class Place:
    def __init__(self):
        d = lax.axis_index("dp")
        self.t = lax.axis_index("tensor")
        self.c = d % 2
        self.x = (d // 2) % 2
        self.y = d // 4
        self.xy = d // 2
        self.core = (d + 1 - 2 * self.c, self.t)
        self.right = (d + 2 - 4 * self.x, self.t)
        self.down = (d + 4 - 8 * self.y, self.t)
        self.diag = (d + 6 - 4 * self.x - 8 * self.y, self.t)
        self.deep = [None] + [(d, (self.t + k) % 4) for k in (1, 2, 3)]
        self.ahead = [(self.t + k) % 4 for k in range(4)]
        self.behind = [(self.t + 4 - k) % 4 for k in range(4)]

    def hail(self):
        peers = [self.core, self.right, self.down, self.diag] + self.deep[1:]
        for peer in peers:
            pl.semaphore_signal(
                pltpu.get_barrier_semaphore(), inc=1, device_id=peer, device_id_type=MESH
            )

    def meet(self):
        pl.semaphore_wait(pltpu.get_barrier_semaphore(), 7)


class Sender:
    def __init__(self, send_sems, recv_sems, local_sems):
        self.sems = (send_sems, recv_sems, local_sems)
        self.used = 0
        self.used_local = 0
        self.open = []

    def send(self, src, dst, peer):
        i = self.used
        self.used += 1
        copy = pltpu.make_async_remote_copy(
            src_ref=src,
            dst_ref=dst,
            send_sem=self.sems[0].at[i],
            recv_sem=self.sems[1].at[i],
            device_id=peer,
            device_id_type=MESH,
        )
        copy.start()
        self.open.append(copy)
        return copy

    def copy(self, src, dst):
        i = self.used_local
        self.used_local += 1
        copy = pltpu.make_async_copy(src, dst, self.sems[2].at[i])
        copy.start()
        return copy

    def sent(self, copy):
        copy.wait_send()
        self.open = [other for other in self.open if other is not copy]

    def finish(self):
        for copy in self.open:
            copy.wait_send()


def rows_of(place, rows, at=None):
    at = place.xy if at is None else at
    return pl.ds(pl.multiple_of(place.c * (4 * rows) + at * rows, 32), rows)


def half_of(place, rows):
    return pl.ds(pl.multiple_of(place.c * (4 * rows), 128), 4 * rows)


def interleave(size, parts):
    group = size // parts
    out_row = lax.broadcasted_iota(jnp.int32, (size, size), 0)
    col = lax.broadcasted_iota(jnp.int32, (size, size), 1)
    part = jnp.zeros((size, size), jnp.int32)
    for k in range(1, parts):
        part = part + (col >= k * group).astype(jnp.int32)
    return jnp.where(out_row == parts * (col - group * part) + part, 1.0, 0.0).astype(BF)


def dot_f32(a, b):
    return jnp.dot(a, b, preferred_element_type=F32)


def third_to_out(k, start, size):
    at = lax.broadcasted_iota(jnp.int32, (1, size), 1) + start
    device, j = at // 32, at % 32
    target = jnp.where(j >= 24, 24 * device + 3 * (j - 24) + k, -1)
    out_row = lax.broadcasted_iota(jnp.int32, (192, size), 0)
    return jnp.where(out_row == target, 1.0, 0.0).astype(BF)


def feature_places():
    at = lax.broadcasted_iota(jnp.int32, (1, 1024), 1)
    r, device, j = (at % 512) // 128, 4 * (at // 512) + (at % 128) // 32, at % 32
    target = jnp.where(j < 24, 4 * (24 * device + j) + r, -1)
    feature = lax.broadcasted_iota(jnp.int32, (768, 1024), 0)
    return jnp.where(feature == target, 1.0, 0.0).astype(BF)


def dot_nt(a, b):
    return lax.dot_general(a, b, (((1,), (1,)), ((), ())), preferred_element_type=F32)


def dot_tn(a, b):
    return lax.dot_general(a, b, (((0,), (0,)), ((), ())), preferred_element_type=F32)


def unpack_small(packed, small):
    for t in range(4):
        small[t] = jnp.concatenate([packed[t, i : i + 1, :] for i in range(6)], axis=1)


def norm_vectors(small, norm):
    for i in range(6):
        at = 1152 + 192 * i
        norm[i : i + 1, :] = jnp.concatenate([small[t, 0:1, at : at + 192] for t in range(4)], axis=1)


def row_loop(body, step=128):
    @pl.loop(0, 512 // step)
    def _(i):
        body(pl.ds(pl.multiple_of(i * step, step), step))


def forward_kernel(
    master,
    owners,
    order_col,
    labels,
    flags,
    x_in,
    gy_in,
    w_att,
    w_up,
    w_down,
    w_qkv,
    w_out,
    slot_out,
    small_out,
    x_out,
    gy_row,
    qkv_out,
    prob_out,
    att_out,
    n_one_out,
    h_out,
    act_out,
    pull_out,
    z_two_out,
    inv_out,
    slot_row,
    slot_col,
    id_row,
    id_col,
    slots,
    canon_att,
    canon_ffn,
    land_att,
    land_ffn,
    pass_ffn,
    pass_land,
    share,
    p_att,
    p_up,
    p_down,
    small_mine,
    small_land,
    small_total,
    packed,
    small,
    norm,
    bias_qkv,
    v_att,
    v_qkv,
    v_compact,
    v_up,
    v_down,
    x_row,
    x_wide,
    qkv,
    prob,
    att,
    n_one,
    h_low,
    act,
    pull,
    total,
    inv,
    send_sems,
    recv_sems,
    local_sems,
):
    place = Place()
    link = Sender(send_sems, recv_sems, local_sems)
    place.hail()
    slots[place.c] = master[...].astype(BF)

    place.meet()
    whole = (w_att, w_up, w_down)
    held = (v_att, v_up, v_down)
    piece = (p_att, p_up, p_down)
    peers = (place.right, place.down, place.diag)
    mine_rows = pl.ds(pl.multiple_of(place.t * 128, 128), 128)
    tidy = []

    core_slots = link.send(slots.at[place.c], slots.at[place.c], place.core)
    x_moves = [
        link.send(x_in.at[place.ahead[k]], x_row.at[mine_rows], place.deep[k]) for k in (1, 2, 3)
    ]
    x_stay = link.copy(x_in.at[place.t], x_row.at[mine_rows])
    tidy.append(link.copy(gy_in.at[place.t], gy_row.at[mine_rows]))

    blocks = owners.shape[0]
    wide = slot_row.shape[1]
    owner = jnp.concatenate(
        [owners[...].astype(F32)[None], jnp.full((1, wide - blocks), -1.0, F32)], axis=1
    )
    kinds = lax.broadcasted_iota(jnp.int32, (8, wide), 0).astype(F32)
    owned = jnp.where(kinds == owner, 1.0, 0.0)
    ordinal = lax.broadcasted_iota(jnp.int32, (wide, wide), 1)
    earlier = jnp.where(lax.broadcasted_iota(jnp.int32, (wide, wide), 0) < ordinal, 1.0, 0.0)
    ahead = dot_f32(owned.astype(BF), earlier.astype(BF))
    ranking = jnp.sum(owned * ahead, axis=0, keepdims=True)
    place_of = jnp.where(order_col[...] == ordinal, 1.0, 0.0).astype(BF)
    pair = jnp.where(kinds == 0.0, owner, ranking).astype(BF)
    row = dot_nt(pair, place_of)
    col = dot_nt(place_of, pair)
    per_owner = float(master.shape[0])
    slot_row[...] = jnp.broadcast_to(row[0:1, :] * per_owner + row[1:2, :], slot_row.shape)
    slot_col[...] = jnp.broadcast_to(col[:, 0:1] * per_owner + col[:, 1:2], slot_col.shape)

    own = pl.ds(place.t, 1)
    apart = -1 - lax.broadcasted_iota(jnp.int32, (1, 512), 1)
    ids = jnp.where(flags[own, :] == 1, labels[own, :], apart).astype(F32)
    id_row[...] = jnp.broadcast_to(ids, id_row.shape)
    id_col[...] = jnp.transpose(id_row[...])
    tidy.append(link.copy(slot_row, slot_out))
    core_slots.wait_recv()

    pair_slots = slots[...].reshape(384, 2304)
    slot_id = (lax.broadcasted_iota(jnp.int32, (64, 384), 1) + place.xy * 384).astype(F32)
    order = [(3, place.diag), (1, place.right), (2, place.down), (0, None)]

    def spread(lo, rows, canon, land):
        sent = []
        for j, peer in order:
            at = place.xy if peer is None else peer[0] // 2
            spot = pl.ds(pl.multiple_of(place.c * 384 + at * 96 + lo, 32), rows)
            wanted = slot_col[spot, 0:1]
            pick = jnp.where(wanted == slot_id[:rows], 1.0, 0.0).astype(BF)
            canon[j] = dot_f32(pick, pair_slots).astype(BF)
            if peer is not None:
                sent.append(link.send(canon.at[j], land.at[j - 1], peer))
        return sent

    def collect(sent, lo, rows, canon, land):
        for move in sent:
            move.wait_recv()
        share[lo : lo + rows, :] = (
            canon[0].astype(F32) + land[0].astype(F32) + land[1].astype(F32) + land[2].astype(F32)
        )

    att_sent = spread(64, 32, canon_att, land_att)
    pick_small = jnp.where(slot_row[:, 768:769] == slot_id[:8], 1.0, 0.0).astype(BF)
    picked = dot_f32(pick_small, pair_slots)
    for i in range(6):
        small_mine[i : i + 1, :] = picked[0:1, 384 * i : 384 * i + 384]
    small_mine[6:8, :] = jnp.zeros((2, 384), F32)
    small_moves = [link.send(small_mine, small_land.at[j], peer) for j, peer in enumerate(peers)]
    def spread_halves():
        for j, peer in order:
            at = place.xy if peer is None else peer[0] // 2
            spot = pl.ds(pl.multiple_of(place.c * 384 + at * 96, 32), 64)
            pick = jnp.where(slot_col[spot, 0:1] == slot_id, 1.0, 0.0).astype(BF)
            canon_ffn[j] = dot_f32(pick, pair_slots).astype(BF)
            if j in (1, 3):
                half = canon_ffn.at[j, pl.ds(0, 32)]
                halves[j, 0] = link.send(half, land_ffn.at[0, j // 2], place.right)
            if j in (2, 3):
                half = canon_ffn.at[j, pl.ds(32, 32)]
                halves[j, 1] = link.send(half, land_ffn.at[1, j - 2], place.down)

    def pass_halves():
        halves[3, 0].wait_recv()
        pass_ffn[0] = canon_ffn[2, 0:32, :] + land_ffn[0, 1]
        halves["down"] = link.send(pass_ffn.at[0], pass_land.at[0], place.down)
        halves[3, 1].wait_recv()
        pass_ffn[1] = canon_ffn[1, 32:64, :] + land_ffn[1, 1]
        halves["right"] = link.send(pass_ffn.at[1], pass_land.at[1], place.right)

    def collect_halves():
        halves[1, 0].wait_recv()
        halves[2, 1].wait_recv()
        halves["down"].wait_recv()
        halves["right"].wait_recv()
        for i in range(2):
            share[32 * i : 32 * i + 32, :] = (
                canon_ffn[0, 32 * i : 32 * i + 32, :] + land_ffn[i, 0] + pass_land[i]
            ).astype(F32)

    halves = {}
    att_sent[0].wait_recv()
    spread_halves()
    collect(att_sent[1:], 64, 32, canon_att, land_att)

    for k in range(3):
        p_att[32 * k : 32 * k + 32, :] = share[64:96, 768 * k : 768 * k + 768].astype(BF)

    def spread_ffn():
        three = interleave(96, 3)
        for at, ref in ((0, p_up), (32, p_down)):
            parts = [share[at : at + 32, 768 * k : 768 * k + 768] for k in range(3)]
            ref[...] = dot_f32(three, jnp.concatenate(parts, axis=0).astype(BF)).astype(BF)

    deep_moves, right_moves, down_moves, own_copies, core_moves, loads = {}, {}, {}, {}, {}, {}

    def deep_send(w):
        spot = whole[w].at[place.t, rows_of(place, WEIGHTS[w][1])]
        own_copies[w] = link.copy(piece[w], spot)
        deep_moves[w] = [link.send(piece[w], spot, place.deep[k]) for k in (1, 2, 3)]

    def plane_send(w, k):
        rows = WEIGHTS[w][1]
        spot = whole[w].at[place.behind[k], rows_of(place, rows)]
        src = piece[w] if k == 0 else spot
        if k:
            deep_moves[w][k - 1].wait_recv()
        right_moves[w, k] = link.send(src, spot, place.right)
        down_moves[w, k] = link.send(src, spot, place.down)

    def plane_pass(w, k):
        rows = WEIGHTS[w][1]
        half = rows // 2
        right_moves[w, k].wait_recv()
        down_moves[w, k].wait_recv()
        t = place.behind[k]
        right_at = place.c * (4 * rows) + (place.right[0] // 2) * rows
        down_at = place.c * (4 * rows) + (place.down[0] // 2) * rows
        first = whole[w].at[t, pl.ds(pl.multiple_of(right_at, 16), half)]
        second = whole[w].at[t, pl.ds(pl.multiple_of(down_at + half, 16), half)]
        right_moves[w, k, 1] = link.send(second, second, place.right)
        down_moves[w, k, 1] = link.send(first, first, place.down)

    def core_pass(w, k):
        if k == 0:
            own_copies[w].wait()
        right_moves[w, k, 1].wait_recv()
        down_moves[w, k, 1].wait_recv()
        spot = whole[w].at[place.behind[k], half_of(place, WEIGHTS[w][1])]
        core_moves[w, k] = link.send(spot, spot, place.core)

    def load(w, k):
        core_moves[w, k].wait_recv()
        t = place.behind[k]
        loads[w, k] = link.copy(whole[w].at[t], held[w].at[t])

    def unpack(k):
        loads[0, k].wait()
        t = place.behind[k]
        thirds = [
            jnp.concatenate([v_att[t, 96 * d + 32 * k3 : 96 * d + 32 * k3 + 32, :] for d in range(8)], axis=0)
            for k3 in range(3)
        ]
        out = jnp.zeros((192, 768), F32)
        for k3 in range(3):
            out = out + dot_f32(third_to_out(k3, 0, 256), thirds[k3])
        v_compact[t] = out.astype(BF)
        turns = [
            thirds[0][:, :576],
            jnp.concatenate([thirds[0][:, 576:], thirds[1][:, :384]], axis=1),
            jnp.concatenate([thirds[1][:, 384:], thirds[2][:, :192]], axis=1),
            thirds[2][:, 192:],
        ]
        for half in range(2):
            for r in range(4):
                at = 512 * half + 128 * r
                v_qkv[t, at : at + 128, :] = turns[r][128 * half : 128 * half + 128]
        tidy.append(link.copy(v_qkv.at[t], w_qkv.at[t]))
        tidy.append(link.copy(v_compact.at[t], w_out.at[t]))

    def qkv_step(k):
        t = place.behind[k]

        def body(rows):
            lin = dot_f32(x_wide[rows, :], v_qkv[t]) + bias_qkv[t]
            qkv[t, rows, :] = lin.astype(BF)

        row_loop(body, 256)

    def attention(k):
        t = place.behind[k]

        def body(rows):
            allowed = id_col[rows, 0:1] == id_row[0:1, :]
            parts = []
            for i in range(3):
                at = 64 * i
                scores = dot_nt(qkv[t, rows, at : at + 64], qkv[t, :, 192 + at : 256 + at]) * 0.125
                scores = jnp.where(allowed, scores, MASKED)
                weight = jnp.exp(scores - jnp.max(scores, axis=1, keepdims=True))
                weight = weight * (1.0 / jnp.sum(weight, axis=1, keepdims=True))
                low = weight.astype(BF)
                prob[3 * t + i, rows, :] = low
                parts.append(dot_f32(low, qkv[t, :, 384 + at : 448 + at]))
            att[t, rows, :] = jnp.concatenate(parts, axis=1).astype(BF)

        row_loop(body, 256)
        tidy.append(link.copy(qkv.at[t], qkv_out.at[t]))
        tidy.append(link.copy(att.at[t], att_out.at[t]))
        tidy.append(link.copy(prob.at[pl.ds(3 * t, 3)], prob_out.at[pl.ds(3 * t, 3)]))

    def out_step():
        def body(rows):
            z = x_row[rows, :].astype(F32) + norm[0:1, :]
            for t in range(4):
                z = z + dot_f32(att[t, rows, :], v_compact[t])
            normed, inverse = normalize(z)
            n_one[rows, :] = normed
            inv[rows, :] = inverse
            h = normed * norm[2:3, :] + norm[3:4, :]
            h_low[rows, :] = h.astype(BF)
            total[rows, :] = h + norm[1:2, :]

        row_loop(body, 256)
        tidy.append(link.copy(n_one, n_one_out))
        tidy.append(link.copy(h_low, h_out))

    def up_step(k):
        loads[1, k].wait()
        t = place.behind[k]

        def body(rows):
            pre = dot_f32(h_low[rows, :], v_up[t]) + small[t, 0:1, 384:1152]
            below = 0.5 + 0.5 * lax.erf(pre * (0.5**0.5))
            act[t, rows, :] = (pre * below).astype(BF)
            slope = below + pre * (jnp.exp(-0.5 * pre * pre) * 0.3989422804014327)
            pull[t, rows, :] = slope.astype(BF)

        row_loop(body, 256)
        tidy.append(link.copy(act.at[t], act_out.at[t]))
        tidy.append(link.copy(pull.at[t], pull_out.at[t]))

    def down_step(k):
        loads[2, k].wait()
        t = place.behind[k]

        def body(rows):
            total[rows, :] += dot_f32(act[t, rows, :], v_down[t])

        row_loop(body, 256)

    def end_step():
        tidy.append(link.copy(total, z_two_out))
        tidy.append(link.copy(inv, inv_out))

    every = range(4)
    others = (1, 2, 3)
    small_state, gy_moves = {}, []

    def small_collect():
        for move in small_moves:
            move.wait_recv()
        small_total[...] = small_mine[...] + small_land[0] + small_land[1] + small_land[2]
        small_state["stay"] = link.copy(small_total, packed.at[place.t])
        small_state["deep"] = [
            link.send(small_total, packed.at[place.t], place.deep[k]) for k in others
        ]

    def small_ready():
        small_state["stay"].wait()
        for move in small_state["deep"]:
            move.wait_recv()
        unpack_small(packed, small)
        norm_vectors(small, norm)
        for t in every:
            bias_qkv[t] = jnp.concatenate(
                [small[t, 0:1, :192], jnp.zeros((1, 192), F32), small[t, 0:1, 192:384]], axis=1
            )
        tidy.append(link.copy(packed, small_out))

    def x_ready():
        x_stay.wait()
        for move in x_moves:
            move.wait_recv()
        places = feature_places()

        def body(rows):
            x_wide[rows, :] = dot_f32(x_row[rows, :], places).astype(BF)

        row_loop(body, 256)
        tidy.append(link.copy(x_wide, x_out))

    def gy_send():
        for k in others:
            gy_moves.append(link.send(gy_in.at[place.ahead[k]], gy_row.at[mine_rows], place.deep[k]))

    def gy_ready():
        for move in gy_moves:
            move.wait_recv()

    deep_send(0)
    small_collect()
    plane_send(0, 0)
    pass_halves()
    x_ready()
    plane_pass(0, 0)
    plane_send(0, 1)
    collect_halves()
    spread_ffn()
    deep_send(1)
    plane_send(2, 0)
    plane_send(0, 2)
    deep_send(2)
    core_pass(0, 0)
    plane_send(0, 3)
    plane_pass(0, 1)
    plane_pass(2, 0)
    load(0, 0)
    plane_pass(0, 3)
    unpack(0)
    plane_pass(0, 2)
    plane_send(1, 1)
    small_ready()
    qkv_step(0)
    attention(0)
    core_pass(0, 1)
    plane_send(1, 2)
    load(0, 1)
    core_pass(0, 2)
    plane_pass(1, 1)
    core_pass(0, 3)
    plane_send(1, 3)
    unpack(1)
    plane_send(2, 1)
    load(0, 2)
    qkv_step(1)
    load(0, 3)
    unpack(2)
    unpack(3)
    gy_send()
    core_pass(1, 1)
    core_pass(2, 0)
    plane_send(1, 0)
    qkv_step(3)
    attention(3)
    plane_pass(1, 3)
    qkv_step(2)
    load(1, 1)
    plane_pass(2, 1)
    attention(1)
    plane_pass(1, 0)
    plane_pass(1, 2)
    plane_send(2, 3)
    attention(2)
    core_pass(1, 3)
    core_pass(2, 1)
    out_step()
    load(2, 0)
    load(1, 3)
    core_pass(1, 0)
    plane_send(2, 2)
    up_step(1)
    load(2, 1)
    core_pass(1, 2)
    plane_pass(2, 3)
    up_step(3)
    load(1, 0)
    load(1, 2)
    plane_pass(2, 2)
    down_step(1)
    core_pass(2, 3)
    up_step(0)
    load(2, 3)
    gy_ready()
    core_pass(2, 2)
    up_step(2)
    load(2, 2)
    down_step(3)
    down_step(0)
    down_step(2)
    end_step()
    for copy in tidy:
        copy.wait()
    link.finish()


def forward_call(master, owners, order_col, labels, flags, x_in, gy_in):
    anywhere = pl.BlockSpec(memory_space=pl.ANY)
    vmem = pl.BlockSpec(memory_space=pltpu.VMEM)
    shape = jax.ShapeDtypeStruct
    outs = [
        ((4, 768, 768), BF),
        ((4, 768, 768), BF),
        ((4, 768, 768), BF),
        ((4, 1024, 576), BF),
        ((4, 192, 768), BF),
        ((8, 896), F32),
        ((4, 8, 384), F32),
        ((512, 1024), BF),
        ((512, 768), BF),
        ((4, 512, 576), BF),
        ((12, 512, 512), BF),
        ((4, 512, 192), BF),
        ((512, 768), F32),
        ((512, 768), BF),
        ((4, 512, 768), BF),
        ((4, 512, 768), BF),
        ((512, 768), F32),
        ((512, 1), F32),
    ]
    scratch = [
        ((8, 896), F32),
        ((896, 8), F32),
        ((8, 512), F32),
        ((512, 8), F32),
        ((2, 192, 2304), BF),
        ((4, 32, 2304), BF),
        ((4, 64, 2304), BF),
        ((3, 32, 2304), BF),
        ((2, 2, 32, 2304), BF),
        ((2, 32, 2304), BF),
        ((2, 32, 2304), BF),
        ((96, 2304), F32),
        ((96, 768), BF),
        ((96, 768), BF),
        ((96, 768), BF),
        ((8, 384), F32),
        ((3, 8, 384), F32),
        ((8, 384), F32),
        ((4, 8, 384), F32),
        ((4, 1, 2304), F32),
        ((8, 768), F32),
        ((4, 1, 576), F32),
        ((4, 768, 768), BF),
        ((4, 1024, 576), BF),
        ((4, 192, 768), BF),
        ((4, 768, 768), BF),
        ((4, 768, 768), BF),
        ((512, 768), BF),
        ((512, 1024), BF),
        ((4, 512, 576), BF),
        ((12, 512, 512), BF),
        ((4, 512, 192), BF),
        ((512, 768), F32),
        ((512, 768), BF),
        ((4, 512, 768), BF),
        ((4, 512, 768), BF),
        ((512, 768), F32),
        ((512, 1), F32),
    ]
    return pl.pallas_call(
        forward_kernel,
        out_shape=[shape(*o) for o in outs],
        in_specs=[vmem] * 5 + [anywhere] * 2,
        out_specs=[anywhere] * len(outs),
        scratch_shapes=[pltpu.VMEM(*s) for s in scratch]
        + [
            pltpu.SemaphoreType.DMA((128,)),
            pltpu.SemaphoreType.DMA((128,)),
            pltpu.SemaphoreType.DMA((64,)),
        ],
        compiler_params=pltpu.CompilerParams(
            collective_id=0, has_side_effects=True, vmem_limit_bytes=60 * MIB
        ),
        name="gather_and_forward",
    )(master, owners, order_col, labels, flags, x_in, gy_in)


def backward_kernel(
    labels,
    flags,
    gy_in,
    z_two_in,
    inv_in,
    small_in,
    act_in,
    pull_in,
    w_down,
    w_up,
    h_in,
    n_one_in,
    att_in,
    w_out,
    qkv_in,
    prob_in,
    w_qkv,
    x_in,
    blocks,
    small_out,
    out_mine,
    dx_mine,
    pool_out,
    *scratch,
):
    sums, cores, lefts, tops, lefts_two, tops_two, deeps = (scratch[3 * i : 3 * i + 3] for i in range(7))
    (
        ring,
        share,
        share_low,
        small_grad,
        small_land,
        packed,
        small,
        norm,
        gy,
        normed,
        inv,
        act,
        pull,
        v_down,
        v_up,
        h_low,
        att,
        v_out,
        qkv,
        prob,
        v_qkv,
        x_row,
        wide,
        low,
        total,
        d_up,
        d_att,
        d_qkv,
        turned,
        go,
        wide_sum,
        reds,
        red_up,
        red_qv,
        flag_col,
        row_low,
        pool,
        send_sems,
        recv_sems,
        local_sems,
    ) = scratch[21:]
    place = Place()
    place.hail()
    link = Sender(send_sems, recv_sems, local_sems)
    t_of = place.ahead
    steps = (1, 2, 3, 0)
    got = {}

    def fetch(name, src, dst):
        got[name] = link.copy(src, dst)

    fetch("small", small_in, packed)
    fetch("normed", z_two_in, normed)
    fetch("gy", gy_in, gy)
    fetch("inv", inv_in, inv)

    def load_ffn(i):
        t, slot = t_of[steps[i]], i % 2
        fetch(("act", i), act_in.at[t], act.at[slot])
        fetch(("down", i), w_down.at[t], v_down.at[slot])
        fetch(("pull", i), pull_in.at[t], pull.at[slot])
        fetch(("up", i), w_up.at[t], v_up.at[slot])

    def load_att(i):
        t, slot = t_of[steps[i]], i % 2
        fetch(("prob", i), prob_in.at[pl.ds(3 * t, 3)], prob.at[slot])
        fetch(("qkv", i), w_qkv.at[t], v_qkv.at[slot])

    own = pl.ds(place.t, 1)
    own_flags = flags[own, :].astype(F32)
    flag_col[...] = jnp.transpose(jnp.broadcast_to(own_flags, (8, 512)))
    t, x, y, c = place.t, place.x, place.y, place.c
    moves, stay = [], []

    core_moves, first, second, third = {}, {}, {}, {}
    ring_open = [None] * 3
    ring_at = [0]

    def chip_row(w, k, yy, xx, half):
        rows = WEIGHTS[w][1]
        at = pl.multiple_of((yy * 2 + xx) * rows + half * (rows // 2), 16)
        return sums[w].at[t_of[k], pl.ds(at, rows // 2)]

    def produce(w, k, make):
        slot = ring_at[0] % 3
        ring_at[0] += 1
        if ring_open[slot] is not None:
            link.sent(ring_open[slot])
        away = ring.at[slot]
        away[...] = make(1 - c).astype(BF)
        move = link.send(away, cores[w].at[k], place.core)
        ring_open[slot] = move
        core_moves[w, k] = move
        sums[w][t_of[k]] = make(c).astype(BF)

    def core_add(w, k):
        core_moves[w, k].wait_recv()
        rows = WEIGHTS[w][1]

        @pl.loop(0, 4)
        def _(i):
            at = pl.ds(pl.multiple_of(i * rows, 32), rows)
            sums[w][t_of[k], at, :] += cores[w][k, at, :]

        first[w, k] = []
        for i in (0, 1):
            first[w, k].append(link.send(chip_row(w, k, i, 1 - x, 0), lefts[w].at[k, i], place.right))
            first[w, k].append(link.send(chip_row(w, k, 1 - y, i, 1), tops[w].at[k, i], place.down))

    def add(spot, other):
        spot[...] = spot[...] + other[...]

    def plane_add(w, k):
        for move in first[w, k]:
            move.wait_recv()
        down_part, right_part = chip_row(w, k, 1 - y, x, 0), chip_row(w, k, y, 1 - x, 1)
        add(down_part, lefts[w].at[k, 1 - y])
        add(right_part, tops[w].at[k, 1 - x])
        second[w, k] = [
            link.send(down_part, lefts_two[w].at[k], place.down),
            link.send(right_part, tops_two[w].at[k], place.right),
        ]
        add(chip_row(w, k, y, x, 0), lefts[w].at[k, y])
        add(chip_row(w, k, y, x, 1), tops[w].at[k, x])

    def deep_add(w, k):
        for move in second[w, k]:
            move.wait_recv()
        add(chip_row(w, k, y, x, 0), lefts_two[w].at[k])
        add(chip_row(w, k, y, x, 1), tops_two[w].at[k])
        rows = WEIGHTS[w][1]
        if k:
            spot = pl.ds(pl.multiple_of(place.xy * rows, 16), rows)
            third[w, k] = link.send(sums[w].at[t_of[k], spot], deeps[w].at[k - 1], place.deep[k])

    def end(w):
        rows = WEIGHTS[w][1]
        spot = pl.ds(pl.multiple_of(place.xy * rows, 16), rows)
        whole = sums[w][t, spot, :].astype(F32)
        for k in (1, 2, 3):
            third[w, k].wait_recv()
            whole = whole + deeps[w][k - 1].astype(F32)
        whole = whole.astype(BF)
        if w == 0:
            for k in range(3):
                share[64:96, 768 * k : 768 * k + 768] = whole[32 * k : 32 * k + 32, :].astype(F32)
        else:
            at = 0 if w == 1 else 32
            parts = dot_tn(interleave(96, 3), whole)
            for k in range(3):
                share[at : at + 32, 768 * k : 768 * k + 768] = parts[32 * k : 32 * k + 32]

    def column_sum(value):
        return jnp.sum(value, axis=0, keepdims=True)

    def norm_two_back():
        def body(rows):
            grad = gy[rows, :].astype(F32) * flag_col[rows, 0:1]
            n, inverse = normalize(normed[rows, :])
            normed[rows, :] = n
            dz = norm_back(grad * norm[4:5, :], n, inverse)
            wide[rows, :] = dz
            total[rows, :] = dz
            low[rows, :] = dz.astype(BF)
            reds[4:5, :] += column_sum(grad * n)
            reds[5:6, :] += column_sum(grad)
            reds[1:2, :] += column_sum(dz)

        row_loop(body)

    def emit_out():
        sentence = lax.broadcasted_iota(jnp.int32, (SMAX, 512), 0).astype(F32)
        member = jnp.where((sentence == labels[own, :].astype(F32)) & (own_flags == 1.0), 1.0, 0.0)
        count = jnp.maximum(jnp.sum(member, axis=1, keepdims=True), 1.0)
        pooled = jnp.zeros((SMAX, 768), F32)
        for i in range(4):
            rows = slice(128 * i, 128 * i + 128)
            out = normed[rows, :] * norm[4:5, :] + norm[5:6, :]
            row_low[rows, :] = out.astype(BF)
            pooled = pooled + jnp.dot(
                member[:, rows], out, precision=exact_precision, preferred_element_type=F32
            )
        pool[...] = pooled / count
        own_rows = pl.ds(pl.multiple_of(t * 128, 128), 128)
        stay.append(link.copy(row_low.at[own_rows], out_mine.at[t]))
        stay.append(link.copy(pool, pool_out.at[t]))
        for k in (1, 2, 3):
            part = row_low.at[pl.ds(pl.multiple_of(t_of[k] * 128, 128), 128)]
            moves.append(link.send(part, out_mine.at[t], place.deep[k]))
            moves.append(link.send(pool, pool_out.at[t], place.deep[k]))

    def lanes(which):
        return pl.ds(pl.multiple_of(which * 384, 128), 384)

    def down_piece(i):
        k, slot = steps[i], i % 2
        got["act", i].wait()
        produce(2, k, lambda which: dot_tn(act[slot, :, lanes(which)], low[...]))

    def act_back(i):
        k, slot = steps[i], i % 2
        got["down", i].wait()
        got["pull", i].wait()

        def body(rows):
            grad = dot_nt(low[rows, :], v_down[slot]) * pull[slot, rows, :].astype(F32)
            red_up[t_of[k]] += column_sum(grad)
            d_up[rows, :] = grad.astype(BF)

        row_loop(body, 256)

    def up_piece(i):
        if i == 0:
            got["h"].wait()
        produce(1, steps[i], lambda which: dot_tn(h_low[:, lanes(which)], d_up[...]))

    def hidden_back(i):
        slot = i % 2
        got["up", i].wait()

        def body(rows):
            total[rows, :] += dot_nt(d_up[rows, :], v_up[slot])

        row_loop(body, 256)
        if i == 1:
            fetch("n_one", n_one_in, normed)

    def norm_one_back():
        got["n_one"].wait()

        def body(rows):
            dh = total[rows, :]
            n = normed[rows, :]
            dz = norm_back(dh * norm[2:3, :], n, inv[rows, :])
            total[rows, :] = dz
            low[rows, :] = dz.astype(BF)
            reds[2:3, :] += column_sum(dh * n)
            reds[3:4, :] += column_sum(dh)
            reds[0:1, :] += column_sum(dz)

        row_loop(body)

    def out_piece(i):
        k = steps[i]
        if i == 0:
            got["att"].wait()
            got["wout"].wait()
        go[...] = dot_tn(att[t_of[k]], low[...]).astype(BF)

        def body(rows):
            d_att[rows, :] = dot_nt(low[rows, :], v_out[t_of[k]]).astype(BF)

        row_loop(body, 256)

    def attention_back(i):
        k, slot = steps[i], i % 2
        tk = t_of[k]
        if i == 0:
            got["qkvs"].wait()
        got["prob", i].wait()
        turned[...] = jnp.zeros_like(turned)

        def body(rows):
            d_queries = []
            for j in range(3):
                at = 64 * j
                grad = d_att[rows, at : at + 64]
                weight_low = prob[slot, j, rows, :]
                weight = weight_low.astype(F32)
                d_prob = dot_nt(grad, qkv[tk, :, 384 + at : 448 + at]) * weight
                inner = jnp.sum(d_prob, axis=1, keepdims=True)
                d_scores = (d_prob - weight * inner).astype(BF)
                d_queries.append(dot_f32(d_scores, qkv[tk, :, 192 + at : 256 + at]))
                turned[at : at + 64, :] += dot_tn(qkv[tk, rows, at : at + 64], d_scores)
                turned[192 + at : 256 + at, :] += dot_tn(grad, weight_low)
            dq = jnp.concatenate(d_queries, axis=1) * 0.125
            red_qv[tk, :, :192] += column_sum(dq)
            d_qkv[rows, :192] = dq.astype(BF)

        row_loop(body, 256)
        dk = jnp.transpose(turned[:192, :]) * 0.125
        dv = jnp.transpose(turned[192:, :])
        red_qv[tk, :, 192:] += column_sum(dv)
        d_qkv[:, 192:] = jnp.concatenate([dk, dv], axis=1).astype(BF)

    def qkv_piece(i):
        k, slot = steps[i], i % 2
        if i == 0:
            got["x"].wait()

        def make(which):
            at = pl.ds(pl.multiple_of(512 * which, 512), 512)
            both = dot_tn(x_row[:, at], d_qkv[...])
            parts = [both[128 * r : 128 * r + 128] for r in range(4)]
            thirds = [
                jnp.concatenate([parts[0], parts[1][:, :192]], axis=1),
                jnp.concatenate([parts[1][:, 192:], parts[2][:, :384]], axis=1),
                jnp.concatenate([parts[2][:, 384:], parts[3]], axis=1),
            ]
            for k3 in range(3):
                thirds[k3] = thirds[k3] + dot_tn(third_to_out(k3, 128 * which, 128), go[...])
            return jnp.concatenate(
                [thirds[k3][32 * d : 32 * d + 32] for d in range(4) for k3 in range(3)], axis=0
            )

        produce(0, k, make)
        got["qkv", i].wait()

        def body(rows):
            wide_sum[rows, :] += dot_nt(d_qkv[rows, :], v_qkv[slot])

        row_loop(body, 256)

    sent, passed, across = {}, {}, {}

    def share_send(lo, hi):
        share_low[lo:hi, :] = share[lo:hi, :].astype(BF)
        mine = c * 4 + place.xy
        rows = pl.ds(lo, hi - lo)
        sent[lo] = (
            link.copy(share_low.at[rows], blocks.at[mine, rows]),
            link.send(share_low.at[rows], blocks.at[mine, rows], place.right),
            link.send(share_low.at[rows], blocks.at[mine, rows], place.down),
        )

    def share_pass(lo, hi):
        half = (hi - lo) // 2
        sent[lo][1].wait_recv()
        sent[lo][2].wait_recv()
        one = blocks.at[c * 4 + place.right[0] // 2, pl.ds(lo, half)]
        two = blocks.at[c * 4 + place.down[0] // 2, pl.ds(lo + half, half)]
        passed[lo] = link.send(one, one, place.down), link.send(two, two, place.right)

    def share_across(lo, hi):
        sent[lo][0].wait()
        passed[lo][0].wait_recv()
        passed[lo][1].wait_recv()
        spot = blocks.at[pl.ds(c * 4, 4), pl.ds(lo, hi - lo)]
        across[lo] = link.send(spot, spot, place.core)

    def share_ready(lo):
        across[lo].wait_recv()

    got["small"].wait()
    unpack_small(packed, small)
    norm_vectors(small, norm)
    reds[...] = jnp.zeros_like(reds)
    red_up[...] = jnp.zeros_like(red_up)
    red_qv[...] = jnp.zeros_like(red_qv)
    small_grad[...] = jnp.zeros_like(small_grad)
    wide_sum[...] = jnp.zeros_like(wide_sum)
    for name in ("normed", "gy", "inv"):
        got[name].wait()
    def load_rest():
        fetch("h", h_in, h_low)
        fetch("att", att_in, att)
        fetch("wout", w_out, v_out)
        fetch("qkvs", qkv_in, qkv)
        fetch("x", x_in, x_row)

    small_state = {}

    def meet():
        place.meet()

    def small_send():
        places = feature_places()

        def dx_body(rows):
            value = wide_sum[rows, :]
            high = value.astype(BF)
            rest = (value - high.astype(F32)).astype(BF)
            back = dot_nt(high, places) + dot_nt(rest, places)
            low[rows, :] = (total[rows, :] + back).astype(BF)

        row_loop(dx_body, 256)
        for q in range(4):
            at = slice(192 * q, 192 * q + 192)
            line = jnp.concatenate(
                [red_qv[q], red_up[q]] + [reds[i : i + 1, at] for i in range(6)], axis=1
            )
            for i in range(6):
                small_grad[q, i : i + 1, :] = line[:, 384 * i : 384 * i + 384]
        small_state["keep"] = link.copy(small_grad.at[t], small_land.at[6])
        small_state["deep"] = [
            link.send(small_grad.at[t_of[k]], small_land.at[k - 1], place.deep[k]) for k in (1, 2, 3)
        ]

    def dx_send():
        own_rows = pl.ds(pl.multiple_of(t * 128, 128), 128)
        stay.append(link.copy(low.at[own_rows], dx_mine.at[t]))
        for k in (1, 2, 3):
            part = low.at[pl.ds(pl.multiple_of(t_of[k] * 128, 128), 128)]
            moves.append(link.send(part, dx_mine.at[t], place.deep[k]))

    def small_core():
        small_state["keep"].wait()
        for move in small_state["deep"]:
            move.wait_recv()
        small_land[7] = small_land[6] + small_land[0] + small_land[1] + small_land[2]
        small_state["core"] = link.send(small_land.at[7], small_land.at[3], place.core)

    def small_right():
        small_state["core"].wait_recv()
        small_land[8] = small_land[7] + small_land[3]
        small_state["right"] = link.send(small_land.at[8], small_land.at[4], place.right)

    def small_down():
        small_state["right"].wait_recv()
        small_land[9] = small_land[8] + small_land[4]
        small_state["down"] = link.send(small_land.at[9], small_land.at[5], place.down)

    def small_end():
        small_state["down"].wait_recv()
        small_out[...] = small_land[9] + small_land[5]

    load_ffn(0)
    norm_two_back()
    meet()
    load_ffn(1)
    down_piece(0)
    load_rest()
    act_back(0)
    load_att(0)
    load_att(1)
    up_piece(0)
    hidden_back(0)
    core_add(2, 1)
    core_add(1, 1)
    load_ffn(2)
    emit_out()
    down_piece(1)
    act_back(1)
    plane_add(2, 1)
    core_add(2, 2)
    up_piece(1)
    hidden_back(1)
    load_ffn(3)
    core_add(1, 2)
    down_piece(2)
    act_back(2)
    up_piece(2)
    hidden_back(2)
    core_add(2, 3)
    plane_add(1, 1)
    plane_add(2, 2)
    deep_add(2, 1)
    down_piece(3)
    act_back(3)
    plane_add(1, 2)
    up_piece(3)
    hidden_back(3)
    norm_one_back()
    core_add(2, 0)
    core_add(1, 3)
    plane_add(2, 3)
    deep_add(1, 1)
    core_add(1, 0)
    out_piece(0)
    attention_back(0)
    deep_add(2, 2)
    deep_add(1, 2)
    qkv_piece(0)
    core_add(0, 1)
    load_att(2)
    out_piece(1)
    attention_back(1)
    qkv_piece(1)
    load_att(3)
    core_add(0, 2)
    out_piece(2)
    deep_add(2, 3)
    plane_add(1, 3)
    attention_back(2)
    qkv_piece(2)
    plane_add(0, 2)
    core_add(0, 3)
    plane_add(1, 0)
    deep_add(1, 3)
    out_piece(3)
    attention_back(3)
    deep_add(0, 2)
    plane_add(0, 1)
    qkv_piece(3)
    plane_add(0, 3)
    deep_add(1, 0)
    core_add(0, 0)
    small_send()
    plane_add(2, 0)
    deep_add(0, 1)
    end(1)
    deep_add(0, 3)
    small_core()
    plane_add(0, 0)
    deep_add(2, 0)
    end(2)
    share_send(0, 64)
    dx_send()
    small_right()
    deep_add(0, 0)
    end(0)
    share_send(64, 96)
    share_pass(0, 64)
    share_pass(64, 96)
    share_across(0, 64)
    small_down()
    share_across(64, 96)
    share_ready(64)
    small_end()
    share_ready(0)
    for move in moves:
        move.wait_recv()
    for copy in stay:
        copy.wait()
    link.finish()


def backward_call(*args):
    anywhere = pl.BlockSpec(memory_space=pl.ANY)
    vmem = pl.BlockSpec(memory_space=pltpu.VMEM)
    shape = jax.ShapeDtypeStruct
    sums = [((4, 4 * rows, cols), BF) for cols, rows in WEIGHTS]
    halves = [((4, 2, rows // 2, cols), BF) for cols, rows in WEIGHTS]
    singles = [((4, rows // 2, cols), BF) for cols, rows in WEIGHTS]
    deeps = [((3, rows, cols), BF) for cols, rows in WEIGHTS]
    rest = [
        ((3, 384, 768), BF),
        ((96, 2304), F32),
        ((96, 2304), BF),
        ((4, 8, 384), F32),
        ((11, 8, 384), F32),
        ((4, 8, 384), F32),
        ((4, 1, 2304), F32),
        ((8, 768), F32),
        ((512, 768), BF),
        ((512, 768), F32),
        ((512, 1), F32),
        ((2, 512, 768), BF),
        ((2, 512, 768), BF),
        ((2, 768, 768), BF),
        ((2, 768, 768), BF),
        ((512, 768), BF),
        ((4, 512, 192), BF),
        ((4, 192, 768), BF),
        ((4, 512, 576), BF),
        ((2, 3, 512, 512), BF),
        ((2, 1024, 576), BF),
        ((512, 1024), BF),
        ((512, 768), F32),
        ((512, 768), BF),
        ((512, 768), F32),
        ((512, 768), BF),
        ((512, 192), BF),
        ((512, 576), BF),
        ((384, 512), F32),
        ((192, 768), BF),
        ((512, 1024), F32),
        ((8, 768), F32),
        ((4, 1, 768), F32),
        ((4, 1, 384), F32),
        ((512, 8), F32),
        ((512, 768), BF),
        ((8, 768), F32),
    ]
    scratch = sums + sums + halves + halves + singles + singles + deeps + rest
    return pl.pallas_call(
        backward_kernel,
        out_shape=[
            shape((8, 96, 2304), BF),
            shape((8, 384), F32),
            shape((4, 128, 768), BF),
            shape((4, 128, 768), BF),
            shape((4, 8, 768), F32),
        ],
        in_specs=[vmem] * 2 + [anywhere] * 16,
        out_specs=[anywhere, vmem, anywhere, anywhere, anywhere],
        scratch_shapes=[pltpu.VMEM(*s) for s in scratch]
        + [
            pltpu.SemaphoreType.DMA((160,)),
            pltpu.SemaphoreType.DMA((160,)),
            pltpu.SemaphoreType.DMA((64,)),
        ],
        compiler_params=pltpu.CompilerParams(
            collective_id=1, has_side_effects=True, vmem_limit_bytes=62 * MIB
        ),
        name="backward_and_reduce",
    )(*args)


def finish_kernel(
    slot_row,
    blocks,
    small,
    pool,
    master,
    first,
    second,
    out_mine,
    dx_mine,
    new_master,
    new_first,
    new_second,
    layer_out,
    input_grad,
    pooled,
    norm_grads,
):
    step = pl.program_id(0)
    rows = master.shape[0]
    t = lax.axis_index("tensor")
    start = lax.axis_index("dp") * (rows * pl.num_programs(0)) + step * rows
    wanted = (lax.broadcasted_iota(jnp.int32, (rows, 1), 0) + start).astype(F32)
    match = slot_row[0:1, :768] == wanted
    gradient = dot_f32(jnp.where(match, 1.0, 0.0).astype(BF), blocks[...])
    is_small = slot_row[0:1, 768:769] == wanted
    small_line = jnp.concatenate([small[i : i + 1, :] for i in range(6)], axis=1)
    gradient = jnp.where(is_small, small_line, gradient)

    at = lax.broadcasted_iota(jnp.int32, (1, 768), 1) % 96
    rates = jnp.where(
        at < 32,
        MODEL_WIDTH ** (-0.5),
        jnp.where(
            at < 64,
            FF ** (-0.5),
            jnp.where(at < 88, MODEL_WIDTH ** (-0.5), 4.0 * MODEL_WIDTH ** (-0.5)),
        ),
    ).astype(F32)
    rate = jnp.sum(jnp.where(match, rates, 0.0), axis=1, keepdims=True)
    filled = (rate > 0.0) | is_small
    offset = lax.broadcasted_iota(jnp.int32, (1, small_line.shape[1]), 1) - 1152
    gain = ((offset >= 384) & (offset < 576)) | ((offset >= 768) & (offset < 960))
    small_rate = jnp.where(gain, 0.2, 0.1).astype(F32)
    step_rate = jnp.where(is_small, small_rate, rate)
    decay_on = jnp.where(is_small, 0.0, 1.0)
    new_master[...], new_first[...], new_second[...] = adamw(
        gradient, first[...], second[...], master[...], step_rate, decay_on, filled
    )
    for src, dst in ((out_mine, layer_out), (dx_mine, input_grad)):
        for row in range(4):
            dst[:, row, :] = src[row].astype(F32)

    @pl.when(step == 0)
    def _():
        total = jnp.zeros((4, 8, 192), F32)
        for q in range(4):
            total = total + jnp.where(t == q, pool[:, :, 192 * q : 192 * q + 192], 0.0)
        pooled[...] = total
        norm_grads[...] = jnp.concatenate(
            [small_line[:, 1152 + 192 * i : 1344 + 192 * i] for i in range(6)], axis=0
        )


def finish_call(slot_row, blocks, small, pool, master, first, second, out_mine, dx_mine):
    steps = 2
    slots, block_len = master.shape
    shape = jax.ShapeDtypeStruct

    def whole(*dims):
        return pl.BlockSpec(dims, lambda i: (0,) * len(dims))

    state = pl.BlockSpec((slots // steps, block_len), lambda i: (i, 0))
    token_in = pl.BlockSpec((4, 128 // steps, 768), lambda i: (0, i, 0))
    token_out = pl.BlockSpec((128 // steps, 4, 768), lambda i: (i, 0, 0))
    return pl.pallas_call(
        finish_kernel,
        grid=(steps,),
        out_shape=[shape((slots, block_len), F32)] * 3
        + [shape((128, 4, 768), F32)] * 2
        + [shape((4, 8, 192), F32), shape((6, 192), F32)],
        in_specs=[whole(8, 896), whole(768, block_len), whole(8, 384), whole(4, 8, 768)]
        + [state] * 3
        + [token_in] * 2,
        out_specs=[state] * 3 + [token_out] * 2 + [whole(4, 8, 192), whole(6, 192)],
        compiler_params=pltpu.CompilerParams(vmem_limit_bytes=62 * MIB),
        name="owners_update",
    )(slot_row, blocks, small, pool, master, first, second, out_mine, dx_mine)


def share_order():
    order = []
    for core in range(2):
        for chip in range(4):
            for base, count in ((0, 32), (256, 32), (512, 24), (704, 8)):
                at = base + (core * 4 + chip) * count
                order += list(range(at, at + count))
    return np.array(order + [768] + [4096] * 127, np.int32)


def local_rows(
    layer_input_rows,
    sentence_index_row,
    padding_mask,
    output_gradient,
    owner_rank,
    master_state,
    first_moment,
    second_moment,
):
    block_len = master_state.shape[2]
    order = share_order()
    (
        _,
        w_up,
        w_down,
        w_qkv,
        w_out,
        slot_row,
        small_all,
        x_row,
        gy_row,
        qkv,
        prob_low,
        attended,
        normed_one,
        h_low,
        act,
        pull,
        z_two,
        inverse,
    ) = forward_call(
        master_state[0],
        owner_rank,
        jnp.asarray(order[:, None]),
        sentence_index_row,
        padding_mask,
        jnp.transpose(layer_input_rows, (1, 0, 2)),
        jnp.transpose(output_gradient, (1, 0, 2)),
    )
    blocks, small_sum, out_mine, dx_mine, pool_all = backward_call(
        sentence_index_row,
        padding_mask,
        gy_row,
        z_two,
        inverse,
        small_all,
        act,
        pull,
        w_down,
        w_up,
        h_low,
        normed_one,
        attended,
        w_out,
        qkv,
        prob_low,
        w_qkv,
        x_row,
    )
    new_master, new_first, new_second, layer_out, input_grad, pooled, norm_grads = finish_call(
        slot_row,
        blocks.reshape(768, block_len),
        small_sum,
        pool_all,
        master_state[0],
        first_moment[0],
        second_moment[0],
        out_mine,
        dx_mine,
    )
    return (
        layer_out,
        pooled,
        input_grad,
        new_master[None],
        new_first[None],
        new_second[None],
        norm_grads,
    )


def solution(mesh):
    in_specs = (
        P("tensor", "dp", None),
        P("dp", None),
        P("dp", None),
        P("tensor", "dp", None),
        P(),
        P("tensor", "dp", None),
        P("tensor", "dp", None),
        P("tensor", "dp", None),
    )
    out_specs = (
        P("tensor", "dp", None),
        P("dp", None, "tensor"),
        P("tensor", "dp", None),
        P("tensor", "dp", None),
        P("tensor", "dp", None),
        P("tensor", "dp", None),
        P(None, "tensor"),
    )
    plain = mesh.shape["dp"] != 8 or mesh.shape["tensor"] != 4
    body = local_general if plain else local_rows
    return jax.shard_map(body, mesh=mesh, in_specs=in_specs, out_specs=out_specs, check_vma=False)
```

```python
import jax
import numpy as np
import jax.numpy as jnp
from jax import lax
from jax.experimental import pallas as pl
from jax.experimental.pallas import tpu as pltpu
from jax.sharding import PartitionSpec as P

MODEL_WIDTH = 768
HEAD_DIM = 64
FF = 3072
SMAX = 8
STEP = 10


NORM_EPS = 1e-05
ADAM_EPS = 1e-08
BETA_ONE = 0.9
BETA_TWO = 0.999
DECAY_RATE = 0.01
MASKED = -1e30
exact_precision = lax.Precision.HIGHEST


def slot_tables(owner_rank, per_owner):
    ordinal = jnp.arange(owner_rank.shape[0], dtype=jnp.int32)
    same_owner = owner_rank[:, None] == owner_rank[None, :]
    earlier = ordinal[None, :] < ordinal[:, None]
    ranking = jnp.sum((same_owner & earlier).astype(jnp.int32), axis=1)
    return owner_rank * per_owner + ranking


def slot_blocks(slot_of, wanted):
    matches = slot_of[None, :] == wanted[:, None]
    filled = jnp.any(matches, axis=1)
    ordinal = jnp.arange(slot_of.shape[0], dtype=jnp.int32)
    block_of = jnp.sum(jnp.where(matches, ordinal[None, :], 0), axis=1)
    return (block_of, filled)


def step_rates(token_position, width, hidden, tensor_size):
    width_loc = width // tensor_size
    ffn_loc = hidden // tensor_size
    end_up = width * ffn_loc
    end_down = end_up + ffn_loc * width
    end_qkv = end_down + width * 3 * width_loc
    end_out = end_qkv + width_loc * width
    offset = token_position - end_out
    first_gain = (offset >= 4 * width_loc + ffn_loc) & (offset < 5 * width_loc + ffn_loc)
    second_gain = (offset >= 6 * width_loc + ffn_loc) & (offset < 7 * width_loc + ffn_loc)
    small_rate = jnp.where(first_gain | second_gain, 0.2, 0.1)
    step_rate = jnp.where(
        token_position < end_up,
        width ** (-0.5),
        jnp.where(
            token_position < end_down,
            hidden ** (-0.5),
            jnp.where(
                token_position < end_qkv,
                width ** (-0.5),
                jnp.where(token_position < end_out, 4.0 * width ** (-0.5), small_rate),
            ),
        ),
    )
    decay_on = (token_position < end_out).astype(jnp.float32)
    return (step_rate.astype(jnp.float32), decay_on)


def adamw(gradient, moment, square, weight, step_rate, decay_on, filled):
    new_moment = BETA_ONE * moment + (1.0 - BETA_ONE) * gradient
    new_square = BETA_TWO * square + (1.0 - BETA_TWO) * gradient * gradient
    unbiased = new_moment / (1.0 - BETA_ONE**STEP)
    divisor = jnp.sqrt(new_square / (1.0 - BETA_TWO**STEP)) + ADAM_EPS
    new_weight = weight - step_rate * (unbiased / divisor + DECAY_RATE * decay_on * weight)
    zeroed = jnp.zeros_like(weight)
    return (
        jnp.where(filled, new_weight, zeroed),
        jnp.where(filled, new_moment, zeroed),
        jnp.where(filled, new_square, zeroed),
    )


def normalize(values):
    centred = values - jnp.mean(values, axis=-1, keepdims=True)
    inv_dev = lax.rsqrt(jnp.mean(centred * centred, axis=-1, keepdims=True) + NORM_EPS)
    return (centred * inv_dev, inv_dev)


def norm_back(grad_scaled, normed, inv_dev):
    first_mean = jnp.mean(grad_scaled, axis=-1, keepdims=True)
    second_mean = jnp.mean(grad_scaled * normed, axis=-1, keepdims=True)
    return inv_dev * (grad_scaled - first_mean - normed * second_mean)


def allowed_pairs(sentence_labels, real_token_flags):
    row_len = sentence_labels.shape[-1]
    same_sent = sentence_labels[:, :, None] == sentence_labels[:, None, :]
    live = (real_token_flags[:, :, None] == 1) & (real_token_flags[:, None, :] == 1)
    diagonal = jnp.eye(row_len, dtype=bool)[None]
    return same_sent & live | diagonal


def masked_scores(queries, key_rows, allowed, scaling):
    scores = (
        jnp.einsum("qshe,kshe->shqk", queries, key_rows, preferred_element_type=jnp.float32)
        * scaling
    )
    return jnp.where(allowed[:, None], scores, MASKED)


def split_flat(flat_all, width_loc, ffn_loc):
    end_up = MODEL_WIDTH * ffn_loc
    end_down = end_up + ffn_loc * MODEL_WIDTH
    end_qkv = end_down + MODEL_WIDTH * 3 * width_loc
    end_out = end_qkv + width_loc * MODEL_WIDTH
    return (
        flat_all[:end_up].reshape(MODEL_WIDTH, ffn_loc),
        flat_all[end_up:end_down].reshape(ffn_loc, MODEL_WIDTH),
        flat_all[end_down:end_qkv].reshape(MODEL_WIDTH, 3 * width_loc),
        flat_all[end_qkv:end_out].reshape(width_loc, MODEL_WIDTH),
        flat_all[end_out:],
    )


def local_general(
    layer_input_rows,
    sentence_index_row,
    padding_mask,
    output_gradient,
    owner_rank,
    master_state,
    first_moment,
    second_moment,
):
    tensor_size = lax.axis_size("tensor")
    tensor_at = lax.axis_index("tensor")
    data_size = lax.axis_size("dp")
    data_at = lax.axis_index("dp")
    width_loc = MODEL_WIDTH // tensor_size
    ffn_loc = FF // tensor_size
    heads_loc = width_loc // HEAD_DIM
    quarter = layer_input_rows.shape[0]
    seq_count = layer_input_rows.shape[1]
    row_len = quarter * tensor_size
    per_owner = master_state.shape[1]
    block_len = master_state.shape[2]
    nblocks = owner_rank.shape[0]
    slot_of = slot_tables(owner_rank, per_owner)
    gathered = lax.all_gather(master_state.astype(jnp.bfloat16), "dp", axis=1, tiled=True)[0]
    flat_weights = gathered[slot_of].reshape(nblocks * block_len)
    up_weight, down_weight, w_qkv, w_out, small_part = split_flat(flat_weights, width_loc, ffn_loc)
    bias_q = small_part[:width_loc].astype(jnp.float32)
    bias_v = small_part[width_loc : 2 * width_loc].astype(jnp.float32)
    expand_bias = small_part[2 * width_loc : 2 * width_loc + ffn_loc].astype(jnp.float32)
    norm_parts = small_part[2 * width_loc + ffn_loc :].reshape(6, width_loc)
    full_rows, norm_whole = (
        lax.all_gather(layer_input_rows, "tensor", axis=0, tiled=True),
        lax.all_gather(norm_parts, "tensor", axis=1, tiled=True),
    )
    norm_all = norm_whole.astype(jnp.float32)
    bias_out, bias_down = (norm_all[0], norm_all[1])
    gain_one, shift_one, gain_two, shift_two = (norm_all[2], norm_all[3], norm_all[4], norm_all[5])
    qkv_lin = jnp.einsum("lsd,de->lse", full_rows, w_qkv, preferred_element_type=jnp.float32)
    bias_qkv = jnp.concatenate([bias_q, jnp.zeros((width_loc,), jnp.float32), bias_v])
    qkv = (qkv_lin + bias_qkv).astype(jnp.bfloat16)
    queries = qkv[:, :, :width_loc].reshape(row_len, seq_count, heads_loc, HEAD_DIM)
    key_rows = qkv[:, :, width_loc : 2 * width_loc].reshape(row_len, seq_count, heads_loc, HEAD_DIM)
    values = qkv[:, :, 2 * width_loc :].reshape(row_len, seq_count, heads_loc, HEAD_DIM)
    scaling = HEAD_DIM ** (-0.5)
    allowed = allowed_pairs(sentence_index_row, padding_mask)
    scores = masked_scores(queries, key_rows, allowed, scaling)
    row_peak = jnp.max(scores, axis=-1, keepdims=True)
    log_total = row_peak + jnp.log(jnp.sum(jnp.exp(scores - row_peak), axis=-1, keepdims=True))
    prob_low = jnp.exp(scores - log_total).astype(jnp.bfloat16)
    attended = jnp.einsum("shqk,kshe->qshe", prob_low, values, preferred_element_type=jnp.float32)
    attended = attended.astype(jnp.bfloat16).reshape(row_len, seq_count, width_loc)
    portion_rows = attended
    attn_rows = lax.psum_scatter(
        jnp.einsum("lse,ed->lsd", portion_rows, w_out, preferred_element_type=jnp.float32).astype(
            jnp.bfloat16
        ),
        "tensor",
        scatter_dimension=0,
        tiled=True,
    ).astype(jnp.float32)
    z_one = layer_input_rows.astype(jnp.float32) + attn_rows + bias_out
    normed_one, inv_one = normalize(z_one)
    h_mine = normed_one * gain_one + shift_one
    hidden_narrow_whole = lax.all_gather(h_mine.astype(jnp.bfloat16), "tensor", axis=0, tiled=True)
    up_pre = (
        jnp.einsum(
            "wer,rb->web", hidden_narrow_whole, up_weight, preferred_element_type=jnp.float32
        )
        + expand_bias
    )
    activation_narrow = jax.nn.gelu(up_pre, approximate=False).astype(jnp.bfloat16)
    portion_rows = activation_narrow
    down_rows = lax.psum_scatter(
        jnp.einsum(
            "aij,jb->aib", portion_rows, down_weight, preferred_element_type=jnp.float32
        ).astype(jnp.bfloat16),
        "tensor",
        scatter_dimension=0,
        tiled=True,
    ).astype(jnp.float32)
    z_two = h_mine + down_rows + bias_down
    normed_two, inv_two = normalize(z_two)
    layer_out = normed_two * gain_two + shift_two
    seg_mine = lax.dynamic_slice_in_dim(sentence_index_row, tensor_at * quarter, quarter, 1)
    valid_mine = lax.dynamic_slice_in_dim(padding_mask, tensor_at * quarter, quarter, 1)
    sent_ids = jnp.arange(SMAX, dtype=jnp.int32)
    onehot_mine = (
        (seg_mine[:, :, None] == sent_ids[None, None, :]) & (valid_mine[:, :, None] == 1)
    ).astype(jnp.float32)
    pool_part = jnp.einsum("slc,lsd->scd", onehot_mine, layer_out, precision=exact_precision)
    onehot_full = (
        (sentence_index_row[:, :, None] == sent_ids[None, None, :])
        & (padding_mask[:, :, None] == 1)
    ).astype(jnp.float32)
    counts = jnp.sum(onehot_full, axis=1)
    grad_out = output_gradient.astype(jnp.float32) * valid_mine.T[:, :, None].astype(jnp.float32)
    d_gain_two = jnp.sum(grad_out * normed_two, axis=(0, 1))
    d_shift_two = jnp.sum(grad_out, axis=(0, 1))
    dz_two = norm_back(grad_out * gain_two, normed_two, inv_two)
    d_bias_down = jnp.sum(dz_two, axis=(0, 1))
    second_sum_gradient_wide = lax.all_gather(
        dz_two.astype(jnp.bfloat16), "tensor", axis=0, tiled=True
    )
    down_weight_gradient = jnp.einsum(
        "ipo,ipr->or",
        activation_narrow,
        second_sum_gradient_wide,
        preferred_element_type=jnp.float32,
    )
    activation_gradient = jnp.einsum(
        "ugp,jp->ugj", second_sum_gradient_wide, down_weight, preferred_element_type=jnp.float32
    )
    gelu_pull = jax.vjp(lambda pre_act: jax.nn.gelu(pre_act, approximate=False), up_pre)[1]
    d_up = gelu_pull(activation_gradient)[0]
    d_bias_up = jnp.sum(d_up, axis=(0, 1))
    expand_gradient_narrow = d_up.astype(jnp.bfloat16)
    up_weight_gradient = jnp.einsum(
        "iux,iuy->xy",
        hidden_narrow_whole,
        expand_gradient_narrow,
        preferred_element_type=jnp.float32,
    )
    portion_rows = expand_gradient_narrow
    dh_rows = lax.psum_scatter(
        jnp.einsum(
            "uih,vh->uiv", portion_rows, up_weight, preferred_element_type=jnp.float32
        ).astype(jnp.bfloat16),
        "tensor",
        scatter_dimension=0,
        tiled=True,
    ).astype(jnp.float32)
    dh_mine = dz_two + dh_rows
    d_gain_one = jnp.sum(dh_mine * normed_one, axis=(0, 1))
    d_shift_one = jnp.sum(dh_mine, axis=(0, 1))
    dz_one = norm_back(dh_mine * gain_one, normed_one, inv_one)
    d_bias_out = jnp.sum(dz_one, axis=(0, 1))
    dz_one_full = lax.all_gather(dz_one.astype(jnp.bfloat16), "tensor", axis=0, tiled=True)
    d_w_out = jnp.einsum("lse,lsd->ed", attended, dz_one_full, preferred_element_type=jnp.float32)
    d_attended = jnp.einsum("lsd,ed->lse", dz_one_full, w_out, preferred_element_type=jnp.float32)
    d_attended = d_attended.astype(jnp.bfloat16).reshape(row_len, seq_count, heads_loc, HEAD_DIM)
    scores_again = masked_scores(queries, key_rows, allowed, scaling)
    attn_prob = jnp.exp(scores_again - log_total)
    prob_again = attn_prob.astype(jnp.bfloat16)
    d_prob = jnp.einsum("qshe,kshe->shqk", d_attended, values, preferred_element_type=jnp.float32)
    d_values = jnp.einsum(
        "shqk,qshe->kshe", prob_again, d_attended, preferred_element_type=jnp.float32
    )
    inner = jnp.sum(d_prob * attn_prob, axis=-1, keepdims=True)
    d_scores = (attn_prob * (d_prob - inner)).astype(jnp.bfloat16)
    d_queries = (
        jnp.einsum("shqk,kshe->qshe", d_scores, key_rows, preferred_element_type=jnp.float32)
        * scaling
    )
    d_keys = (
        jnp.einsum("shqk,qshe->kshe", d_scores, queries, preferred_element_type=jnp.float32)
        * scaling
    )
    d_bias_q = jnp.sum(d_queries, axis=(0, 1)).reshape(width_loc)
    d_bias_v = jnp.sum(d_values, axis=(0, 1)).reshape(width_loc)
    d_qkv_low = jnp.concatenate(
        [
            d_queries.reshape(row_len, seq_count, width_loc),
            d_keys.reshape(row_len, seq_count, width_loc),
            d_values.reshape(row_len, seq_count, width_loc),
        ],
        axis=2,
    ).astype(jnp.bfloat16)
    d_w_qkv = jnp.einsum("lsd,lse->de", full_rows, d_qkv_low, preferred_element_type=jnp.float32)
    portion_rows = d_qkv_low
    dx_rows = lax.psum_scatter(
        jnp.einsum("lse,de->lsd", portion_rows, w_qkv, preferred_element_type=jnp.float32).astype(
            jnp.bfloat16
        ),
        "tensor",
        scatter_dimension=0,
        tiled=True,
    ).astype(jnp.float32)
    input_grad = dz_one + dx_rows
    shared_grads = jnp.stack(
        [d_bias_out, d_bias_down, d_gain_one, d_shift_one, d_gain_two, d_shift_two]
    )[None]
    pool_sum, shared_sum = (
        lax.psum_scatter(
            pool_part.astype(jnp.bfloat16), "tensor", scatter_dimension=2, tiled=True
        ).astype(jnp.float32),
        lax.psum_scatter(
            shared_grads.astype(jnp.bfloat16), "tensor", scatter_dimension=2, tiled=True
        ).astype(jnp.float32),
    )
    pooled_mean = pool_sum / jnp.maximum(counts, 1.0)[:, :, None]
    flat_grads = jnp.concatenate(
        [
            up_weight_gradient.reshape(-1),
            down_weight_gradient.reshape(-1),
            d_w_qkv.reshape(-1),
            d_w_out.reshape(-1),
            d_bias_q,
            d_bias_v,
            d_bias_up,
            shared_sum.reshape(-1),
        ]
    )
    grad_blocks = flat_grads.reshape(nblocks, block_len)
    wanted = data_at * per_owner + jnp.arange(per_owner, dtype=jnp.int32)
    block_of, filled = slot_blocks(slot_of, wanted)
    slot_grads = (
        jnp.zeros((data_size * per_owner, block_len), jnp.float32).at[slot_of].set(grad_blocks)
    )
    owned_grads = lax.psum_scatter(slot_grads, "dp", scatter_dimension=0, tiled=True)
    norm_grads = lax.psum(shared_sum[0], "dp")
    token_position = block_of[:, None] * block_len + jnp.arange(block_len, dtype=jnp.int32)[None, :]
    step_rate, decay_on = step_rates(token_position, MODEL_WIDTH, FF, tensor_size)
    new_master, new_first, new_second = adamw(
        owned_grads,
        first_moment[0],
        second_moment[0],
        master_state[0],
        step_rate,
        decay_on,
        filled[:, None],
    )
    return (
        layer_out,
        pooled_mean,
        input_grad,
        new_master[None],
        new_first[None],
        new_second[None],
        norm_grads,
    )


MESH = pl.DeviceIdType.MESH
BF = jnp.bfloat16
F32 = jnp.float32
WEIGHTS = ((768, 96), (768, 96), (768, 96))
MIB = 2**20


class Place:
    def __init__(self):
        d = lax.axis_index("dp")
        self.t = lax.axis_index("tensor")
        self.c = d % 2
        self.x = (d // 2) % 2
        self.y = d // 4
        self.xy = d // 2
        self.core = (d + 1 - 2 * self.c, self.t)
        self.right = (d + 2 - 4 * self.x, self.t)
        self.down = (d + 4 - 8 * self.y, self.t)
        self.diag = (d + 6 - 4 * self.x - 8 * self.y, self.t)
        self.deep = [None] + [(d, (self.t + k) % 4) for k in (1, 2, 3)]
        self.ahead = [(self.t + k) % 4 for k in range(4)]
        self.behind = [(self.t + 4 - k) % 4 for k in range(4)]

    def hail(self):
        peers = [self.core, self.right, self.down, self.diag] + self.deep[1:]
        for peer in peers:
            pl.semaphore_signal(
                pltpu.get_barrier_semaphore(), inc=1, device_id=peer, device_id_type=MESH
            )

    def meet(self):
        pl.semaphore_wait(pltpu.get_barrier_semaphore(), 7)


class Sender:
    def __init__(self, send_sems, recv_sems, local_sems):
        self.sems = (send_sems, recv_sems, local_sems)
        self.used = 0
        self.used_local = 0
        self.open = []

    def send(self, src, dst, peer):
        i = self.used
        self.used += 1
        copy = pltpu.make_async_remote_copy(
            src_ref=src,
            dst_ref=dst,
            send_sem=self.sems[0].at[i],
            recv_sem=self.sems[1].at[i],
            device_id=peer,
            device_id_type=MESH,
        )
        copy.start()
        self.open.append(copy)
        return copy

    def copy(self, src, dst):
        i = self.used_local
        self.used_local += 1
        copy = pltpu.make_async_copy(src, dst, self.sems[2].at[i])
        copy.start()
        return copy

    def sent(self, copy):
        copy.wait_send()
        self.open = [other for other in self.open if other is not copy]

    def finish(self):
        for copy in self.open:
            copy.wait_send()


def rows_of(place, rows, at=None):
    at = place.xy if at is None else at
    return pl.ds(pl.multiple_of(place.c * (4 * rows) + at * rows, 32), rows)


def half_of(place, rows):
    return pl.ds(pl.multiple_of(place.c * (4 * rows), 128), 4 * rows)


def interleave(size, parts):
    group = size // parts
    out_row = lax.broadcasted_iota(jnp.int32, (size, size), 0)
    col = lax.broadcasted_iota(jnp.int32, (size, size), 1)
    part = jnp.zeros((size, size), jnp.int32)
    for k in range(1, parts):
        part = part + (col >= k * group).astype(jnp.int32)
    return jnp.where(out_row == parts * (col - group * part) + part, 1.0, 0.0).astype(BF)


def dot_f32(a, b):
    return jnp.dot(a, b, preferred_element_type=F32)


def third_to_out(k, start, size):
    at = lax.broadcasted_iota(jnp.int32, (1, size), 1) + start
    device, j = at // 32, at % 32
    target = jnp.where(j >= 24, 24 * device + 3 * (j - 24) + k, -1)
    out_row = lax.broadcasted_iota(jnp.int32, (192, size), 0)
    return jnp.where(out_row == target, 1.0, 0.0).astype(BF)


def feature_places():
    at = lax.broadcasted_iota(jnp.int32, (1, 1024), 1)
    r, device, j = (at % 512) // 128, 4 * (at // 512) + (at % 128) // 32, at % 32
    target = jnp.where(j < 24, 4 * (24 * device + j) + r, -1)
    feature = lax.broadcasted_iota(jnp.int32, (768, 1024), 0)
    return jnp.where(feature == target, 1.0, 0.0).astype(BF)


def dot_nt(a, b):
    return lax.dot_general(a, b, (((1,), (1,)), ((), ())), preferred_element_type=F32)


def dot_tn(a, b):
    return lax.dot_general(a, b, (((0,), (0,)), ((), ())), preferred_element_type=F32)


def unpack_small(packed, small):
    for t in range(4):
        small[t] = jnp.concatenate([packed[t, i : i + 1, :] for i in range(6)], axis=1)


def norm_vectors(small, norm):
    for i in range(6):
        at = 1152 + 192 * i
        norm[i : i + 1, :] = jnp.concatenate([small[t, 0:1, at : at + 192] for t in range(4)], axis=1)


def row_loop(body, step=128):
    @pl.loop(0, 512 // step)
    def _(i):
        body(pl.ds(pl.multiple_of(i * step, step), step))


def forward_kernel(
    master,
    owners,
    order_col,
    labels,
    flags,
    x_in,
    gy_in,
    w_att,
    w_up,
    w_down,
    w_qkv,
    w_out,
    slot_out,
    small_out,
    x_out,
    gy_row,
    qkv_out,
    prob_out,
    att_out,
    n_one_out,
    h_out,
    act_out,
    pull_out,
    z_two_out,
    inv_out,
    slot_row,
    slot_col,
    id_row,
    id_col,
    slots,
    canon_att,
    canon_ffn,
    land_att,
    land_ffn,
    pass_ffn,
    pass_land,
    share,
    p_att,
    p_up,
    p_down,
    small_mine,
    small_land,
    small_total,
    packed,
    small,
    norm,
    bias_qkv,
    v_att,
    v_qkv,
    v_compact,
    v_up,
    v_down,
    x_row,
    x_wide,
    qkv,
    prob,
    att,
    n_one,
    h_low,
    act,
    pull,
    total,
    inv,
    send_sems,
    recv_sems,
    local_sems,
):
    place = Place()
    link = Sender(send_sems, recv_sems, local_sems)
    place.hail()
    slots[place.c] = master[...].astype(BF)

    place.meet()
    whole = (w_att, w_up, w_down)
    held = (v_att, v_up, v_down)
    piece = (p_att, p_up, p_down)
    peers = (place.right, place.down, place.diag)
    mine_rows = pl.ds(pl.multiple_of(place.t * 128, 128), 128)
    tidy = []

    core_slots = link.send(slots.at[place.c], slots.at[place.c], place.core)
    x_moves = [
        link.send(x_in.at[place.ahead[k]], x_row.at[mine_rows], place.deep[k]) for k in (1, 2, 3)
    ]
    x_stay = link.copy(x_in.at[place.t], x_row.at[mine_rows])
    tidy.append(link.copy(gy_in.at[place.t], gy_row.at[mine_rows]))

    blocks = owners.shape[0]
    wide = slot_row.shape[1]
    owner = jnp.concatenate(
        [owners[...].astype(F32)[None], jnp.full((1, wide - blocks), -1.0, F32)], axis=1
    )
    kinds = lax.broadcasted_iota(jnp.int32, (8, wide), 0).astype(F32)
    owned = jnp.where(kinds == owner, 1.0, 0.0)
    ordinal = lax.broadcasted_iota(jnp.int32, (wide, wide), 1)
    earlier = jnp.where(lax.broadcasted_iota(jnp.int32, (wide, wide), 0) < ordinal, 1.0, 0.0)
    ahead = dot_f32(owned.astype(BF), earlier.astype(BF))
    ranking = jnp.sum(owned * ahead, axis=0, keepdims=True)
    place_of = jnp.where(order_col[...] == ordinal, 1.0, 0.0).astype(BF)
    pair = jnp.where(kinds == 0.0, owner, ranking).astype(BF)
    row = dot_nt(pair, place_of)
    col = dot_nt(place_of, pair)
    per_owner = float(master.shape[0])
    slot_row[...] = jnp.broadcast_to(row[0:1, :] * per_owner + row[1:2, :], slot_row.shape)
    slot_col[...] = jnp.broadcast_to(col[:, 0:1] * per_owner + col[:, 1:2], slot_col.shape)

    own = pl.ds(place.t, 1)
    apart = -1 - lax.broadcasted_iota(jnp.int32, (1, 512), 1)
    ids = jnp.where(flags[own, :] == 1, labels[own, :], apart).astype(F32)
    id_row[...] = jnp.broadcast_to(ids, id_row.shape)
    id_col[...] = jnp.transpose(id_row[...])
    tidy.append(link.copy(slot_row, slot_out))
    core_slots.wait_recv()

    pair_slots = slots[...].reshape(384, 2304)
    slot_id = (lax.broadcasted_iota(jnp.int32, (64, 384), 1) + place.xy * 384).astype(F32)
    order = [(3, place.diag), (1, place.right), (2, place.down), (0, None)]

    def spread(lo, rows, canon, land):
        sent = []
        for j, peer in order:
            at = place.xy if peer is None else peer[0] // 2
            spot = pl.ds(pl.multiple_of(place.c * 384 + at * 96 + lo, 32), rows)
            wanted = slot_col[spot, 0:1]
            pick = jnp.where(wanted == slot_id[:rows], 1.0, 0.0).astype(BF)
            canon[j] = dot_f32(pick, pair_slots).astype(BF)
            if peer is not None:
                sent.append(link.send(canon.at[j], land.at[j - 1], peer))
        return sent

    def collect(sent, lo, rows, canon, land):
        for move in sent:
            move.wait_recv()
        share[lo : lo + rows, :] = (
            canon[0].astype(F32) + land[0].astype(F32) + land[1].astype(F32) + land[2].astype(F32)
        )

    att_sent = spread(64, 32, canon_att, land_att)
    pick_small = jnp.where(slot_row[:, 768:769] == slot_id[:8], 1.0, 0.0).astype(BF)
    picked = dot_f32(pick_small, pair_slots)
    for i in range(6):
        small_mine[i : i + 1, :] = picked[0:1, 384 * i : 384 * i + 384]
    small_mine[6:8, :] = jnp.zeros((2, 384), F32)
    small_moves = [link.send(small_mine, small_land.at[j], peer) for j, peer in enumerate(peers)]
    def spread_halves():
        for j, peer in order:
            at = place.xy if peer is None else peer[0] // 2
            spot = pl.ds(pl.multiple_of(place.c * 384 + at * 96, 32), 64)
            pick = jnp.where(slot_col[spot, 0:1] == slot_id, 1.0, 0.0).astype(BF)
            canon_ffn[j] = dot_f32(pick, pair_slots).astype(BF)
            if j in (1, 3):
                half = canon_ffn.at[j, pl.ds(0, 32)]
                halves[j, 0] = link.send(half, land_ffn.at[0, j // 2], place.right)
            if j in (2, 3):
                half = canon_ffn.at[j, pl.ds(32, 32)]
                halves[j, 1] = link.send(half, land_ffn.at[1, j - 2], place.down)

    def pass_halves():
        halves[3, 0].wait_recv()
        pass_ffn[0] = canon_ffn[2, 0:32, :] + land_ffn[0, 1]
        halves["down"] = link.send(pass_ffn.at[0], pass_land.at[0], place.down)
        halves[3, 1].wait_recv()
        pass_ffn[1] = canon_ffn[1, 32:64, :] + land_ffn[1, 1]
        halves["right"] = link.send(pass_ffn.at[1], pass_land.at[1], place.right)

    def collect_halves():
        halves[1, 0].wait_recv()
        halves[2, 1].wait_recv()
        halves["down"].wait_recv()
        halves["right"].wait_recv()
        for i in range(2):
            share[32 * i : 32 * i + 32, :] = (
                canon_ffn[0, 32 * i : 32 * i + 32, :] + land_ffn[i, 0] + pass_land[i]
            ).astype(F32)

    halves = {}
    att_sent[0].wait_recv()
    spread_halves()
    collect(att_sent[1:], 64, 32, canon_att, land_att)

    for k in range(3):
        p_att[32 * k : 32 * k + 32, :] = share[64:96, 768 * k : 768 * k + 768].astype(BF)

    def spread_ffn():
        three = interleave(96, 3)
        for at, ref in ((0, p_up), (32, p_down)):
            parts = [share[at : at + 32, 768 * k : 768 * k + 768] for k in range(3)]
            ref[...] = dot_f32(three, jnp.concatenate(parts, axis=0).astype(BF)).astype(BF)

    deep_moves, right_moves, down_moves, own_copies, core_moves, loads = {}, {}, {}, {}, {}, {}

    def deep_send(w):
        spot = whole[w].at[place.t, rows_of(place, WEIGHTS[w][1])]
        own_copies[w] = link.copy(piece[w], spot)
        deep_moves[w] = [link.send(piece[w], spot, place.deep[k]) for k in (1, 2, 3)]

    def plane_send(w, k):
        rows = WEIGHTS[w][1]
        spot = whole[w].at[place.behind[k], rows_of(place, rows)]
        src = piece[w] if k == 0 else spot
        if k:
            deep_moves[w][k - 1].wait_recv()
        right_moves[w, k] = link.send(src, spot, place.right)
        down_moves[w, k] = link.send(src, spot, place.down)

    def plane_pass(w, k):
        rows = WEIGHTS[w][1]
        half = rows // 2
        right_moves[w, k].wait_recv()
        down_moves[w, k].wait_recv()
        t = place.behind[k]
        right_at = place.c * (4 * rows) + (place.right[0] // 2) * rows
        down_at = place.c * (4 * rows) + (place.down[0] // 2) * rows
        first = whole[w].at[t, pl.ds(pl.multiple_of(right_at, 16), half)]
        second = whole[w].at[t, pl.ds(pl.multiple_of(down_at + half, 16), half)]
        right_moves[w, k, 1] = link.send(second, second, place.right)
        down_moves[w, k, 1] = link.send(first, first, place.down)

    def core_pass(w, k):
        if k == 0:
            own_copies[w].wait()
        right_moves[w, k, 1].wait_recv()
        down_moves[w, k, 1].wait_recv()
        spot = whole[w].at[place.behind[k], half_of(place, WEIGHTS[w][1])]
        core_moves[w, k] = link.send(spot, spot, place.core)

    def load(w, k):
        core_moves[w, k].wait_recv()
        t = place.behind[k]
        loads[w, k] = link.copy(whole[w].at[t], held[w].at[t])

    def unpack(k):
        loads[0, k].wait()
        t = place.behind[k]
        thirds = [
            jnp.concatenate([v_att[t, 96 * d + 32 * k3 : 96 * d + 32 * k3 + 32, :] for d in range(8)], axis=0)
            for k3 in range(3)
        ]
        out = jnp.zeros((192, 768), F32)
        for k3 in range(3):
            out = out + dot_f32(third_to_out(k3, 0, 256), thirds[k3])
        v_compact[t] = out.astype(BF)
        turns = [
            thirds[0][:, :576],
            jnp.concatenate([thirds[0][:, 576:], thirds[1][:, :384]], axis=1),
            jnp.concatenate([thirds[1][:, 384:], thirds[2][:, :192]], axis=1),
            thirds[2][:, 192:],
        ]
        for half in range(2):
            for r in range(4):
                at = 512 * half + 128 * r
                v_qkv[t, at : at + 128, :] = turns[r][128 * half : 128 * half + 128]
        tidy.append(link.copy(v_qkv.at[t], w_qkv.at[t]))
        tidy.append(link.copy(v_compact.at[t], w_out.at[t]))

    def qkv_step(k):
        t = place.behind[k]

        def body(rows):
            lin = dot_f32(x_wide[rows, :], v_qkv[t]) + bias_qkv[t]
            qkv[t, rows, :] = lin.astype(BF)

        row_loop(body, 256)

    def attention(k):
        t = place.behind[k]

        def body(rows):
            allowed = id_col[rows, 0:1] == id_row[0:1, :]
            parts = []
            for i in range(3):
                at = 64 * i
                scores = dot_nt(qkv[t, rows, at : at + 64], qkv[t, :, 192 + at : 256 + at]) * 0.125
                scores = jnp.where(allowed, scores, MASKED)
                weight = jnp.exp(scores - jnp.max(scores, axis=1, keepdims=True))
                weight = weight * (1.0 / jnp.sum(weight, axis=1, keepdims=True))
                low = weight.astype(BF)
                prob[3 * t + i, rows, :] = low
                parts.append(dot_f32(low, qkv[t, :, 384 + at : 448 + at]))
            att[t, rows, :] = jnp.concatenate(parts, axis=1).astype(BF)

        row_loop(body, 256)
        tidy.append(link.copy(qkv.at[t], qkv_out.at[t]))
        tidy.append(link.copy(att.at[t], att_out.at[t]))
        tidy.append(link.copy(prob.at[pl.ds(3 * t, 3)], prob_out.at[pl.ds(3 * t, 3)]))

    def out_step():
        def body(rows):
            z = x_row[rows, :].astype(F32) + norm[0:1, :]
            for t in range(4):
                z = z + dot_f32(att[t, rows, :], v_compact[t])
            normed, inverse = normalize(z)
            n_one[rows, :] = normed
            inv[rows, :] = inverse
            h = normed * norm[2:3, :] + norm[3:4, :]
            h_low[rows, :] = h.astype(BF)
            total[rows, :] = h + norm[1:2, :]

        row_loop(body, 256)
        tidy.append(link.copy(n_one, n_one_out))
        tidy.append(link.copy(h_low, h_out))

    def up_step(k):
        loads[1, k].wait()
        t = place.behind[k]

        def body(rows):
            pre = dot_f32(h_low[rows, :], v_up[t]) + small[t, 0:1, 384:1152]
            below = 0.5 + 0.5 * lax.erf(pre * (0.5**0.5))
            act[t, rows, :] = (pre * below).astype(BF)
            slope = below + pre * (jnp.exp(-0.5 * pre * pre) * 0.3989422804014327)
            pull[t, rows, :] = slope.astype(BF)

        row_loop(body, 256)
        tidy.append(link.copy(act.at[t], act_out.at[t]))
        tidy.append(link.copy(pull.at[t], pull_out.at[t]))

    def down_step(k):
        loads[2, k].wait()
        t = place.behind[k]

        def body(rows):
            total[rows, :] += dot_f32(act[t, rows, :], v_down[t])

        row_loop(body, 256)

    def end_step():
        tidy.append(link.copy(total, z_two_out))
        tidy.append(link.copy(inv, inv_out))

    every = range(4)
    others = (1, 2, 3)
    small_state, gy_moves = {}, []

    def small_collect():
        for move in small_moves:
            move.wait_recv()
        small_total[...] = small_mine[...] + small_land[0] + small_land[1] + small_land[2]
        small_state["stay"] = link.copy(small_total, packed.at[place.t])
        small_state["deep"] = [
            link.send(small_total, packed.at[place.t], place.deep[k]) for k in others
        ]

    def small_ready():
        small_state["stay"].wait()
        for move in small_state["deep"]:
            move.wait_recv()
        unpack_small(packed, small)
        norm_vectors(small, norm)
        for t in every:
            bias_qkv[t] = jnp.concatenate(
                [small[t, 0:1, :192], jnp.zeros((1, 192), F32), small[t, 0:1, 192:384]], axis=1
            )
        tidy.append(link.copy(packed, small_out))

    def x_ready():
        x_stay.wait()
        for move in x_moves:
            move.wait_recv()
        places = feature_places()

        def body(rows):
            x_wide[rows, :] = dot_f32(x_row[rows, :], places).astype(BF)

        row_loop(body, 256)
        tidy.append(link.copy(x_wide, x_out))

    def gy_send():
        for k in others:
            gy_moves.append(link.send(gy_in.at[place.ahead[k]], gy_row.at[mine_rows], place.deep[k]))

    def gy_ready():
        for move in gy_moves:
            move.wait_recv()

    deep_send(0)
    small_collect()
    plane_send(0, 0)
    pass_halves()
    plane_pass(0, 0)
    plane_send(0, 1)
    collect_halves()
    spread_ffn()
    deep_send(1)
    plane_send(1, 0)
    plane_send(0, 2)
    plane_pass(0, 1)
    small_ready()
    core_pass(0, 0)
    plane_send(0, 3)
    x_ready()
    core_pass(0, 1)
    plane_pass(0, 2)
    load(0, 0)
    plane_send(1, 1)
    unpack(0)
    load(0, 1)
    plane_pass(0, 3)
    qkv_step(0)
    plane_send(2, 0)
    deep_send(2)
    core_pass(0, 2)
    unpack(1)
    plane_send(1, 2)
    load(0, 2)
    qkv_step(1)
    plane_pass(1, 0)
    core_pass(0, 3)
    plane_send(1, 3)
    attention(1)
    gy_send()
    unpack(2)
    plane_pass(2, 0)
    load(0, 3)
    attention(0)
    qkv_step(2)
    plane_pass(1, 2)
    core_pass(1, 0)
    plane_pass(1, 1)
    unpack(3)
    attention(2)
    plane_send(2, 2)
    qkv_step(3)
    plane_pass(1, 3)
    load(1, 0)
    plane_send(2, 3)
    plane_send(2, 1)
    core_pass(2, 0)
    attention(3)
    core_pass(1, 1)
    out_step()
    load(1, 1)
    core_pass(1, 2)
    load(2, 0)
    core_pass(1, 3)
    up_step(0)
    plane_pass(2, 2)
    load(1, 2)
    load(1, 3)
    plane_pass(2, 3)
    up_step(1)
    plane_pass(2, 1)
    up_step(2)
    core_pass(2, 2)
    gy_ready()
    core_pass(2, 3)
    up_step(3)
    load(2, 2)
    core_pass(2, 1)
    down_step(0)
    load(2, 3)
    down_step(2)
    load(2, 1)
    down_step(3)
    down_step(1)
    end_step()
    for copy in tidy:
        copy.wait()
    link.finish()


def forward_call(master, owners, order_col, labels, flags, x_in, gy_in):
    anywhere = pl.BlockSpec(memory_space=pl.ANY)
    vmem = pl.BlockSpec(memory_space=pltpu.VMEM)
    shape = jax.ShapeDtypeStruct
    outs = [
        ((4, 768, 768), BF),
        ((4, 768, 768), BF),
        ((4, 768, 768), BF),
        ((4, 1024, 576), BF),
        ((4, 192, 768), BF),
        ((8, 896), F32),
        ((4, 8, 384), F32),
        ((512, 1024), BF),
        ((512, 768), BF),
        ((4, 512, 576), BF),
        ((12, 512, 512), BF),
        ((4, 512, 192), BF),
        ((512, 768), F32),
        ((512, 768), BF),
        ((4, 512, 768), BF),
        ((4, 512, 768), BF),
        ((512, 768), F32),
        ((512, 1), F32),
    ]
    scratch = [
        ((8, 896), F32),
        ((896, 8), F32),
        ((8, 512), F32),
        ((512, 8), F32),
        ((2, 192, 2304), BF),
        ((4, 32, 2304), BF),
        ((4, 64, 2304), BF),
        ((3, 32, 2304), BF),
        ((2, 2, 32, 2304), BF),
        ((2, 32, 2304), BF),
        ((2, 32, 2304), BF),
        ((96, 2304), F32),
        ((96, 768), BF),
        ((96, 768), BF),
        ((96, 768), BF),
        ((8, 384), F32),
        ((3, 8, 384), F32),
        ((8, 384), F32),
        ((4, 8, 384), F32),
        ((4, 1, 2304), F32),
        ((8, 768), F32),
        ((4, 1, 576), F32),
        ((4, 768, 768), BF),
        ((4, 1024, 576), BF),
        ((4, 192, 768), BF),
        ((4, 768, 768), BF),
        ((4, 768, 768), BF),
        ((512, 768), BF),
        ((512, 1024), BF),
        ((4, 512, 576), BF),
        ((12, 512, 512), BF),
        ((4, 512, 192), BF),
        ((512, 768), F32),
        ((512, 768), BF),
        ((4, 512, 768), BF),
        ((4, 512, 768), BF),
        ((512, 768), F32),
        ((512, 1), F32),
    ]
    return pl.pallas_call(
        forward_kernel,
        out_shape=[shape(*o) for o in outs],
        in_specs=[vmem] * 5 + [anywhere] * 2,
        out_specs=[anywhere] * len(outs),
        scratch_shapes=[pltpu.VMEM(*s) for s in scratch]
        + [
            pltpu.SemaphoreType.DMA((128,)),
            pltpu.SemaphoreType.DMA((128,)),
            pltpu.SemaphoreType.DMA((64,)),
        ],
        compiler_params=pltpu.CompilerParams(
            collective_id=0, has_side_effects=True, vmem_limit_bytes=60 * MIB
        ),
        name="gather_and_forward",
    )(master, owners, order_col, labels, flags, x_in, gy_in)


def backward_kernel(
    labels,
    flags,
    gy_in,
    z_two_in,
    inv_in,
    small_in,
    act_in,
    pull_in,
    w_down,
    w_up,
    h_in,
    n_one_in,
    att_in,
    w_out,
    qkv_in,
    prob_in,
    w_qkv,
    x_in,
    blocks,
    small_out,
    out_mine,
    dx_mine,
    pool_out,
    *scratch,
):
    sums, cores, lefts, tops, lefts_two, tops_two, deeps = (scratch[3 * i : 3 * i + 3] for i in range(7))
    (
        ring,
        share,
        share_low,
        small_grad,
        small_land,
        packed,
        small,
        norm,
        gy,
        normed,
        inv,
        act,
        pull,
        v_down,
        v_up,
        h_low,
        att,
        v_out,
        qkv,
        prob,
        v_qkv,
        x_row,
        wide,
        low,
        total,
        d_up,
        d_att,
        d_qkv,
        turned,
        go,
        wide_sum,
        reds,
        red_up,
        red_qv,
        flag_col,
        row_low,
        pool,
        send_sems,
        recv_sems,
        local_sems,
    ) = scratch[21:]
    place = Place()
    place.hail()
    link = Sender(send_sems, recv_sems, local_sems)
    t_of = place.ahead
    steps = (1, 2, 3, 0)
    got = {}

    def fetch(name, src, dst):
        got[name] = link.copy(src, dst)

    fetch("small", small_in, packed)
    fetch("normed", z_two_in, normed)
    fetch("gy", gy_in, gy)
    fetch("inv", inv_in, inv)

    def load_ffn(i):
        t, slot = t_of[steps[i]], i % 2
        fetch(("act", i), act_in.at[t], act.at[slot])
        fetch(("down", i), w_down.at[t], v_down.at[slot])
        fetch(("pull", i), pull_in.at[t], pull.at[slot])
        fetch(("up", i), w_up.at[t], v_up.at[slot])

    def load_att(i):
        t, slot = t_of[steps[i]], i % 2
        fetch(("prob", i), prob_in.at[pl.ds(3 * t, 3)], prob.at[slot])
        fetch(("qkv", i), w_qkv.at[t], v_qkv.at[slot])

    own = pl.ds(place.t, 1)
    own_flags = flags[own, :].astype(F32)
    flag_col[...] = jnp.transpose(jnp.broadcast_to(own_flags, (8, 512)))
    t, x, y, c = place.t, place.x, place.y, place.c
    moves, stay = [], []

    core_moves, first, second, third = {}, {}, {}, {}
    ring_open = [None] * 3
    ring_at = [0]

    def chip_row(w, k, yy, xx, half):
        rows = WEIGHTS[w][1]
        at = pl.multiple_of((yy * 2 + xx) * rows + half * (rows // 2), 16)
        return sums[w].at[t_of[k], pl.ds(at, rows // 2)]

    def produce(w, k, make):
        slot = ring_at[0] % 3
        ring_at[0] += 1
        if ring_open[slot] is not None:
            link.sent(ring_open[slot])
        away = ring.at[slot]
        away[...] = make(1 - c).astype(BF)
        move = link.send(away, cores[w].at[k], place.core)
        ring_open[slot] = move
        core_moves[w, k] = move
        sums[w][t_of[k]] = make(c).astype(BF)

    def core_add(w, k):
        core_moves[w, k].wait_recv()
        rows = WEIGHTS[w][1]

        @pl.loop(0, 4)
        def _(i):
            at = pl.ds(pl.multiple_of(i * rows, 32), rows)
            sums[w][t_of[k], at, :] += cores[w][k, at, :]

        first[w, k] = []
        for i in (0, 1):
            first[w, k].append(link.send(chip_row(w, k, i, 1 - x, 0), lefts[w].at[k, i], place.right))
            first[w, k].append(link.send(chip_row(w, k, 1 - y, i, 1), tops[w].at[k, i], place.down))

    def add(spot, other):
        spot[...] = spot[...] + other[...]

    def plane_add(w, k):
        for move in first[w, k]:
            move.wait_recv()
        down_part, right_part = chip_row(w, k, 1 - y, x, 0), chip_row(w, k, y, 1 - x, 1)
        add(down_part, lefts[w].at[k, 1 - y])
        add(right_part, tops[w].at[k, 1 - x])
        second[w, k] = [
            link.send(down_part, lefts_two[w].at[k], place.down),
            link.send(right_part, tops_two[w].at[k], place.right),
        ]
        add(chip_row(w, k, y, x, 0), lefts[w].at[k, y])
        add(chip_row(w, k, y, x, 1), tops[w].at[k, x])

    def deep_add(w, k):
        for move in second[w, k]:
            move.wait_recv()
        add(chip_row(w, k, y, x, 0), lefts_two[w].at[k])
        add(chip_row(w, k, y, x, 1), tops_two[w].at[k])
        rows = WEIGHTS[w][1]
        if k:
            spot = pl.ds(pl.multiple_of(place.xy * rows, 16), rows)
            third[w, k] = link.send(sums[w].at[t_of[k], spot], deeps[w].at[k - 1], place.deep[k])

    def end(w):
        rows = WEIGHTS[w][1]
        spot = pl.ds(pl.multiple_of(place.xy * rows, 16), rows)
        whole = sums[w][t, spot, :].astype(F32)
        for k in (1, 2, 3):
            third[w, k].wait_recv()
            whole = whole + deeps[w][k - 1].astype(F32)
        whole = whole.astype(BF)
        if w == 0:
            for k in range(3):
                share[64:96, 768 * k : 768 * k + 768] = whole[32 * k : 32 * k + 32, :].astype(F32)
        else:
            at = 0 if w == 1 else 32
            parts = dot_tn(interleave(96, 3), whole)
            for k in range(3):
                share[at : at + 32, 768 * k : 768 * k + 768] = parts[32 * k : 32 * k + 32]

    def column_sum(value):
        return jnp.sum(value, axis=0, keepdims=True)

    def norm_two_back():
        def body(rows):
            grad = gy[rows, :].astype(F32) * flag_col[rows, 0:1]
            n, inverse = normalize(normed[rows, :])
            normed[rows, :] = n
            dz = norm_back(grad * norm[4:5, :], n, inverse)
            wide[rows, :] = dz
            total[rows, :] = dz
            low[rows, :] = dz.astype(BF)
            reds[4:5, :] += column_sum(grad * n)
            reds[5:6, :] += column_sum(grad)
            reds[1:2, :] += column_sum(dz)

        row_loop(body)

    def emit_out():
        sentence = lax.broadcasted_iota(jnp.int32, (SMAX, 512), 0).astype(F32)
        member = jnp.where((sentence == labels[own, :].astype(F32)) & (own_flags == 1.0), 1.0, 0.0)
        count = jnp.maximum(jnp.sum(member, axis=1, keepdims=True), 1.0)
        pooled = jnp.zeros((SMAX, 768), F32)
        for i in range(4):
            rows = slice(128 * i, 128 * i + 128)
            out = normed[rows, :] * norm[4:5, :] + norm[5:6, :]
            row_low[rows, :] = out.astype(BF)
            pooled = pooled + jnp.dot(
                member[:, rows], out, precision=exact_precision, preferred_element_type=F32
            )
        pool[...] = pooled / count
        own_rows = pl.ds(pl.multiple_of(t * 128, 128), 128)
        stay.append(link.copy(row_low.at[own_rows], out_mine.at[t]))
        stay.append(link.copy(pool, pool_out.at[t]))
        for k in (1, 2, 3):
            part = row_low.at[pl.ds(pl.multiple_of(t_of[k] * 128, 128), 128)]
            moves.append(link.send(part, out_mine.at[t], place.deep[k]))
            moves.append(link.send(pool, pool_out.at[t], place.deep[k]))

    def lanes(which):
        return pl.ds(pl.multiple_of(which * 384, 128), 384)

    def down_piece(i):
        k, slot = steps[i], i % 2
        got["act", i].wait()
        produce(2, k, lambda which: dot_tn(act[slot, :, lanes(which)], low[...]))

    def act_back(i):
        k, slot = steps[i], i % 2
        got["down", i].wait()
        got["pull", i].wait()

        def body(rows):
            grad = dot_nt(low[rows, :], v_down[slot]) * pull[slot, rows, :].astype(F32)
            red_up[t_of[k]] += column_sum(grad)
            d_up[rows, :] = grad.astype(BF)

        row_loop(body, 256)

    def up_piece(i):
        if i == 0:
            got["h"].wait()
        produce(1, steps[i], lambda which: dot_tn(h_low[:, lanes(which)], d_up[...]))

    def hidden_back(i):
        slot = i % 2
        got["up", i].wait()

        def body(rows):
            total[rows, :] += dot_nt(d_up[rows, :], v_up[slot])

        row_loop(body, 256)
        if i == 1:
            fetch("n_one", n_one_in, normed)

    def norm_one_back():
        got["n_one"].wait()

        def body(rows):
            dh = total[rows, :]
            n = normed[rows, :]
            dz = norm_back(dh * norm[2:3, :], n, inv[rows, :])
            total[rows, :] = dz
            low[rows, :] = dz.astype(BF)
            reds[2:3, :] += column_sum(dh * n)
            reds[3:4, :] += column_sum(dh)
            reds[0:1, :] += column_sum(dz)

        row_loop(body)

    def out_piece(i):
        k = steps[i]
        if i == 0:
            got["att"].wait()
            got["wout"].wait()
        go[...] = dot_tn(att[t_of[k]], low[...]).astype(BF)

        def body(rows):
            d_att[rows, :] = dot_nt(low[rows, :], v_out[t_of[k]]).astype(BF)

        row_loop(body, 256)

    def attention_back(i):
        k, slot = steps[i], i % 2
        tk = t_of[k]
        if i == 0:
            got["qkvs"].wait()
        got["prob", i].wait()
        turned[...] = jnp.zeros_like(turned)

        def body(rows):
            d_queries = []
            for j in range(3):
                at = 64 * j
                grad = d_att[rows, at : at + 64]
                weight_low = prob[slot, j, rows, :]
                weight = weight_low.astype(F32)
                d_prob = dot_nt(grad, qkv[tk, :, 384 + at : 448 + at]) * weight
                inner = jnp.sum(d_prob, axis=1, keepdims=True)
                d_scores = (d_prob - weight * inner).astype(BF)
                d_queries.append(dot_f32(d_scores, qkv[tk, :, 192 + at : 256 + at]))
                turned[at : at + 64, :] += dot_tn(qkv[tk, rows, at : at + 64], d_scores)
                turned[192 + at : 256 + at, :] += dot_tn(grad, weight_low)
            dq = jnp.concatenate(d_queries, axis=1) * 0.125
            red_qv[tk, :, :192] += column_sum(dq)
            d_qkv[rows, :192] = dq.astype(BF)

        row_loop(body, 256)
        dk = jnp.transpose(turned[:192, :]) * 0.125
        dv = jnp.transpose(turned[192:, :])
        red_qv[tk, :, 192:] += column_sum(dv)
        d_qkv[:, 192:] = jnp.concatenate([dk, dv], axis=1).astype(BF)

    def qkv_piece(i):
        k, slot = steps[i], i % 2
        if i == 0:
            got["x"].wait()

        def make(which):
            at = pl.ds(pl.multiple_of(512 * which, 512), 512)
            both = dot_tn(x_row[:, at], d_qkv[...])
            parts = [both[128 * r : 128 * r + 128] for r in range(4)]
            thirds = [
                jnp.concatenate([parts[0], parts[1][:, :192]], axis=1),
                jnp.concatenate([parts[1][:, 192:], parts[2][:, :384]], axis=1),
                jnp.concatenate([parts[2][:, 384:], parts[3]], axis=1),
            ]
            for k3 in range(3):
                thirds[k3] = thirds[k3] + dot_tn(third_to_out(k3, 128 * which, 128), go[...])
            return jnp.concatenate(
                [thirds[k3][32 * d : 32 * d + 32] for d in range(4) for k3 in range(3)], axis=0
            )

        produce(0, k, make)
        got["qkv", i].wait()

        def body(rows):
            wide_sum[rows, :] += dot_nt(d_qkv[rows, :], v_qkv[slot])

        row_loop(body, 256)

    sent, passed, across = {}, {}, {}

    def share_send(lo, hi):
        share_low[lo:hi, :] = share[lo:hi, :].astype(BF)
        mine = c * 4 + place.xy
        rows = pl.ds(lo, hi - lo)
        sent[lo] = (
            link.copy(share_low.at[rows], blocks.at[mine, rows]),
            link.send(share_low.at[rows], blocks.at[mine, rows], place.right),
            link.send(share_low.at[rows], blocks.at[mine, rows], place.down),
        )

    def share_pass(lo, hi):
        half = (hi - lo) // 2
        sent[lo][1].wait_recv()
        sent[lo][2].wait_recv()
        one = blocks.at[c * 4 + place.right[0] // 2, pl.ds(lo, half)]
        two = blocks.at[c * 4 + place.down[0] // 2, pl.ds(lo + half, half)]
        passed[lo] = link.send(one, one, place.down), link.send(two, two, place.right)

    def share_across(lo, hi):
        sent[lo][0].wait()
        passed[lo][0].wait_recv()
        passed[lo][1].wait_recv()
        spot = blocks.at[pl.ds(c * 4, 4), pl.ds(lo, hi - lo)]
        across[lo] = link.send(spot, spot, place.core)

    def share_ready(lo):
        across[lo].wait_recv()

    got["small"].wait()
    unpack_small(packed, small)
    norm_vectors(small, norm)
    reds[...] = jnp.zeros_like(reds)
    red_up[...] = jnp.zeros_like(red_up)
    red_qv[...] = jnp.zeros_like(red_qv)
    small_grad[...] = jnp.zeros_like(small_grad)
    wide_sum[...] = jnp.zeros_like(wide_sum)
    for name in ("normed", "gy", "inv"):
        got[name].wait()
    def load_rest():
        fetch("h", h_in, h_low)
        fetch("att", att_in, att)
        fetch("wout", w_out, v_out)
        fetch("qkvs", qkv_in, qkv)
        fetch("x", x_in, x_row)

    small_state = {}

    def meet():
        place.meet()

    def small_send():
        places = feature_places()

        def dx_body(rows):
            value = wide_sum[rows, :]
            high = value.astype(BF)
            rest = (value - high.astype(F32)).astype(BF)
            back = dot_nt(high, places) + dot_nt(rest, places)
            low[rows, :] = (total[rows, :] + back).astype(BF)

        row_loop(dx_body, 256)
        for q in range(4):
            at = slice(192 * q, 192 * q + 192)
            line = jnp.concatenate(
                [red_qv[q], red_up[q]] + [reds[i : i + 1, at] for i in range(6)], axis=1
            )
            for i in range(6):
                small_grad[q, i : i + 1, :] = line[:, 384 * i : 384 * i + 384]
        small_state["keep"] = link.copy(small_grad.at[t], small_land.at[6])
        small_state["deep"] = [
            link.send(small_grad.at[t_of[k]], small_land.at[k - 1], place.deep[k]) for k in (1, 2, 3)
        ]

    def dx_send():
        own_rows = pl.ds(pl.multiple_of(t * 128, 128), 128)
        stay.append(link.copy(low.at[own_rows], dx_mine.at[t]))
        for k in (1, 2, 3):
            part = low.at[pl.ds(pl.multiple_of(t_of[k] * 128, 128), 128)]
            moves.append(link.send(part, dx_mine.at[t], place.deep[k]))

    def small_core():
        small_state["keep"].wait()
        for move in small_state["deep"]:
            move.wait_recv()
        small_land[7] = small_land[6] + small_land[0] + small_land[1] + small_land[2]
        small_state["core"] = link.send(small_land.at[7], small_land.at[3], place.core)

    def small_right():
        small_state["core"].wait_recv()
        small_land[8] = small_land[7] + small_land[3]
        small_state["right"] = link.send(small_land.at[8], small_land.at[4], place.right)

    def small_down():
        small_state["right"].wait_recv()
        small_land[9] = small_land[8] + small_land[4]
        small_state["down"] = link.send(small_land.at[9], small_land.at[5], place.down)

    def small_end():
        small_state["down"].wait_recv()
        small_out[...] = small_land[9] + small_land[5]

    load_ffn(0)
    norm_two_back()
    meet()
    load_ffn(1)
    down_piece(0)
    load_rest()
    act_back(0)
    load_att(0)
    core_add(2, 1)
    load_att(1)
    up_piece(0)
    emit_out()
    core_add(1, 1)
    hidden_back(0)
    load_ffn(2)
    down_piece(1)
    plane_add(2, 1)
    act_back(1)
    core_add(2, 2)
    up_piece(1)
    hidden_back(1)
    load_ffn(3)
    plane_add(1, 1)
    core_add(1, 2)
    down_piece(2)
    act_back(2)
    plane_add(2, 2)
    core_add(2, 3)
    deep_add(2, 1)
    up_piece(2)
    deep_add(1, 1)
    hidden_back(2)
    down_piece(3)
    core_add(1, 3)
    act_back(3)
    up_piece(3)
    hidden_back(3)
    norm_one_back()
    out_piece(0)
    plane_add(1, 2)
    deep_add(2, 2)
    core_add(1, 0)
    attention_back(0)
    plane_add(1, 3)
    qkv_piece(0)
    deep_add(1, 2)
    plane_add(2, 3)
    load_att(2)
    core_add(0, 1)
    core_add(2, 0)
    out_piece(1)
    attention_back(1)
    deep_add(2, 3)
    deep_add(1, 3)
    qkv_piece(1)
    core_add(0, 2)
    load_att(3)
    plane_add(0, 1)
    out_piece(2)
    plane_add(1, 0)
    attention_back(2)
    qkv_piece(2)
    plane_add(0, 2)
    core_add(0, 3)
    deep_add(0, 1)
    out_piece(3)
    attention_back(3)
    plane_add(2, 0)
    deep_add(0, 2)
    qkv_piece(3)
    plane_add(0, 3)
    core_add(0, 0)
    deep_add(2, 0)
    small_send()
    deep_add(0, 3)
    end(2)
    dx_send()
    plane_add(0, 0)
    deep_add(1, 0)
    end(1)
    share_send(0, 64)
    deep_add(0, 0)
    end(0)
    share_send(64, 96)
    share_pass(0, 64)
    small_core()
    share_pass(64, 96)
    small_right()
    share_across(0, 64)
    small_down()
    share_across(64, 96)
    share_ready(64)
    small_end()
    share_ready(0)
    for move in moves:
        move.wait_recv()
    for copy in stay:
        copy.wait()
    link.finish()


def backward_call(*args):
    anywhere = pl.BlockSpec(memory_space=pl.ANY)
    vmem = pl.BlockSpec(memory_space=pltpu.VMEM)
    shape = jax.ShapeDtypeStruct
    sums = [((4, 4 * rows, cols), BF) for cols, rows in WEIGHTS]
    halves = [((4, 2, rows // 2, cols), BF) for cols, rows in WEIGHTS]
    singles = [((4, rows // 2, cols), BF) for cols, rows in WEIGHTS]
    deeps = [((3, rows, cols), BF) for cols, rows in WEIGHTS]
    rest = [
        ((3, 384, 768), BF),
        ((96, 2304), F32),
        ((96, 2304), BF),
        ((4, 8, 384), F32),
        ((11, 8, 384), F32),
        ((4, 8, 384), F32),
        ((4, 1, 2304), F32),
        ((8, 768), F32),
        ((512, 768), BF),
        ((512, 768), F32),
        ((512, 1), F32),
        ((2, 512, 768), BF),
        ((2, 512, 768), BF),
        ((2, 768, 768), BF),
        ((2, 768, 768), BF),
        ((512, 768), BF),
        ((4, 512, 192), BF),
        ((4, 192, 768), BF),
        ((4, 512, 576), BF),
        ((2, 3, 512, 512), BF),
        ((2, 1024, 576), BF),
        ((512, 1024), BF),
        ((512, 768), F32),
        ((512, 768), BF),
        ((512, 768), F32),
        ((512, 768), BF),
        ((512, 192), BF),
        ((512, 576), BF),
        ((384, 512), F32),
        ((192, 768), BF),
        ((512, 1024), F32),
        ((8, 768), F32),
        ((4, 1, 768), F32),
        ((4, 1, 384), F32),
        ((512, 8), F32),
        ((512, 768), BF),
        ((8, 768), F32),
    ]
    scratch = sums + sums + halves + halves + singles + singles + deeps + rest
    return pl.pallas_call(
        backward_kernel,
        out_shape=[
            shape((8, 96, 2304), BF),
            shape((8, 384), F32),
            shape((4, 128, 768), BF),
            shape((4, 128, 768), BF),
            shape((4, 8, 768), F32),
        ],
        in_specs=[vmem] * 2 + [anywhere] * 16,
        out_specs=[anywhere, vmem, anywhere, anywhere, anywhere],
        scratch_shapes=[pltpu.VMEM(*s) for s in scratch]
        + [
            pltpu.SemaphoreType.DMA((160,)),
            pltpu.SemaphoreType.DMA((160,)),
            pltpu.SemaphoreType.DMA((64,)),
        ],
        compiler_params=pltpu.CompilerParams(
            collective_id=1, has_side_effects=True, vmem_limit_bytes=62 * MIB
        ),
        name="backward_and_reduce",
    )(*args)


def finish_kernel(
    slot_row,
    blocks,
    small,
    pool,
    master,
    first,
    second,
    out_mine,
    dx_mine,
    new_master,
    new_first,
    new_second,
    layer_out,
    input_grad,
    pooled,
    norm_grads,
):
    step = pl.program_id(0)
    rows = master.shape[0]
    t = lax.axis_index("tensor")
    start = lax.axis_index("dp") * (rows * pl.num_programs(0)) + step * rows
    wanted = (lax.broadcasted_iota(jnp.int32, (rows, 1), 0) + start).astype(F32)
    match = slot_row[0:1, :768] == wanted
    gradient = dot_f32(jnp.where(match, 1.0, 0.0).astype(BF), blocks[...])
    is_small = slot_row[0:1, 768:769] == wanted
    small_line = jnp.concatenate([small[i : i + 1, :] for i in range(6)], axis=1)
    gradient = jnp.where(is_small, small_line, gradient)

    at = lax.broadcasted_iota(jnp.int32, (1, 768), 1) % 96
    rates = jnp.where(
        at < 32,
        MODEL_WIDTH ** (-0.5),
        jnp.where(
            at < 64,
            FF ** (-0.5),
            jnp.where(at < 88, MODEL_WIDTH ** (-0.5), 4.0 * MODEL_WIDTH ** (-0.5)),
        ),
    ).astype(F32)
    rate = jnp.sum(jnp.where(match, rates, 0.0), axis=1, keepdims=True)
    filled = (rate > 0.0) | is_small
    offset = lax.broadcasted_iota(jnp.int32, (1, small_line.shape[1]), 1) - 1152
    gain = ((offset >= 384) & (offset < 576)) | ((offset >= 768) & (offset < 960))
    small_rate = jnp.where(gain, 0.2, 0.1).astype(F32)
    step_rate = jnp.where(is_small, small_rate, rate)
    decay_on = jnp.where(is_small, 0.0, 1.0)
    new_master[...], new_first[...], new_second[...] = adamw(
        gradient, first[...], second[...], master[...], step_rate, decay_on, filled
    )
    for src, dst in ((out_mine, layer_out), (dx_mine, input_grad)):
        for row in range(4):
            dst[:, row, :] = src[row].astype(F32)

    @pl.when(step == 0)
    def _():
        total = jnp.zeros((4, 8, 192), F32)
        for q in range(4):
            total = total + jnp.where(t == q, pool[:, :, 192 * q : 192 * q + 192], 0.0)
        pooled[...] = total
        norm_grads[...] = jnp.concatenate(
            [small_line[:, 1152 + 192 * i : 1344 + 192 * i] for i in range(6)], axis=0
        )


def finish_call(slot_row, blocks, small, pool, master, first, second, out_mine, dx_mine):
    steps = 2
    slots, block_len = master.shape
    shape = jax.ShapeDtypeStruct

    def whole(*dims):
        return pl.BlockSpec(dims, lambda i: (0,) * len(dims))

    state = pl.BlockSpec((slots // steps, block_len), lambda i: (i, 0))
    token_in = pl.BlockSpec((4, 128 // steps, 768), lambda i: (0, i, 0))
    token_out = pl.BlockSpec((128 // steps, 4, 768), lambda i: (i, 0, 0))
    return pl.pallas_call(
        finish_kernel,
        grid=(steps,),
        out_shape=[shape((slots, block_len), F32)] * 3
        + [shape((128, 4, 768), F32)] * 2
        + [shape((4, 8, 192), F32), shape((6, 192), F32)],
        in_specs=[whole(8, 896), whole(768, block_len), whole(8, 384), whole(4, 8, 768)]
        + [state] * 3
        + [token_in] * 2,
        out_specs=[state] * 3 + [token_out] * 2 + [whole(4, 8, 192), whole(6, 192)],
        compiler_params=pltpu.CompilerParams(vmem_limit_bytes=62 * MIB),
        name="owners_update",
    )(slot_row, blocks, small, pool, master, first, second, out_mine, dx_mine)


def share_order():
    order = []
    for core in range(2):
        for chip in range(4):
            for base, count in ((0, 32), (256, 32), (512, 24), (704, 8)):
                at = base + (core * 4 + chip) * count
                order += list(range(at, at + count))
    return np.array(order + [768] + [4096] * 127, np.int32)


def local_rows(
    layer_input_rows,
    sentence_index_row,
    padding_mask,
    output_gradient,
    owner_rank,
    master_state,
    first_moment,
    second_moment,
):
    block_len = master_state.shape[2]
    order = share_order()
    (
        _,
        w_up,
        w_down,
        w_qkv,
        w_out,
        slot_row,
        small_all,
        x_row,
        gy_row,
        qkv,
        prob_low,
        attended,
        normed_one,
        h_low,
        act,
        pull,
        z_two,
        inverse,
    ) = forward_call(
        master_state[0],
        owner_rank,
        jnp.asarray(order[:, None]),
        sentence_index_row,
        padding_mask,
        jnp.transpose(layer_input_rows, (1, 0, 2)),
        jnp.transpose(output_gradient, (1, 0, 2)),
    )
    blocks, small_sum, out_mine, dx_mine, pool_all = backward_call(
        sentence_index_row,
        padding_mask,
        gy_row,
        z_two,
        inverse,
        small_all,
        act,
        pull,
        w_down,
        w_up,
        h_low,
        normed_one,
        attended,
        w_out,
        qkv,
        prob_low,
        w_qkv,
        x_row,
    )
    new_master, new_first, new_second, layer_out, input_grad, pooled, norm_grads = finish_call(
        slot_row,
        blocks.reshape(768, block_len),
        small_sum,
        pool_all,
        master_state[0],
        first_moment[0],
        second_moment[0],
        out_mine,
        dx_mine,
    )
    return (
        layer_out,
        pooled,
        input_grad,
        new_master[None],
        new_first[None],
        new_second[None],
        norm_grads,
    )


def solution(mesh):
    in_specs = (
        P("tensor", "dp", None),
        P("dp", None),
        P("dp", None),
        P("tensor", "dp", None),
        P(),
        P("tensor", "dp", None),
        P("tensor", "dp", None),
        P("tensor", "dp", None),
    )
    out_specs = (
        P("tensor", "dp", None),
        P("dp", None, "tensor"),
        P("tensor", "dp", None),
        P("tensor", "dp", None),
        P("tensor", "dp", None),
        P("tensor", "dp", None),
        P(None, "tensor"),
    )
    plain = mesh.shape["dp"] != 8 or mesh.shape["tensor"] != 4
    body = local_general if plain else local_rows
    return jax.shard_map(body, mesh=mesh, in_specs=in_specs, out_specs=out_specs, check_vma=False)
```
